32 devices in a mesh: grp: 2 (over y), src: 4 (over z), tile: 4 (over x, core).
Axes of the slice: x: 2, y: 2, z: 4, core: 2. Of those that a mesh axis runs over, the one named last changes fastest.
Arguments:
- mask: bfloat16 [4096, 2048], P(('grp', 'tile')), parts along dimension 0, may hold values from -1 to 1
- cotangent: bfloat16 [4096, 2048], P(('grp', 'tile')), parts along dimension 0, may hold values from -6 to 6
- pupil_phase: float32 [64, 64], replicated, may hold values from -3.140625 to 3.140625
- source_weight: float32 [12288], replicated, may hold values from 0.2 to 1
- shift_table: int32 [12288, 2], replicated, may hold values from 0 to 64
- source_ids: int32 [8, 8], P(('grp', 'src')), parts along dimension 0, may hold values from 0 to 12287
- source_count: int32 [8], P(('grp', 'src')), parts along dimension 0, may hold values from 1 to 8, as said below
Outputs:
- grad_mask: float32 [8, 512, 2048], P(('grp', 'tile'), 'src'), parts along dimension 0
The draws below stay inside these ranges and needn't reach their ends.
There are 2 independent parts, one for each index of `grp`. The reference program is written for one: setup_inputs(seed, part) draws one part's arguments, and reference() takes and returns one part's arrays. A program takes and returns all parts, laid end to end along the dimension named above; an argument that names none is the same for every part. Nothing has to cross between parts.
Inputs may be any that keep to these rules, and one draw needn't show every extreme that they name: `source_count`: every src index has at least one used slot, and in every draw some src index uses all 8 slots.
All inputs are finite; a program needn't handle non-finite values.
Results may differ from the reference program's by a relative error of at most 0.008.
Values sent between devices are 32-bit elements; how exact they have to be, the bound alone decides.
No kernel may reach another device: no remote copies, remote signals or barrier semaphores. Data moves between devices by JAX's collectives and lax.ppermute only.
A program may use at most 64 MiB of HBM per device.

```python
import math
import jax
import jax.numpy as jnp
from jax import lax

COLS = 2048
TILE_ROWS = 2048
BAND = 128
PUPIL = 64
CAND = 12288
SLOTS = 8
ROWS_DEV = 512
N_SRC = 4
N_TILE = 4


def draw_source_count(key, part):
    key = jax.random.fold_in(key, 7)
    first_key, second_key, third_key = jax.random.split(key, 3)
    first = jax.random.randint(first_key, (N_SRC,), 1, SLOTS + 1)
    second = jax.random.randint(second_key, (N_SRC,), 1, SLOTS + 1)
    counts = (first * second + SLOTS - 1) // SLOTS
    busiest = jax.random.randint(third_key, (), 0, N_SRC)
    counts = jnp.where(jnp.arange(N_SRC) == busiest, SLOTS, counts)
    return counts.astype(jnp.int32)


def with_ends(values, rng, smallest, top_value):
    dims = values.shape
    index_at = [jax.random.randint(jax.random.fold_in(rng, axis), (), 0, dims[axis]) for axis in range(len(dims))]
    values = values.at[tuple(index_at)].set(smallest)
    longest = dims.index(max(dims))
    index_at[longest] = (index_at[longest] + 1) % dims[longest]
    return values.at[tuple(index_at)].set(top_value)


def steps_of(key, shape, cuts, least, high):
    factor_of, own = 1.0, jax.random.fold_in(key, 6)
    for dim, blocks in cuts:
        heights = jnp.exp(jax.random.uniform(jax.random.fold_in(own, dim), (blocks,), jnp.float32, least / len(cuts), high / len(cuts)))
        factor_of = factor_of * jnp.repeat(heights, shape[dim] // blocks).reshape([-1 if axis == dim else 1 for axis in range(len(shape))])
    return factor_of


def bell_draw(rng, dims, scale, limit, cuts=(), held_as=jnp.bfloat16):
    gain = steps_of(rng, dims, cuts, -0.22, 0.18) if cuts else 1.0
    array = jax.random.normal(rng, dims, jnp.float32) * scale * gain
    return jnp.minimum(jnp.maximum(array, -limit), limit).astype(held_as)


def setup_inputs(seed: int = 0, part: int = 0) -> dict:
    key_of = jax.random.split(jax.random.key(seed), 8)
    own_keys = jax.random.split(jax.random.fold_in(key_of[7], part), 8)
    return {
        "mask": jnp.clip(jax.random.uniform(own_keys[0], (TILE_ROWS, COLS), jnp.float32, -1.0, 1.0) * steps_of(own_keys[0], (TILE_ROWS, COLS), ((0, 4),), -0.4, 0.0), -1.0, 1.0).astype(jnp.bfloat16),
        "cotangent": bell_draw(own_keys[1], (TILE_ROWS, COLS), 1.0, 6.0, ((0, 4),)),
        "pupil_phase": jnp.clip(jax.random.uniform(key_of[2], (PUPIL, PUPIL), jnp.float32, -3.140625, 3.140625), -3.140625, 3.140625),
        "source_weight": jnp.clip(jnp.exp(jax.random.uniform(key_of[3], (CAND,), jnp.float32, math.log(0.2), math.log(1.0))), 0.2, 1.0),
        "shift_table": with_ends(jax.random.randint(key_of[4], (CAND, 2), 0, BAND - PUPIL + 1), jax.random.fold_in(key_of[4], 1), 0, BAND - PUPIL).astype(jnp.int32),
        "source_ids": with_ends(jax.random.randint(own_keys[5], (N_SRC, SLOTS), 0, CAND), jax.random.fold_in(own_keys[5], 1), 0, CAND - 1).astype(jnp.int32),
        "source_count": draw_source_count(jax.random.fold_in(jax.random.fold_in(key_of[7], part), 71), part),
    }


def angles(positions, freqs, length):
    product = positions[:, None] * freqs[None, :] % length
    return product.astype(jnp.float32) * (2.0 * math.pi / length)

def centered(count):
    return jnp.arange(count, dtype=jnp.int32) - count // 2

def contract_rows(left, right):
    return lax.dot_general(left, right, (((0,), (0,)), ((), ())), precision=lax.Precision.HIGHEST, preferred_element_type=jnp.float32)

def reference(mask, cotangent, pupil_phase, source_weight, shift_table, source_ids, source_count):
    scale = 1.0 / math.sqrt(TILE_ROWS * COLS)
    row_positions = jnp.arange(TILE_ROWS, dtype=jnp.int32)
    col_positions = jnp.arange(COLS, dtype=jnp.int32)
    column_angle = angles(col_positions, centered(BAND), COLS)
    column_cos = jnp.cos(column_angle)
    column_sin = jnp.sin(column_angle)
    forward_cols = jnp.concatenate([column_cos, -column_sin], 1).astype(jnp.bfloat16)
    row_angle = angles(row_positions, centered(BAND), TILE_ROWS)
    forward_rows = jnp.concatenate([jnp.cos(row_angle), jnp.sin(row_angle)], 1).astype(jnp.bfloat16)
    column_part = jnp.dot(mask, forward_cols, preferred_element_type=jnp.float32).astype(jnp.bfloat16)
    blocks = lax.dot_general(forward_rows, column_part, (((0,), (0,)), ((), ())), preferred_element_type=jnp.float32)
    spectrum = jnp.stack([blocks[:BAND, :BAND] + blocks[BAND:, BAND:], blocks[:BAND, BAND:] - blocks[BAND:, :BAND]]) * scale
    spectrum = spectrum.astype(jnp.bfloat16)
    grid_u = jnp.arange(PUPIL, dtype=jnp.int32)
    radius = (2 * grid_u[:, None] - PUPIL + 1) ** 2 + (2 * grid_u[None, :] - PUPIL + 1) ** 2
    inside = radius <= PUPIL * PUPIL
    pupil_real = jnp.where(inside, jnp.cos(pupil_phase), 0.0).astype(jnp.float32)
    pupil_imag = jnp.where(inside, jnp.sin(pupil_phase), 0.0).astype(jnp.float32)
    pupil_angle = angles(col_positions, centered(PUPIL), COLS)
    pupil_cols = jnp.concatenate([jnp.cos(pupil_angle).T, jnp.sin(pupil_angle).T], 0).astype(jnp.bfloat16)
    image_angle = angles(row_positions, centered(PUPIL), TILE_ROWS)
    image_cos = jnp.cos(image_angle)
    image_sin = jnp.sin(image_angle)
    image_rows = jnp.concatenate([jnp.concatenate([image_cos, -image_sin], 1), jnp.concatenate([image_sin, image_cos], 1)], 0).astype(jnp.bfloat16)
    flat_ids = source_ids.reshape(-1).astype(jnp.int32)
    valid = (jnp.arange(SLOTS, dtype=jnp.int32)[None, :] < source_count[:, None]).reshape(-1).astype(jnp.float32)

    def contribution(totals, item):
        source, keep = item
        offset_x = shift_table[source, 0].astype(jnp.int32)
        offset_y = shift_table[source, 1].astype(jnp.int32)
        start = (jnp.int32(0), offset_y, offset_x)
        window = lax.dynamic_slice(spectrum, start, (2, PUPIL, PUPIL)).astype(jnp.float32)
        amp_real = pupil_real * window[0] - pupil_imag * window[1]
        amp_imag = pupil_real * window[1] + pupil_imag * window[0]
        amplitude = jnp.concatenate([jnp.concatenate([amp_real, -amp_imag], 1), jnp.concatenate([amp_imag, amp_real], 1)], 0).astype(jnp.bfloat16)
        halfway = jnp.dot(amplitude, pupil_cols, preferred_element_type=jnp.float32).astype(jnp.bfloat16)
        field = jnp.dot(image_rows, halfway, preferred_element_type=jnp.float32) * (1.0 / PUPIL)
        factor = 2.0 / SLOTS * (source_weight[source] * keep)
        field_grad = (field.reshape(2, TILE_ROWS, COLS) * factor * cotangent[None]).astype(jnp.bfloat16).reshape(2 * TILE_ROWS, COLS)
        back = lax.dot_general(field_grad, pupil_cols, (((1,), (1,)), ((), ())), preferred_element_type=jnp.float32)
        back_real = back[:TILE_ROWS, :PUPIL] + back[TILE_ROWS:, PUPIL:]
        back_imag = back[TILE_ROWS:, :PUPIL] - back[:TILE_ROWS, PUPIL:]
        grad_real = (contract_rows(image_cos, back_real) + contract_rows(image_sin, back_imag)) / PUPIL
        grad_imag = (contract_rows(image_cos, back_imag) - contract_rows(image_sin, back_real)) / PUPIL
        spec_real = pupil_real * grad_real + pupil_imag * grad_imag
        spec_imag = pupil_real * grad_imag - pupil_imag * grad_real
        current = lax.dynamic_slice(totals, start, (2, PUPIL, PUPIL))
        return (lax.dynamic_update_slice(totals, current + jnp.stack([spec_real, spec_imag]), start), None)
    band_grad, unused = lax.scan(contribution, jnp.zeros((2, BAND, BAND), jnp.float32), (flat_ids, valid))
    left_side = jnp.concatenate([jnp.concatenate([band_grad[0], -band_grad[1]], 1), jnp.concatenate([band_grad[1], band_grad[0]], 1)], 0)
    back_cols = jnp.concatenate([column_cos, column_sin], 1)
    spread = lax.dot_general(left_side, back_cols, (((1,), (1,)), ((), ())), precision=lax.Precision.HIGHEST, preferred_element_type=jnp.float32)
    row_side = jnp.concatenate([jnp.cos(row_angle), -jnp.sin(row_angle)], 1)
    result = jnp.dot(row_side, spread, precision=lax.Precision.HIGHEST, preferred_element_type=jnp.float32) * scale
    return result.reshape(N_TILE, ROWS_DEV, COLS)
```

```python
import functools
import math

import jax
import jax.numpy as jnp
import ml_dtypes
import numpy as np
from jax import lax
from jax.experimental import pallas as pl
from jax.experimental.pallas import tpu as pltpu
from jax.sharding import PartitionSpec as P

COLS = 2048
TILE_ROWS = 2048
BAND = 128
PUPIL = 64
SLOTS = 8
GRID = 128
CHUNKS = 4
GROUP = 4
OX, OY, WEIGHT, USED = range(4)

VMEM = pl.BlockSpec(memory_space=pltpu.VMEM)
SMEM = pl.BlockSpec(memory_space=pltpu.SMEM)
ANY = pl.BlockSpec(memory_space=pl.ANY)


def waves(positions, freqs, length):
    product = np.multiply.outer(positions, freqs) % length
    angle = product.astype(np.float64) * (2.0 * math.pi / length)
    return np.cos(angle), np.sin(angle)


def lowpass(positions, length):
    freqs = np.arange(1, PUPIL)
    step = length // GRID
    apart = np.arange(GRID)[None, :] * step - positions[:, None]
    product = (apart[:, :, None] * freqs) % length
    return (1.0 + 2.0 * np.cos(product * (2.0 * math.pi / length)).sum(2)) / GRID


def low(array):
    return np.ascontiguousarray(array).astype(ml_dtypes.bfloat16)


@functools.cache
def image_tables(columns, height, n_tile, n_src):
    band = np.arange(BAND) - BAND // 2
    cols = np.arange(columns)
    rows = np.arange(TILE_ROWS)
    cos, sin = waves(cols, band, columns)
    col_table = low(np.concatenate([cos, -sin, lowpass(cols, columns)], 1))
    cos, sin = waves(rows, band, TILE_ROWS)
    row_table = np.concatenate([cos, sin, lowpass(rows, TILE_ROWS)], 1)
    row_table = low(row_table.reshape(n_tile, height, 2 * BAND + GRID).transpose(0, 2, 1))
    portion = height // n_src
    out_table = np.concatenate([cos, -sin], 1).astype(np.float32)
    return col_table, row_table, out_table.reshape(n_tile * n_src, portion, 2 * BAND)


@functools.cache
def grid_tables():
    points = np.arange(GRID)
    cos, sin = waves(points, np.arange(BAND) - BAND // 2, GRID)
    cols_in = np.block([[cos.T, sin.T], [-sin.T, cos.T]])
    cols_out = np.block([[cos, -sin], [sin, cos]])
    cos, sin = waves(points, np.arange(PUPIL) - PUPIL // 2, GRID)
    rows_in = np.block([[cos, -sin], [sin, cos]])
    rows_out = np.block([[cos.T, sin.T], [-sin.T, cos.T]])
    return low(cols_in), low(rows_in), low(rows_out), low(cols_out)


def dot(left, right):
    return jnp.dot(left, right, preferred_element_type=jnp.float32)


def forward_kernel(
    ids, count, mask, cotangent, phase, weight, shift, col_table, row_table,
    partial, pupil, slots,
    mask_v, cot_v, col_v, row_v, shift_v, weight_v, sems,
):
    height, columns = mask.shape
    width = columns // CHUNKS
    tile = lax.axis_index("tile")
    chunk_copies = []
    for step in range(CHUNKS):
        part = pl.ds(step * width, width)
        copies = [
            pltpu.make_async_copy(col_table.at[part, :], col_v.at[part, :], sems.at[step, 0]),
            pltpu.make_async_copy(mask.at[:, part], mask_v.at[step], sems.at[step, 1]),
            pltpu.make_async_copy(cotangent.at[:, part], cot_v.at[step], sems.at[step, 2]),
        ]
        for copy in copies:
            copy.start()
        chunk_copies.append(copies)
    row_copy = pltpu.make_async_copy(row_table.at[tile], row_v, sems.at[CHUNKS, 0])
    row_copy.start()
    shift_copy = pltpu.make_async_copy(shift, shift_v, sems.at[CHUNKS, 1])
    shift_copy.start()
    weight_copy = pltpu.make_async_copy(weight, weight_v, sems.at[CHUNKS, 2])
    weight_copy.start()

    grid_u = lax.broadcasted_iota(jnp.int32, (PUPIL, PUPIL), 0)
    grid_v = lax.broadcasted_iota(jnp.int32, (PUPIL, PUPIL), 1)
    radius = (2 * grid_u - PUPIL + 1) ** 2 + (2 * grid_v - PUPIL + 1) ** 2
    inside = radius <= PUPIL * PUPIL
    rest = jnp.zeros((PUPIL, BAND - PUPIL), jnp.float32)
    pupil[:PUPIL, :] = jnp.concatenate([jnp.where(inside, jnp.cos(phase[...]), 0.0), rest], 1)
    pupil[PUPIL:, :] = jnp.concatenate([jnp.where(inside, jnp.sin(phase[...]), 0.0), rest], 1)

    for step in range(CHUNKS):
        for copy in chunk_copies[step]:
            copy.wait()
        part = pl.ds(step * width, width)
        mask_add = dot(mask_v[step], col_v[part, : 2 * BAND])
        cot_add = dot(cot_v[step], col_v[part, 2 * BAND :])
        mask_part = mask_add if step == 0 else mask_part + mask_add
        cot_part = cot_add if step == 0 else cot_part + cot_add

    row_copy.wait()
    blocks = dot(row_v[: 2 * BAND, :], mask_part.astype(jnp.bfloat16))
    partial[:BAND, :] = blocks[:BAND, :BAND] + blocks[BAND:, BAND:]
    partial[BAND : 2 * BAND, :] = blocks[:BAND, BAND:] - blocks[BAND:, :BAND]
    partial[2 * BAND :, :] = dot(row_v[2 * BAND :, :], cot_part.astype(jnp.bfloat16))

    shift_copy.wait()
    weight_copy.wait()
    lane = lax.broadcasted_iota(jnp.int32, (1, 128), 1)
    lines = []
    for slot in range(SLOTS):
        source = ids[0, slot]
        start = pl.multiple_of(source // 128 * 128, 128)
        here = lane == source % 128
        found = []
        for line in (shift_v[0:1, pl.ds(start, 128)], shift_v[1:2, pl.ds(start, 128)]):
            found.append(jnp.sum(jnp.where(here, line.astype(jnp.float32), 0.0), 1, keepdims=True))
        line = weight_v[pl.ds(source // 128, 1), :]
        found.append(jnp.sum(jnp.where(here, line, 0.0), 1, keepdims=True))
        used = jnp.where(slot < count[0], 1.0, 0.0)
        row = jnp.where(lane == OX, found[0], 0.0) + jnp.where(lane == OY, found[1], 0.0)
        row += jnp.where(lane == WEIGHT, found[2] * used, 0.0) + jnp.where(lane == USED, used, 0.0)
        lines.append(row)
    slots[...] = jnp.concatenate(lines, 0)


def forward(ids, count, mask, cotangent, phase, weight, shift, col_table, row_table):
    height, columns = mask.shape
    width = columns // CHUNKS
    lines = 2 * BAND + GRID
    return pl.pallas_call(
        forward_kernel,
        out_shape=(
            jax.ShapeDtypeStruct((lines, BAND), jnp.float32),
            jax.ShapeDtypeStruct((2 * PUPIL, BAND), jnp.float32),
            jax.ShapeDtypeStruct((SLOTS, 128), jnp.float32),
        ),
        in_specs=[SMEM, SMEM, ANY, ANY, VMEM, ANY, ANY, ANY, ANY],
        out_specs=(VMEM, VMEM, VMEM),
        scratch_shapes=[
            pltpu.VMEM((CHUNKS, height, width), jnp.bfloat16),
            pltpu.VMEM((CHUNKS, height, width), jnp.bfloat16),
            pltpu.VMEM(col_table.shape, jnp.bfloat16),
            pltpu.VMEM(row_table.shape[1:], jnp.bfloat16),
            pltpu.VMEM(shift.shape, jnp.int32),
            pltpu.VMEM(weight.shape, jnp.float32),
            pltpu.SemaphoreType.DMA((CHUNKS + 1, 3)),
        ],
        compiler_params=pltpu.CompilerParams(vmem_limit_bytes=32 * 1024 * 1024),
        cost_estimate=pl.CostEstimate(
            flops=2 * height * columns * lines, bytes_accessed=6 * 1024 * 1024, transcendentals=0
        ),
        name="forward",
    )(ids, count, mask, cotangent, phase, weight, shift, col_table, row_table)


def adjoint_kernel(n_src, n_tile, *refs):
    own, other = refs[:2]
    infos = refs[2 : 2 + n_src]
    (
        pupil, cols_in, rows_in, rows_out, cols_out, col_table, out_table,
        result,
        spec, image, band, col_v, out_v, list_x, list_y, list_w, sems,
    ) = refs[2 + n_src :]
    place = lax.axis_index("tile") * n_src + lax.axis_index("src")
    col_copy = pltpu.make_async_copy(col_table.at[:, pl.ds(0, 2 * BAND)], col_v, sems.at[0])
    col_copy.start()
    out_copy = pltpu.make_async_copy(out_table.at[place], out_v, sems.at[1])
    out_copy.start()

    scale = 1.0 / math.sqrt(TILE_ROWS * COLS)
    whole = own[...] + other[...]
    spec[...] = (whole[: 2 * BAND] * scale).astype(jnp.bfloat16).astype(jnp.float32)
    image[:GRID, :] = whole[2 * BAND :]
    image[GRID:, :] = whole[2 * BAND :]
    band[...] = jnp.zeros_like(band)

    total = jnp.int32(0)
    for info in infos:
        for slot in range(SLOTS):
            list_x[total] = info[slot, OX].astype(jnp.int32)
            list_y[total] = info[slot, OY].astype(jnp.int32)
            list_w[total] = info[slot, WEIGHT] * (2.0 / SLOTS / PUPIL / PUPIL)
            total = total + info[slot, USED].astype(jnp.int32)
    for slot in range(GROUP):
        list_x[total + slot] = jnp.int32(0)
        list_y[total + slot] = jnp.int32(0)
        list_w[total + slot] = jnp.float32(0.0)

    def group(step, carry):
        offsets, pupils, amplitudes = [], [], []
        for slot in range(GROUP):
            index = step * GROUP + slot
            offset_x, offset_y = list_x[index], list_y[index]
            real = pltpu.roll(pupil[:PUPIL, :], offset_x, 1)
            imag = pltpu.roll(pupil[PUPIL:, :], offset_x, 1)
            spec_real = spec[pl.ds(offset_y, PUPIL), :]
            spec_imag = spec[pl.ds(BAND + offset_y, PUPIL), :]
            amp_real = real * spec_real - imag * spec_imag
            amp_imag = real * spec_imag + imag * spec_real
            offsets.append(offset_y)
            pupils.append((real, imag, list_w[index]))
            amplitudes.append(jnp.concatenate([amp_real, amp_imag], 1).astype(jnp.bfloat16))
        halfway = dot(jnp.concatenate(amplitudes, 0), cols_in[...]).astype(jnp.bfloat16)
        halfway = jnp.concatenate(
            [
                jnp.concatenate(
                    [
                        halfway[slot * PUPIL : (slot + 1) * PUPIL, :GRID],
                        halfway[slot * PUPIL : (slot + 1) * PUPIL, GRID:],
                    ],
                    0,
                )
                for slot in range(GROUP)
            ],
            1,
        )
        field = dot(rows_in[...], halfway)
        field_grad = jnp.concatenate(
            [
                (field[:, slot * GRID : (slot + 1) * GRID] * image[...]).astype(jnp.bfloat16)
                for slot in range(GROUP)
            ],
            1,
        )
        back = dot(rows_out[...], field_grad).astype(jnp.bfloat16)
        back = jnp.concatenate(
            [
                jnp.concatenate(
                    [
                        back[:PUPIL, slot * GRID : (slot + 1) * GRID],
                        back[PUPIL:, slot * GRID : (slot + 1) * GRID],
                    ],
                    1,
                )
                for slot in range(GROUP)
            ],
            0,
        )
        grad = dot(back, cols_out[...])
        for slot in range(GROUP):
            real, imag, factor = pupils[slot]
            grad_real = grad[slot * PUPIL : (slot + 1) * PUPIL, :BAND] * factor
            grad_imag = grad[slot * PUPIL : (slot + 1) * PUPIL, BAND:] * factor
            rows = pl.ds(offsets[slot], PUPIL)
            band[rows, :] = band[rows, :] + (real * grad_real + imag * grad_imag)
            rows = pl.ds(BAND + offsets[slot], PUPIL)
            band[rows, :] = band[rows, :] + (real * grad_imag - imag * grad_real)
        return carry

    lax.fori_loop(0, (total + GROUP - 1) // GROUP, group, jnp.int32(0))

    col_copy.wait()
    out_copy.wait()
    real = band[:BAND, :] * scale
    imag = band[BAND:, :] * scale
    left = jnp.concatenate(
        [jnp.concatenate([real, imag], 1), jnp.concatenate([imag, -real], 1)], 0
    ).astype(jnp.bfloat16)
    mixed = dot(out_v[...].astype(jnp.bfloat16), left).astype(jnp.bfloat16)
    result[0] = lax.dot_general(
        mixed, col_v[...], (((1,), (1,)), ((), ())), preferred_element_type=jnp.float32
    )


def adjoint(own, other, infos, pupil, tables, col_table, out_table, n_tile):
    n_src = len(infos)
    portion = out_table.shape[1]
    columns = col_table.shape[0]
    places = n_src * SLOTS + GROUP
    return pl.pallas_call(
        functools.partial(adjoint_kernel, n_src, n_tile),
        out_shape=jax.ShapeDtypeStruct((1, portion, columns), jnp.float32),
        in_specs=[VMEM, VMEM] + [SMEM] * n_src + [VMEM] * 5 + [ANY, ANY],
        out_specs=VMEM,
        scratch_shapes=[
            pltpu.VMEM((2 * BAND, BAND), jnp.float32),
            pltpu.VMEM((2 * GRID, GRID), jnp.float32),
            pltpu.VMEM((2 * BAND, BAND), jnp.float32),
            pltpu.VMEM((columns, 2 * BAND), jnp.bfloat16),
            pltpu.VMEM(out_table.shape[1:], jnp.float32),
            pltpu.SMEM((places,), jnp.int32),
            pltpu.SMEM((places,), jnp.int32),
            pltpu.SMEM((places,), jnp.float32),
            pltpu.SemaphoreType.DMA((2,)),
        ],
        compiler_params=pltpu.CompilerParams(vmem_limit_bytes=32 * 1024 * 1024),
        cost_estimate=pl.CostEstimate(
            flops=2 * 128 * 4096 * 256, bytes_accessed=4 * 1024 * 1024, transcendentals=0
        ),
        name="adjoint",
    )(own, other, *infos, pupil, *tables, col_table, out_table)


def body(mask, cotangent, pupil_phase, source_weight, shift_table, source_ids, source_count):
    height, columns = mask.shape
    n_tile, n_src = lax.axis_size("tile"), lax.axis_size("src")
    col_table, row_table, out_table = image_tables(columns, height, n_tile, n_src)
    partial, pupil, slots = forward(
        source_ids,
        source_count,
        mask,
        cotangent,
        pupil_phase,
        source_weight.reshape(-1, 128),
        shift_table.T,
        col_table,
        row_table,
    )
    infos = [slots]
    for step in range(1, n_src):
        turn = [(place, (place + step) % n_src) for place in range(n_src)]
        infos.append(lax.ppermute(slots, "src", turn))
    other = jnp.zeros_like(partial)
    if n_tile & (n_tile - 1):
        partial = lax.psum(partial, "tile")
    else:
        step = 1
        while step < n_tile:
            partial = partial + other if step > 1 else partial
            swap = [(place, place ^ step) for place in range(n_tile)]
            other = lax.ppermute(partial, "tile", swap)
            step *= 2
    return adjoint(
        partial, other, infos, pupil, grid_tables(), col_table, out_table, n_tile
    )


def solution(mesh):
    placed = (
        P(("grp", "tile"), None),
        P(("grp", "tile"), None),
        P(),
        P(),
        P(),
        P(("grp", "src"), None),
        P(("grp", "src")),
    )
    return jax.shard_map(
        body, mesh=mesh, in_specs=placed, out_specs=P(("grp", "tile"), "src", None), check_vma=False
    )
```

```python
import functools
import math

import jax
import jax.numpy as jnp
import ml_dtypes
import numpy as np
from jax import lax
from jax.experimental import pallas as pl
from jax.experimental.pallas import tpu as pltpu
from jax.sharding import PartitionSpec as P

COLS = 2048
TILE_ROWS = 2048
BAND = 128
PUPIL = 64
SLOTS = 8
GRID = 128
CHUNKS = 4
GROUP = 4
OX, OY, TOTAL = range(3)

VMEM = pl.BlockSpec(memory_space=pltpu.VMEM)
SMEM = pl.BlockSpec(memory_space=pltpu.SMEM)
HBM = pl.BlockSpec(memory_space=pltpu.HBM)


def waves(positions, freqs, length):
    product = np.multiply.outer(positions, freqs) % length
    angle = product.astype(np.float64) * (2.0 * math.pi / length)
    return np.cos(angle), np.sin(angle)


def lowpass(positions, length):
    freqs = np.arange(1, PUPIL)
    step = length // GRID
    apart = np.arange(GRID)[None, :] * step - positions[:, None]
    product = (apart[:, :, None] * freqs) % length
    return (1.0 + 2.0 * np.cos(product * (2.0 * math.pi / length)).sum(2)) / GRID


def low(array):
    return np.ascontiguousarray(array).astype(ml_dtypes.bfloat16)


@functools.cache
def image_tables(columns, height, n_tile, n_src):
    band = np.arange(BAND) - BAND // 2
    cols = np.arange(columns)
    rows = np.arange(TILE_ROWS)
    cos, sin = waves(cols, band, columns)
    col_table = low(np.concatenate([cos, -sin, lowpass(cols, columns)], 1))
    cos, sin = waves(rows, band, TILE_ROWS)
    row_table = np.concatenate([cos, sin, lowpass(rows, TILE_ROWS)], 1)
    row_table = low(row_table.reshape(n_tile, height, 2 * BAND + GRID).transpose(0, 2, 1))
    portion = height // n_src
    out_table = np.concatenate([cos, -sin], 1).astype(np.float32)
    return col_table, row_table, out_table.reshape(n_tile * n_src, portion, 2 * BAND)


@functools.cache
def grid_tables():
    points = np.arange(GRID)
    cos, sin = waves(points, np.arange(BAND) - BAND // 2, GRID)
    cols_in = np.block([[cos.T, sin.T], [-sin.T, cos.T]])
    cols_out = np.block([[cos, -sin], [sin, cos]])
    cos, sin = waves(points, np.arange(PUPIL) - PUPIL // 2, GRID)
    rows_in = np.block([[cos, -sin], [sin, cos]])
    rows_out = np.block([[cos.T, sin.T], [-sin.T, cos.T]])
    return low(cols_in), low(rows_in), low(rows_out), low(cols_out)


def dot(left, right):
    return jnp.dot(left, right, preferred_element_type=jnp.float32)


def forward_kernel(
    mask, cotangent, phase, col_table, row_table,
    partial, pupil,
    mask_v, cot_v, col_v, row_v, sems,
):
    height, columns = mask.shape
    width = columns // CHUNKS
    tile = lax.axis_index("tile")
    chunk_copies = []
    for step in range(CHUNKS):
        part = pl.ds(step * width, width)
        copies = [
            pltpu.make_async_copy(col_table.at[part, :], col_v.at[part, :], sems.at[step, 0]),
            pltpu.make_async_copy(mask.at[:, part], mask_v.at[step], sems.at[step, 1]),
            pltpu.make_async_copy(cotangent.at[:, part], cot_v.at[step], sems.at[step, 2]),
        ]
        for copy in copies:
            copy.start()
        chunk_copies.append(copies)
    row_copy = pltpu.make_async_copy(row_table.at[tile], row_v, sems.at[CHUNKS, 0])
    row_copy.start()

    grid_u = lax.broadcasted_iota(jnp.int32, (PUPIL, PUPIL), 0)
    grid_v = lax.broadcasted_iota(jnp.int32, (PUPIL, PUPIL), 1)
    radius = (2 * grid_u - PUPIL + 1) ** 2 + (2 * grid_v - PUPIL + 1) ** 2
    inside = radius <= PUPIL * PUPIL
    rest = jnp.zeros((PUPIL, BAND - PUPIL), jnp.float32)
    pupil[:PUPIL, :] = jnp.concatenate([jnp.where(inside, jnp.cos(phase[...]), 0.0), rest], 1)
    pupil[PUPIL:, :] = jnp.concatenate([jnp.where(inside, jnp.sin(phase[...]), 0.0), rest], 1)

    for step in range(CHUNKS):
        for copy in chunk_copies[step]:
            copy.wait()
        part = pl.ds(step * width, width)
        mask_add = dot(mask_v[step], col_v[part, : 2 * BAND])
        cot_add = dot(cot_v[step], col_v[part, 2 * BAND :])
        mask_part = mask_add if step == 0 else mask_part + mask_add
        cot_part = cot_add if step == 0 else cot_part + cot_add

    row_copy.wait()
    blocks = dot(row_v[: 2 * BAND, :], mask_part.astype(jnp.bfloat16))
    partial[:BAND, :] = blocks[:BAND, :BAND] + blocks[BAND:, BAND:]
    partial[BAND : 2 * BAND, :] = blocks[:BAND, BAND:] - blocks[BAND:, :BAND]
    partial[2 * BAND :, :] = dot(row_v[2 * BAND :, :], cot_part.astype(jnp.bfloat16))


def forward(mask, cotangent, phase, col_table, row_table):
    height, columns = mask.shape
    width = columns // CHUNKS
    lines = 2 * BAND + GRID
    return pl.pallas_call(
        forward_kernel,
        out_shape=(
            jax.ShapeDtypeStruct((lines, BAND), jnp.float32),
            jax.ShapeDtypeStruct((2 * PUPIL, BAND), jnp.float32),
        ),
        in_specs=[HBM, HBM, VMEM, HBM, HBM],
        out_specs=(VMEM, VMEM),
        scratch_shapes=[
            pltpu.VMEM((CHUNKS, height, width), jnp.bfloat16),
            pltpu.VMEM((CHUNKS, height, width), jnp.bfloat16),
            pltpu.VMEM(col_table.shape, jnp.bfloat16),
            pltpu.VMEM(row_table.shape[1:], jnp.bfloat16),
            pltpu.SemaphoreType.DMA((CHUNKS + 1, 3)),
        ],
        compiler_params=pltpu.CompilerParams(vmem_limit_bytes=62 * 1024 * 1024),
        cost_estimate=pl.CostEstimate(
            flops=2 * height * columns * lines, bytes_accessed=6 * 1024 * 1024, transcendentals=0
        ),
        name="forward",
    )(mask, cotangent, phase, col_table, row_table)


def list_kernel(ids, shift, weight, offsets, factors):
    def add(index, total):
        source = ids[index // SLOTS, index % SLOTS]
        used = source >= 0
        source = jnp.maximum(source, 0)
        offsets[OX, total] = shift[0, source]
        offsets[OY, total] = shift[1, source]
        factors[total] = weight[source] * (2.0 / SLOTS / PUPIL / PUPIL)
        return total + used.astype(jnp.int32)

    total = lax.fori_loop(0, ids.shape[0] * SLOTS, add, jnp.int32(0))
    offsets[TOTAL, 0] = total
    for slot in range(GROUP):
        offsets[OX, total + slot] = jnp.int32(0)
        offsets[OY, total + slot] = jnp.int32(0)
        factors[total + slot] = jnp.float32(0.0)


def used_slots(ids, shift, weight):
    places = ids.shape[0] * SLOTS + GROUP
    return pl.pallas_call(
        list_kernel,
        out_shape=(
            jax.ShapeDtypeStruct((3, places), jnp.int32),
            jax.ShapeDtypeStruct((places,), jnp.float32),
        ),
        in_specs=[SMEM, SMEM, SMEM],
        out_specs=(SMEM, SMEM),
        name="used_slots",
    )(ids, shift, weight)


def adjoint_kernel(
    n_src, own, other, offsets, factors, pupil, cols_in, rows_in, rows_out, cols_out, col_table,
    out_table,
    result,
    spec, image, band, col_v, out_v, sems,
):
    place = lax.axis_index("tile") * n_src + lax.axis_index("src")
    col_copy = pltpu.make_async_copy(col_table.at[:, pl.ds(0, 2 * BAND)], col_v, sems.at[0])
    col_copy.start()
    out_copy = pltpu.make_async_copy(out_table.at[place], out_v, sems.at[1])
    out_copy.start()

    scale = 1.0 / math.sqrt(TILE_ROWS * COLS)
    whole = own[...] + other[...]
    spec[...] = (whole[: 2 * BAND] * scale).astype(jnp.bfloat16).astype(jnp.float32)
    image[:GRID, :] = whole[2 * BAND :]
    image[GRID:, :] = whole[2 * BAND :]
    band[...] = jnp.zeros_like(band)

    def group(step, carry):
        starts, pupils, amplitudes = [], [], []
        for slot in range(GROUP):
            index = step * GROUP + slot
            offset_x, offset_y = offsets[OX, index], offsets[OY, index]
            real = pltpu.roll(pupil[:PUPIL, :], offset_x, 1)
            imag = pltpu.roll(pupil[PUPIL:, :], offset_x, 1)
            spec_real = spec[pl.ds(offset_y, PUPIL), :]
            spec_imag = spec[pl.ds(BAND + offset_y, PUPIL), :]
            amp_real = real * spec_real - imag * spec_imag
            amp_imag = real * spec_imag + imag * spec_real
            starts.append(offset_y)
            pupils.append((real, imag, factors[index]))
            amplitudes.append(jnp.concatenate([amp_real, amp_imag], 1).astype(jnp.bfloat16))
        halfway = dot(jnp.concatenate(amplitudes, 0), cols_in[...]).astype(jnp.bfloat16)
        halfway = jnp.concatenate(
            [
                jnp.concatenate(
                    [
                        halfway[slot * PUPIL : (slot + 1) * PUPIL, :GRID],
                        halfway[slot * PUPIL : (slot + 1) * PUPIL, GRID:],
                    ],
                    0,
                )
                for slot in range(GROUP)
            ],
            1,
        )
        field = dot(rows_in[...], halfway)
        field_grad = jnp.concatenate(
            [
                (field[:, slot * GRID : (slot + 1) * GRID] * image[...]).astype(jnp.bfloat16)
                for slot in range(GROUP)
            ],
            1,
        )
        back = dot(rows_out[...], field_grad).astype(jnp.bfloat16)
        back = jnp.concatenate(
            [
                jnp.concatenate(
                    [
                        back[:PUPIL, slot * GRID : (slot + 1) * GRID],
                        back[PUPIL:, slot * GRID : (slot + 1) * GRID],
                    ],
                    1,
                )
                for slot in range(GROUP)
            ],
            0,
        )
        grad = dot(back, cols_out[...])
        for slot in range(GROUP):
            real, imag, factor = pupils[slot]
            grad_real = grad[slot * PUPIL : (slot + 1) * PUPIL, :BAND] * factor
            grad_imag = grad[slot * PUPIL : (slot + 1) * PUPIL, BAND:] * factor
            rows = pl.ds(starts[slot], PUPIL)
            band[rows, :] = band[rows, :] + (real * grad_real + imag * grad_imag)
            rows = pl.ds(BAND + starts[slot], PUPIL)
            band[rows, :] = band[rows, :] + (real * grad_imag - imag * grad_real)
        return carry

    lax.fori_loop(0, (offsets[TOTAL, 0] + GROUP - 1) // GROUP, group, jnp.int32(0))

    col_copy.wait()
    out_copy.wait()
    real = band[:BAND, :] * scale
    imag = band[BAND:, :] * scale
    left = jnp.concatenate(
        [jnp.concatenate([real, imag], 1), jnp.concatenate([imag, -real], 1)], 0
    ).astype(jnp.bfloat16)
    mixed = dot(out_v[...].astype(jnp.bfloat16), left).astype(jnp.bfloat16)
    result[0] = lax.dot_general(
        mixed, col_v[...], (((1,), (1,)), ((), ())), preferred_element_type=jnp.float32
    )


def adjoint(own, other, offsets, factors, pupil, tables, col_table, out_table, n_src):
    portion = out_table.shape[1]
    columns = col_table.shape[0]
    return pl.pallas_call(
        functools.partial(adjoint_kernel, n_src),
        out_shape=jax.ShapeDtypeStruct((1, portion, columns), jnp.float32),
        in_specs=[VMEM, VMEM, SMEM, SMEM] + [VMEM] * 5 + [HBM, HBM],
        out_specs=VMEM,
        scratch_shapes=[
            pltpu.VMEM((2 * BAND, BAND), jnp.float32),
            pltpu.VMEM((2 * GRID, GRID), jnp.float32),
            pltpu.VMEM((2 * BAND, BAND), jnp.float32),
            pltpu.VMEM((columns, 2 * BAND), jnp.bfloat16),
            pltpu.VMEM(out_table.shape[1:], jnp.float32),
            pltpu.SemaphoreType.DMA((2,)),
        ],
        compiler_params=pltpu.CompilerParams(vmem_limit_bytes=8 * 1024 * 1024),
        cost_estimate=pl.CostEstimate(
            flops=2 * 128 * 4096 * 256, bytes_accessed=4 * 1024 * 1024, transcendentals=0
        ),
        name="adjoint",
    )(own, other, offsets, factors, pupil, *tables, col_table, out_table)


def body(mask, cotangent, pupil_phase, source_weight, shift_table, source_ids, source_count):
    height, columns = mask.shape
    n_tile, n_src = lax.axis_size("tile"), lax.axis_size("src")
    col_table, row_table, out_table = image_tables(columns, height, n_tile, n_src)
    used = jnp.arange(SLOTS, dtype=jnp.int32)[None, :] < source_count[0]
    ids = lax.all_gather(jnp.where(used, source_ids, -1), "src", axis=0, tiled=True)
    partial, pupil = forward(mask, cotangent, pupil_phase, col_table, row_table)
    offsets, factors = used_slots(ids, shift_table.T, source_weight)
    other = jnp.zeros_like(partial)
    if n_tile & (n_tile - 1):
        partial = lax.psum(partial, "tile")
    else:
        step = 1
        while step < n_tile:
            partial = partial + other if step > 1 else partial
            swap = [(place, place ^ step) for place in range(n_tile)]
            other = lax.ppermute(partial, "tile", swap)
            step *= 2
    return adjoint(
        partial, other, offsets, factors, pupil, grid_tables(), col_table, out_table, n_src
    )


def solution(mesh):
    placed = (
        P(("grp", "tile"), None),
        P(("grp", "tile"), None),
        P(),
        P(),
        P(),
        P(("grp", "src"), None),
        P(("grp", "src")),
    )
    return jax.shard_map(
        body, mesh=mesh, in_specs=placed, out_specs=P(("grp", "tile"), "src", None), check_vma=False
    )
```

```python
import functools
import math

import jax
import jax.numpy as jnp
import ml_dtypes
import numpy as np
from jax import lax
from jax.experimental import pallas as pl
from jax.experimental.pallas import tpu as pltpu
from jax.sharding import PartitionSpec as P

COLS = 2048
TILE_ROWS = 2048
BAND = 128
PUPIL = 64
SLOTS = 8
GRID = 128
CHUNKS = 4
GROUP = 4
OX, OY, WEIGHT, USED = range(4)
LANES = 128
SUMS = 2 * BAND + GRID
GRANT = 53 * 1024 * 1024

VMEM = pl.BlockSpec(memory_space=pltpu.VMEM)
SMEM = pl.BlockSpec(memory_space=pltpu.SMEM)
HBM = pl.BlockSpec(memory_space=pltpu.HBM)


def waves(positions, freqs, length):
    product = np.multiply.outer(positions, freqs) % length
    angle = product.astype(np.float64) * (2.0 * math.pi / length)
    return np.cos(angle), np.sin(angle)


def lowpass(positions, length):
    freqs = np.arange(1, PUPIL)
    step = length // GRID
    apart = np.arange(GRID)[None, :] * step - positions[:, None]
    product = (apart[:, :, None] * freqs) % length
    return (1.0 + 2.0 * np.cos(product * (2.0 * math.pi / length)).sum(2)) / GRID


def low(array):
    return np.ascontiguousarray(array).astype(ml_dtypes.bfloat16)


@functools.cache
def image_tables(columns, height, n_tile, n_src):
    band = np.arange(BAND) - BAND // 2
    cols = np.arange(columns)
    rows = np.arange(TILE_ROWS)
    cos, sin = waves(cols, band, columns)
    col_table = low(np.concatenate([cos, -sin, lowpass(cols, columns)], 1))
    cos, sin = waves(rows, band, TILE_ROWS)
    row_table = np.concatenate([cos, sin, lowpass(rows, TILE_ROWS)], 1)
    row_table = low(row_table.reshape(n_tile, height, 2 * BAND + GRID).transpose(0, 2, 1))
    portion = height // n_src
    out_table = np.concatenate([cos, -sin], 1).astype(np.float32)
    return col_table, row_table, out_table.reshape(n_tile * n_src, portion, 2 * BAND)


COLS_IN, COLS_OUT = slice(0, 2 * BAND), slice(2 * BAND, 2 * BAND + 2 * GRID)
ROWS_IN = slice(COLS_OUT.stop, COLS_OUT.stop + GRID)
ROWS_OUT = slice(ROWS_IN.stop, ROWS_IN.stop + 2 * PUPIL)
GRID_ROWS = ROWS_OUT.stop


@functools.cache
def grid_tables(columns):
    points = np.arange(GRID)
    band = np.arange(BAND) - BAND // 2
    cos, sin = waves(points, band, GRID)
    cols_in = np.block([[cos.T, sin.T], [-sin.T, cos.T]])
    cols_out = np.block([[cos, -sin], [sin, cos]])
    cos, sin = waves(points, np.arange(PUPIL) - PUPIL // 2, GRID)
    rows_in = np.block([[cos, -sin, sin, cos]])
    rows_out = np.block([[cos.T, sin.T], [-sin.T, cos.T]])
    cos, sin = waves(np.arange(columns), band, columns)
    return low(np.concatenate([cols_in, cols_out, rows_in, rows_out, np.block([cos, -sin])], 0))


def dot(left, right):
    return jnp.dot(left, right, preferred_element_type=jnp.float32)


def forward_kernel(
    ids, count, mask, cotangent, shift, weight, col_table, row_table,
    partial, slots,
    mask_v, cot_v, col_v, row_v, shift_s, weight_s, sems, slot_sems,
):
    height, columns = mask.shape
    width = columns // CHUNKS
    tile = lax.axis_index("tile")
    look_ups = []
    for slot in range(SLOTS):
        source = ids[0, slot]
        lanes = pl.ds(pl.multiple_of(source // LANES * LANES, LANES), LANES)
        rows = pl.ds(pl.multiple_of(source // (8 * LANES) * 8, 8), 8)
        look_ups += [
            pltpu.make_async_copy(shift.at[:, lanes], shift_s.at[slot], slot_sems.at[slot, 0]),
            pltpu.make_async_copy(weight.at[rows, :], weight_s.at[slot], slot_sems.at[slot, 1]),
        ]
    chunk_copies = []
    for step in range(CHUNKS):
        part = pl.ds(step * width, width)
        copies = [
            pltpu.make_async_copy(col_table.at[part, :], col_v.at[part, :], sems.at[step, 0]),
            pltpu.make_async_copy(mask.at[:, part], mask_v.at[step], sems.at[step, 1]),
            pltpu.make_async_copy(cotangent.at[:, part], cot_v.at[step], sems.at[step, 2]),
        ]
        for copy in copies:
            copy.start()
        chunk_copies.append(copies)
    row_copy = pltpu.make_async_copy(row_table.at[tile], row_v, sems.at[CHUNKS, 0])
    row_copy.start()
    for copy in look_ups:
        copy.start()

    for step in range(CHUNKS):
        for copy in chunk_copies[step]:
            copy.wait()
        part = pl.ds(step * width, width)
        mask_add = dot(mask_v[step], col_v[part, : 2 * BAND])
        cot_add = dot(cot_v[step], col_v[part, 2 * BAND :])
        mask_part = mask_add if step == 0 else mask_part + mask_add
        cot_part = cot_add if step == 0 else cot_part + cot_add

    for copy in look_ups:
        copy.wait()
    lane = lax.broadcasted_iota(jnp.int32, (1, LANES), 1)
    lines = []
    for slot in range(SLOTS):
        source = ids[0, slot]
        used = jnp.where(slot < count[0], 1.0, 0.0)
        line = jnp.where(lane == OX, shift_s[slot, 0, source % LANES].astype(jnp.float32), 0.0)
        line = jnp.where(lane == OY, shift_s[slot, 1, source % LANES].astype(jnp.float32), line)
        line = jnp.where(lane == WEIGHT, weight_s[slot, source // LANES % 8, source % LANES], line)
        lines.append(jnp.where(lane == USED, used, line))
    slots[...] = jnp.concatenate(lines, 0)

    row_copy.wait()
    blocks = dot(row_v[: 2 * BAND, :], mask_part.astype(jnp.bfloat16))
    partial[:BAND, :] = blocks[:BAND, :BAND] + blocks[BAND:, BAND:]
    partial[BAND : 2 * BAND, :] = blocks[:BAND, BAND:] - blocks[BAND:, :BAND]
    partial[2 * BAND :, :] = dot(row_v[2 * BAND :, :], cot_part.astype(jnp.bfloat16))


def forward(ids, count, mask, cotangent, shift, weight, col_table, row_table):
    height, columns = mask.shape
    width = columns // CHUNKS
    return pl.pallas_call(
        forward_kernel,
        out_shape=(
            jax.ShapeDtypeStruct((SUMS, BAND), jnp.float32),
            jax.ShapeDtypeStruct((SLOTS, LANES), jnp.float32),
        ),
        in_specs=[SMEM, SMEM] + [HBM] * 6,
        out_specs=(VMEM, VMEM),
        scratch_shapes=[
            pltpu.VMEM((CHUNKS, height, width), jnp.bfloat16),
            pltpu.VMEM((CHUNKS, height, width), jnp.bfloat16),
            pltpu.VMEM(col_table.shape, jnp.bfloat16),
            pltpu.VMEM(row_table.shape[1:], jnp.bfloat16),
            pltpu.SMEM((SLOTS, 2, LANES), jnp.int32),
            pltpu.SMEM((SLOTS, 8, LANES), jnp.float32),
            pltpu.SemaphoreType.DMA((CHUNKS + 1, 3)),
            pltpu.SemaphoreType.DMA((SLOTS, 2)),
        ],
        compiler_params=pltpu.CompilerParams(vmem_limit_bytes=GRANT),
        cost_estimate=pl.CostEstimate(
            flops=2 * height * columns * SUMS, bytes_accessed=6 * 1024 * 1024, transcendentals=0
        ),
        name="forward",
    )(ids, count, mask, cotangent, shift, weight, col_table, row_table)


def adjoint_kernel(
    n_src, own, other, pupil, table, out_table,
    result,
    spec, image, band, table_v, out_v, own_s, other_s, list_x, list_y, list_w, sems,
):
    place = lax.axis_index("tile") * n_src + lax.axis_index("src")
    own_copy = pltpu.make_async_copy(own.at[SUMS:, :], own_s, sems.at[0])
    other_copy = pltpu.make_async_copy(other.at[SUMS:, :], other_s, sems.at[1])
    small, columns = GRID_ROWS, table.shape[0] - GRID_ROWS
    grid_part, col_part = pl.ds(0, small), pl.ds(small, columns)
    grid_copy = pltpu.make_async_copy(table.at[grid_part, :], table_v.at[grid_part, :], sems.at[2])
    col_copy = pltpu.make_async_copy(table.at[col_part, :], table_v.at[col_part, :], sems.at[3])
    out_copy = pltpu.make_async_copy(out_table.at[place], out_v, sems.at[4])
    for copy in (own_copy, other_copy, grid_copy, col_copy, out_copy):
        copy.start()

    scale = 1.0 / math.sqrt(TILE_ROWS * COLS)
    whole = own[:SUMS, :] + other[:SUMS, :]
    spec[...] = (whole[: 2 * BAND] * scale).astype(jnp.bfloat16).astype(jnp.float32)
    image[:GRID, :] = whole[2 * BAND :]
    image[GRID:, :] = whole[2 * BAND :]
    band[...] = jnp.zeros_like(band)

    own_copy.wait()
    other_copy.wait()

    def add_from(lines):
        def add(line, total):
            list_x[total] = lines[line, OX].astype(jnp.int32)
            list_y[total] = lines[line, OY].astype(jnp.int32)
            list_w[total] = lines[line, WEIGHT] * (2.0 / SLOTS / PUPIL / PUPIL)
            return total + lines[line, USED].astype(jnp.int32)

        return add

    total = jnp.int32(0)
    for lines in (own_s, other_s):
        total = lax.fori_loop(0, lines.shape[0], add_from(lines), total)
    for slot in range(GROUP):
        list_x[total + slot] = jnp.int32(0)
        list_y[total + slot] = jnp.int32(0)
        list_w[total + slot] = jnp.float32(0.0)
    grid_copy.wait()

    def group(step, carry):
        starts, pupils, amplitudes = [], [], []
        for slot in range(GROUP):
            index = step * GROUP + slot
            offset_x, offset_y = list_x[index], list_y[index]
            real = pltpu.roll(pupil[:PUPIL, :], offset_x, 1)
            imag = pltpu.roll(pupil[PUPIL:, :], offset_x, 1)
            spec_real = spec[pl.ds(offset_y, PUPIL), :]
            spec_imag = spec[pl.ds(BAND + offset_y, PUPIL), :]
            amp_real = real * spec_real - imag * spec_imag
            amp_imag = real * spec_imag + imag * spec_real
            starts.append(offset_y)
            pupils.append((real, imag, list_w[index]))
            amplitudes.append(jnp.concatenate([amp_real, amp_imag], 1).astype(jnp.bfloat16))
        halfway = dot(jnp.concatenate(amplitudes, 0), table_v[COLS_IN, :]).astype(jnp.bfloat16)
        halfway = jnp.concatenate(
            [
                jnp.concatenate(
                    [
                        halfway[slot * PUPIL : (slot + 1) * PUPIL, :GRID],
                        halfway[slot * PUPIL : (slot + 1) * PUPIL, GRID:],
                    ],
                    0,
                )
                for slot in range(GROUP)
            ],
            1,
        )
        rows_in = table_v[ROWS_IN, :]
        rows_in = jnp.concatenate([rows_in[:, : 2 * PUPIL], rows_in[:, 2 * PUPIL :]], 0)
        field = dot(rows_in, halfway)
        field_grad = jnp.concatenate(
            [
                (field[:, slot * GRID : (slot + 1) * GRID] * image[...]).astype(jnp.bfloat16)
                for slot in range(GROUP)
            ],
            1,
        )
        back = dot(table_v[ROWS_OUT, :], field_grad).astype(jnp.bfloat16)
        back = jnp.concatenate(
            [
                jnp.concatenate(
                    [
                        back[:PUPIL, slot * GRID : (slot + 1) * GRID],
                        back[PUPIL:, slot * GRID : (slot + 1) * GRID],
                    ],
                    1,
                )
                for slot in range(GROUP)
            ],
            0,
        )
        grad = dot(back, table_v[COLS_OUT, :])
        for slot in range(GROUP):
            real, imag, factor = pupils[slot]
            grad_real = grad[slot * PUPIL : (slot + 1) * PUPIL, :BAND] * factor
            grad_imag = grad[slot * PUPIL : (slot + 1) * PUPIL, BAND:] * factor
            rows = pl.ds(starts[slot], PUPIL)
            band[rows, :] = band[rows, :] + (real * grad_real + imag * grad_imag)
            rows = pl.ds(BAND + starts[slot], PUPIL)
            band[rows, :] = band[rows, :] + (real * grad_imag - imag * grad_real)
        return carry

    lax.fori_loop(0, (total + GROUP - 1) // GROUP, group, jnp.int32(0))

    col_copy.wait()
    out_copy.wait()
    real = band[:BAND, :] * scale
    imag = band[BAND:, :] * scale
    left = jnp.concatenate(
        [jnp.concatenate([real, imag], 1), jnp.concatenate([imag, -real], 1)], 0
    ).astype(jnp.bfloat16)
    mixed = dot(out_v[...].astype(jnp.bfloat16), left).astype(jnp.bfloat16)
    result[0] = lax.dot_general(
        mixed, table_v[col_part, :], (((1,), (1,)), ((), ())), preferred_element_type=jnp.float32
    )


def adjoint(own, other, pupil, table, out_table, n_src):
    portion = out_table.shape[1]
    columns = table.shape[0] - GRID_ROWS
    lines = own.shape[0] - SUMS
    places = 2 * lines + GROUP
    return pl.pallas_call(
        functools.partial(adjoint_kernel, n_src),
        out_shape=jax.ShapeDtypeStruct((1, portion, columns), jnp.float32),
        in_specs=[VMEM, VMEM, VMEM, HBM, HBM],
        out_specs=VMEM,
        scratch_shapes=[
            pltpu.VMEM((2 * BAND, BAND), jnp.float32),
            pltpu.VMEM((2 * GRID, GRID), jnp.float32),
            pltpu.VMEM((2 * BAND, BAND), jnp.float32),
            pltpu.VMEM(table.shape, jnp.bfloat16),
            pltpu.VMEM(out_table.shape[1:], jnp.float32),
            pltpu.SMEM((lines, LANES), jnp.float32),
            pltpu.SMEM((lines, LANES), jnp.float32),
            pltpu.SMEM((places,), jnp.int32),
            pltpu.SMEM((places,), jnp.int32),
            pltpu.SMEM((places,), jnp.float32),
            pltpu.SemaphoreType.DMA((5,)),
        ],
        compiler_params=pltpu.CompilerParams(vmem_limit_bytes=GRANT),
        cost_estimate=pl.CostEstimate(
            flops=2 * 128 * 4096 * 256, bytes_accessed=4 * 1024 * 1024, transcendentals=0
        ),
        name="adjoint",
    )(own, other, pupil, table, out_table)


def pupil_rows(phase):
    grid = jnp.arange(PUPIL, dtype=jnp.int32)
    radius = (2 * grid[:, None] - PUPIL + 1) ** 2 + (2 * grid[None, :] - PUPIL + 1) ** 2
    inside = radius <= PUPIL * PUPIL
    both = jnp.concatenate(
        [jnp.where(inside, jnp.cos(phase), 0.0), jnp.where(inside, jnp.sin(phase), 0.0)], 0
    )
    return jnp.pad(both, ((0, 0), (0, BAND - PUPIL)))


def swapped(array, sizes, steps):
    axes = tuple(sizes)
    places = np.arange(math.prod(sizes.values())).reshape(tuple(sizes.values()))
    there = places
    for dim, axis in enumerate(axes):
        there = np.take(there, np.arange(sizes[axis]) ^ steps.get(axis, 0), dim)
    turn = [(int(a), int(b)) for a, b in zip(places.ravel(), there.ravel())]
    return lax.ppermute(array, axes, turn)


def body(mask, cotangent, pupil_phase, source_weight, shift_table, source_ids, source_count):
    height, columns = mask.shape
    n_tile, n_src = lax.axis_size("tile"), lax.axis_size("src")
    col_table, row_table, out_table = image_tables(columns, height, n_tile, n_src)
    partial, lines = forward(
        source_ids,
        source_count,
        mask,
        cotangent,
        shift_table.T,
        source_weight.reshape(-1, LANES),
        col_table,
        row_table,
    )
    sizes = {"src": n_src, "tile": n_tile}
    step = 2
    while step < n_src:
        lines = jnp.concatenate([lines, swapped(lines, sizes, {"src": step})], 0)
        step *= 2
    step = 1
    while step < n_tile // 2:
        partial = partial + swapped(partial, sizes, {"tile": step})
        step *= 2
    own = jnp.concatenate([partial, lines], 0)
    other = swapped(own, sizes, {"src": 1, "tile": step})
    return adjoint(own, other, pupil_rows(pupil_phase), grid_tables(columns), out_table, n_src)


def solution(mesh):
    placed = (
        P(("grp", "tile"), None),
        P(("grp", "tile"), None),
        P(),
        P(),
        P(),
        P(("grp", "src"), None),
        P(("grp", "src")),
    )
    return jax.shard_map(
        body, mesh=mesh, in_specs=placed, out_specs=P(("grp", "tile"), "src", None), check_vma=False
    )
```

```python
import functools
import math

import jax
import jax.numpy as jnp
import ml_dtypes
import numpy as np
from jax import lax
from jax.experimental import pallas as pl
from jax.experimental.pallas import tpu as pltpu
from jax.sharding import PartitionSpec as P

COLS = 2048
TILE_ROWS = 2048
BAND = 128
PUPIL = 64
SLOTS = 8
GRID = 128
CHUNKS = 4
GROUP = 4
OX, OY, WEIGHT, USED = range(4)
LANES = 128
GRANT = 53 * 1024 * 1024

VMEM = pl.BlockSpec(memory_space=pltpu.VMEM)
SMEM = pl.BlockSpec(memory_space=pltpu.SMEM)
HBM = pl.BlockSpec(memory_space=pltpu.HBM)


def waves(positions, freqs, length):
    product = np.multiply.outer(positions, freqs) % length
    angle = product.astype(np.float64) * (2.0 * math.pi / length)
    return np.cos(angle), np.sin(angle)


def lowpass(positions, length):
    freqs = np.arange(1, PUPIL)
    step = length // GRID
    apart = np.arange(GRID)[None, :] * step - positions[:, None]
    product = (apart[:, :, None] * freqs) % length
    return (1.0 + 2.0 * np.cos(product * (2.0 * math.pi / length)).sum(2)) / GRID


def low(array):
    return np.ascontiguousarray(array).astype(ml_dtypes.bfloat16)


@functools.cache
def image_tables(columns, height, n_tile, n_src):
    band = np.arange(BAND) - BAND // 2
    cols = np.arange(columns)
    rows = np.arange(TILE_ROWS)

    def by_tile(table):
        return low(table.reshape(n_tile, height, table.shape[1]).transpose(0, 2, 1))

    cos, sin = waves(cols, band, columns)
    mask_cols = low(np.concatenate([cos, -sin], 1))
    cos, sin = waves(rows, band, TILE_ROWS)
    mask_rows = by_tile(np.concatenate([cos, sin], 1))
    grid_cols = low(lowpass(cols, columns))
    grid_rows = by_tile(lowpass(rows, TILE_ROWS))
    out_table = np.concatenate([cos, -sin], 1).astype(np.float32)
    out_table = out_table.reshape(n_tile * n_src, height // n_src, 2 * BAND)
    return (mask_cols, mask_rows), (grid_cols, grid_rows), out_table


COLS_IN, COLS_OUT = slice(0, 2 * BAND), slice(2 * BAND, 2 * BAND + 2 * GRID)
ROWS_IN = slice(COLS_OUT.stop, COLS_OUT.stop + GRID)
ROWS_OUT = slice(ROWS_IN.stop, ROWS_IN.stop + 2 * PUPIL)
GRID_ROWS = ROWS_OUT.stop


@functools.cache
def grid_tables(columns):
    points = np.arange(GRID)
    band = np.arange(BAND) - BAND // 2
    cos, sin = waves(points, band, GRID)
    cols_in = np.block([[cos.T, sin.T], [-sin.T, cos.T]])
    cols_out = np.block([[cos, -sin], [sin, cos]])
    cos, sin = waves(points, np.arange(PUPIL) - PUPIL // 2, GRID)
    rows_in = np.block([[cos, -sin, sin, cos]])
    rows_out = np.block([[cos.T, sin.T], [-sin.T, cos.T]])
    cos, sin = waves(np.arange(columns), band, columns)
    return low(np.concatenate([cols_in, cols_out, rows_in, rows_out, np.block([cos, -sin])], 0))


def dot(left, right):
    return jnp.dot(left, right, preferred_element_type=jnp.float32)


def column_sums(pixels, col_table, row_table, pixels_v, col_v, row_v, sems):
    width = pixels.shape[1] // CHUNKS
    chunk_copies = []
    for step in range(CHUNKS):
        part = pl.ds(step * width, width)
        copies = (
            pltpu.make_async_copy(col_table.at[part, :], col_v.at[part, :], sems.at[step, 0]),
            pltpu.make_async_copy(pixels.at[:, part], pixels_v.at[step], sems.at[step, 1]),
        )
        for copy in copies:
            copy.start()
        chunk_copies.append(copies)
    tile = lax.axis_index("tile")
    row_copy = pltpu.make_async_copy(row_table.at[tile], row_v, sems.at[CHUNKS, 0])
    row_copy.start()

    def finish():
        for step in range(CHUNKS):
            for copy in chunk_copies[step]:
                copy.wait()
            add = dot(pixels_v[step], col_v[pl.ds(step * width, width), :])
            total = add if step == 0 else total + add
        row_copy.wait()
        return total.astype(jnp.bfloat16)

    return finish


def mask_kernel(mask, col_table, row_table, partial, *scratch):
    sums = column_sums(mask, col_table, row_table, *scratch)()
    row_v = scratch[2]
    blocks = dot(row_v[...], sums)
    partial[:BAND, :] = blocks[:BAND, :BAND] + blocks[BAND:, BAND:]
    partial[BAND:, :] = blocks[:BAND, BAND:] - blocks[BAND:, :BAND]


def cotangent_kernel(
    ids, shift, weight, cotangent, col_table, row_table, partial, shift_s, weight_s, slot_sems, *scratch
):
    finish = column_sums(cotangent, col_table, row_table, *scratch)
    look_up(ids, shift, weight, partial.at[GRID:, :], shift_s, weight_s, slot_sems)
    row_v = scratch[2]
    partial[:GRID, :] = dot(row_v[...], finish())


def look_up(ids, shift, weight, lines, shift_s, weight_s, sems):
    count = lines.shape[0]

    def each(work):
        def step(line, carry):
            work(line, ids[line // SLOTS, line % SLOTS])
            return carry

        lax.fori_loop(0, count, step, jnp.int32(0), unroll=count <= 32)

    def copies(line, source):
        source = jnp.maximum(source, 0)
        lanes = pl.ds(pl.multiple_of(source // LANES * LANES, LANES), LANES)
        rows = pl.ds(pl.multiple_of(source // (8 * LANES) * 8, 8), 8)
        return (
            pltpu.make_async_copy(shift.at[:, lanes], shift_s.at[line], sems.at[line, 0]),
            pltpu.make_async_copy(weight.at[rows, :], weight_s.at[line], sems.at[line, 1]),
        )

    def start(line, source):
        for copy in copies(line, source):
            copy.start()

    def wait(line, source):
        for copy in copies(line, source):
            copy.wait()

    def write(line, source):
        used = jnp.where(source >= 0, 1.0, 0.0)
        source = jnp.maximum(source, 0)
        lane = lax.broadcasted_iota(jnp.int32, (1, LANES), 1)
        found = jnp.where(lane == OX, shift_s[line, 0, source % LANES].astype(jnp.float32), 0.0)
        found = jnp.where(lane == OY, shift_s[line, 1, source % LANES].astype(jnp.float32), found)
        factor = weight_s[line, source // LANES % 8, source % LANES]
        found = jnp.where(lane == WEIGHT, factor, found)
        lines[pl.ds(line, 1), :] = jnp.where(lane == USED, used, found)

    each(start)
    each(wait)
    each(write)


def sums_scratch(pixels, col_table, row_table):
    height, columns = pixels.shape
    return [
        pltpu.VMEM((CHUNKS, height, columns // CHUNKS), jnp.bfloat16),
        pltpu.VMEM(col_table.shape, jnp.bfloat16),
        pltpu.VMEM(row_table.shape[1:], jnp.bfloat16),
        pltpu.SemaphoreType.DMA((CHUNKS + 1, 2)),
    ]


def sums_params(pixels, lines):
    return dict(
        compiler_params=pltpu.CompilerParams(vmem_limit_bytes=GRANT),
        cost_estimate=pl.CostEstimate(
            flops=2 * pixels.size * lines, bytes_accessed=2 * pixels.size, transcendentals=0
        ),
    )


def mask_part(mask, tables):
    return pl.pallas_call(
        mask_kernel,
        out_shape=jax.ShapeDtypeStruct((2 * BAND, BAND), jnp.float32),
        in_specs=[HBM] * 3,
        out_specs=VMEM,
        scratch_shapes=sums_scratch(mask, *tables),
        name="mask_part",
        **sums_params(mask, 2 * BAND),
    )(mask, *tables)


def cotangent_part(ids, shift, weight, cotangent, tables):
    return pl.pallas_call(
        cotangent_kernel,
        out_shape=jax.ShapeDtypeStruct((GRID + ids.size, BAND), jnp.float32),
        in_specs=[SMEM] + [HBM] * 5,
        out_specs=VMEM,
        scratch_shapes=[
            pltpu.SMEM((ids.size, 2, LANES), jnp.int32),
            pltpu.SMEM((ids.size, 8, LANES), jnp.float32),
            pltpu.SemaphoreType.DMA((ids.size, 2)),
        ]
        + sums_scratch(cotangent, *tables),
        name="cotangent_part",
        **sums_params(cotangent, GRID),
    )(ids, shift, weight, cotangent, *tables)


def adjoint_kernel(
    n_src, own_mask, other_mask, own, other, pupil, table, out_table,
    result,
    spec, image, band, table_v, out_v, own_s, other_s, list_x, list_y, list_w, sems,
):
    place = lax.axis_index("tile") * n_src + lax.axis_index("src")
    own_copy = pltpu.make_async_copy(own.at[GRID:, :], own_s, sems.at[0])
    other_copy = pltpu.make_async_copy(other.at[GRID:, :], other_s, sems.at[1])
    small, columns = GRID_ROWS, table.shape[0] - GRID_ROWS
    grid_part, col_part = pl.ds(0, small), pl.ds(small, columns)
    grid_copy = pltpu.make_async_copy(table.at[grid_part, :], table_v.at[grid_part, :], sems.at[2])
    col_copy = pltpu.make_async_copy(table.at[col_part, :], table_v.at[col_part, :], sems.at[3])
    out_copy = pltpu.make_async_copy(out_table.at[place], out_v, sems.at[4])
    for copy in (own_copy, other_copy, grid_copy, col_copy, out_copy):
        copy.start()

    scale = 1.0 / math.sqrt(TILE_ROWS * COLS)
    spec[...] = ((own_mask[...] + other_mask[...]) * scale).astype(jnp.bfloat16).astype(jnp.float32)
    image[:GRID, :] = own[:GRID, :] + other[:GRID, :]
    image[GRID:, :] = image[:GRID, :]
    band[...] = jnp.zeros_like(band)

    own_copy.wait()
    other_copy.wait()

    def add_from(lines):
        def add(line, total):
            list_x[total] = lines[line, OX].astype(jnp.int32)
            list_y[total] = lines[line, OY].astype(jnp.int32)
            list_w[total] = lines[line, WEIGHT] * (2.0 / SLOTS / PUPIL / PUPIL)
            return total + lines[line, USED].astype(jnp.int32)

        return add

    total = jnp.int32(0)
    for lines in (own_s, other_s):
        total = lax.fori_loop(0, lines.shape[0], add_from(lines), total)
    for slot in range(GROUP):
        list_x[total + slot] = jnp.int32(0)
        list_y[total + slot] = jnp.int32(0)
        list_w[total + slot] = jnp.float32(0.0)
    grid_copy.wait()

    def group(step, carry):
        starts, pupils, amplitudes = [], [], []
        for slot in range(GROUP):
            index = step * GROUP + slot
            offset_x, offset_y = list_x[index], list_y[index]
            real = pltpu.roll(pupil[:PUPIL, :], offset_x, 1)
            imag = pltpu.roll(pupil[PUPIL:, :], offset_x, 1)
            spec_real = spec[pl.ds(offset_y, PUPIL), :]
            spec_imag = spec[pl.ds(BAND + offset_y, PUPIL), :]
            amp_real = real * spec_real - imag * spec_imag
            amp_imag = real * spec_imag + imag * spec_real
            starts.append(offset_y)
            pupils.append((real, imag, list_w[index]))
            amplitudes.append(jnp.concatenate([amp_real, amp_imag], 1).astype(jnp.bfloat16))
        halfway = dot(jnp.concatenate(amplitudes, 0), table_v[COLS_IN, :]).astype(jnp.bfloat16)
        halfway = jnp.concatenate(
            [
                jnp.concatenate(
                    [
                        halfway[slot * PUPIL : (slot + 1) * PUPIL, :GRID],
                        halfway[slot * PUPIL : (slot + 1) * PUPIL, GRID:],
                    ],
                    0,
                )
                for slot in range(GROUP)
            ],
            1,
        )
        rows_in = table_v[ROWS_IN, :]
        rows_in = jnp.concatenate([rows_in[:, : 2 * PUPIL], rows_in[:, 2 * PUPIL :]], 0)
        field = dot(rows_in, halfway)
        field_grad = jnp.concatenate(
            [
                (field[:, slot * GRID : (slot + 1) * GRID] * image[...]).astype(jnp.bfloat16)
                for slot in range(GROUP)
            ],
            1,
        )
        back = dot(table_v[ROWS_OUT, :], field_grad).astype(jnp.bfloat16)
        back = jnp.concatenate(
            [
                jnp.concatenate(
                    [
                        back[:PUPIL, slot * GRID : (slot + 1) * GRID],
                        back[PUPIL:, slot * GRID : (slot + 1) * GRID],
                    ],
                    1,
                )
                for slot in range(GROUP)
            ],
            0,
        )
        grad = dot(back, table_v[COLS_OUT, :])
        for slot in range(GROUP):
            real, imag, factor = pupils[slot]
            grad_real = grad[slot * PUPIL : (slot + 1) * PUPIL, :BAND] * factor
            grad_imag = grad[slot * PUPIL : (slot + 1) * PUPIL, BAND:] * factor
            rows = pl.ds(starts[slot], PUPIL)
            band[rows, :] = band[rows, :] + (real * grad_real + imag * grad_imag)
            rows = pl.ds(BAND + starts[slot], PUPIL)
            band[rows, :] = band[rows, :] + (real * grad_imag - imag * grad_real)
        return carry

    lax.fori_loop(0, (total + GROUP - 1) // GROUP, group, jnp.int32(0))

    col_copy.wait()
    out_copy.wait()
    real = band[:BAND, :] * scale
    imag = band[BAND:, :] * scale
    left = jnp.concatenate(
        [jnp.concatenate([real, imag], 1), jnp.concatenate([imag, -real], 1)], 0
    ).astype(jnp.bfloat16)
    mixed = dot(out_v[...].astype(jnp.bfloat16), left).astype(jnp.bfloat16)
    result[0] = lax.dot_general(
        mixed, table_v[col_part, :], (((1,), (1,)), ((), ())), preferred_element_type=jnp.float32
    )


def adjoint(own_mask, other_mask, own, other, pupil, table, out_table, n_src):
    portion = out_table.shape[1]
    columns = table.shape[0] - GRID_ROWS
    lines = own.shape[0] - GRID
    places = 2 * lines + GROUP
    return pl.pallas_call(
        functools.partial(adjoint_kernel, n_src),
        out_shape=jax.ShapeDtypeStruct((1, portion, columns), jnp.float32),
        in_specs=[VMEM] * 5 + [HBM, HBM],
        out_specs=VMEM,
        scratch_shapes=[
            pltpu.VMEM((2 * BAND, BAND), jnp.float32),
            pltpu.VMEM((2 * GRID, GRID), jnp.float32),
            pltpu.VMEM((2 * BAND, BAND), jnp.float32),
            pltpu.VMEM(table.shape, jnp.bfloat16),
            pltpu.VMEM(out_table.shape[1:], jnp.float32),
            pltpu.SMEM((lines, LANES), jnp.float32),
            pltpu.SMEM((lines, LANES), jnp.float32),
            pltpu.SMEM((places,), jnp.int32),
            pltpu.SMEM((places,), jnp.int32),
            pltpu.SMEM((places,), jnp.float32),
            pltpu.SemaphoreType.DMA((5,)),
        ],
        compiler_params=pltpu.CompilerParams(vmem_limit_bytes=GRANT),
        cost_estimate=pl.CostEstimate(
            flops=2 * 128 * 4096 * 256, bytes_accessed=4 * 1024 * 1024, transcendentals=0
        ),
        name="adjoint",
    )(own_mask, other_mask, own, other, pupil, table, out_table)


def pupil_rows(phase):
    grid = jnp.arange(PUPIL, dtype=jnp.int32)
    radius = (2 * grid[:, None] - PUPIL + 1) ** 2 + (2 * grid[None, :] - PUPIL + 1) ** 2
    inside = radius <= PUPIL * PUPIL
    both = jnp.concatenate(
        [jnp.where(inside, jnp.cos(phase), 0.0), jnp.where(inside, jnp.sin(phase), 0.0)], 0
    )
    return jnp.pad(both, ((0, 0), (0, BAND - PUPIL)))


def swapped(array, sizes, steps):
    axes = tuple(sizes)
    places = np.arange(math.prod(sizes.values())).reshape(tuple(sizes.values()))
    there = places
    for dim, axis in enumerate(axes):
        there = np.take(there, np.arange(sizes[axis]) ^ steps.get(axis, 0), dim)
    turn = [(int(a), int(b)) for a, b in zip(places.ravel(), there.ravel())]
    return lax.ppermute(array, axes, turn)


def body(mask, cotangent, pupil_phase, source_weight, shift_table, source_ids, source_count):
    height, columns = mask.shape
    n_tile, n_src = lax.axis_size("tile"), lax.axis_size("src")
    mask_tables, grid_part, out_table = image_tables(columns, height, n_tile, n_src)
    sizes = {"src": n_src, "tile": n_tile}
    used = jnp.arange(SLOTS, dtype=jnp.int32)[None, :] < source_count[0]
    ids = jnp.where(used, source_ids, -1)
    step = 2
    while step < n_src:
        ids = jnp.concatenate([ids, swapped(ids, sizes, {"src": step})], 0)
        step *= 2
    own_mask = mask_part(mask, mask_tables)
    own = cotangent_part(
        ids, shift_table.T, source_weight.reshape(-1, LANES), cotangent, grid_part
    )
    step = 1
    while step < n_tile // 2:
        own_mask = own_mask + swapped(own_mask, sizes, {"tile": step})
        image = own[:GRID] + swapped(own[:GRID], sizes, {"tile": step})
        own = jnp.concatenate([image, own[GRID:]], 0)
        step *= 2
    other_mask = swapped(own_mask, sizes, {"tile": step})
    other = swapped(own, sizes, {"src": 1, "tile": step})
    return adjoint(
        own_mask, other_mask, own, other, pupil_rows(pupil_phase), grid_tables(columns), out_table, n_src
    )


def solution(mesh):
    placed = (
        P(("grp", "tile"), None),
        P(("grp", "tile"), None),
        P(),
        P(),
        P(),
        P(("grp", "src"), None),
        P(("grp", "src")),
    )
    return jax.shard_map(
        body, mesh=mesh, in_specs=placed, out_specs=P(("grp", "tile"), "src", None), check_vma=False
    )
```

```python
import functools
import math

import jax
import jax.numpy as jnp
import ml_dtypes
import numpy as np
from jax import lax
from jax.experimental import pallas as pl
from jax.experimental.pallas import tpu as pltpu
from jax.sharding import PartitionSpec as P

COLS = 2048
TILE_ROWS = 2048
BAND = 128
PUPIL = 64
SLOTS = 8
GRID = 128
CHUNKS = 4
GROUP = 4
OX, OY, WEIGHT, USED = range(4)
LANES = 128
SUMS = 2 * BAND + GRID
GRANT = 53 * 1024 * 1024

VMEM = pl.BlockSpec(memory_space=pltpu.VMEM)
SMEM = pl.BlockSpec(memory_space=pltpu.SMEM)
HBM = pl.BlockSpec(memory_space=pltpu.HBM)


def waves(positions, freqs, length):
    product = np.multiply.outer(positions, freqs) % length
    angle = product.astype(np.float64) * (2.0 * math.pi / length)
    return np.cos(angle), np.sin(angle)


def lowpass(positions, length):
    freqs = np.arange(1, PUPIL)
    step = length // GRID
    apart = np.arange(GRID)[None, :] * step - positions[:, None]
    product = (apart[:, :, None] * freqs) % length
    return (1.0 + 2.0 * np.cos(product * (2.0 * math.pi / length)).sum(2)) / GRID


def low(array):
    return np.ascontiguousarray(array).astype(ml_dtypes.bfloat16)


@functools.cache
def image_tables(columns, height, n_tile, n_src):
    band = np.arange(BAND) - BAND // 2
    cols = np.arange(columns)
    rows = np.arange(TILE_ROWS)
    cos, sin = waves(cols, band, columns)
    col_table = low(np.concatenate([cos, -sin, lowpass(cols, columns)], 1))
    cos, sin = waves(rows, band, TILE_ROWS)
    row_table = np.concatenate([cos, sin, lowpass(rows, TILE_ROWS)], 1)
    row_table = low(row_table.reshape(n_tile, height, 2 * BAND + GRID).transpose(0, 2, 1))
    portion = height // n_src
    out_table = np.concatenate([cos, -sin], 1).astype(np.float32)
    return col_table, row_table, out_table.reshape(n_tile * n_src, portion, 2 * BAND)


COLS_IN, COLS_OUT = slice(0, 2 * BAND), slice(2 * BAND, 2 * BAND + 2 * GRID)
ROWS_IN = slice(COLS_OUT.stop, COLS_OUT.stop + GRID)
ROWS_OUT = slice(ROWS_IN.stop, ROWS_IN.stop + 2 * PUPIL)
GRID_ROWS = ROWS_OUT.stop


@functools.cache
def grid_tables(columns):
    points = np.arange(GRID)
    band = np.arange(BAND) - BAND // 2
    cos, sin = waves(points, band, GRID)
    cols_in = np.block([[cos.T, sin.T], [-sin.T, cos.T]])
    cols_out = np.block([[cos, -sin], [sin, cos]])
    cos, sin = waves(points, np.arange(PUPIL) - PUPIL // 2, GRID)
    rows_in = np.block([[cos, -sin, sin, cos]])
    rows_out = np.block([[cos.T, sin.T], [-sin.T, cos.T]])
    cos, sin = waves(np.arange(columns), band, columns)
    return low(np.concatenate([cols_in, cols_out, rows_in, rows_out, np.block([cos, -sin])], 0))


def dot(left, right):
    return jnp.dot(left, right, preferred_element_type=jnp.float32)


def forward_kernel(
    mask, cotangent, col_table, row_table,
    partial,
    mask_v, cot_v, col_v, row_v, sems,
):
    height, columns = mask.shape
    width = columns // CHUNKS
    tile = lax.axis_index("tile")
    chunk_copies = []
    for step in range(CHUNKS):
        part = pl.ds(step * width, width)
        copies = [
            pltpu.make_async_copy(col_table.at[part, :], col_v.at[part, :], sems.at[step, 0]),
            pltpu.make_async_copy(mask.at[:, part], mask_v.at[step], sems.at[step, 1]),
            pltpu.make_async_copy(cotangent.at[:, part], cot_v.at[step], sems.at[step, 2]),
        ]
        for copy in copies:
            copy.start()
        chunk_copies.append(copies)
    row_copy = pltpu.make_async_copy(row_table.at[tile], row_v, sems.at[CHUNKS, 0])
    row_copy.start()

    for step in range(CHUNKS):
        for copy in chunk_copies[step]:
            copy.wait()
        part = pl.ds(step * width, width)
        mask_add = dot(mask_v[step], col_v[part, : 2 * BAND])
        cot_add = dot(cot_v[step], col_v[part, 2 * BAND :])
        mask_part = mask_add if step == 0 else mask_part + mask_add
        cot_part = cot_add if step == 0 else cot_part + cot_add

    row_copy.wait()
    blocks = dot(row_v[: 2 * BAND, :], mask_part.astype(jnp.bfloat16))
    partial[:BAND, :] = blocks[:BAND, :BAND] + blocks[BAND:, BAND:]
    partial[BAND : 2 * BAND, :] = blocks[:BAND, BAND:] - blocks[BAND:, :BAND]
    partial[2 * BAND :, :] = dot(row_v[2 * BAND :, :], cot_part.astype(jnp.bfloat16))


def forward(mask, cotangent, col_table, row_table):
    height, columns = mask.shape
    width = columns // CHUNKS
    return pl.pallas_call(
        forward_kernel,
        out_shape=jax.ShapeDtypeStruct((SUMS, BAND), jnp.float32),
        in_specs=[HBM] * 4,
        out_specs=VMEM,
        scratch_shapes=[
            pltpu.VMEM((CHUNKS, height, width), jnp.bfloat16),
            pltpu.VMEM((CHUNKS, height, width), jnp.bfloat16),
            pltpu.VMEM(col_table.shape, jnp.bfloat16),
            pltpu.VMEM(row_table.shape[1:], jnp.bfloat16),
            pltpu.SemaphoreType.DMA((CHUNKS + 1, 3)),
        ],
        compiler_params=pltpu.CompilerParams(vmem_limit_bytes=GRANT),
        cost_estimate=pl.CostEstimate(
            flops=2 * height * columns * SUMS, bytes_accessed=6 * 1024 * 1024, transcendentals=0
        ),
        name="forward",
    )(mask, cotangent, col_table, row_table)


def list_kernel(ids, shift, weight, lines):
    lane = lax.broadcasted_iota(jnp.int32, (SLOTS, LANES), 1)
    place = lax.broadcasted_iota(jnp.int32, (SLOTS, LANES), 0)

    def one(row, carry):
        blocks, weights, there = [], [], jnp.zeros_like(lane)
        for slot in range(SLOTS):
            source = jnp.maximum(ids[row, slot], 0)
            start = pl.multiple_of(source // LANES * LANES, LANES)
            blocks.append(shift[:, pl.ds(start, LANES)])
            weights.append(weight[pl.ds(source // LANES, 1), :])
            there = jnp.where(place == slot, source % LANES, there)
        here = lane == there
        line = jnp.zeros((SLOTS, LANES), jnp.float32)
        for dim, into in ((0, OX), (1, OY)):
            values = jnp.concatenate([block[dim : dim + 1, :] for block in blocks], 0)
            found = jnp.sum(jnp.where(here, values.astype(jnp.float32), 0.0), 1, keepdims=True)
            line = jnp.where(lane == into, found, line)
        found = jnp.sum(jnp.where(here, jnp.concatenate(weights, 0), 0.0), 1, keepdims=True)
        line = jnp.where(lane == WEIGHT, found, line)
        for slot in range(SLOTS):
            used = jnp.where(ids[row, slot] >= 0, 1.0, 0.0)
            line = jnp.where((lane == USED) & (place == slot), used, line)
        lines[pl.ds(pl.multiple_of(row * SLOTS, SLOTS), SLOTS), :] = line
        return carry

    lax.fori_loop(0, ids.shape[0], one, jnp.int32(0), unroll=ids.shape[0] <= 4)


def slot_lines(ids, shift, weight):
    count = ids.size
    return pl.pallas_call(
        list_kernel,
        out_shape=jax.ShapeDtypeStruct((count, LANES), jnp.float32),
        in_specs=[SMEM, VMEM, VMEM],
        out_specs=VMEM,
        name="slot_lines",
    )(ids, shift, weight)


def adjoint_kernel(
    n_src, own, other, lines, pupil, table, out_table,
    result,
    spec, image, band, table_v, out_v, lines_s, list_x, list_y, list_w, sems,
):
    place = lax.axis_index("tile") * n_src + lax.axis_index("src")
    lines_copy = pltpu.make_async_copy(lines, lines_s, sems.at[0])
    small, columns = GRID_ROWS, table.shape[0] - GRID_ROWS
    grid_part, col_part = pl.ds(0, small), pl.ds(small, columns)
    grid_copy = pltpu.make_async_copy(table.at[grid_part, :], table_v.at[grid_part, :], sems.at[1])
    col_copy = pltpu.make_async_copy(table.at[col_part, :], table_v.at[col_part, :], sems.at[2])
    out_copy = pltpu.make_async_copy(out_table.at[place], out_v, sems.at[3])
    for copy in (lines_copy, grid_copy, col_copy, out_copy):
        copy.start()

    scale = 1.0 / math.sqrt(TILE_ROWS * COLS)
    whole = own[...] + other[...]
    spec[...] = (whole[: 2 * BAND] * scale).astype(jnp.bfloat16).astype(jnp.float32)
    image[:GRID, :] = whole[2 * BAND :]
    image[GRID:, :] = whole[2 * BAND :]
    band[...] = jnp.zeros_like(band)

    lines_copy.wait()

    def add(line, total):
        list_x[total] = lines_s[line, OX].astype(jnp.int32)
        list_y[total] = lines_s[line, OY].astype(jnp.int32)
        list_w[total] = lines_s[line, WEIGHT] * (2.0 / SLOTS / PUPIL / PUPIL)
        return total + lines_s[line, USED].astype(jnp.int32)

    count = lines.shape[0]
    total = lax.fori_loop(0, count, add, jnp.int32(0), unroll=count <= 32)
    for slot in range(GROUP):
        list_x[total + slot] = jnp.int32(0)
        list_y[total + slot] = jnp.int32(0)
        list_w[total + slot] = jnp.float32(0.0)
    grid_copy.wait()

    def group(step, carry):
        starts, pupils, amplitudes = [], [], []
        for slot in range(GROUP):
            index = step * GROUP + slot
            offset_x, offset_y = list_x[index], list_y[index]
            real = pltpu.roll(pupil[:PUPIL, :], offset_x, 1)
            imag = pltpu.roll(pupil[PUPIL:, :], offset_x, 1)
            spec_real = spec[pl.ds(offset_y, PUPIL), :]
            spec_imag = spec[pl.ds(BAND + offset_y, PUPIL), :]
            amp_real = real * spec_real - imag * spec_imag
            amp_imag = real * spec_imag + imag * spec_real
            starts.append(offset_y)
            pupils.append((real, imag, list_w[index]))
            amplitudes.append(jnp.concatenate([amp_real, amp_imag], 1).astype(jnp.bfloat16))
        halfway = dot(jnp.concatenate(amplitudes, 0), table_v[COLS_IN, :]).astype(jnp.bfloat16)
        halfway = jnp.concatenate(
            [
                jnp.concatenate(
                    [
                        halfway[slot * PUPIL : (slot + 1) * PUPIL, :GRID],
                        halfway[slot * PUPIL : (slot + 1) * PUPIL, GRID:],
                    ],
                    0,
                )
                for slot in range(GROUP)
            ],
            1,
        )
        rows_in = table_v[ROWS_IN, :]
        rows_in = jnp.concatenate([rows_in[:, : 2 * PUPIL], rows_in[:, 2 * PUPIL :]], 0)
        field = dot(rows_in, halfway)
        field_grad = jnp.concatenate(
            [
                (field[:, slot * GRID : (slot + 1) * GRID] * image[...]).astype(jnp.bfloat16)
                for slot in range(GROUP)
            ],
            1,
        )
        back = dot(table_v[ROWS_OUT, :], field_grad).astype(jnp.bfloat16)
        back = jnp.concatenate(
            [
                jnp.concatenate(
                    [
                        back[:PUPIL, slot * GRID : (slot + 1) * GRID],
                        back[PUPIL:, slot * GRID : (slot + 1) * GRID],
                    ],
                    1,
                )
                for slot in range(GROUP)
            ],
            0,
        )
        grad = dot(back, table_v[COLS_OUT, :])
        for slot in range(GROUP):
            real, imag, factor = pupils[slot]
            grad_real = grad[slot * PUPIL : (slot + 1) * PUPIL, :BAND] * factor
            grad_imag = grad[slot * PUPIL : (slot + 1) * PUPIL, BAND:] * factor
            rows = pl.ds(starts[slot], PUPIL)
            band[rows, :] = band[rows, :] + (real * grad_real + imag * grad_imag)
            rows = pl.ds(BAND + starts[slot], PUPIL)
            band[rows, :] = band[rows, :] + (real * grad_imag - imag * grad_real)
        return carry

    lax.fori_loop(0, (total + GROUP - 1) // GROUP, group, jnp.int32(0))

    col_copy.wait()
    out_copy.wait()
    real = band[:BAND, :] * scale
    imag = band[BAND:, :] * scale
    left = jnp.concatenate(
        [jnp.concatenate([real, imag], 1), jnp.concatenate([imag, -real], 1)], 0
    ).astype(jnp.bfloat16)
    mixed = dot(out_v[...].astype(jnp.bfloat16), left).astype(jnp.bfloat16)
    result[0] = lax.dot_general(
        mixed, table_v[col_part, :], (((1,), (1,)), ((), ())), preferred_element_type=jnp.float32
    )


def adjoint(own, other, lines, pupil, table, out_table, n_src):
    portion = out_table.shape[1]
    columns = table.shape[0] - GRID_ROWS
    places = lines.shape[0] + GROUP
    return pl.pallas_call(
        functools.partial(adjoint_kernel, n_src),
        out_shape=jax.ShapeDtypeStruct((1, portion, columns), jnp.float32),
        in_specs=[VMEM] * 4 + [HBM, HBM],
        out_specs=VMEM,
        scratch_shapes=[
            pltpu.VMEM((2 * BAND, BAND), jnp.float32),
            pltpu.VMEM((2 * GRID, GRID), jnp.float32),
            pltpu.VMEM((2 * BAND, BAND), jnp.float32),
            pltpu.VMEM(table.shape, jnp.bfloat16),
            pltpu.VMEM(out_table.shape[1:], jnp.float32),
            pltpu.SMEM(lines.shape, jnp.float32),
            pltpu.SMEM((places,), jnp.int32),
            pltpu.SMEM((places,), jnp.int32),
            pltpu.SMEM((places,), jnp.float32),
            pltpu.SemaphoreType.DMA((4,)),
        ],
        compiler_params=pltpu.CompilerParams(vmem_limit_bytes=GRANT),
        cost_estimate=pl.CostEstimate(
            flops=2 * 128 * 4096 * 256, bytes_accessed=4 * 1024 * 1024, transcendentals=0
        ),
        name="adjoint",
    )(own, other, lines, pupil, table, out_table)


def pupil_rows(phase):
    grid = jnp.arange(PUPIL, dtype=jnp.int32)
    radius = (2 * grid[:, None] - PUPIL + 1) ** 2 + (2 * grid[None, :] - PUPIL + 1) ** 2
    inside = radius <= PUPIL * PUPIL
    both = jnp.concatenate(
        [jnp.where(inside, jnp.cos(phase), 0.0), jnp.where(inside, jnp.sin(phase), 0.0)], 0
    )
    return jnp.pad(both, ((0, 0), (0, BAND - PUPIL)))


def swapped(array, sizes, steps):
    axes = tuple(sizes)
    places = np.arange(math.prod(sizes.values())).reshape(tuple(sizes.values()))
    there = places
    for dim, axis in enumerate(axes):
        there = np.take(there, np.arange(sizes[axis]) ^ steps.get(axis, 0), dim)
    turn = [(int(a), int(b)) for a, b in zip(places.ravel(), there.ravel())]
    return lax.ppermute(array, axes, turn)


def body(mask, cotangent, pupil_phase, source_weight, shift_table, source_ids, source_count):
    height, columns = mask.shape
    n_tile, n_src = lax.axis_size("tile"), lax.axis_size("src")
    col_table, row_table, out_table = image_tables(columns, height, n_tile, n_src)
    sizes = {"src": n_src, "tile": n_tile}
    used = jnp.arange(SLOTS, dtype=jnp.int32)[None, :] < source_count[0]
    ids = jnp.where(used, source_ids, -1)
    step = 1
    while step < n_src:
        ids = jnp.concatenate([ids, swapped(ids, sizes, {"src": step})], 0)
        step *= 2
    lines = slot_lines(ids, shift_table.T, source_weight.reshape(-1, LANES))
    own = forward(mask, cotangent, col_table, row_table)
    step = 1
    while step < n_tile // 2:
        own = own + swapped(own, sizes, {"tile": step})
        step *= 2
    other = swapped(own, sizes, {"tile": step})
    return adjoint(
        own, other, lines, pupil_rows(pupil_phase), grid_tables(columns), out_table, n_src
    )


def solution(mesh):
    placed = (
        P(("grp", "tile"), None),
        P(("grp", "tile"), None),
        P(),
        P(),
        P(),
        P(("grp", "src"), None),
        P(("grp", "src")),
    )
    return jax.shard_map(
        body, mesh=mesh, in_specs=placed, out_specs=P(("grp", "tile"), "src", None), check_vma=False
    )
```

```python
import functools
import math

import jax
import jax.numpy as jnp
import ml_dtypes
import numpy as np
from jax import lax
from jax.experimental import pallas as pl
from jax.experimental.pallas import tpu as pltpu
from jax.sharding import PartitionSpec as P

COLS = 2048
TILE_ROWS = 2048
BAND = 128
PUPIL = 64
SLOTS = 8
GRID = 128
CHUNKS = 4
GROUP = 8
OX, OY, WEIGHT, USED = range(4)
LANES = 128
SUMS = 2 * BAND + GRID
GRANT = 53 * 1024 * 1024

VMEM = pl.BlockSpec(memory_space=pltpu.VMEM)
SMEM = pl.BlockSpec(memory_space=pltpu.SMEM)
HBM = pl.BlockSpec(memory_space=pltpu.HBM)


def waves(positions, freqs, length):
    product = np.multiply.outer(positions, freqs) % length
    angle = product.astype(np.float64) * (2.0 * math.pi / length)
    return np.cos(angle), np.sin(angle)


def lowpass(positions, length):
    freqs = np.arange(1, PUPIL)
    step = length // GRID
    apart = np.arange(GRID)[None, :] * step - positions[:, None]
    product = (apart[:, :, None] * freqs) % length
    return (1.0 + 2.0 * np.cos(product * (2.0 * math.pi / length)).sum(2)) / GRID


def low(array):
    return np.ascontiguousarray(array).astype(ml_dtypes.bfloat16)


@functools.cache
def image_tables(columns, height, n_tile, n_src):
    band = np.arange(BAND) - BAND // 2
    cols = np.arange(columns)
    rows = np.arange(TILE_ROWS)
    cos, sin = waves(cols, band, columns)
    col_table = low(np.concatenate([cos, -sin, lowpass(cols, columns)], 1))
    cos, sin = waves(rows, band, TILE_ROWS)
    row_table = np.concatenate([cos, sin, lowpass(rows, TILE_ROWS)], 1)
    row_table = low(row_table.reshape(n_tile, height, 2 * BAND + GRID).transpose(0, 2, 1))
    portion = height // n_src
    out_table = np.concatenate([cos, -sin], 1).astype(np.float32)
    return col_table, row_table, out_table.reshape(n_tile * n_src, portion, 2 * BAND)


COLS_IN, COLS_OUT = slice(0, 2 * BAND), slice(2 * BAND, 2 * BAND + 2 * GRID)
ROWS_IN = slice(COLS_OUT.stop, COLS_OUT.stop + GRID)
ROWS_OUT = slice(ROWS_IN.stop, ROWS_IN.stop + 2 * PUPIL)
GRID_ROWS = ROWS_OUT.stop


@functools.cache
def grid_tables(columns):
    points = np.arange(GRID)
    band = np.arange(BAND) - BAND // 2
    cos, sin = waves(points, band, GRID)
    cols_in = np.block([[cos.T, sin.T], [-sin.T, cos.T]])
    cols_out = np.block([[cos, -sin], [sin, cos]])
    cos, sin = waves(points, np.arange(PUPIL) - PUPIL // 2, GRID)
    rows_in = np.block([[cos, -sin, sin, cos]])
    rows_out = np.block([[cos.T, sin.T], [-sin.T, cos.T]])
    cos, sin = waves(np.arange(columns), band, columns)
    return low(np.concatenate([cols_in, cols_out, rows_in, rows_out, np.block([cos, -sin])], 0))


def dot(left, right):
    return jnp.dot(left, right, preferred_element_type=jnp.float32)


def forward_kernel(
    mask, cotangent, col_table, row_table,
    partial, zeros,
    mask_v, cot_v, col_v, row_v, sems,
):
    height, columns = mask.shape
    width = columns // CHUNKS
    tile = lax.axis_index("tile")
    chunk_copies = []
    for step in range(CHUNKS):
        part = pl.ds(step * width, width)
        copies = [
            pltpu.make_async_copy(col_table.at[part, :], col_v.at[part, :], sems.at[step, 0]),
            pltpu.make_async_copy(mask.at[:, part], mask_v.at[step], sems.at[step, 1]),
            pltpu.make_async_copy(cotangent.at[:, part], cot_v.at[step], sems.at[step, 2]),
        ]
        for copy in copies:
            copy.start()
        chunk_copies.append(copies)
    row_copy = pltpu.make_async_copy(row_table.at[tile], row_v, sems.at[CHUNKS, 0])
    row_copy.start()

    for step in range(CHUNKS):
        for copy in chunk_copies[step]:
            copy.wait()
        part = pl.ds(step * width, width)
        mask_add = dot(mask_v[step], col_v[part, : 2 * BAND])
        cot_add = dot(cot_v[step], col_v[part, 2 * BAND :])
        mask_part = mask_add if step == 0 else mask_part + mask_add
        cot_part = cot_add if step == 0 else cot_part + cot_add

    row_copy.wait()
    blocks = dot(row_v[: 2 * BAND, :], mask_part.astype(jnp.bfloat16))
    partial[:BAND, :] = blocks[:BAND, :BAND] + blocks[BAND:, BAND:]
    partial[BAND : 2 * BAND, :] = blocks[:BAND, BAND:] - blocks[BAND:, :BAND]
    partial[2 * BAND :, :] = dot(row_v[2 * BAND :, :], cot_part.astype(jnp.bfloat16))
    zeros[...] = jnp.zeros_like(zeros)


def forward(mask, cotangent, col_table, row_table):
    height, columns = mask.shape
    width = columns // CHUNKS
    return pl.pallas_call(
        forward_kernel,
        out_shape=(
            jax.ShapeDtypeStruct((SUMS, BAND), jnp.float32),
            jax.ShapeDtypeStruct((1, SLOTS), jnp.int32),
        ),
        in_specs=[HBM] * 4,
        out_specs=(VMEM, VMEM),
        scratch_shapes=[
            pltpu.VMEM((CHUNKS, height, width), jnp.bfloat16),
            pltpu.VMEM((CHUNKS, height, width), jnp.bfloat16),
            pltpu.VMEM(col_table.shape, jnp.bfloat16),
            pltpu.VMEM(row_table.shape[1:], jnp.bfloat16),
            pltpu.SemaphoreType.DMA((CHUNKS + 1, 3)),
        ],
        compiler_params=pltpu.CompilerParams(vmem_limit_bytes=GRANT),
        cost_estimate=pl.CostEstimate(
            flops=2 * height * columns * SUMS, bytes_accessed=6 * 1024 * 1024, transcendentals=0
        ),
        name="forward",
    )(mask, cotangent, col_table, row_table)


def list_kernel(ids, shift, weight, lines):
    lane = lax.broadcasted_iota(jnp.int32, (SLOTS, LANES), 1)
    place = lax.broadcasted_iota(jnp.int32, (SLOTS, LANES), 0)

    def one(row, carry):
        blocks, weights, there = [], [], jnp.zeros_like(lane)
        for slot in range(SLOTS):
            source = jnp.maximum(ids[row, slot], 0)
            start = pl.multiple_of(source // LANES * LANES, LANES)
            blocks.append(shift[:, pl.ds(start, LANES)])
            weights.append(weight[pl.ds(source // LANES, 1), :])
            there = jnp.where(place == slot, source % LANES, there)
        here = lane == there
        line = jnp.zeros((SLOTS, LANES), jnp.float32)
        for dim, into in ((0, OX), (1, OY)):
            values = jnp.concatenate([block[dim : dim + 1, :] for block in blocks], 0)
            found = jnp.sum(jnp.where(here, values.astype(jnp.float32), 0.0), 1, keepdims=True)
            line = jnp.where(lane == into, found, line)
        found = jnp.sum(jnp.where(here, jnp.concatenate(weights, 0), 0.0), 1, keepdims=True)
        line = jnp.where(lane == WEIGHT, found, line)
        for slot in range(SLOTS):
            used = jnp.where(ids[row, slot] >= 0, 1.0, 0.0)
            line = jnp.where((lane == USED) & (place == slot), used, line)
        lines[pl.ds(pl.multiple_of(row * SLOTS, SLOTS), SLOTS), :] = line
        return carry

    lax.fori_loop(0, ids.shape[0], one, jnp.int32(0), unroll=ids.shape[0] <= 4)


def slot_lines(ids, shift, weight):
    count = ids.size
    return pl.pallas_call(
        list_kernel,
        out_shape=jax.ShapeDtypeStruct((count, LANES), jnp.float32),
        in_specs=[SMEM, VMEM, VMEM],
        out_specs=VMEM,
        compiler_params=pltpu.CompilerParams(vmem_limit_bytes=2 * 1024 * 1024),
        cost_estimate=pl.CostEstimate(flops=1, bytes_accessed=1, transcendentals=0),
        name="slot_lines",
    )(ids, shift, weight)


def adjoint_kernel(
    n_src, own, other, lines, pupil, table, out_table,
    result,
    spec, image, band, table_v, out_v, lines_s, list_x, list_y, list_w, sems,
):
    place = lax.axis_index("tile") * n_src + lax.axis_index("src")
    lines_copy = pltpu.make_async_copy(lines, lines_s, sems.at[0])
    small, columns = GRID_ROWS, table.shape[0] - GRID_ROWS
    grid_part, col_part = pl.ds(0, small), pl.ds(small, columns)
    grid_copy = pltpu.make_async_copy(table.at[grid_part, :], table_v.at[grid_part, :], sems.at[1])
    col_copy = pltpu.make_async_copy(table.at[col_part, :], table_v.at[col_part, :], sems.at[2])
    out_copy = pltpu.make_async_copy(out_table.at[place], out_v, sems.at[3])
    for copy in (lines_copy, grid_copy, col_copy, out_copy):
        copy.start()

    scale = 1.0 / math.sqrt(TILE_ROWS * COLS)
    whole = own[...] + other[...]
    spec[...] = (whole[: 2 * BAND] * scale).astype(jnp.bfloat16).astype(jnp.float32)
    image[:GRID, :] = whole[2 * BAND :]
    image[GRID:, :] = whole[2 * BAND :]
    band[...] = jnp.zeros_like(band)

    lines_copy.wait()

    def add(line, total):
        list_x[total] = lines_s[line, OX].astype(jnp.int32)
        list_y[total] = lines_s[line, OY].astype(jnp.int32)
        list_w[total] = lines_s[line, WEIGHT] * (2.0 / SLOTS / PUPIL / PUPIL)
        return total + lines_s[line, USED].astype(jnp.int32)

    count = lines.shape[0]
    total = lax.fori_loop(0, count, add, jnp.int32(0), unroll=count <= 32)
    for slot in range(GROUP):
        list_x[total + slot] = jnp.int32(0)
        list_y[total + slot] = jnp.int32(0)
        list_w[total + slot] = jnp.float32(0.0)
    grid_copy.wait()

    def group(step, carry):
        starts, pupils, amplitudes = [], [], []
        for slot in range(GROUP):
            index = step * GROUP + slot
            offset_x, offset_y = list_x[index], list_y[index]
            real = pltpu.roll(pupil[:PUPIL, :], offset_x, 1)
            imag = pltpu.roll(pupil[PUPIL:, :], offset_x, 1)
            spec_real = spec[pl.ds(offset_y, PUPIL), :]
            spec_imag = spec[pl.ds(BAND + offset_y, PUPIL), :]
            amp_real = real * spec_real - imag * spec_imag
            amp_imag = real * spec_imag + imag * spec_real
            starts.append(offset_y)
            pupils.append((real, imag, list_w[index]))
            amplitudes.append(jnp.concatenate([amp_real, amp_imag], 1).astype(jnp.bfloat16))
        halfway = dot(jnp.concatenate(amplitudes, 0), table_v[COLS_IN, :]).astype(jnp.bfloat16)
        halfway = jnp.concatenate(
            [
                jnp.concatenate(
                    [
                        halfway[slot * PUPIL : (slot + 1) * PUPIL, :GRID],
                        halfway[slot * PUPIL : (slot + 1) * PUPIL, GRID:],
                    ],
                    0,
                )
                for slot in range(GROUP)
            ],
            1,
        )
        rows_in = table_v[ROWS_IN, :]
        rows_in = jnp.concatenate([rows_in[:, : 2 * PUPIL], rows_in[:, 2 * PUPIL :]], 0)
        field = dot(rows_in, halfway)
        field_grad = jnp.concatenate(
            [
                (field[:, slot * GRID : (slot + 1) * GRID] * image[...]).astype(jnp.bfloat16)
                for slot in range(GROUP)
            ],
            1,
        )
        back = dot(table_v[ROWS_OUT, :], field_grad).astype(jnp.bfloat16)
        back = jnp.concatenate(
            [
                jnp.concatenate(
                    [
                        back[:PUPIL, slot * GRID : (slot + 1) * GRID],
                        back[PUPIL:, slot * GRID : (slot + 1) * GRID],
                    ],
                    1,
                )
                for slot in range(GROUP)
            ],
            0,
        )
        grad = dot(back, table_v[COLS_OUT, :])
        for slot in range(GROUP):
            real, imag, factor = pupils[slot]
            grad_real = grad[slot * PUPIL : (slot + 1) * PUPIL, :BAND] * factor
            grad_imag = grad[slot * PUPIL : (slot + 1) * PUPIL, BAND:] * factor
            rows = pl.ds(starts[slot], PUPIL)
            band[rows, :] = band[rows, :] + (real * grad_real + imag * grad_imag)
            rows = pl.ds(BAND + starts[slot], PUPIL)
            band[rows, :] = band[rows, :] + (real * grad_imag - imag * grad_real)
        return carry

    lax.fori_loop(0, (total + GROUP - 1) // GROUP, group, jnp.int32(0))

    col_copy.wait()
    out_copy.wait()
    real = band[:BAND, :] * scale
    imag = band[BAND:, :] * scale
    left = jnp.concatenate(
        [jnp.concatenate([real, imag], 1), jnp.concatenate([imag, -real], 1)], 0
    ).astype(jnp.bfloat16)
    mixed = dot(out_v[...].astype(jnp.bfloat16), left).astype(jnp.bfloat16)
    result[0] = lax.dot_general(
        mixed, table_v[col_part, :], (((1,), (1,)), ((), ())), preferred_element_type=jnp.float32
    )


def adjoint(own, other, lines, pupil, table, out_table, n_src):
    portion = out_table.shape[1]
    columns = table.shape[0] - GRID_ROWS
    places = lines.shape[0] + GROUP
    return pl.pallas_call(
        functools.partial(adjoint_kernel, n_src),
        out_shape=jax.ShapeDtypeStruct((1, portion, columns), jnp.float32),
        in_specs=[VMEM] * 4 + [HBM, HBM],
        out_specs=VMEM,
        scratch_shapes=[
            pltpu.VMEM((2 * BAND, BAND), jnp.float32),
            pltpu.VMEM((2 * GRID, GRID), jnp.float32),
            pltpu.VMEM((2 * BAND, BAND), jnp.float32),
            pltpu.VMEM(table.shape, jnp.bfloat16),
            pltpu.VMEM(out_table.shape[1:], jnp.float32),
            pltpu.SMEM(lines.shape, jnp.float32),
            pltpu.SMEM((places,), jnp.int32),
            pltpu.SMEM((places,), jnp.int32),
            pltpu.SMEM((places,), jnp.float32),
            pltpu.SemaphoreType.DMA((4,)),
        ],
        compiler_params=pltpu.CompilerParams(vmem_limit_bytes=GRANT),
        cost_estimate=pl.CostEstimate(
            flops=2 * 128 * 4096 * 256, bytes_accessed=4 * 1024 * 1024, transcendentals=0
        ),
        name="adjoint",
    )(own, other, lines, pupil, table, out_table)


def pupil_rows(phase):
    grid = jnp.arange(PUPIL, dtype=jnp.int32)
    radius = (2 * grid[:, None] - PUPIL + 1) ** 2 + (2 * grid[None, :] - PUPIL + 1) ** 2
    inside = radius <= PUPIL * PUPIL
    both = jnp.concatenate(
        [jnp.where(inside, jnp.cos(phase), 0.0), jnp.where(inside, jnp.sin(phase), 0.0)], 0
    )
    return jnp.pad(both, ((0, 0), (0, BAND - PUPIL)))


def swapped(array, sizes, steps):
    axes = tuple(sizes)
    places = np.arange(math.prod(sizes.values())).reshape(tuple(sizes.values()))
    there = places
    for dim, axis in enumerate(axes):
        there = np.take(there, np.arange(sizes[axis]) ^ steps.get(axis, 0), dim)
    turn = [(int(a), int(b)) for a, b in zip(places.ravel(), there.ravel())]
    return lax.ppermute(array, axes, turn)


def body(mask, cotangent, pupil_phase, source_weight, shift_table, source_ids, source_count):
    height, columns = mask.shape
    n_tile, n_src = lax.axis_size("tile"), lax.axis_size("src")
    col_table, row_table, out_table = image_tables(columns, height, n_tile, n_src)
    sizes = {"src": n_src, "tile": n_tile}
    own, zeros = forward(mask, cotangent, col_table, row_table)
    used = jnp.arange(SLOTS, dtype=jnp.int32)[None, :] < source_count[0]
    ids = jnp.where(used, source_ids, -1) + zeros
    step = 1
    while step < n_src:
        ids = jnp.concatenate([ids, swapped(ids, sizes, {"src": step})], 0)
        step *= 2
    lines = slot_lines(ids, shift_table.T, source_weight.reshape(-1, LANES))
    step = 1
    while step < n_tile // 2:
        own = own + swapped(own, sizes, {"tile": step})
        step *= 2
    other = swapped(own, sizes, {"tile": step})
    return adjoint(
        own, other, lines, pupil_rows(pupil_phase), grid_tables(columns), out_table, n_src
    )


def solution(mesh):
    placed = (
        P(("grp", "tile"), None),
        P(("grp", "tile"), None),
        P(),
        P(),
        P(),
        P(("grp", "src"), None),
        P(("grp", "src")),
    )
    return jax.shard_map(
        body, mesh=mesh, in_specs=placed, out_specs=P(("grp", "tile"), "src", None), check_vma=False
    )
```

```python
import functools
import math

import jax
import jax.numpy as jnp
import ml_dtypes
import numpy as np
from jax import lax
from jax.experimental import pallas as pl
from jax.experimental.pallas import tpu as pltpu
from jax.sharding import PartitionSpec as P

COLS = 2048
TILE_ROWS = 2048
BAND = 128
PUPIL = 64
SLOTS = 8
GRID = 128
CHUNKS = 4
GROUP = 24
OX, OY, WEIGHT, USED = range(4)
TOTAL = 2
PARTS = 4
LANES = 128
SUMS = 2 * BAND + GRID
GRANT = 53 * 1024 * 1024

VMEM = pl.BlockSpec(memory_space=pltpu.VMEM)
SMEM = pl.BlockSpec(memory_space=pltpu.SMEM)
HBM = pl.BlockSpec(memory_space=pltpu.HBM)


def waves(positions, freqs, length):
    product = np.multiply.outer(positions, freqs) % length
    angle = product.astype(np.float64) * (2.0 * math.pi / length)
    return np.cos(angle), np.sin(angle)


def lowpass(positions, length):
    freqs = np.arange(1, PUPIL)
    step = length // GRID
    apart = np.arange(GRID)[None, :] * step - positions[:, None]
    product = (apart[:, :, None] * freqs) % length
    return (1.0 + 2.0 * np.cos(product * (2.0 * math.pi / length)).sum(2)) / GRID


def low(array):
    return np.ascontiguousarray(array).astype(ml_dtypes.bfloat16)


@functools.cache
def image_tables(columns, height, n_tile, n_src):
    band = np.arange(BAND) - BAND // 2
    cols = np.arange(columns)
    rows = np.arange(TILE_ROWS)
    cos, sin = waves(cols, band, columns)
    col_table = low(np.concatenate([cos, -sin, lowpass(cols, columns)], 1))
    cos, sin = waves(rows, band, TILE_ROWS)
    row_table = np.concatenate([cos, sin, lowpass(rows, TILE_ROWS)], 1)
    row_table = low(row_table.reshape(n_tile, height, 2 * BAND + GRID).transpose(0, 2, 1))
    portion = height // n_src
    out_table = np.concatenate([cos, -sin], 1).astype(np.float32)
    out_table = out_table.reshape(n_tile * n_src, portion, 2 * BAND)
    cos, sin = waves(cols, band, columns)
    return col_table, row_table, out_table, low(np.concatenate([cos, -sin], 1).T)


COLS_IN, COLS_OUT = slice(0, 2 * BAND), slice(2 * BAND, 2 * BAND + 2 * GRID)
ROWS_IN = slice(COLS_OUT.stop, COLS_OUT.stop + GRID)
ROWS_OUT = slice(ROWS_IN.stop, ROWS_IN.stop + 2 * PUPIL)


@functools.cache
def grid_tables():
    points = np.arange(GRID)
    band = np.arange(BAND) - BAND // 2
    cos, sin = waves(points, band, GRID)
    cols_in = np.block([[cos.T, sin.T], [-sin.T, cos.T]])
    cols_out = np.block([[cos, -sin], [sin, cos]])
    cos, sin = waves(points, np.arange(PUPIL) - PUPIL // 2, GRID)
    rows_in = np.block([[cos, -sin, sin, cos]])
    rows_out = np.block([[cos.T, sin.T], [-sin.T, cos.T]])
    return low(np.concatenate([cols_in, cols_out, rows_in, rows_out], 0))


def dot(left, right):
    return jnp.dot(left, right, preferred_element_type=jnp.float32)


def forward_kernel(
    mask, cotangent, col_table, row_table,
    partial, zeros,
    mask_v, cot_v, col_v, row_v, sems,
):
    height, columns = mask.shape
    width = columns // CHUNKS
    tile = lax.axis_index("tile")
    chunk_copies = []
    for step in range(CHUNKS):
        part = pl.ds(step * width, width)
        copies = [
            pltpu.make_async_copy(col_table.at[part, :], col_v.at[part, :], sems.at[step, 0]),
            pltpu.make_async_copy(mask.at[:, part], mask_v.at[step], sems.at[step, 1]),
            pltpu.make_async_copy(cotangent.at[:, part], cot_v.at[step], sems.at[step, 2]),
        ]
        for copy in copies:
            copy.start()
        chunk_copies.append(copies)
    row_copy = pltpu.make_async_copy(row_table.at[tile], row_v, sems.at[CHUNKS, 0])
    row_copy.start()

    for step in range(CHUNKS):
        for copy in chunk_copies[step]:
            copy.wait()
        part = pl.ds(step * width, width)
        mask_add = dot(mask_v[step], col_v[part, : 2 * BAND])
        cot_add = dot(cot_v[step], col_v[part, 2 * BAND :])
        mask_part = mask_add if step == 0 else mask_part + mask_add
        cot_part = cot_add if step == 0 else cot_part + cot_add

    row_copy.wait()
    blocks = dot(row_v[: 2 * BAND, :], mask_part.astype(jnp.bfloat16))
    partial[:BAND, :] = blocks[:BAND, :BAND] + blocks[BAND:, BAND:]
    partial[BAND : 2 * BAND, :] = blocks[:BAND, BAND:] - blocks[BAND:, :BAND]
    partial[2 * BAND :, :] = dot(row_v[2 * BAND :, :], cot_part.astype(jnp.bfloat16))
    zeros[...] = jnp.zeros_like(zeros)


def forward(mask, cotangent, col_table, row_table):
    height, columns = mask.shape
    width = columns // CHUNKS
    return pl.pallas_call(
        forward_kernel,
        out_shape=(
            jax.ShapeDtypeStruct((SUMS, BAND), jnp.float32),
            jax.ShapeDtypeStruct((1, SLOTS), jnp.int32),
        ),
        in_specs=[HBM] * 4,
        out_specs=(VMEM, VMEM),
        scratch_shapes=[
            pltpu.VMEM((CHUNKS, height, width), jnp.bfloat16),
            pltpu.VMEM((CHUNKS, height, width), jnp.bfloat16),
            pltpu.VMEM(col_table.shape, jnp.bfloat16),
            pltpu.VMEM(row_table.shape[1:], jnp.bfloat16),
            pltpu.SemaphoreType.DMA((CHUNKS + 1, 3)),
        ],
        compiler_params=pltpu.CompilerParams(vmem_limit_bytes=GRANT),
        cost_estimate=pl.CostEstimate(
            flops=2 * height * columns * SUMS, bytes_accessed=6 * 1024 * 1024, transcendentals=0
        ),
        name="forward",
    )(mask, cotangent, col_table, row_table)


def list_kernel(*refs):
    *id_parts, shift, weight, offsets, factors, lines, lines_s, sem = refs
    lane = lax.broadcasted_iota(jnp.int32, (SLOTS, LANES), 1)
    place = lax.broadcasted_iota(jnp.int32, (SLOTS, LANES), 0)

    def line_block(ids, row):
        blocks, weights, there = [], [], jnp.zeros_like(lane)
        for slot in range(SLOTS):
            source = jnp.maximum(ids[row, slot], 0)
            start = pl.multiple_of(source // LANES * LANES, LANES)
            blocks.append(shift[:, pl.ds(start, LANES)])
            weights.append(weight[pl.ds(source // LANES, 1), :])
            there = jnp.where(place == slot, source % LANES, there)
        here = lane == there
        line = jnp.zeros((SLOTS, LANES), jnp.float32)
        for dim, into in ((0, OX), (1, OY)):
            values = jnp.concatenate([block[dim : dim + 1, :] for block in blocks], 0)
            found = jnp.sum(jnp.where(here, values.astype(jnp.float32), 0.0), 1, keepdims=True)
            line = jnp.where(lane == into, found, line)
        found = jnp.sum(jnp.where(here, jnp.concatenate(weights, 0), 0.0), 1, keepdims=True)
        line = jnp.where(lane == WEIGHT, found, line)
        for slot in range(SLOTS):
            used = jnp.where(ids[row, slot] >= 0, 1.0, 0.0)
            line = jnp.where((lane == USED) & (place == slot), used, line)
        return line

    first = 0
    for ids in id_parts:
        rows = ids.shape[0]

        def one(row, carry, ids=ids, first=first):
            start = pl.multiple_of((first + row) * SLOTS, SLOTS)
            lines[pl.ds(start, SLOTS), :] = line_block(ids, row)
            return carry

        lax.fori_loop(0, rows, one, jnp.int32(0), unroll=rows <= 4)
        first += rows

    copy = pltpu.make_async_copy(lines, lines_s, sem)
    copy.start()
    copy.wait()

    def add(line, total):
        offsets[OX, total] = lines_s[line, OX].astype(jnp.int32)
        offsets[OY, total] = lines_s[line, OY].astype(jnp.int32)
        factors[total] = lines_s[line, WEIGHT] * (2.0 / SLOTS / PUPIL / PUPIL)
        return total + lines_s[line, USED].astype(jnp.int32)

    count = lines.shape[0]
    total = lax.fori_loop(0, count, add, jnp.int32(0), unroll=count <= 32)
    offsets[TOTAL, 0] = total
    for slot in range(GROUP):
        offsets[OX, total + slot] = jnp.int32(0)
        offsets[OY, total + slot] = jnp.int32(0)
        factors[total + slot] = jnp.float32(0.0)


def used_slots(id_parts, shift, weight):
    count = sum(ids.size for ids in id_parts)
    places = count + GROUP
    return pl.pallas_call(
        list_kernel,
        out_shape=(
            jax.ShapeDtypeStruct((3, places), jnp.int32),
            jax.ShapeDtypeStruct((places,), jnp.float32),
        ),
        in_specs=[SMEM] * len(id_parts) + [VMEM, VMEM],
        out_specs=(SMEM, SMEM),
        scratch_shapes=[
            pltpu.VMEM((count, LANES), jnp.float32),
            pltpu.SMEM((count, LANES), jnp.float32),
            pltpu.SemaphoreType.DMA,
        ],
        compiler_params=pltpu.CompilerParams(vmem_limit_bytes=2 * 1024 * 1024),
        cost_estimate=pl.CostEstimate(flops=1, bytes_accessed=1, transcendentals=0),
        name="used_slots",
    )(*id_parts, shift, weight)


def adjoint_kernel(
    n_src, own, other, offsets, factors, pupil, table, col_table, out_table,
    result,
    spec_real, spec_imag, image, table_v, col_v, out_v, result_v, sems, out_sems, *bands,
):
    place = lax.axis_index("tile") * n_src + lax.axis_index("src")
    grid_copy = pltpu.make_async_copy(table, table_v, sems.at[0])
    out_copy = pltpu.make_async_copy(out_table.at[place], out_v, sems.at[1])
    col_copy = pltpu.make_async_copy(col_table, col_v, sems.at[2])
    for copy in (grid_copy, out_copy, col_copy):
        copy.start()

    scale = 1.0 / math.sqrt(TILE_ROWS * COLS)
    whole = own[...] + other[...]
    spec = (whole[: 2 * BAND] * scale).astype(jnp.bfloat16).astype(jnp.float32)
    spec_real[...] = spec[:BAND]
    spec_imag[...] = spec[BAND:]
    image[:GRID, :] = whole[2 * BAND :]
    image[GRID:, :] = whole[2 * BAND :]
    for band in bands:
        band[...] = jnp.zeros_like(band)
    total = offsets[TOTAL, 0]
    grid_copy.wait()

    def group(step, carry):
        starts, pupils, amplitudes = [], [], []
        for slot in range(GROUP):
            index = step * GROUP + slot
            offset_x, offset_y = offsets[OX, index], offsets[OY, index]
            real = pltpu.roll(pupil[:PUPIL, :], offset_x, 1)
            imag = pltpu.roll(pupil[PUPIL:, :], offset_x, 1)
            rows = pl.ds(offset_y, PUPIL)
            amp_real = real * spec_real[rows, :] - imag * spec_imag[rows, :]
            amp_imag = real * spec_imag[rows, :] + imag * spec_real[rows, :]
            starts.append(offset_y)
            pupils.append((real, imag, factors[index]))
            amplitudes.append(jnp.concatenate([amp_real, amp_imag], 1).astype(jnp.bfloat16))
        halfway = dot(jnp.concatenate(amplitudes, 0), table_v[COLS_IN, :]).astype(jnp.bfloat16)
        halfway = jnp.concatenate(
            [
                jnp.concatenate(
                    [
                        halfway[slot * PUPIL : (slot + 1) * PUPIL, :GRID],
                        halfway[slot * PUPIL : (slot + 1) * PUPIL, GRID:],
                    ],
                    0,
                )
                for slot in range(GROUP)
            ],
            1,
        )
        rows_in = table_v[ROWS_IN, :]
        rows_in = jnp.concatenate([rows_in[:, : 2 * PUPIL], rows_in[:, 2 * PUPIL :]], 0)
        field = dot(rows_in, halfway)
        field_grad = jnp.concatenate(
            [
                (field[:, slot * GRID : (slot + 1) * GRID] * image[...]).astype(jnp.bfloat16)
                for slot in range(GROUP)
            ],
            1,
        )
        back = dot(table_v[ROWS_OUT, :], field_grad).astype(jnp.bfloat16)
        back = jnp.concatenate(
            [
                jnp.concatenate(
                    [
                        back[:PUPIL, slot * GRID : (slot + 1) * GRID],
                        back[PUPIL:, slot * GRID : (slot + 1) * GRID],
                    ],
                    1,
                )
                for slot in range(GROUP)
            ],
            0,
        )
        grad = dot(back, table_v[COLS_OUT, :])
        for slot in range(GROUP):
            real, imag, factor = pupils[slot]
            grad_real = grad[slot * PUPIL : (slot + 1) * PUPIL, :BAND] * factor
            grad_imag = grad[slot * PUPIL : (slot + 1) * PUPIL, BAND:] * factor
            rows = pl.ds(starts[slot], PUPIL)
            band_real, band_imag = bands[slot % 2], bands[2 + slot % 2]
            band_real[rows, :] = band_real[rows, :] + (real * grad_real + imag * grad_imag)
            band_imag[rows, :] = band_imag[rows, :] + (real * grad_imag - imag * grad_real)
        return carry

    lax.fori_loop(0, (total + GROUP - 1) // GROUP, group, jnp.int32(0))

    real = (bands[0][...] + bands[1][...]) * scale
    imag = (bands[2][...] + bands[3][...]) * scale
    left = jnp.concatenate(
        [jnp.concatenate([real, imag], 1), jnp.concatenate([imag, -real], 1)], 0
    ).astype(jnp.bfloat16)
    out_copy.wait()
    mixed = dot(out_v[...].astype(jnp.bfloat16), left).astype(jnp.bfloat16)
    col_copy.wait()
    width = result.shape[2] // PARTS
    copies = []
    for step in range(PARTS):
        part = pl.ds(step * width, width)
        result_v[:, part] = dot(mixed, col_v[:, part])
        copy = pltpu.make_async_copy(
            result_v.at[:, part], result.at[0, :, part], out_sems.at[step]
        )
        copy.start()
        copies.append(copy)
    for copy in copies:
        copy.wait()


def adjoint(own, other, offsets, factors, pupil, table, col_table, out_table, n_src):
    portion = out_table.shape[1]
    columns = col_table.shape[1]
    band = pltpu.VMEM((BAND, BAND), jnp.float32)
    return pl.pallas_call(
        functools.partial(adjoint_kernel, n_src),
        out_shape=jax.ShapeDtypeStruct((1, portion, columns), jnp.float32),
        in_specs=[VMEM, VMEM, SMEM, SMEM, VMEM, HBM, HBM, HBM],
        out_specs=HBM,
        scratch_shapes=[
            band,
            band,
            pltpu.VMEM((2 * GRID, GRID), jnp.float32),
            pltpu.VMEM(table.shape, jnp.bfloat16),
            pltpu.VMEM(col_table.shape, jnp.bfloat16),
            pltpu.VMEM(out_table.shape[1:], jnp.float32),
            pltpu.VMEM((portion, columns), jnp.float32),
            pltpu.SemaphoreType.DMA((3,)),
            pltpu.SemaphoreType.DMA((PARTS,)),
            band,
            band,
            band,
            band,
        ],
        compiler_params=pltpu.CompilerParams(vmem_limit_bytes=GRANT),
        cost_estimate=pl.CostEstimate(
            flops=2 * 128 * 4096 * 256, bytes_accessed=4 * 1024 * 1024, transcendentals=0
        ),
        name="adjoint",
    )(own, other, offsets, factors, pupil, table, col_table, out_table)


def pupil_rows(phase):
    grid = jnp.arange(PUPIL, dtype=jnp.int32)
    radius = (2 * grid[:, None] - PUPIL + 1) ** 2 + (2 * grid[None, :] - PUPIL + 1) ** 2
    inside = radius <= PUPIL * PUPIL
    both = jnp.concatenate(
        [jnp.where(inside, jnp.cos(phase), 0.0), jnp.where(inside, jnp.sin(phase), 0.0)], 0
    )
    return jnp.pad(both, ((0, 0), (0, BAND - PUPIL)))


def swapped(array, sizes, steps):
    axes = tuple(sizes)
    places = np.arange(math.prod(sizes.values())).reshape(tuple(sizes.values()))
    there = places
    for dim, axis in enumerate(axes):
        there = np.take(there, np.arange(sizes[axis]) ^ steps.get(axis, 0), dim)
    turn = [(int(a), int(b)) for a, b in zip(places.ravel(), there.ravel())]
    return lax.ppermute(array, axes, turn)


def body(mask, cotangent, pupil_phase, source_weight, shift_table, source_ids, source_count):
    height, columns = mask.shape
    n_tile, n_src = lax.axis_size("tile"), lax.axis_size("src")
    col_table, row_table, out_table, out_cols = image_tables(columns, height, n_tile, n_src)
    sizes = {"src": n_src, "tile": n_tile}
    own, zeros = forward(mask, cotangent, col_table, row_table)
    used = jnp.arange(SLOTS, dtype=jnp.int32)[None, :] < source_count[0]
    ids = jnp.where(used, source_ids, -1) + zeros
    id_parts = (ids,)
    step = 1
    while step < n_src:
        ids = jnp.concatenate(id_parts, 0) if len(id_parts) > 1 else ids
        id_parts = (ids, swapped(ids, sizes, {"src": step}))
        step *= 2
    offsets, factors = used_slots(
        id_parts, shift_table.T, source_weight.reshape(-1, LANES)
    )
    step = 1
    while step < n_tile // 2:
        own = own + swapped(own, sizes, {"tile": step})
        step *= 2
    other = swapped(own, sizes, {"tile": step})
    pupil = pupil_rows(pupil_phase)
    return adjoint(own, other, offsets, factors, pupil, grid_tables(), out_cols, out_table, n_src)


def solution(mesh):
    placed = (
        P(("grp", "tile"), None),
        P(("grp", "tile"), None),
        P(),
        P(),
        P(),
        P(("grp", "src"), None),
        P(("grp", "src")),
    )
    return jax.shard_map(
        body, mesh=mesh, in_specs=placed, out_specs=P(("grp", "tile"), "src", None), check_vma=False
    )
```

```python
import functools
import math

import jax
import jax.numpy as jnp
import ml_dtypes
import numpy as np
from jax import lax
from jax.experimental import pallas as pl
from jax.experimental.pallas import tpu as pltpu
from jax.sharding import PartitionSpec as P

COLS = 2048
TILE_ROWS = 2048
BAND = 128
PUPIL = 64
SLOTS = 8
GRID = 128
CHUNKS = 4
GROUP = 32
OX, OY, FACTOR = range(3)
PARTS = 4
LANES = 128
SUMS = 2 * BAND + GRID
GRANT = 53 * 1024 * 1024

VMEM = pl.BlockSpec(memory_space=pltpu.VMEM)
SMEM = pl.BlockSpec(memory_space=pltpu.SMEM)
HBM = pl.BlockSpec(memory_space=pltpu.HBM)


def waves(positions, freqs, length):
    product = np.multiply.outer(positions, freqs) % length
    angle = product.astype(np.float64) * (2.0 * math.pi / length)
    return np.cos(angle), np.sin(angle)


def lowpass(positions, length):
    freqs = np.arange(1, PUPIL)
    step = length // GRID
    apart = np.arange(GRID)[None, :] * step - positions[:, None]
    product = (apart[:, :, None] * freqs) % length
    return (1.0 + 2.0 * np.cos(product * (2.0 * math.pi / length)).sum(2)) / GRID


def low(array):
    return np.ascontiguousarray(array).astype(ml_dtypes.bfloat16)


@functools.cache
def image_tables(columns, height, n_tile, n_src):
    band = np.arange(BAND) - BAND // 2
    cols = np.arange(columns)
    rows = np.arange(TILE_ROWS)
    cos, sin = waves(cols, band, columns)
    col_table = low(np.concatenate([cos, -sin, lowpass(cols, columns)], 1))
    cos, sin = waves(rows, band, TILE_ROWS)
    row_table = np.concatenate([cos, sin, lowpass(rows, TILE_ROWS)], 1)
    row_table = low(row_table.reshape(n_tile, height, 2 * BAND + GRID).transpose(0, 2, 1))
    portion = height // n_src
    out_table = np.concatenate([cos, -sin], 1).astype(np.float32)
    out_table = out_table.reshape(n_tile * n_src, portion, 2 * BAND)
    cos, sin = waves(cols, band, columns)
    return col_table, row_table, out_table, low(np.concatenate([cos, -sin], 1).T)


COLS_IN, COLS_OUT = slice(0, 2 * BAND), slice(2 * BAND, 2 * BAND + 2 * GRID)
ROWS_IN = slice(COLS_OUT.stop, COLS_OUT.stop + GRID)
ROWS_OUT = slice(ROWS_IN.stop, ROWS_IN.stop + 2 * PUPIL)


@functools.cache
def grid_tables():
    points = np.arange(GRID)
    band = np.arange(BAND) - BAND // 2
    cos, sin = waves(points, band, GRID)
    cols_in = np.block([[cos.T, sin.T], [-sin.T, cos.T]])
    cols_out = np.block([[cos, -sin], [sin, cos]])
    cos, sin = waves(points, np.arange(PUPIL) - PUPIL // 2, GRID)
    rows_in = np.block([[cos, -sin, sin, cos]])
    rows_out = np.block([[cos.T, sin.T], [-sin.T, cos.T]])
    return low(np.concatenate([cols_in, cols_out, rows_in, rows_out], 0))


def dot(left, right):
    return jnp.dot(left, right, preferred_element_type=jnp.float32)


def forward_kernel(
    mask, cotangent, col_table, row_table,
    partial, zeros,
    mask_v, cot_v, col_v, row_v, sems,
):
    height, columns = mask.shape
    width = columns // CHUNKS
    tile = lax.axis_index("tile")
    chunk_copies = []
    for step in range(CHUNKS):
        part = pl.ds(step * width, width)
        copies = [
            pltpu.make_async_copy(col_table.at[part, :], col_v.at[part, :], sems.at[step, 0]),
            pltpu.make_async_copy(mask.at[:, part], mask_v.at[step], sems.at[step, 1]),
            pltpu.make_async_copy(cotangent.at[:, part], cot_v.at[step], sems.at[step, 2]),
        ]
        for copy in copies:
            copy.start()
        chunk_copies.append(copies)
    row_copy = pltpu.make_async_copy(row_table.at[tile], row_v, sems.at[CHUNKS, 0])
    row_copy.start()

    for step in range(CHUNKS):
        for copy in chunk_copies[step]:
            copy.wait()
        part = pl.ds(step * width, width)
        mask_add = dot(mask_v[step], col_v[part, : 2 * BAND])
        cot_add = dot(cot_v[step], col_v[part, 2 * BAND :])
        mask_part = mask_add if step == 0 else mask_part + mask_add
        cot_part = cot_add if step == 0 else cot_part + cot_add

    row_copy.wait()
    blocks = dot(row_v[: 2 * BAND, :], mask_part.astype(jnp.bfloat16))
    partial[:BAND, :] = blocks[:BAND, :BAND] + blocks[BAND:, BAND:]
    partial[BAND : 2 * BAND, :] = blocks[:BAND, BAND:] - blocks[BAND:, :BAND]
    partial[2 * BAND :, :] = dot(row_v[2 * BAND :, :], cot_part.astype(jnp.bfloat16))
    zeros[...] = jnp.zeros_like(zeros)


def forward(mask, cotangent, col_table, row_table):
    height, columns = mask.shape
    width = columns // CHUNKS
    return pl.pallas_call(
        forward_kernel,
        out_shape=(
            jax.ShapeDtypeStruct((SUMS, BAND), jnp.float32),
            jax.ShapeDtypeStruct((1, SLOTS), jnp.int32),
        ),
        in_specs=[HBM] * 4,
        out_specs=(VMEM, VMEM),
        scratch_shapes=[
            pltpu.VMEM((CHUNKS, height, width), jnp.bfloat16),
            pltpu.VMEM((CHUNKS, height, width), jnp.bfloat16),
            pltpu.VMEM(col_table.shape, jnp.bfloat16),
            pltpu.VMEM(row_table.shape[1:], jnp.bfloat16),
            pltpu.SemaphoreType.DMA((CHUNKS + 1, 3)),
        ],
        compiler_params=pltpu.CompilerParams(vmem_limit_bytes=GRANT),
        cost_estimate=pl.CostEstimate(
            flops=2 * height * columns * SUMS, bytes_accessed=6 * 1024 * 1024, transcendentals=0
        ),
        name="forward",
    )(mask, cotangent, col_table, row_table)


def lines_kernel(ids, shift, weight, lines):
    lane = lax.broadcasted_iota(jnp.int32, (SLOTS, LANES), 1)
    place = lax.broadcasted_iota(jnp.int32, (SLOTS, LANES), 0)

    def one(row, carry):
        blocks, weights, there = [], [], jnp.full_like(lane, -1)
        for slot in range(SLOTS):
            source = jnp.maximum(ids[row, slot], 0)
            start = pl.multiple_of(source // LANES * LANES, LANES)
            blocks.append(shift[:, pl.ds(start, LANES)])
            weights.append(weight[pl.ds(source // LANES, 1), :])
            found = jnp.where(ids[row, slot] >= 0, source % LANES, -1)
            there = jnp.where(place == slot, found, there)
        here = lane == there
        line = jnp.zeros((SLOTS, LANES), jnp.float32)
        for dim, into in ((0, OX), (1, OY)):
            values = jnp.concatenate([block[dim : dim + 1, :] for block in blocks], 0)
            found = jnp.sum(jnp.where(here, values.astype(jnp.float32), 0.0), 1, keepdims=True)
            line = jnp.where(lane == into, found, line)
        found = jnp.sum(jnp.where(here, jnp.concatenate(weights, 0), 0.0), 1, keepdims=True)
        line = jnp.where(lane == FACTOR, found * (2.0 / SLOTS / PUPIL / PUPIL), line)
        lines[pl.ds(pl.multiple_of(row * SLOTS, SLOTS), SLOTS), :] = line
        return carry

    lax.fori_loop(0, ids.shape[0], one, jnp.int32(0), unroll=ids.shape[0] <= 4)


def slot_lines(ids, shift, weight):
    return pl.pallas_call(
        lines_kernel,
        out_shape=jax.ShapeDtypeStruct((ids.size, LANES), jnp.float32),
        in_specs=[SMEM, VMEM, VMEM],
        out_specs=VMEM,
        compiler_params=pltpu.CompilerParams(vmem_limit_bytes=2 * 1024 * 1024),
        cost_estimate=pl.CostEstimate(flops=1, bytes_accessed=1, transcendentals=0),
        name="slot_lines",
    )(ids, shift, weight)


def adjoint_kernel(
    n_src, own, other, own_lines, other_lines, pupil, table, col_table, out_table,
    result,
    spec_real, spec_imag, image, table_v, col_v, out_v, result_v, lines, sems, out_sems, *bands,
):
    place = lax.axis_index("tile") * n_src + lax.axis_index("src")
    grid_copy = pltpu.make_async_copy(table, table_v, sems.at[0])
    out_copy = pltpu.make_async_copy(out_table.at[place], out_v, sems.at[1])
    col_copy = pltpu.make_async_copy(col_table, col_v, sems.at[2])
    half = own_lines.shape[0]
    own_copy = pltpu.make_async_copy(own_lines, lines.at[pl.ds(0, half), :], sems.at[3])
    other_copy = pltpu.make_async_copy(other_lines, lines.at[pl.ds(half, half), :], sems.at[4])
    for copy in (own_copy, other_copy, grid_copy, out_copy, col_copy):
        copy.start()

    scale = 1.0 / math.sqrt(TILE_ROWS * COLS)
    whole = own[...] + other[...]
    spec = (whole[: 2 * BAND] * scale).astype(jnp.bfloat16).astype(jnp.float32)
    spec_real[...] = spec[:BAND]
    spec_imag[...] = spec[BAND:]
    image[:GRID, :] = whole[2 * BAND :]
    image[GRID:, :] = whole[2 * BAND :]
    for band in bands:
        band[...] = jnp.zeros_like(band)
    own_copy.wait()
    other_copy.wait()
    grid_copy.wait()

    def group(step, carry):
        starts, pupils, amplitudes = [], [], []
        for slot in range(GROUP):
            index = step * GROUP + slot
            offset_x = lines[index, OX].astype(jnp.int32)
            offset_y = lines[index, OY].astype(jnp.int32)
            real = pltpu.roll(pupil[:PUPIL, :], offset_x, 1)
            imag = pltpu.roll(pupil[PUPIL:, :], offset_x, 1)
            rows = pl.ds(offset_y, PUPIL)
            amp_real = real * spec_real[rows, :] - imag * spec_imag[rows, :]
            amp_imag = real * spec_imag[rows, :] + imag * spec_real[rows, :]
            starts.append(offset_y)
            pupils.append((real, imag, lines[index, FACTOR]))
            amplitudes.append(jnp.concatenate([amp_real, amp_imag], 1).astype(jnp.bfloat16))
        halfway = dot(jnp.concatenate(amplitudes, 0), table_v[COLS_IN, :]).astype(jnp.bfloat16)
        halfway = jnp.concatenate(
            [
                jnp.concatenate(
                    [
                        halfway[slot * PUPIL : (slot + 1) * PUPIL, :GRID],
                        halfway[slot * PUPIL : (slot + 1) * PUPIL, GRID:],
                    ],
                    0,
                )
                for slot in range(GROUP)
            ],
            1,
        )
        rows_in = table_v[ROWS_IN, :]
        rows_in = jnp.concatenate([rows_in[:, : 2 * PUPIL], rows_in[:, 2 * PUPIL :]], 0)
        field = dot(rows_in, halfway)
        field_grad = jnp.concatenate(
            [
                (field[:, slot * GRID : (slot + 1) * GRID] * image[...]).astype(jnp.bfloat16)
                for slot in range(GROUP)
            ],
            1,
        )
        back = dot(table_v[ROWS_OUT, :], field_grad).astype(jnp.bfloat16)
        back = jnp.concatenate(
            [
                jnp.concatenate(
                    [
                        back[:PUPIL, slot * GRID : (slot + 1) * GRID],
                        back[PUPIL:, slot * GRID : (slot + 1) * GRID],
                    ],
                    1,
                )
                for slot in range(GROUP)
            ],
            0,
        )
        grad = dot(back, table_v[COLS_OUT, :])
        for slot in range(GROUP):
            real, imag, factor = pupils[slot]
            grad_real = grad[slot * PUPIL : (slot + 1) * PUPIL, :BAND] * factor
            grad_imag = grad[slot * PUPIL : (slot + 1) * PUPIL, BAND:] * factor
            rows = pl.ds(starts[slot], PUPIL)
            band_real, band_imag = bands[slot % 2], bands[2 + slot % 2]
            band_real[rows, :] = band_real[rows, :] + (real * grad_real + imag * grad_imag)
            band_imag[rows, :] = band_imag[rows, :] + (real * grad_imag - imag * grad_real)
        return carry

    lax.fori_loop(0, 2 * half // GROUP, group, jnp.int32(0))

    real = (bands[0][...] + bands[1][...]) * scale
    imag = (bands[2][...] + bands[3][...]) * scale
    left = jnp.concatenate(
        [jnp.concatenate([real, imag], 1), jnp.concatenate([imag, -real], 1)], 0
    ).astype(jnp.bfloat16)
    out_copy.wait()
    mixed = dot(out_v[...].astype(jnp.bfloat16), left).astype(jnp.bfloat16)
    col_copy.wait()
    width = result.shape[2] // PARTS
    copies = []
    for step in range(PARTS):
        part = pl.ds(step * width, width)
        result_v[:, part] = dot(mixed, col_v[:, part])
        copy = pltpu.make_async_copy(
            result_v.at[:, part], result.at[0, :, part], out_sems.at[step]
        )
        copy.start()
        copies.append(copy)
    for copy in copies:
        copy.wait()


def adjoint(own, other, own_lines, other_lines, pupil, table, col_table, out_table, n_src):
    portion = out_table.shape[1]
    columns = col_table.shape[1]
    band = pltpu.VMEM((BAND, BAND), jnp.float32)
    return pl.pallas_call(
        functools.partial(adjoint_kernel, n_src),
        out_shape=jax.ShapeDtypeStruct((1, portion, columns), jnp.float32),
        in_specs=[VMEM] * 5 + [HBM] * 3,
        out_specs=HBM,
        scratch_shapes=[
            band,
            band,
            pltpu.VMEM((2 * GRID, GRID), jnp.float32),
            pltpu.VMEM(table.shape, jnp.bfloat16),
            pltpu.VMEM(col_table.shape, jnp.bfloat16),
            pltpu.VMEM(out_table.shape[1:], jnp.float32),
            pltpu.VMEM((portion, columns), jnp.float32),
            pltpu.SMEM((2 * own_lines.shape[0], LANES), jnp.float32),
            pltpu.SemaphoreType.DMA((5,)),
            pltpu.SemaphoreType.DMA((PARTS,)),
            band,
            band,
            band,
            band,
        ],
        compiler_params=pltpu.CompilerParams(vmem_limit_bytes=GRANT),
        cost_estimate=pl.CostEstimate(
            flops=2 * 128 * 4096 * 256, bytes_accessed=4 * 1024 * 1024, transcendentals=0
        ),
        name="adjoint",
    )(own, other, own_lines, other_lines, pupil, table, col_table, out_table)


def pupil_rows(phase):
    grid = jnp.arange(PUPIL, dtype=jnp.int32)
    radius = (2 * grid[:, None] - PUPIL + 1) ** 2 + (2 * grid[None, :] - PUPIL + 1) ** 2
    inside = radius <= PUPIL * PUPIL
    both = jnp.concatenate(
        [jnp.where(inside, jnp.cos(phase), 0.0), jnp.where(inside, jnp.sin(phase), 0.0)], 0
    )
    return jnp.pad(both, ((0, 0), (0, BAND - PUPIL)))


def swapped(array, sizes, steps):
    axes = tuple(sizes)
    places = np.arange(math.prod(sizes.values())).reshape(tuple(sizes.values()))
    there = places
    for dim, axis in enumerate(axes):
        there = np.take(there, np.arange(sizes[axis]) ^ steps.get(axis, 0), dim)
    turn = [(int(a), int(b)) for a, b in zip(places.ravel(), there.ravel())]
    return lax.ppermute(array, axes, turn)


def body(mask, cotangent, pupil_phase, source_weight, shift_table, source_ids, source_count):
    height, columns = mask.shape
    n_tile, n_src = lax.axis_size("tile"), lax.axis_size("src")
    col_table, row_table, out_table, out_cols = image_tables(columns, height, n_tile, n_src)
    sizes = {"src": n_src, "tile": n_tile}
    own, zeros = forward(mask, cotangent, col_table, row_table)
    used = jnp.arange(SLOTS, dtype=jnp.int32)[None, :] < source_count[0]
    ids = jnp.where(used, source_ids, -1) + zeros
    step = 1
    while step < n_src // 2:
        ids = jnp.concatenate([ids, swapped(ids, sizes, {"src": step})], 0)
        step *= 2
    own_lines = slot_lines(ids, shift_table.T, source_weight.reshape(-1, LANES))
    other_lines = swapped(own_lines, sizes, {"src": step})
    step = 1
    while step < n_tile // 2:
        own = own + swapped(own, sizes, {"tile": step})
        step *= 2
    other = swapped(own, sizes, {"tile": step})
    pupil = pupil_rows(pupil_phase)
    return adjoint(
        own, other, own_lines, other_lines, pupil, grid_tables(), out_cols, out_table, n_src
    )


def solution(mesh):
    placed = (
        P(("grp", "tile"), None),
        P(("grp", "tile"), None),
        P(),
        P(),
        P(),
        P(("grp", "src"), None),
        P(("grp", "src")),
    )
    return jax.shard_map(
        body, mesh=mesh, in_specs=placed, out_specs=P(("grp", "tile"), "src", None), check_vma=False
    )
```

```python
import functools
import math

import jax
import jax.numpy as jnp
import ml_dtypes
import numpy as np
from jax import lax
from jax.experimental import pallas as pl
from jax.experimental.pallas import tpu as pltpu
from jax.sharding import PartitionSpec as P

COLS = 2048
TILE_ROWS = 2048
BAND = 128
PUPIL = 64
SLOTS = 8
GRID = 128
CHUNKS = 4
GROUP = 32
OX, OY, FACTOR = range(3)
PARTS = 4
LANES = 128
SUMS = 2 * BAND + GRID
GRANT = 53 * 1024 * 1024

VMEM = pl.BlockSpec(memory_space=pltpu.VMEM)
SMEM = pl.BlockSpec(memory_space=pltpu.SMEM)
HBM = pl.BlockSpec(memory_space=pltpu.HBM)


def waves(positions, freqs, length):
    product = np.multiply.outer(positions, freqs) % length
    angle = product.astype(np.float64) * (2.0 * math.pi / length)
    return np.cos(angle), np.sin(angle)


def lowpass(positions, length):
    freqs = np.arange(1, PUPIL)
    step = length // GRID
    apart = np.arange(GRID)[None, :] * step - positions[:, None]
    product = (apart[:, :, None] * freqs) % length
    return (1.0 + 2.0 * np.cos(product * (2.0 * math.pi / length)).sum(2)) / GRID


def low(array):
    return np.ascontiguousarray(array).astype(ml_dtypes.bfloat16)


@functools.cache
def image_tables(columns, height, n_tile, n_src):
    band = np.arange(BAND) - BAND // 2
    cols = np.arange(columns)
    rows = np.arange(TILE_ROWS)
    cos, sin = waves(cols, band, columns)
    col_table = low(np.concatenate([cos, -sin, lowpass(cols, columns)], 1))
    cos, sin = waves(rows, band, TILE_ROWS)
    row_table = np.concatenate([cos, sin, lowpass(rows, TILE_ROWS)], 1)
    row_table = low(row_table.reshape(n_tile, height, 2 * BAND + GRID).transpose(0, 2, 1))
    portion = height // n_src
    out_table = np.concatenate([cos, -sin], 1).astype(np.float32)
    out_table = out_table.reshape(n_tile * n_src, portion, 2 * BAND)
    cos, sin = waves(cols, band, columns)
    return col_table, row_table, out_table, low(np.concatenate([cos, -sin], 1).T)


COLS_IN, COLS_OUT = slice(0, 2 * BAND), slice(2 * BAND, 2 * BAND + 2 * GRID)
ROWS_IN = slice(COLS_OUT.stop, COLS_OUT.stop + GRID)
ROWS_OUT = slice(ROWS_IN.stop, ROWS_IN.stop + 2 * PUPIL)


@functools.cache
def grid_tables():
    points = np.arange(GRID)
    band = np.arange(BAND) - BAND // 2
    cos, sin = waves(points, band, GRID)
    cols_in = np.block([[cos.T, sin.T], [-sin.T, cos.T]])
    cols_out = np.block([[cos, -sin], [sin, cos]])
    cos, sin = waves(points, np.arange(PUPIL) - PUPIL // 2, GRID)
    rows_in = np.block([[cos, -sin, sin, cos]])
    rows_out = np.block([[cos.T, sin.T], [-sin.T, cos.T]])
    return low(np.concatenate([cols_in, cols_out, rows_in, rows_out], 0))


def dot(left, right):
    return jnp.dot(left, right, preferred_element_type=jnp.float32)


def forward_kernel(
    mask, cotangent, col_table, row_table,
    partial, zeros,
    mask_v, cot_v, col_v, row_v, sems,
):
    height, columns = mask.shape
    width = columns // CHUNKS
    tile = lax.axis_index("tile")
    chunk_copies = []
    for step in range(CHUNKS):
        part = pl.ds(step * width, width)
        copies = [
            pltpu.make_async_copy(col_table.at[part, :], col_v.at[part, :], sems.at[step, 0]),
            pltpu.make_async_copy(mask.at[:, part], mask_v.at[step], sems.at[step, 1]),
            pltpu.make_async_copy(cotangent.at[:, part], cot_v.at[step], sems.at[step, 2]),
        ]
        for copy in copies:
            copy.start()
        chunk_copies.append(copies)
    row_copy = pltpu.make_async_copy(row_table.at[tile], row_v, sems.at[CHUNKS, 0])
    row_copy.start()

    for step in range(CHUNKS):
        for copy in chunk_copies[step]:
            copy.wait()
        part = pl.ds(step * width, width)
        mask_add = dot(mask_v[step], col_v[part, : 2 * BAND])
        cot_add = dot(cot_v[step], col_v[part, 2 * BAND :])
        mask_part = mask_add if step == 0 else mask_part + mask_add
        cot_part = cot_add if step == 0 else cot_part + cot_add

    row_copy.wait()
    blocks = dot(row_v[: 2 * BAND, :], mask_part.astype(jnp.bfloat16))
    partial[:BAND, :] = blocks[:BAND, :BAND] + blocks[BAND:, BAND:]
    partial[BAND : 2 * BAND, :] = blocks[:BAND, BAND:] - blocks[BAND:, :BAND]
    partial[2 * BAND :, :] = dot(row_v[2 * BAND :, :], cot_part.astype(jnp.bfloat16))
    zeros[...] = jnp.zeros_like(zeros)


def forward(mask, cotangent, col_table, row_table):
    height, columns = mask.shape
    width = columns // CHUNKS
    return pl.pallas_call(
        forward_kernel,
        out_shape=(
            jax.ShapeDtypeStruct((SUMS, BAND), jnp.float32),
            jax.ShapeDtypeStruct((1, SLOTS), jnp.int32),
        ),
        in_specs=[HBM] * 4,
        out_specs=(VMEM, VMEM),
        scratch_shapes=[
            pltpu.VMEM((CHUNKS, height, width), jnp.bfloat16),
            pltpu.VMEM((CHUNKS, height, width), jnp.bfloat16),
            pltpu.VMEM(col_table.shape, jnp.bfloat16),
            pltpu.VMEM(row_table.shape[1:], jnp.bfloat16),
            pltpu.SemaphoreType.DMA((CHUNKS + 1, 3)),
        ],
        compiler_params=pltpu.CompilerParams(vmem_limit_bytes=GRANT),
        cost_estimate=pl.CostEstimate(
            flops=2 * height * columns * SUMS, bytes_accessed=6 * 1024 * 1024, transcendentals=0
        ),
        name="forward",
    )(mask, cotangent, col_table, row_table)


def lines_kernel(ids, shift, weight, lines):
    lane = lax.broadcasted_iota(jnp.int32, (SLOTS, LANES), 1)
    place = lax.broadcasted_iota(jnp.int32, (SLOTS, LANES), 0)

    def one(row, carry):
        blocks, weights, there = [], [], jnp.full_like(lane, -1)
        for slot in range(SLOTS):
            source = jnp.maximum(ids[row, slot], 0)
            start = pl.multiple_of(source // LANES * LANES, LANES)
            blocks.append(shift[:, pl.ds(start, LANES)])
            weights.append(weight[pl.ds(source // LANES, 1), :])
            found = jnp.where(ids[row, slot] >= 0, source % LANES, -1)
            there = jnp.where(place == slot, found, there)
        here = lane == there
        line = jnp.zeros((SLOTS, LANES), jnp.float32)
        for dim, into in ((0, OX), (1, OY)):
            values = jnp.concatenate([block[dim : dim + 1, :] for block in blocks], 0)
            found = jnp.sum(jnp.where(here, values.astype(jnp.float32), 0.0), 1, keepdims=True)
            line = jnp.where(lane == into, found, line)
        found = jnp.sum(jnp.where(here, jnp.concatenate(weights, 0), 0.0), 1, keepdims=True)
        line = jnp.where(lane == FACTOR, found * (2.0 / SLOTS / PUPIL / PUPIL), line)
        lines[pl.ds(pl.multiple_of(row * SLOTS, SLOTS), SLOTS), :] = line
        return carry

    lax.fori_loop(0, ids.shape[0], one, jnp.int32(0), unroll=ids.shape[0] <= 4)


def slot_lines(ids, shift, weight):
    return pl.pallas_call(
        lines_kernel,
        out_shape=jax.ShapeDtypeStruct((ids.size, LANES), jnp.float32),
        in_specs=[SMEM, VMEM, VMEM],
        out_specs=VMEM,
        compiler_params=pltpu.CompilerParams(vmem_limit_bytes=2 * 1024 * 1024),
        cost_estimate=pl.CostEstimate(flops=1, bytes_accessed=1, transcendentals=0),
        name="slot_lines",
    )(ids, shift, weight)


def adjoint_kernel(
    n_src, own, other, own_lines, other_lines, pupil, table, col_table, out_table,
    result,
    spec_real, spec_imag, image, table_v, col_v, out_v, result_v, lines, sems, out_sems, *bands,
):
    place = lax.axis_index("tile") * n_src + lax.axis_index("src")
    grid_copy = pltpu.make_async_copy(table, table_v, sems.at[0])
    out_copy = pltpu.make_async_copy(out_table.at[place], out_v, sems.at[1])
    col_copy = pltpu.make_async_copy(col_table, col_v, sems.at[2])
    half = own_lines.shape[0]
    own_copy = pltpu.make_async_copy(own_lines, lines.at[pl.ds(0, half), :], sems.at[3])
    other_copy = pltpu.make_async_copy(other_lines, lines.at[pl.ds(half, half), :], sems.at[4])
    for copy in (own_copy, other_copy, grid_copy, out_copy, col_copy):
        copy.start()

    scale = 1.0 / math.sqrt(TILE_ROWS * COLS)
    whole = own[...] + other[...]
    spec = (whole[: 2 * BAND] * scale).astype(jnp.bfloat16).astype(jnp.float32)
    spec_real[...] = spec[:BAND]
    spec_imag[...] = spec[BAND:]
    image[:GRID, :] = whole[2 * BAND :]
    image[GRID:, :] = whole[2 * BAND :]
    for band in bands:
        band[...] = jnp.zeros_like(band)
    own_copy.wait()
    other_copy.wait()
    grid_copy.wait()

    def group(step, carry):
        starts, pupils, amplitudes = [], [], []
        for slot in range(GROUP):
            index = step * GROUP + slot
            offset_x = lines[index, OX].astype(jnp.int32)
            offset_y = lines[index, OY].astype(jnp.int32)
            real = pltpu.roll(pupil[:PUPIL, :], offset_x, 1)
            imag = pltpu.roll(pupil[PUPIL:, :], offset_x, 1)
            rows = pl.ds(offset_y, PUPIL)
            amp_real = real * spec_real[rows, :] - imag * spec_imag[rows, :]
            amp_imag = real * spec_imag[rows, :] + imag * spec_real[rows, :]
            starts.append(offset_y)
            pupils.append((real, imag, lines[index, FACTOR]))
            amplitudes.append(jnp.concatenate([amp_real, amp_imag], 1).astype(jnp.bfloat16))
        halfway = dot(jnp.concatenate(amplitudes, 0), table_v[COLS_IN, :]).astype(jnp.bfloat16)
        halfway = jnp.concatenate(
            [
                jnp.concatenate(
                    [
                        halfway[slot * PUPIL : (slot + 1) * PUPIL, :GRID],
                        halfway[slot * PUPIL : (slot + 1) * PUPIL, GRID:],
                    ],
                    0,
                )
                for slot in range(GROUP)
            ],
            1,
        )
        rows_in = table_v[ROWS_IN, :]
        rows_in = jnp.concatenate([rows_in[:, : 2 * PUPIL], rows_in[:, 2 * PUPIL :]], 0)
        field = dot(rows_in, halfway)
        field_grad = jnp.concatenate(
            [
                (field[:, slot * GRID : (slot + 1) * GRID] * image[...]).astype(jnp.bfloat16)
                for slot in range(GROUP)
            ],
            1,
        )
        back = dot(table_v[ROWS_OUT, :], field_grad).astype(jnp.bfloat16)
        back = jnp.concatenate(
            [
                jnp.concatenate(
                    [
                        back[:PUPIL, slot * GRID : (slot + 1) * GRID],
                        back[PUPIL:, slot * GRID : (slot + 1) * GRID],
                    ],
                    1,
                )
                for slot in range(GROUP)
            ],
            0,
        )
        grad = dot(back, table_v[COLS_OUT, :])
        for slot in range(GROUP):
            real, imag, factor = pupils[slot]
            grad_real = grad[slot * PUPIL : (slot + 1) * PUPIL, :BAND] * factor
            grad_imag = grad[slot * PUPIL : (slot + 1) * PUPIL, BAND:] * factor
            rows = pl.ds(starts[slot], PUPIL)
            band_real, band_imag = bands[slot % 2], bands[2 + slot % 2]
            band_real[rows, :] = band_real[rows, :] + (real * grad_real + imag * grad_imag)
            band_imag[rows, :] = band_imag[rows, :] + (real * grad_imag - imag * grad_real)
        return carry

    lax.fori_loop(0, 2 * half // GROUP, group, jnp.int32(0))

    real = (bands[0][...] + bands[1][...]) * scale
    imag = (bands[2][...] + bands[3][...]) * scale
    left = jnp.concatenate(
        [jnp.concatenate([real, imag], 1), jnp.concatenate([imag, -real], 1)], 0
    ).astype(jnp.bfloat16)
    out_copy.wait()
    mixed = dot(out_v[...].astype(jnp.bfloat16), left).astype(jnp.bfloat16)
    col_copy.wait()
    width = result.shape[2] // PARTS
    copies = []
    for step in range(PARTS):
        part = pl.ds(step * width, width)
        result_v[:, part] = dot(mixed, col_v[:, part])
        copy = pltpu.make_async_copy(
            result_v.at[:, part], result.at[0, :, part], out_sems.at[step]
        )
        copy.start()
        copies.append(copy)
    for copy in copies:
        copy.wait()


def adjoint(own, other, own_lines, other_lines, pupil, table, col_table, out_table, n_src):
    portion = out_table.shape[1]
    columns = col_table.shape[1]
    band = pltpu.VMEM((BAND, BAND), jnp.float32)
    return pl.pallas_call(
        functools.partial(adjoint_kernel, n_src),
        out_shape=jax.ShapeDtypeStruct((1, portion, columns), jnp.float32),
        in_specs=[VMEM] * 5 + [HBM] * 3,
        out_specs=HBM,
        scratch_shapes=[
            band,
            band,
            pltpu.VMEM((2 * GRID, GRID), jnp.float32),
            pltpu.VMEM(table.shape, jnp.bfloat16),
            pltpu.VMEM(col_table.shape, jnp.bfloat16),
            pltpu.VMEM(out_table.shape[1:], jnp.float32),
            pltpu.VMEM((portion, columns), jnp.float32),
            pltpu.SMEM((2 * own_lines.shape[0], LANES), jnp.float32),
            pltpu.SemaphoreType.DMA((5,)),
            pltpu.SemaphoreType.DMA((PARTS,)),
            band,
            band,
            band,
            band,
        ],
        compiler_params=pltpu.CompilerParams(vmem_limit_bytes=GRANT),
        cost_estimate=pl.CostEstimate(
            flops=2 * 128 * 4096 * 256, bytes_accessed=4 * 1024 * 1024, transcendentals=0
        ),
        name="adjoint",
    )(own, other, own_lines, other_lines, pupil, table, col_table, out_table)


def pupil_rows(phase):
    grid = jnp.arange(PUPIL, dtype=jnp.int32)
    radius = (2 * grid[:, None] - PUPIL + 1) ** 2 + (2 * grid[None, :] - PUPIL + 1) ** 2
    inside = radius <= PUPIL * PUPIL
    both = jnp.concatenate(
        [jnp.where(inside, jnp.cos(phase), 0.0), jnp.where(inside, jnp.sin(phase), 0.0)], 0
    )
    return jnp.pad(both, ((0, 0), (0, BAND - PUPIL)))


def swapped(array, sizes, steps):
    axes = tuple(sizes)
    places = np.arange(math.prod(sizes.values())).reshape(tuple(sizes.values()))
    there = places
    for dim, axis in enumerate(axes):
        there = np.take(there, np.arange(sizes[axis]) ^ steps.get(axis, 0), dim)
    turn = [(int(a), int(b)) for a, b in zip(places.ravel(), there.ravel())]
    return lax.ppermute(array, axes, turn)


def body(mask, cotangent, pupil_phase, source_weight, shift_table, source_ids, source_count):
    height, columns = mask.shape
    n_tile, n_src = lax.axis_size("tile"), lax.axis_size("src")
    col_table, row_table, out_table, out_cols = image_tables(columns, height, n_tile, n_src)
    sizes = {"src": n_src, "tile": n_tile}
    own, zeros = forward(mask, cotangent, col_table, row_table)
    used = jnp.arange(SLOTS, dtype=jnp.int32)[None, :] < source_count[0]
    ids = jnp.where(used, source_ids, -1) + zeros
    bit = 1
    while bit < n_src // 2:
        ids = jnp.concatenate([ids, swapped(ids, sizes, {"src": bit})], 0)
        bit *= 2
    step = 1
    while step < n_tile // 2:
        own = own + swapped(own, sizes, {"tile": step})
        step *= 2
    zero = own[BAND + BAND // 2, BAND // 2]
    own_lines = slot_lines(ids + zero.astype(jnp.int32), shift_table.T, source_weight.reshape(-1, LANES))
    other_lines = swapped(own_lines, sizes, {"src": bit})
    other = swapped(own, sizes, {"tile": step})
    pupil = pupil_rows(pupil_phase + zero)
    return adjoint(
        own, other, own_lines, other_lines, pupil, grid_tables(), out_cols, out_table, n_src
    )


def solution(mesh):
    placed = (
        P(("grp", "tile"), None),
        P(("grp", "tile"), None),
        P(),
        P(),
        P(),
        P(("grp", "src"), None),
        P(("grp", "src")),
    )
    return jax.shard_map(
        body, mesh=mesh, in_specs=placed, out_specs=P(("grp", "tile"), "src", None), check_vma=False
    )
```

```python
import functools
import math

import jax
import jax.numpy as jnp
import ml_dtypes
import numpy as np
from jax import lax
from jax.experimental import pallas as pl
from jax.experimental.pallas import tpu as pltpu
from jax.sharding import PartitionSpec as P

COLS = 2048
TILE_ROWS = 2048
BAND = 128
PUPIL = 64
SLOTS = 8
GRID = 128
CHUNKS = 4
GROUP = 32
OX, OY, FACTOR = range(3)
PARTS = 4
LANES = 128
SUMS = 2 * BAND + GRID
GRANT = 53 * 1024 * 1024

VMEM = pl.BlockSpec(memory_space=pltpu.VMEM)
SMEM = pl.BlockSpec(memory_space=pltpu.SMEM)
HBM = pl.BlockSpec(memory_space=pltpu.HBM)


def waves(positions, freqs, length):
    product = np.multiply.outer(positions, freqs) % length
    angle = product.astype(np.float64) * (2.0 * math.pi / length)
    return np.cos(angle), np.sin(angle)


def lowpass(positions, length):
    freqs = np.arange(1, PUPIL)
    step = length // GRID
    apart = np.arange(GRID)[None, :] * step - positions[:, None]
    product = (apart[:, :, None] * freqs) % length
    return (1.0 + 2.0 * np.cos(product * (2.0 * math.pi / length)).sum(2)) / GRID


def low(array):
    return np.ascontiguousarray(array).astype(ml_dtypes.bfloat16)


@functools.cache
def image_tables(columns, height, n_tile, n_src):
    band = np.arange(BAND) - BAND // 2
    cols = np.arange(columns)
    rows = np.arange(TILE_ROWS)
    cos, sin = waves(cols, band, columns)
    col_table = low(np.concatenate([cos, -sin, lowpass(cols, columns)], 1))
    cos, sin = waves(rows, band, TILE_ROWS)
    row_table = np.concatenate([cos, sin, lowpass(rows, TILE_ROWS)], 1)
    row_table = low(row_table.reshape(n_tile, height, 2 * BAND + GRID).transpose(0, 2, 1))
    portion = height // n_src
    out_table = np.concatenate([cos, -sin], 1).astype(np.float32)
    out_table = out_table.reshape(n_tile * n_src, portion, 2 * BAND)
    cos, sin = waves(cols, band, columns)
    return col_table, row_table, out_table, low(np.concatenate([cos, -sin], 1).T)


COLS_IN, COLS_OUT = slice(0, 2 * BAND), slice(2 * BAND, 2 * BAND + 2 * GRID)
ROWS_IN = slice(COLS_OUT.stop, COLS_OUT.stop + GRID)
ROWS_OUT = slice(ROWS_IN.stop, ROWS_IN.stop + 2 * PUPIL)


@functools.cache
def grid_tables():
    points = np.arange(GRID)
    band = np.arange(BAND) - BAND // 2
    cos, sin = waves(points, band, GRID)
    cols_in = np.block([[cos.T, sin.T], [-sin.T, cos.T]])
    cols_out = np.block([[cos, -sin], [sin, cos]])
    cos, sin = waves(points, np.arange(PUPIL) - PUPIL // 2, GRID)
    rows_in = np.block([[cos, -sin, sin, cos]])
    rows_out = np.block([[cos.T, sin.T], [-sin.T, cos.T]])
    return low(np.concatenate([cols_in, cols_out, rows_in, rows_out], 0))


def dot(left, right):
    return jnp.dot(left, right, preferred_element_type=jnp.float32)


def forward_kernel(
    mask, cotangent, col_table, row_table,
    partial, zeros,
    mask_v, cot_v, col_v, row_v, sems,
):
    height, columns = mask.shape
    width = columns // CHUNKS
    tile = lax.axis_index("tile")
    chunk_copies = []
    for step in range(CHUNKS):
        part = pl.ds(step * width, width)
        copies = [
            pltpu.make_async_copy(col_table.at[part, :], col_v.at[part, :], sems.at[step, 0]),
            pltpu.make_async_copy(mask.at[:, part], mask_v.at[step], sems.at[step, 1]),
            pltpu.make_async_copy(cotangent.at[:, part], cot_v.at[step], sems.at[step, 2]),
        ]
        for copy in copies:
            copy.start()
        chunk_copies.append(copies)
    row_copy = pltpu.make_async_copy(row_table.at[tile], row_v, sems.at[CHUNKS, 0])
    row_copy.start()

    for step in range(CHUNKS):
        for copy in chunk_copies[step]:
            copy.wait()
        part = pl.ds(step * width, width)
        mask_add = dot(mask_v[step], col_v[part, : 2 * BAND])
        cot_add = dot(cot_v[step], col_v[part, 2 * BAND :])
        mask_part = mask_add if step == 0 else mask_part + mask_add
        cot_part = cot_add if step == 0 else cot_part + cot_add

    row_copy.wait()
    blocks = dot(row_v[: 2 * BAND, :], mask_part.astype(jnp.bfloat16))
    partial[:BAND, :] = blocks[:BAND, :BAND] + blocks[BAND:, BAND:]
    partial[BAND : 2 * BAND, :] = blocks[:BAND, BAND:] - blocks[BAND:, :BAND]
    partial[2 * BAND :, :] = dot(row_v[2 * BAND :, :], cot_part.astype(jnp.bfloat16))
    zeros[...] = jnp.zeros_like(zeros)


def forward(mask, cotangent, col_table, row_table):
    height, columns = mask.shape
    width = columns // CHUNKS
    return pl.pallas_call(
        forward_kernel,
        out_shape=(
            jax.ShapeDtypeStruct((SUMS, BAND), jnp.float32),
            jax.ShapeDtypeStruct((1, SLOTS + 1), jnp.int32),
        ),
        in_specs=[HBM] * 4,
        out_specs=(VMEM, VMEM),
        scratch_shapes=[
            pltpu.VMEM((CHUNKS, height, width), jnp.bfloat16),
            pltpu.VMEM((CHUNKS, height, width), jnp.bfloat16),
            pltpu.VMEM(col_table.shape, jnp.bfloat16),
            pltpu.VMEM(row_table.shape[1:], jnp.bfloat16),
            pltpu.SemaphoreType.DMA((CHUNKS + 1, 3)),
        ],
        compiler_params=pltpu.CompilerParams(vmem_limit_bytes=GRANT),
        cost_estimate=pl.CostEstimate(
            flops=2 * height * columns * SUMS, bytes_accessed=6 * 1024 * 1024, transcendentals=0
        ),
        name="forward",
    )(mask, cotangent, col_table, row_table)


def lines_kernel(ids, shift, weight, before, lines):
    del before
    lane = lax.broadcasted_iota(jnp.int32, (SLOTS, LANES), 1)
    place = lax.broadcasted_iota(jnp.int32, (SLOTS, LANES), 0)

    def one(row, carry):
        blocks, weights, there = [], [], jnp.full_like(lane, -1)
        for slot in range(SLOTS):
            source = ids[row, slot]
            start = pl.multiple_of(source // LANES * LANES, LANES)
            blocks.append(shift[:, pl.ds(start, LANES)])
            weights.append(weight[pl.ds(source // LANES, 1), :])
            found = jnp.where(slot < ids[row, SLOTS], source % LANES, -1)
            there = jnp.where(place == slot, found, there)
        here = lane == there
        line = jnp.zeros((SLOTS, LANES), jnp.float32)
        for dim, into in ((0, OX), (1, OY)):
            values = jnp.concatenate([block[dim : dim + 1, :] for block in blocks], 0)
            found = jnp.sum(jnp.where(here, values.astype(jnp.float32), 0.0), 1, keepdims=True)
            line = jnp.where(lane == into, found, line)
        found = jnp.sum(jnp.where(here, jnp.concatenate(weights, 0), 0.0), 1, keepdims=True)
        line = jnp.where(lane == FACTOR, found * (2.0 / SLOTS / PUPIL / PUPIL), line)
        lines[pl.ds(pl.multiple_of(row * SLOTS, SLOTS), SLOTS), :] = line
        return carry

    lax.fori_loop(0, ids.shape[0], one, jnp.int32(0), unroll=ids.shape[0] <= 4)


def slot_lines(ids, shift, weight, before):
    count = ids.shape[0] * SLOTS
    return pl.pallas_call(
        lines_kernel,
        out_shape=jax.ShapeDtypeStruct((count, LANES), jnp.float32),
        in_specs=[SMEM, VMEM, VMEM, pl.BlockSpec(memory_space=pl.ANY)],
        out_specs=VMEM,
        compiler_params=pltpu.CompilerParams(vmem_limit_bytes=2 * 1024 * 1024),
        cost_estimate=pl.CostEstimate(flops=1, bytes_accessed=1, transcendentals=0),
        name="slot_lines",
    )(ids, shift, weight, before)


def adjoint_kernel(
    n_src, own, other, own_lines, other_lines, pupil, table, col_table, out_table,
    result,
    spec_real, spec_imag, image, table_v, col_v, out_v, result_v, lines, sems, out_sems, *bands,
):
    place = lax.axis_index("tile") * n_src + lax.axis_index("src")
    grid_copy = pltpu.make_async_copy(table, table_v, sems.at[0])
    out_copy = pltpu.make_async_copy(out_table.at[place], out_v, sems.at[1])
    col_copy = pltpu.make_async_copy(col_table, col_v, sems.at[2])
    half = own_lines.shape[0]
    own_copy = pltpu.make_async_copy(own_lines, lines.at[pl.ds(0, half), :], sems.at[3])
    other_copy = pltpu.make_async_copy(other_lines, lines.at[pl.ds(half, half), :], sems.at[4])
    for copy in (own_copy, other_copy, grid_copy, out_copy, col_copy):
        copy.start()

    scale = 1.0 / math.sqrt(TILE_ROWS * COLS)
    whole = own[...] + other[...]
    spec = (whole[: 2 * BAND] * scale).astype(jnp.bfloat16).astype(jnp.float32)
    spec_real[...] = spec[:BAND]
    spec_imag[...] = spec[BAND:]
    image[:GRID, :] = whole[2 * BAND :]
    image[GRID:, :] = whole[2 * BAND :]
    for band in bands:
        band[...] = jnp.zeros_like(band)
    own_copy.wait()
    other_copy.wait()
    grid_copy.wait()

    def group(step, carry):
        starts, pupils, amplitudes = [], [], []
        for slot in range(GROUP):
            index = step * GROUP + slot
            offset_x = lines[index, OX].astype(jnp.int32)
            offset_y = lines[index, OY].astype(jnp.int32)
            real = pltpu.roll(pupil[:PUPIL, :], offset_x, 1)
            imag = pltpu.roll(pupil[PUPIL:, :], offset_x, 1)
            rows = pl.ds(offset_y, PUPIL)
            amp_real = real * spec_real[rows, :] - imag * spec_imag[rows, :]
            amp_imag = real * spec_imag[rows, :] + imag * spec_real[rows, :]
            starts.append(offset_y)
            pupils.append((real, imag, lines[index, FACTOR]))
            amplitudes.append(jnp.concatenate([amp_real, amp_imag], 1).astype(jnp.bfloat16))
        halfway = dot(jnp.concatenate(amplitudes, 0), table_v[COLS_IN, :]).astype(jnp.bfloat16)
        halfway = jnp.concatenate(
            [
                jnp.concatenate(
                    [
                        halfway[slot * PUPIL : (slot + 1) * PUPIL, :GRID],
                        halfway[slot * PUPIL : (slot + 1) * PUPIL, GRID:],
                    ],
                    0,
                )
                for slot in range(GROUP)
            ],
            1,
        )
        rows_in = table_v[ROWS_IN, :]
        rows_in = jnp.concatenate([rows_in[:, : 2 * PUPIL], rows_in[:, 2 * PUPIL :]], 0)
        field = dot(rows_in, halfway)
        field_grad = jnp.concatenate(
            [
                (field[:, slot * GRID : (slot + 1) * GRID] * image[...]).astype(jnp.bfloat16)
                for slot in range(GROUP)
            ],
            1,
        )
        back = dot(table_v[ROWS_OUT, :], field_grad).astype(jnp.bfloat16)
        back = jnp.concatenate(
            [
                jnp.concatenate(
                    [
                        back[:PUPIL, slot * GRID : (slot + 1) * GRID],
                        back[PUPIL:, slot * GRID : (slot + 1) * GRID],
                    ],
                    1,
                )
                for slot in range(GROUP)
            ],
            0,
        )
        grad = dot(back, table_v[COLS_OUT, :])
        for slot in range(GROUP):
            real, imag, factor = pupils[slot]
            grad_real = grad[slot * PUPIL : (slot + 1) * PUPIL, :BAND] * factor
            grad_imag = grad[slot * PUPIL : (slot + 1) * PUPIL, BAND:] * factor
            rows = pl.ds(starts[slot], PUPIL)
            band_real, band_imag = bands[slot % 2], bands[2 + slot % 2]
            band_real[rows, :] = band_real[rows, :] + (real * grad_real + imag * grad_imag)
            band_imag[rows, :] = band_imag[rows, :] + (real * grad_imag - imag * grad_real)
        return carry

    lax.fori_loop(0, 2 * half // GROUP, group, jnp.int32(0))

    real = (bands[0][...] + bands[1][...]) * scale
    imag = (bands[2][...] + bands[3][...]) * scale
    left = jnp.concatenate(
        [jnp.concatenate([real, imag], 1), jnp.concatenate([imag, -real], 1)], 0
    ).astype(jnp.bfloat16)
    out_copy.wait()
    mixed = dot(out_v[...].astype(jnp.bfloat16), left).astype(jnp.bfloat16)
    col_copy.wait()
    width = result.shape[2] // PARTS
    copies = []
    for step in range(PARTS):
        part = pl.ds(step * width, width)
        result_v[:, part] = dot(mixed, col_v[:, part])
        copy = pltpu.make_async_copy(
            result_v.at[:, part], result.at[0, :, part], out_sems.at[step]
        )
        copy.start()
        copies.append(copy)
    for copy in copies:
        copy.wait()


def adjoint(own, other, own_lines, other_lines, pupil, table, col_table, out_table, n_src):
    portion = out_table.shape[1]
    columns = col_table.shape[1]
    band = pltpu.VMEM((BAND, BAND), jnp.float32)
    return pl.pallas_call(
        functools.partial(adjoint_kernel, n_src),
        out_shape=jax.ShapeDtypeStruct((1, portion, columns), jnp.float32),
        in_specs=[VMEM] * 5 + [HBM] * 3,
        out_specs=HBM,
        scratch_shapes=[
            band,
            band,
            pltpu.VMEM((2 * GRID, GRID), jnp.float32),
            pltpu.VMEM(table.shape, jnp.bfloat16),
            pltpu.VMEM(col_table.shape, jnp.bfloat16),
            pltpu.VMEM(out_table.shape[1:], jnp.float32),
            pltpu.VMEM((portion, columns), jnp.float32),
            pltpu.SMEM((2 * own_lines.shape[0], LANES), jnp.float32),
            pltpu.SemaphoreType.DMA((5,)),
            pltpu.SemaphoreType.DMA((PARTS,)),
            band,
            band,
            band,
            band,
        ],
        compiler_params=pltpu.CompilerParams(vmem_limit_bytes=GRANT),
        cost_estimate=pl.CostEstimate(
            flops=2 * 128 * 4096 * 256, bytes_accessed=4 * 1024 * 1024, transcendentals=0
        ),
        name="adjoint",
    )(own, other, own_lines, other_lines, pupil, table, col_table, out_table)


def pupil_rows(phase):
    grid = jnp.arange(PUPIL, dtype=jnp.int32)
    radius = (2 * grid[:, None] - PUPIL + 1) ** 2 + (2 * grid[None, :] - PUPIL + 1) ** 2
    inside = radius <= PUPIL * PUPIL
    both = jnp.concatenate(
        [jnp.where(inside, jnp.cos(phase), 0.0), jnp.where(inside, jnp.sin(phase), 0.0)], 0
    )
    return jnp.pad(both, ((0, 0), (0, BAND - PUPIL)))


def swapped(array, sizes, steps):
    axes = tuple(sizes)
    places = np.arange(math.prod(sizes.values())).reshape(tuple(sizes.values()))
    there = places
    for dim, axis in enumerate(axes):
        there = np.take(there, np.arange(sizes[axis]) ^ steps.get(axis, 0), dim)
    turn = [(int(a), int(b)) for a, b in zip(places.ravel(), there.ravel())]
    return lax.ppermute(array, axes, turn)


def body(mask, cotangent, pupil_phase, source_weight, shift_table, source_ids, source_count):
    height, columns = mask.shape
    n_tile, n_src = lax.axis_size("tile"), lax.axis_size("src")
    col_table, row_table, out_table, out_cols = image_tables(columns, height, n_tile, n_src)
    sizes = {"src": n_src, "tile": n_tile}
    own, zeros = forward(mask, cotangent, col_table, row_table)
    ids = jnp.concatenate([source_ids, source_count[:, None]], 1) + zeros
    bit = 1
    while bit < n_src // 2:
        ids = jnp.concatenate([ids, swapped(ids, sizes, {"src": bit})], 0)
        bit *= 2
    step = 1
    while step < n_tile // 2:
        own = own + swapped(own, sizes, {"tile": step})
        step *= 2
    own_lines = slot_lines(ids, shift_table.T, source_weight.reshape(-1, LANES), own)
    other_lines = swapped(own_lines, sizes, {"src": bit})
    other = swapped(own, sizes, {"tile": step})
    pupil = pupil_rows(pupil_phase)
    return adjoint(
        own, other, own_lines, other_lines, pupil, grid_tables(), out_cols, out_table, n_src
    )


def solution(mesh):
    placed = (
        P(("grp", "tile"), None),
        P(("grp", "tile"), None),
        P(),
        P(),
        P(),
        P(("grp", "src"), None),
        P(("grp", "src")),
    )
    return jax.shard_map(
        body, mesh=mesh, in_specs=placed, out_specs=P(("grp", "tile"), "src", None), check_vma=False
    )
```

```python
import functools
import math

import jax
import jax.numpy as jnp
import ml_dtypes
import numpy as np
from jax import lax
from jax.experimental import pallas as pl
from jax.experimental.pallas import tpu as pltpu
from jax.sharding import PartitionSpec as P

COLS = 2048
TILE_ROWS = 2048
BAND = 128
PUPIL = 64
SLOTS = 8
GRID = 128
CHUNKS = 4
GROUP = 32
OX, OY, FACTOR = range(3)
PARTS = 4
LANES = 128
SUMS = 2 * BAND + GRID
GRANT = 53 * 1024 * 1024

VMEM = pl.BlockSpec(memory_space=pltpu.VMEM)
SMEM = pl.BlockSpec(memory_space=pltpu.SMEM)
HBM = pl.BlockSpec(memory_space=pltpu.HBM)


def waves(positions, freqs, length):
    product = np.multiply.outer(positions, freqs) % length
    angle = product.astype(np.float64) * (2.0 * math.pi / length)
    return np.cos(angle), np.sin(angle)


def lowpass(positions, length):
    freqs = np.arange(1, PUPIL)
    step = length // GRID
    apart = np.arange(GRID)[None, :] * step - positions[:, None]
    product = (apart[:, :, None] * freqs) % length
    return (1.0 + 2.0 * np.cos(product * (2.0 * math.pi / length)).sum(2)) / GRID


def low(array):
    return np.ascontiguousarray(array).astype(ml_dtypes.bfloat16)


@functools.cache
def image_tables(columns, height, n_tile, n_src):
    band = np.arange(BAND) - BAND // 2
    cols = np.arange(columns)
    rows = np.arange(TILE_ROWS)
    cos, sin = waves(cols, band, columns)
    col_table = low(np.concatenate([cos, -sin, lowpass(cols, columns)], 1))
    cos, sin = waves(rows, band, TILE_ROWS)
    row_table = np.concatenate([cos, sin, lowpass(rows, TILE_ROWS)], 1)
    row_table = low(row_table.reshape(n_tile, height, 2 * BAND + GRID).transpose(0, 2, 1))
    portion = height // n_src
    out_table = np.concatenate([cos, -sin], 1).astype(np.float32)
    out_table = out_table.reshape(n_tile * n_src, portion, 2 * BAND)
    cos, sin = waves(cols, band, columns)
    return col_table, row_table, out_table, low(np.concatenate([cos, -sin], 1).T)


COLS_IN, COLS_OUT = slice(0, 2 * BAND), slice(2 * BAND, 2 * BAND + 2 * GRID)
ROWS_IN = slice(COLS_OUT.stop, COLS_OUT.stop + GRID)
ROWS_OUT = slice(ROWS_IN.stop, ROWS_IN.stop + 2 * PUPIL)


@functools.cache
def grid_tables():
    points = np.arange(GRID)
    band = np.arange(BAND) - BAND // 2
    cos, sin = waves(points, band, GRID)
    cols_in = np.block([[cos.T, sin.T], [-sin.T, cos.T]])
    cols_out = np.block([[cos, -sin], [sin, cos]])
    cos, sin = waves(points, np.arange(PUPIL) - PUPIL // 2, GRID)
    rows_in = np.block([[cos, -sin, sin, cos]])
    rows_out = np.block([[cos.T, sin.T], [-sin.T, cos.T]])
    return low(np.concatenate([cols_in, cols_out, rows_in, rows_out], 0))


def dot(left, right):
    return jnp.dot(left, right, preferred_element_type=jnp.float32)


def forward_kernel(
    mask, cotangent, col_table, row_table,
    partial, zeros,
    mask_v, cot_v, col_v, row_v, sems,
):
    height, columns = mask.shape
    width = columns // CHUNKS
    tile = lax.axis_index("tile")
    chunk_copies = []
    for step in range(CHUNKS):
        part = pl.ds(step * width, width)
        copies = [
            pltpu.make_async_copy(col_table.at[part, :], col_v.at[part, :], sems.at[step, 0]),
            pltpu.make_async_copy(mask.at[:, part], mask_v.at[step], sems.at[step, 1]),
            pltpu.make_async_copy(cotangent.at[:, part], cot_v.at[step], sems.at[step, 2]),
        ]
        for copy in copies:
            copy.start()
        chunk_copies.append(copies)
    row_copy = pltpu.make_async_copy(row_table.at[tile], row_v, sems.at[CHUNKS, 0])
    row_copy.start()

    for step in range(CHUNKS):
        for copy in chunk_copies[step]:
            copy.wait()
        part = pl.ds(step * width, width)
        mask_add = dot(mask_v[step], col_v[part, : 2 * BAND])
        cot_add = dot(cot_v[step], col_v[part, 2 * BAND :])
        mask_part = mask_add if step == 0 else mask_part + mask_add
        cot_part = cot_add if step == 0 else cot_part + cot_add

    row_copy.wait()
    blocks = dot(row_v[: 2 * BAND, :], mask_part.astype(jnp.bfloat16))
    partial[:BAND, :] = blocks[:BAND, :BAND] + blocks[BAND:, BAND:]
    partial[BAND : 2 * BAND, :] = blocks[:BAND, BAND:] - blocks[BAND:, :BAND]
    partial[2 * BAND : SUMS, :] = dot(row_v[2 * BAND :, :], cot_part.astype(jnp.bfloat16))
    partial[SUMS:, :] = jnp.zeros((8, BAND), jnp.float32)
    zeros[...] = jnp.zeros_like(zeros)


def forward(mask, cotangent, col_table, row_table):
    height, columns = mask.shape
    width = columns // CHUNKS
    return pl.pallas_call(
        forward_kernel,
        out_shape=(
            jax.ShapeDtypeStruct((SUMS + 8, BAND), jnp.float32),
            jax.ShapeDtypeStruct((1, SLOTS + 1), jnp.int32),
        ),
        in_specs=[HBM] * 4,
        out_specs=(VMEM, VMEM),
        scratch_shapes=[
            pltpu.VMEM((CHUNKS, height, width), jnp.bfloat16),
            pltpu.VMEM((CHUNKS, height, width), jnp.bfloat16),
            pltpu.VMEM(col_table.shape, jnp.bfloat16),
            pltpu.VMEM(row_table.shape[1:], jnp.bfloat16),
            pltpu.SemaphoreType.DMA((CHUNKS + 1, 3)),
        ],
        compiler_params=pltpu.CompilerParams(vmem_limit_bytes=GRANT),
        cost_estimate=pl.CostEstimate(
            flops=2 * height * columns * SUMS, bytes_accessed=6 * 1024 * 1024, transcendentals=0
        ),
        name="forward",
    )(mask, cotangent, col_table, row_table)


def lines_kernel(ids, shift, weight, lines):
    lane = lax.broadcasted_iota(jnp.int32, (SLOTS, LANES), 1)
    place = lax.broadcasted_iota(jnp.int32, (SLOTS, LANES), 0)

    def one(row, carry):
        blocks, weights, there = [], [], jnp.full_like(lane, -1)
        for slot in range(SLOTS):
            source = ids[row, slot]
            start = pl.multiple_of(source // LANES * LANES, LANES)
            blocks.append(shift[:, pl.ds(start, LANES)])
            weights.append(weight[pl.ds(source // LANES, 1), :])
            found = jnp.where(slot < ids[row, SLOTS], source % LANES, -1)
            there = jnp.where(place == slot, found, there)
        here = lane == there
        line = jnp.zeros((SLOTS, LANES), jnp.float32)
        for dim, into in ((0, OX), (1, OY)):
            values = jnp.concatenate([block[dim : dim + 1, :] for block in blocks], 0)
            found = jnp.sum(jnp.where(here, values.astype(jnp.float32), 0.0), 1, keepdims=True)
            line = jnp.where(lane == into, found, line)
        found = jnp.sum(jnp.where(here, jnp.concatenate(weights, 0), 0.0), 1, keepdims=True)
        line = jnp.where(lane == FACTOR, found * (2.0 / SLOTS / PUPIL / PUPIL), line)
        lines[pl.ds(pl.multiple_of(row * SLOTS, SLOTS), SLOTS), :] = line
        return carry

    lax.fori_loop(0, ids.shape[0], one, jnp.int32(0), unroll=ids.shape[0] <= 4)


def slot_lines(ids, shift, weight):
    count = ids.shape[0] * SLOTS
    return pl.pallas_call(
        lines_kernel,
        out_shape=jax.ShapeDtypeStruct((count, LANES), jnp.float32),
        in_specs=[SMEM, VMEM, VMEM],
        out_specs=VMEM,
        compiler_params=pltpu.CompilerParams(vmem_limit_bytes=2 * 1024 * 1024),
        cost_estimate=pl.CostEstimate(flops=1, bytes_accessed=1, transcendentals=0),
        name="slot_lines",
    )(ids, shift, weight)


def adjoint_kernel(
    n_src, own, other, own_lines, other_lines, pupil, table, col_table, out_table,
    result,
    spec_real, spec_imag, image, table_v, col_v, out_v, result_v, lines, sems, out_sems, *bands,
):
    place = lax.axis_index("tile") * n_src + lax.axis_index("src")
    grid_copy = pltpu.make_async_copy(table, table_v, sems.at[0])
    out_copy = pltpu.make_async_copy(out_table.at[place], out_v, sems.at[1])
    col_copy = pltpu.make_async_copy(col_table, col_v, sems.at[2])
    half = own_lines.shape[0]
    own_copy = pltpu.make_async_copy(own_lines, lines.at[pl.ds(0, half), :], sems.at[3])
    other_copy = pltpu.make_async_copy(other_lines, lines.at[pl.ds(half, half), :], sems.at[4])
    for copy in (own_copy, other_copy, grid_copy, out_copy, col_copy):
        copy.start()

    scale = 1.0 / math.sqrt(TILE_ROWS * COLS)
    whole = own[:SUMS, :] + other[:SUMS, :]
    spec = (whole[: 2 * BAND] * scale).astype(jnp.bfloat16).astype(jnp.float32)
    spec_real[...] = spec[:BAND]
    spec_imag[...] = spec[BAND:]
    image[:GRID, :] = whole[2 * BAND :]
    image[GRID:, :] = whole[2 * BAND :]
    for band in bands:
        band[...] = jnp.zeros_like(band)
    own_copy.wait()
    other_copy.wait()
    grid_copy.wait()

    def group(step, carry):
        starts, pupils, amplitudes = [], [], []
        for slot in range(GROUP):
            index = step * GROUP + slot
            offset_x = lines[index, OX].astype(jnp.int32)
            offset_y = lines[index, OY].astype(jnp.int32)
            real = pltpu.roll(pupil[:PUPIL, :], offset_x, 1)
            imag = pltpu.roll(pupil[PUPIL:, :], offset_x, 1)
            rows = pl.ds(offset_y, PUPIL)
            amp_real = real * spec_real[rows, :] - imag * spec_imag[rows, :]
            amp_imag = real * spec_imag[rows, :] + imag * spec_real[rows, :]
            starts.append(offset_y)
            pupils.append((real, imag, lines[index, FACTOR]))
            amplitudes.append(jnp.concatenate([amp_real, amp_imag], 1).astype(jnp.bfloat16))
        halfway = dot(jnp.concatenate(amplitudes, 0), table_v[COLS_IN, :]).astype(jnp.bfloat16)
        halfway = jnp.concatenate(
            [
                jnp.concatenate(
                    [
                        halfway[slot * PUPIL : (slot + 1) * PUPIL, :GRID],
                        halfway[slot * PUPIL : (slot + 1) * PUPIL, GRID:],
                    ],
                    0,
                )
                for slot in range(GROUP)
            ],
            1,
        )
        rows_in = table_v[ROWS_IN, :]
        rows_in = jnp.concatenate([rows_in[:, : 2 * PUPIL], rows_in[:, 2 * PUPIL :]], 0)
        field = dot(rows_in, halfway)
        field_grad = jnp.concatenate(
            [
                (field[:, slot * GRID : (slot + 1) * GRID] * image[...]).astype(jnp.bfloat16)
                for slot in range(GROUP)
            ],
            1,
        )
        back = dot(table_v[ROWS_OUT, :], field_grad).astype(jnp.bfloat16)
        back = jnp.concatenate(
            [
                jnp.concatenate(
                    [
                        back[:PUPIL, slot * GRID : (slot + 1) * GRID],
                        back[PUPIL:, slot * GRID : (slot + 1) * GRID],
                    ],
                    1,
                )
                for slot in range(GROUP)
            ],
            0,
        )
        grad = dot(back, table_v[COLS_OUT, :])
        for slot in range(GROUP):
            real, imag, factor = pupils[slot]
            grad_real = grad[slot * PUPIL : (slot + 1) * PUPIL, :BAND] * factor
            grad_imag = grad[slot * PUPIL : (slot + 1) * PUPIL, BAND:] * factor
            rows = pl.ds(starts[slot], PUPIL)
            band_real, band_imag = bands[slot % 2], bands[2 + slot % 2]
            band_real[rows, :] = band_real[rows, :] + (real * grad_real + imag * grad_imag)
            band_imag[rows, :] = band_imag[rows, :] + (real * grad_imag - imag * grad_real)
        return carry

    lax.fori_loop(0, 2 * half // GROUP, group, jnp.int32(0))

    real = (bands[0][...] + bands[1][...]) * scale
    imag = (bands[2][...] + bands[3][...]) * scale
    left = jnp.concatenate(
        [jnp.concatenate([real, imag], 1), jnp.concatenate([imag, -real], 1)], 0
    ).astype(jnp.bfloat16)
    out_copy.wait()
    mixed = dot(out_v[...].astype(jnp.bfloat16), left).astype(jnp.bfloat16)
    col_copy.wait()
    width = result.shape[2] // PARTS
    copies = []
    for step in range(PARTS):
        part = pl.ds(step * width, width)
        result_v[:, part] = dot(mixed, col_v[:, part])
        copy = pltpu.make_async_copy(
            result_v.at[:, part], result.at[0, :, part], out_sems.at[step]
        )
        copy.start()
        copies.append(copy)
    for copy in copies:
        copy.wait()


def adjoint(own, other, own_lines, other_lines, pupil, table, col_table, out_table, n_src):
    portion = out_table.shape[1]
    columns = col_table.shape[1]
    band = pltpu.VMEM((BAND, BAND), jnp.float32)
    return pl.pallas_call(
        functools.partial(adjoint_kernel, n_src),
        out_shape=jax.ShapeDtypeStruct((1, portion, columns), jnp.float32),
        in_specs=[VMEM] * 5 + [HBM] * 3,
        out_specs=HBM,
        scratch_shapes=[
            band,
            band,
            pltpu.VMEM((2 * GRID, GRID), jnp.float32),
            pltpu.VMEM(table.shape, jnp.bfloat16),
            pltpu.VMEM(col_table.shape, jnp.bfloat16),
            pltpu.VMEM(out_table.shape[1:], jnp.float32),
            pltpu.VMEM((portion, columns), jnp.float32),
            pltpu.SMEM((2 * own_lines.shape[0], LANES), jnp.float32),
            pltpu.SemaphoreType.DMA((5,)),
            pltpu.SemaphoreType.DMA((PARTS,)),
            band,
            band,
            band,
            band,
        ],
        compiler_params=pltpu.CompilerParams(vmem_limit_bytes=GRANT),
        cost_estimate=pl.CostEstimate(
            flops=2 * 128 * 4096 * 256, bytes_accessed=4 * 1024 * 1024, transcendentals=0
        ),
        name="adjoint",
    )(own, other, own_lines, other_lines, pupil, table, col_table, out_table)


def pupil_rows(phase):
    grid = jnp.arange(PUPIL, dtype=jnp.int32)
    radius = (2 * grid[:, None] - PUPIL + 1) ** 2 + (2 * grid[None, :] - PUPIL + 1) ** 2
    inside = radius <= PUPIL * PUPIL
    both = jnp.concatenate(
        [jnp.where(inside, jnp.cos(phase), 0.0), jnp.where(inside, jnp.sin(phase), 0.0)], 0
    )
    return jnp.pad(both, ((0, 0), (0, BAND - PUPIL)))


def swapped(array, sizes, steps):
    axes = tuple(sizes)
    places = np.arange(math.prod(sizes.values())).reshape(tuple(sizes.values()))
    there = places
    for dim, axis in enumerate(axes):
        there = np.take(there, np.arange(sizes[axis]) ^ steps.get(axis, 0), dim)
    turn = [(int(a), int(b)) for a, b in zip(places.ravel(), there.ravel())]
    return lax.ppermute(array, axes, turn)


def body(mask, cotangent, pupil_phase, source_weight, shift_table, source_ids, source_count):
    height, columns = mask.shape
    n_tile, n_src = lax.axis_size("tile"), lax.axis_size("src")
    col_table, row_table, out_table, out_cols = image_tables(columns, height, n_tile, n_src)
    sizes = {"src": n_src, "tile": n_tile}
    own, zeros = forward(mask, cotangent, col_table, row_table)
    ids = jnp.concatenate([source_ids, source_count[:, None]], 1) + zeros
    bit = 1
    while bit < n_src // 2:
        ids = jnp.concatenate([ids, swapped(ids, sizes, {"src": bit})], 0)
        bit *= 2
    step = 1
    while step < n_tile // 2:
        own = own + swapped(own, sizes, {"tile": step})
        step *= 2
    own_lines = slot_lines(ids + own[SUMS : SUMS + 1, : SLOTS + 1].astype(jnp.int32), shift_table.T, source_weight.reshape(-1, LANES))
    other_lines = swapped(own_lines, sizes, {"src": bit})
    other = swapped(own, sizes, {"tile": step})
    pupil = pupil_rows(pupil_phase + own[SUMS : SUMS + 1, :PUPIL])
    return adjoint(
        own, other, own_lines, other_lines, pupil, grid_tables(), out_cols, out_table, n_src
    )


def solution(mesh):
    placed = (
        P(("grp", "tile"), None),
        P(("grp", "tile"), None),
        P(),
        P(),
        P(),
        P(("grp", "src"), None),
        P(("grp", "src")),
    )
    return jax.shard_map(
        body, mesh=mesh, in_specs=placed, out_specs=P(("grp", "tile"), "src", None), check_vma=False
    )
```

```python
import functools
import math

import jax
import jax.numpy as jnp
import ml_dtypes
import numpy as np
from jax import lax
from jax.experimental import pallas as pl
from jax.experimental.pallas import tpu as pltpu
from jax.sharding import PartitionSpec as P

COLS = 2048
TILE_ROWS = 2048
BAND = 128
PUPIL = 64
SLOTS = 8
GRID = 128
CHUNKS = (1, 1, 2, 2, 1, 1)
GROUPS = (16, 20, 24, 32)
OX, OY, FACTOR, COUNT = range(4)
PARTS = 4
LANES = 128
SUMS = 2 * BAND + GRID
GRANT = 53 * 1024 * 1024

VMEM = pl.BlockSpec(memory_space=pltpu.VMEM)
SMEM = pl.BlockSpec(memory_space=pltpu.SMEM)
HBM = pl.BlockSpec(memory_space=pltpu.HBM)


def waves(positions, freqs, length):
    product = np.multiply.outer(positions, freqs) % length
    angle = product.astype(np.float64) * (2.0 * math.pi / length)
    return np.cos(angle), np.sin(angle)


def lowpass(positions, length):
    freqs = np.arange(1, PUPIL)
    step = length // GRID
    apart = np.arange(GRID)[None, :] * step - positions[:, None]
    product = (apart[:, :, None] * freqs) % length
    return (1.0 + 2.0 * np.cos(product * (2.0 * math.pi / length)).sum(2)) / GRID


def low(array):
    return np.ascontiguousarray(array).astype(ml_dtypes.bfloat16)


@functools.cache
def image_tables(columns, height, n_tile, n_src):
    band = np.arange(BAND) - BAND // 2
    cols = np.arange(columns)
    rows = np.arange(TILE_ROWS)
    cos, sin = waves(cols, band, columns)
    col_table = low(np.concatenate([cos, -sin, lowpass(cols, columns)], 1))
    cos, sin = waves(rows, band, TILE_ROWS)
    row_table = np.concatenate([cos, sin, lowpass(rows, TILE_ROWS)], 1)
    row_table = low(row_table.reshape(n_tile, height, 2 * BAND + GRID).transpose(0, 2, 1))
    portion = height // n_src
    out_table = np.concatenate([cos, -sin], 1).astype(np.float32)
    out_table = out_table.reshape(n_tile * n_src, portion, 2 * BAND)
    cos, sin = waves(cols, band, columns)
    return col_table, row_table, out_table, low(np.concatenate([cos, -sin], 1).T)


COLS_IN, COLS_OUT = slice(0, 2 * BAND), slice(2 * BAND, 2 * BAND + 2 * GRID)
ROWS_IN = slice(COLS_OUT.stop, COLS_OUT.stop + GRID)
ROWS_OUT = slice(ROWS_IN.stop, ROWS_IN.stop + 2 * PUPIL)


@functools.cache
def grid_tables():
    points = np.arange(GRID)
    band = np.arange(BAND) - BAND // 2
    cos, sin = waves(points, band, GRID)
    cols_in = np.block([[cos.T, sin.T], [-sin.T, cos.T]])
    cols_out = np.block([[cos, -sin], [sin, cos]])
    cos, sin = waves(points, np.arange(PUPIL) - PUPIL // 2, GRID)
    rows_in = np.block([[cos, -sin, sin, cos]])
    rows_out = np.block([[cos.T, sin.T], [-sin.T, cos.T]])
    return low(np.concatenate([cols_in, cols_out, rows_in, rows_out], 0))


def dot(left, right):
    return jnp.dot(left, right, preferred_element_type=jnp.float32)


def forward_kernel(
    mask, cotangent, col_table, row_table,
    partial, zeros,
    mask_v, cot_v, col_v, row_v, sems,
):
    columns = mask.shape[1]
    ends = np.cumsum(CHUNKS) * (columns // sum(CHUNKS))
    parts = [pl.ds(int(low), int(high - low)) for low, high in zip([0, *ends], ends)]
    tile = lax.axis_index("tile")
    chunk_copies = []
    for step, part in enumerate(parts):
        copies = [
            pltpu.make_async_copy(col_table.at[part, :], col_v.at[part, :], sems.at[step, 0]),
            pltpu.make_async_copy(mask.at[:, part], mask_v.at[:, part], sems.at[step, 1]),
            pltpu.make_async_copy(cotangent.at[:, part], cot_v.at[:, part], sems.at[step, 2]),
        ]
        for copy in copies:
            copy.start()
        chunk_copies.append(copies)
    row_copy = pltpu.make_async_copy(row_table.at[tile], row_v, sems.at[len(CHUNKS), 0])
    row_copy.start()

    for step, part in enumerate(parts):
        for copy in chunk_copies[step]:
            copy.wait()
        mask_add = dot(mask_v[:, part], col_v[part, : 2 * BAND])
        cot_add = dot(cot_v[:, part], col_v[part, 2 * BAND :])
        mask_part = mask_add if step == 0 else mask_part + mask_add
        cot_part = cot_add if step == 0 else cot_part + cot_add

    row_copy.wait()
    blocks = dot(row_v[: 2 * BAND, :], mask_part.astype(jnp.bfloat16))
    partial[:BAND, :] = blocks[:BAND, :BAND] + blocks[BAND:, BAND:]
    partial[BAND : 2 * BAND, :] = blocks[:BAND, BAND:] - blocks[BAND:, :BAND]
    partial[2 * BAND : SUMS, :] = dot(row_v[2 * BAND :, :], cot_part.astype(jnp.bfloat16))
    partial[SUMS:, :] = jnp.zeros((8, BAND), jnp.float32)
    zeros[...] = jnp.zeros_like(zeros)


def forward(mask, cotangent, col_table, row_table):
    height, columns = mask.shape
    return pl.pallas_call(
        forward_kernel,
        out_shape=(
            jax.ShapeDtypeStruct((SUMS + 8, BAND), jnp.float32),
            jax.ShapeDtypeStruct((1, SLOTS + 1), jnp.int32),
        ),
        in_specs=[HBM] * 4,
        out_specs=(VMEM, VMEM),
        scratch_shapes=[
            pltpu.VMEM(mask.shape, jnp.bfloat16),
            pltpu.VMEM(mask.shape, jnp.bfloat16),
            pltpu.VMEM(col_table.shape, jnp.bfloat16),
            pltpu.VMEM(row_table.shape[1:], jnp.bfloat16),
            pltpu.SemaphoreType.DMA((len(CHUNKS) + 1, 3)),
        ],
        compiler_params=pltpu.CompilerParams(vmem_limit_bytes=GRANT),
        cost_estimate=pl.CostEstimate(
            flops=2 * height * columns * SUMS, bytes_accessed=6 * 1024 * 1024, transcendentals=0
        ),
        name="forward",
    )(mask, cotangent, col_table, row_table)


def lines_kernel(ids, shift, weight, lines):
    lane = lax.broadcasted_iota(jnp.int32, (SLOTS, LANES), 1)
    place = lax.broadcasted_iota(jnp.int32, (SLOTS, LANES), 0)

    def one(row, carry):
        blocks, weights, there = [], [], jnp.full_like(lane, -1)
        for slot in range(SLOTS):
            source = ids[row, slot]
            start = pl.multiple_of(source // LANES * LANES, LANES)
            blocks.append(shift[:, pl.ds(start, LANES)])
            weights.append(weight[pl.ds(source // LANES, 1), :])
            found = jnp.where(slot < ids[row, SLOTS], source % LANES, -1)
            there = jnp.where(place == slot, found, there)
        here = lane == there
        line = jnp.zeros((SLOTS, LANES), jnp.float32)
        for dim, into in ((0, OX), (1, OY)):
            values = jnp.concatenate([block[dim : dim + 1, :] for block in blocks], 0)
            found = jnp.sum(jnp.where(here, values.astype(jnp.float32), 0.0), 1, keepdims=True)
            line = jnp.where(lane == into, found, line)
        found = jnp.sum(jnp.where(here, jnp.concatenate(weights, 0), 0.0), 1, keepdims=True)
        line = jnp.where(lane == FACTOR, found * (2.0 / SLOTS / PUPIL / PUPIL), line)
        line = jnp.where(lane == COUNT, ids[row, SLOTS].astype(jnp.float32), line)
        lines[pl.ds(pl.multiple_of(row * SLOTS, SLOTS), SLOTS), :] = line
        return carry

    lax.fori_loop(0, ids.shape[0], one, jnp.int32(0), unroll=ids.shape[0] <= 4)


def slot_lines(ids, shift, weight):
    count = ids.shape[0] * SLOTS
    return pl.pallas_call(
        lines_kernel,
        out_shape=jax.ShapeDtypeStruct((count, LANES), jnp.float32),
        in_specs=[SMEM, VMEM, VMEM],
        out_specs=VMEM,
        compiler_params=pltpu.CompilerParams(vmem_limit_bytes=2 * 1024 * 1024),
        cost_estimate=pl.CostEstimate(flops=1, bytes_accessed=1, transcendentals=0),
        name="slot_lines",
    )(ids, shift, weight)


def adjoint_kernel(
    n_src, own, other, own_lines, other_lines, pupil, table, col_table, out_table,
    result,
    spec_real, spec_imag, image, table_v, col_v, out_v, result_v, lines, used, sems, out_sems, *bands,
):
    place = lax.axis_index("tile") * n_src + lax.axis_index("src")
    grid_copy = pltpu.make_async_copy(table, table_v, sems.at[0])
    out_copy = pltpu.make_async_copy(out_table.at[place], out_v, sems.at[1])
    col_copy = pltpu.make_async_copy(col_table, col_v, sems.at[2])
    half = own_lines.shape[0]
    own_copy = pltpu.make_async_copy(own_lines, lines.at[pl.ds(0, half), :], sems.at[3])
    other_copy = pltpu.make_async_copy(other_lines, lines.at[pl.ds(half, half), :], sems.at[4])
    for copy in (own_copy, other_copy, grid_copy, out_copy, col_copy):
        copy.start()

    scale = 1.0 / math.sqrt(TILE_ROWS * COLS)
    whole = own[:SUMS, :] + other[:SUMS, :]
    spec = (whole[: 2 * BAND] * scale).astype(jnp.bfloat16).astype(jnp.float32)
    spec_real[...] = spec[:BAND]
    spec_imag[...] = spec[BAND:]
    image[:GRID, :] = whole[2 * BAND :]
    image[GRID:, :] = whole[2 * BAND :]
    for band in bands:
        band[...] = jnp.zeros_like(band)
    for slot in range(2 * half + GROUPS[-1]):
        used[slot] = jnp.int32(0)
    own_copy.wait()
    other_copy.wait()

    def add(block, total):
        first = block * SLOTS
        for slot in range(SLOTS):
            used[total + slot] = first + slot
        return total + lines[first, COUNT].astype(jnp.int32)

    blocks = 2 * half // SLOTS
    total = lax.fori_loop(0, blocks, add, jnp.int32(0), unroll=blocks <= 8)
    grid_copy.wait()

    def group(first, size):
        starts, pupils, amplitudes = [], [], []
        for slot in range(size):
            place = first + slot
            index = used[place]
            factor = jnp.where(place < total, lines[index, FACTOR], 0.0)
            offset_x = lines[index, OX].astype(jnp.int32)
            offset_y = lines[index, OY].astype(jnp.int32)
            real = pltpu.roll(pupil[:PUPIL, :], offset_x, 1)
            imag = pltpu.roll(pupil[PUPIL:, :], offset_x, 1)
            rows = pl.ds(offset_y, PUPIL)
            amp_real = real * spec_real[rows, :] - imag * spec_imag[rows, :]
            amp_imag = real * spec_imag[rows, :] + imag * spec_real[rows, :]
            starts.append(offset_y)
            pupils.append((real, imag, factor))
            amplitudes.append(jnp.concatenate([amp_real, amp_imag], 1).astype(jnp.bfloat16))
        halfway = dot(jnp.concatenate(amplitudes, 0), table_v[COLS_IN, :]).astype(jnp.bfloat16)
        halfway = jnp.concatenate(
            [
                jnp.concatenate(
                    [
                        halfway[slot * PUPIL : (slot + 1) * PUPIL, :GRID],
                        halfway[slot * PUPIL : (slot + 1) * PUPIL, GRID:],
                    ],
                    0,
                )
                for slot in range(size)
            ],
            1,
        )
        rows_in = table_v[ROWS_IN, :]
        rows_in = jnp.concatenate([rows_in[:, : 2 * PUPIL], rows_in[:, 2 * PUPIL :]], 0)
        field = dot(rows_in, halfway)
        field_grad = jnp.concatenate(
            [
                (field[:, slot * GRID : (slot + 1) * GRID] * image[...]).astype(jnp.bfloat16)
                for slot in range(size)
            ],
            1,
        )
        back = dot(table_v[ROWS_OUT, :], field_grad).astype(jnp.bfloat16)
        back = jnp.concatenate(
            [
                jnp.concatenate(
                    [
                        back[:PUPIL, slot * GRID : (slot + 1) * GRID],
                        back[PUPIL:, slot * GRID : (slot + 1) * GRID],
                    ],
                    1,
                )
                for slot in range(size)
            ],
            0,
        )
        grad = dot(back, table_v[COLS_OUT, :])
        for slot in range(size):
            real, imag, factor = pupils[slot]
            grad_real = grad[slot * PUPIL : (slot + 1) * PUPIL, :BAND] * factor
            grad_imag = grad[slot * PUPIL : (slot + 1) * PUPIL, BAND:] * factor
            rows = pl.ds(starts[slot], PUPIL)
            band_real, band_imag = bands[slot % 2], bands[2 + slot % 2]
            band_real[rows, :] = band_real[rows, :] + (real * grad_real + imag * grad_imag)
            band_imag[rows, :] = band_imag[rows, :] + (real * grad_imag - imag * grad_real)

    largest, second = GROUPS[-1], GROUPS[-2]
    whole_groups = (total + largest - 1 - second) // largest

    def whole_group(step, carry):
        group(step * largest, largest)
        return carry

    lax.fori_loop(0, whole_groups, whole_group, jnp.int32(0))
    rest = total - whole_groups * largest
    for below, size in zip((0, *GROUPS), GROUPS[:-1]):

        @pl.when((rest > below) & (rest <= size))
        def _():
            group(whole_groups * largest, size)

    real = (bands[0][...] + bands[1][...]) * scale
    imag = (bands[2][...] + bands[3][...]) * scale
    left = jnp.concatenate(
        [jnp.concatenate([real, imag], 1), jnp.concatenate([imag, -real], 1)], 0
    ).astype(jnp.bfloat16)
    out_copy.wait()
    mixed = dot(out_v[...].astype(jnp.bfloat16), left).astype(jnp.bfloat16)
    col_copy.wait()
    width = result.shape[2] // PARTS
    copies = []
    for step in range(PARTS):
        part = pl.ds(step * width, width)
        result_v[:, part] = dot(mixed, col_v[:, part])
        copy = pltpu.make_async_copy(
            result_v.at[:, part], result.at[0, :, part], out_sems.at[step]
        )
        copy.start()
        copies.append(copy)
    for copy in copies:
        copy.wait()


def adjoint(own, other, own_lines, other_lines, pupil, table, col_table, out_table, n_src):
    portion = out_table.shape[1]
    columns = col_table.shape[1]
    band = pltpu.VMEM((BAND, BAND), jnp.float32)
    return pl.pallas_call(
        functools.partial(adjoint_kernel, n_src),
        out_shape=jax.ShapeDtypeStruct((1, portion, columns), jnp.float32),
        in_specs=[VMEM] * 5 + [HBM] * 3,
        out_specs=HBM,
        scratch_shapes=[
            band,
            band,
            pltpu.VMEM((2 * GRID, GRID), jnp.float32),
            pltpu.VMEM(table.shape, jnp.bfloat16),
            pltpu.VMEM(col_table.shape, jnp.bfloat16),
            pltpu.VMEM(out_table.shape[1:], jnp.float32),
            pltpu.VMEM((portion, columns), jnp.float32),
            pltpu.SMEM((2 * own_lines.shape[0], LANES), jnp.float32),
            pltpu.SMEM((2 * own_lines.shape[0] + GROUPS[-1],), jnp.int32),
            pltpu.SemaphoreType.DMA((5,)),
            pltpu.SemaphoreType.DMA((PARTS,)),
            band,
            band,
            band,
            band,
        ],
        compiler_params=pltpu.CompilerParams(vmem_limit_bytes=GRANT),
        cost_estimate=pl.CostEstimate(
            flops=2 * 128 * 4096 * 256, bytes_accessed=4 * 1024 * 1024, transcendentals=0
        ),
        name="adjoint",
    )(own, other, own_lines, other_lines, pupil, table, col_table, out_table)


def pupil_rows(phase):
    grid = jnp.arange(PUPIL, dtype=jnp.int32)
    radius = (2 * grid[:, None] - PUPIL + 1) ** 2 + (2 * grid[None, :] - PUPIL + 1) ** 2
    inside = radius <= PUPIL * PUPIL
    both = jnp.concatenate(
        [jnp.where(inside, jnp.cos(phase), 0.0), jnp.where(inside, jnp.sin(phase), 0.0)], 0
    )
    return jnp.pad(both, ((0, 0), (0, BAND - PUPIL)))


def swapped(array, sizes, steps):
    axes = tuple(sizes)
    places = np.arange(math.prod(sizes.values())).reshape(tuple(sizes.values()))
    there = places
    for dim, axis in enumerate(axes):
        there = np.take(there, np.arange(sizes[axis]) ^ steps.get(axis, 0), dim)
    turn = [(int(a), int(b)) for a, b in zip(places.ravel(), there.ravel())]
    return lax.ppermute(array, axes, turn)


def body(mask, cotangent, pupil_phase, source_weight, shift_table, source_ids, source_count):
    height, columns = mask.shape
    n_tile, n_src = lax.axis_size("tile"), lax.axis_size("src")
    col_table, row_table, out_table, out_cols = image_tables(columns, height, n_tile, n_src)
    sizes = {"src": n_src, "tile": n_tile}
    own, zeros = forward(mask, cotangent, col_table, row_table)
    ids = jnp.concatenate([source_ids, source_count[:, None]], 1) + zeros
    bit = 1
    while bit < n_src // 2:
        ids = jnp.concatenate([ids, swapped(ids, sizes, {"src": bit})], 0)
        bit *= 2
    step = 1
    while step < n_tile // 2:
        own = own + swapped(own, sizes, {"tile": step})
        step *= 2
    own_lines = slot_lines(ids + own[SUMS : SUMS + 1, : SLOTS + 1].astype(jnp.int32), shift_table.T, source_weight.reshape(-1, LANES))
    other_lines = swapped(own_lines, sizes, {"src": bit})
    other = swapped(own, sizes, {"tile": step})
    pupil = pupil_rows(pupil_phase + own[SUMS : SUMS + 1, :PUPIL])
    return adjoint(
        own, other, own_lines, other_lines, pupil, grid_tables(), out_cols, out_table, n_src
    )


def solution(mesh):
    placed = (
        P(("grp", "tile"), None),
        P(("grp", "tile"), None),
        P(),
        P(),
        P(),
        P(("grp", "src"), None),
        P(("grp", "src")),
    )
    return jax.shard_map(
        body, mesh=mesh, in_specs=placed, out_specs=P(("grp", "tile"), "src", None), check_vma=False
    )
```

```python
import functools
import math

import jax
import jax.numpy as jnp
import ml_dtypes
import numpy as np
from jax import lax
from jax.experimental import pallas as pl
from jax.experimental.pallas import tpu as pltpu
from jax.sharding import PartitionSpec as P

COLS = 2048
TILE_ROWS = 2048
BAND = 128
PUPIL = 64
SLOTS = 8
GRID = 128
CHUNKS = (1, 1, 2, 2, 1, 1)
GROUPS = (16, 20, 24, 32)
PACK = 4
OX, OY, FACTOR, COUNT = range(4)
PARTS = 4
LANES = 128
SUMS = 2 * BAND + GRID
GRANT = 53 * 1024 * 1024

VMEM = pl.BlockSpec(memory_space=pltpu.VMEM)
SMEM = pl.BlockSpec(memory_space=pltpu.SMEM)
HBM = pl.BlockSpec(memory_space=pltpu.HBM)


def waves(positions, freqs, length):
    product = np.multiply.outer(positions, freqs) % length
    angle = product.astype(np.float64) * (2.0 * math.pi / length)
    return np.cos(angle), np.sin(angle)


def lowpass(positions, length):
    freqs = np.arange(1, PUPIL)
    step = length // GRID
    apart = np.arange(GRID)[None, :] * step - positions[:, None]
    product = (apart[:, :, None] * freqs) % length
    return (1.0 + 2.0 * np.cos(product * (2.0 * math.pi / length)).sum(2)) / GRID


def low(array):
    return np.ascontiguousarray(array).astype(ml_dtypes.bfloat16)


@functools.cache
def image_tables(columns, height, n_tile, n_src):
    band = np.arange(BAND) - BAND // 2
    cols = np.arange(columns)
    rows = np.arange(TILE_ROWS)
    cos, sin = waves(cols, band, columns)
    col_table = low(np.concatenate([cos, -sin, lowpass(cols, columns)], 1))
    cos, sin = waves(rows, band, TILE_ROWS)
    row_table = np.concatenate([cos, sin, lowpass(rows, TILE_ROWS)], 1)
    row_table = low(row_table.reshape(n_tile, height, 2 * BAND + GRID).transpose(0, 2, 1))
    portion = height // n_src
    out_table = np.concatenate([cos, -sin], 1).astype(np.float32)
    out_table = out_table.reshape(n_tile * n_src, portion, 2 * BAND)
    cos, sin = waves(cols, band, columns)
    return col_table, row_table, out_table, low(np.concatenate([cos, -sin], 1).T)


COLS_IN, COLS_OUT = slice(0, 2 * BAND), slice(2 * BAND, 2 * BAND + 2 * GRID)
ROWS_IN = slice(COLS_OUT.stop, COLS_OUT.stop + GRID)
ROWS_OUT = slice(ROWS_IN.stop, ROWS_IN.stop + 2 * PUPIL)


@functools.cache
def grid_tables():
    points = np.arange(GRID)
    band = np.arange(BAND) - BAND // 2
    cos, sin = waves(points, band, GRID)
    cols_in = np.block([[cos.T, sin.T], [-sin.T, cos.T]])
    cols_out = np.block([[cos, -sin], [sin, cos]])
    cos, sin = waves(points, np.arange(PUPIL) - PUPIL // 2, GRID)
    rows_in = np.block([[cos, -sin, sin, cos]])
    rows_out = np.block([[cos.T, sin.T], [-sin.T, cos.T]])
    return low(np.concatenate([cols_in, cols_out, rows_in, rows_out], 0))


def dot(left, right):
    return jnp.dot(left, right, preferred_element_type=jnp.float32)


def forward_kernel(
    mask, cotangent, col_table, row_table,
    partial, zeros,
    mask_v, cot_v, col_v, row_v, sems,
):
    columns = mask.shape[1]
    ends = np.cumsum(CHUNKS) * (columns // sum(CHUNKS))
    parts = [pl.ds(int(low), int(high - low)) for low, high in zip([0, *ends], ends)]
    tile = lax.axis_index("tile")
    chunk_copies = []
    for step, part in enumerate(parts):
        copies = [
            pltpu.make_async_copy(col_table.at[part, :], col_v.at[part, :], sems.at[step, 0]),
            pltpu.make_async_copy(mask.at[:, part], mask_v.at[:, part], sems.at[step, 1]),
            pltpu.make_async_copy(cotangent.at[:, part], cot_v.at[:, part], sems.at[step, 2]),
        ]
        for copy in copies:
            copy.start()
        chunk_copies.append(copies)
    row_copy = pltpu.make_async_copy(row_table.at[tile], row_v, sems.at[len(CHUNKS), 0])
    row_copy.start()

    for step, part in enumerate(parts):
        for copy in chunk_copies[step]:
            copy.wait()
        mask_add = dot(mask_v[:, part], col_v[part, : 2 * BAND])
        cot_add = dot(cot_v[:, part], col_v[part, 2 * BAND :])
        mask_part = mask_add if step == 0 else mask_part + mask_add
        cot_part = cot_add if step == 0 else cot_part + cot_add

    row_copy.wait()
    blocks = dot(row_v[: 2 * BAND, :], mask_part.astype(jnp.bfloat16))
    partial[:BAND, :] = blocks[:BAND, :BAND] + blocks[BAND:, BAND:]
    partial[BAND : 2 * BAND, :] = blocks[:BAND, BAND:] - blocks[BAND:, :BAND]
    partial[2 * BAND : SUMS, :] = dot(row_v[2 * BAND :, :], cot_part.astype(jnp.bfloat16))
    partial[SUMS:, :] = jnp.zeros((8, BAND), jnp.float32)
    zeros[...] = jnp.zeros_like(zeros)


def forward(mask, cotangent, col_table, row_table):
    height, columns = mask.shape
    return pl.pallas_call(
        forward_kernel,
        out_shape=(
            jax.ShapeDtypeStruct((SUMS + 8, BAND), jnp.float32),
            jax.ShapeDtypeStruct((1, SLOTS + 1), jnp.int32),
        ),
        in_specs=[HBM] * 4,
        out_specs=(VMEM, VMEM),
        scratch_shapes=[
            pltpu.VMEM(mask.shape, jnp.bfloat16),
            pltpu.VMEM(mask.shape, jnp.bfloat16),
            pltpu.VMEM(col_table.shape, jnp.bfloat16),
            pltpu.VMEM(row_table.shape[1:], jnp.bfloat16),
            pltpu.SemaphoreType.DMA((len(CHUNKS) + 1, 3)),
        ],
        compiler_params=pltpu.CompilerParams(vmem_limit_bytes=GRANT),
        cost_estimate=pl.CostEstimate(
            flops=2 * height * columns * SUMS, bytes_accessed=6 * 1024 * 1024, transcendentals=0
        ),
        name="forward",
    )(mask, cotangent, col_table, row_table)


def lines_kernel(ids, shift, weight, lines):
    lane = lax.broadcasted_iota(jnp.int32, (SLOTS, LANES), 1)
    place = lax.broadcasted_iota(jnp.int32, (SLOTS, LANES), 0)

    def one(row, carry):
        blocks, weights, there = [], [], jnp.full_like(lane, -1)
        for slot in range(SLOTS):
            source = ids[row, slot]
            start = pl.multiple_of(source // LANES * LANES, LANES)
            blocks.append(shift[:, pl.ds(start, LANES)])
            weights.append(weight[pl.ds(source // LANES, 1), :])
            found = jnp.where(slot < ids[row, SLOTS], source % LANES, -1)
            there = jnp.where(place == slot, found, there)
        here = lane == there
        line = jnp.zeros((SLOTS, LANES), jnp.float32)
        for dim, into in ((0, OX), (1, OY)):
            values = jnp.concatenate([block[dim : dim + 1, :] for block in blocks], 0)
            found = jnp.sum(jnp.where(here, values.astype(jnp.float32), 0.0), 1, keepdims=True)
            line = jnp.where(lane == into, found, line)
        found = jnp.sum(jnp.where(here, jnp.concatenate(weights, 0), 0.0), 1, keepdims=True)
        line = jnp.where(lane == FACTOR, found * (2.0 / SLOTS / PUPIL / PUPIL), line)
        line = jnp.where(lane == COUNT, ids[row, SLOTS].astype(jnp.float32), line)
        lines[pl.ds(pl.multiple_of(row * SLOTS, SLOTS), SLOTS), :] = line
        return carry

    lax.fori_loop(0, ids.shape[0], one, jnp.int32(0), unroll=ids.shape[0] <= 4)


def slot_lines(ids, shift, weight):
    count = ids.shape[0] * SLOTS
    return pl.pallas_call(
        lines_kernel,
        out_shape=jax.ShapeDtypeStruct((count, LANES), jnp.float32),
        in_specs=[SMEM, VMEM, VMEM],
        out_specs=VMEM,
        compiler_params=pltpu.CompilerParams(vmem_limit_bytes=2 * 1024 * 1024),
        cost_estimate=pl.CostEstimate(flops=1, bytes_accessed=1, transcendentals=0),
        name="slot_lines",
    )(ids, shift, weight)


def adjoint_kernel(
    n_src, own, other, own_lines, other_lines, pupil, table, col_table, out_table,
    result,
    spec_real, spec_imag, image, col_v, out_v, result_v, lines, used, sems, out_sems, *bands,
):
    place = lax.axis_index("tile") * n_src + lax.axis_index("src")
    out_copy = pltpu.make_async_copy(out_table.at[place], out_v, sems.at[1])
    col_copy = pltpu.make_async_copy(col_table, col_v, sems.at[2])
    half = own_lines.shape[0]
    own_copy = pltpu.make_async_copy(own_lines, lines.at[pl.ds(0, half), :], sems.at[3])
    other_copy = pltpu.make_async_copy(other_lines, lines.at[pl.ds(half, half), :], sems.at[0])
    for copy in (own_copy, other_copy, out_copy, col_copy):
        copy.start()

    scale = 1.0 / math.sqrt(TILE_ROWS * COLS)
    whole = own[:SUMS, :] + other[:SUMS, :]
    spec = (whole[: 2 * BAND] * scale).astype(jnp.bfloat16).astype(jnp.float32)
    spec_real[...] = spec[:BAND]
    spec_imag[...] = spec[BAND:]
    image[:GRID, :] = whole[2 * BAND :]
    image[GRID:, :] = whole[2 * BAND :]
    for band in bands:
        band[...] = jnp.zeros_like(band)
    for slot in range(2 * half + GROUPS[-1]):
        used[slot] = jnp.int32(0)
    own_copy.wait()
    other_copy.wait()

    def add(block, total):
        first = block * SLOTS
        for slot in range(SLOTS):
            used[total + slot] = first + slot
        return total + lines[first, COUNT].astype(jnp.int32)

    blocks = 2 * half // SLOTS
    total = lax.fori_loop(0, blocks, add, jnp.int32(0), unroll=blocks <= 8)

    def group(first, size):
        held = [None] * (size // PACK)
        slots = [None] * (size // PACK)

        def amplitude(pack):
            slots[pack], parts = [], []
            for slot in range(PACK):
                place = first + pack * PACK + slot
                index = used[place]
                factor = jnp.where(place < total, lines[index, FACTOR], 0.0)
                offset_x = lines[index, OX].astype(jnp.int32)
                rows = pl.ds(lines[index, OY].astype(jnp.int32), PUPIL)
                real = pltpu.roll(pupil[:PUPIL, :], offset_x, 1)
                imag = pltpu.roll(pupil[PUPIL:, :], offset_x, 1)
                amp_real = real * spec_real[rows, :] - imag * spec_imag[rows, :]
                amp_imag = real * spec_imag[rows, :] + imag * spec_real[rows, :]
                slots[pack].append((rows, real, imag, factor))
                parts.append(jnp.concatenate([amp_real, amp_imag], 1).astype(jnp.bfloat16))
            held[pack] = jnp.concatenate(parts, 0)

        def halfway(pack):
            found = dot(held[pack], table[COLS_IN, :]).astype(jnp.bfloat16)
            parts = []
            for slot in range(PACK):
                block = found[slot * PUPIL : (slot + 1) * PUPIL, :]
                parts.append(jnp.concatenate([block[:, :GRID], block[:, GRID:]], 0))
            held[pack] = jnp.concatenate(parts, 1)

        def field_grad(pack):
            rows_in = table[ROWS_IN, :]
            rows_in = jnp.concatenate([rows_in[:, : 2 * PUPIL], rows_in[:, 2 * PUPIL :]], 0)
            field = dot(rows_in, held[pack])
            parts = []
            for slot in range(PACK):
                block = field[:, slot * GRID : (slot + 1) * GRID]
                parts.append((block * image[...]).astype(jnp.bfloat16))
            held[pack] = jnp.concatenate(parts, 1)

        def back(pack):
            found = dot(table[ROWS_OUT, :], held[pack]).astype(jnp.bfloat16)
            parts = []
            for slot in range(PACK):
                block = found[:, slot * GRID : (slot + 1) * GRID]
                parts.append(jnp.concatenate([block[:PUPIL], block[PUPIL:]], 1))
            held[pack] = jnp.concatenate(parts, 0)

        def gradient(pack):
            grad = dot(held[pack], table[COLS_OUT, :])
            for slot, (rows, real, imag, factor) in enumerate(slots[pack]):
                block = grad[slot * PUPIL : (slot + 1) * PUPIL, :] * factor
                grad_real, grad_imag = block[:, :BAND], block[:, BAND:]
                band_real, band_imag = bands[slot % 2], bands[2 + slot % 2]
                band_real[rows, :] = band_real[rows, :] + (real * grad_real + imag * grad_imag)
                band_imag[rows, :] = band_imag[rows, :] + (real * grad_imag - imag * grad_real)

        stages = (amplitude, halfway, field_grad, back, gradient)
        for step in range(len(held) + len(stages) - 1):
            for late, stage in reversed(list(enumerate(stages))):
                if 0 <= step - late < len(held):
                    stage(step - late)

    largest, second = GROUPS[-1], GROUPS[-2]
    whole_groups = (total + largest - 1 - second) // largest

    def whole_group(step, carry):
        group(step * largest, largest)
        return carry

    lax.fori_loop(0, whole_groups, whole_group, jnp.int32(0))
    rest = total - whole_groups * largest
    for below, size in zip((0, *GROUPS), GROUPS[:-1]):

        @pl.when((rest > below) & (rest <= size))
        def _():
            group(whole_groups * largest, size)

    real = (bands[0][...] + bands[1][...]) * scale
    imag = (bands[2][...] + bands[3][...]) * scale
    left = jnp.concatenate(
        [jnp.concatenate([real, imag], 1), jnp.concatenate([imag, -real], 1)], 0
    ).astype(jnp.bfloat16)
    out_copy.wait()
    mixed = dot(out_v[...].astype(jnp.bfloat16), left).astype(jnp.bfloat16)
    col_copy.wait()
    width = result.shape[2] // PARTS
    copies = []
    for step in range(PARTS):
        part = pl.ds(step * width, width)
        result_v[:, part] = dot(mixed, col_v[:, part])
        copy = pltpu.make_async_copy(
            result_v.at[:, part], result.at[0, :, part], out_sems.at[step]
        )
        copy.start()
        copies.append(copy)
    for copy in copies:
        copy.wait()


def adjoint(own, other, own_lines, other_lines, pupil, table, col_table, out_table, n_src):
    portion = out_table.shape[1]
    columns = col_table.shape[1]
    band = pltpu.VMEM((BAND, BAND), jnp.float32)
    return pl.pallas_call(
        functools.partial(adjoint_kernel, n_src),
        out_shape=jax.ShapeDtypeStruct((1, portion, columns), jnp.float32),
        in_specs=[VMEM] * 6 + [HBM] * 2,
        out_specs=HBM,
        scratch_shapes=[
            band,
            band,
            pltpu.VMEM((2 * GRID, GRID), jnp.float32),
            pltpu.VMEM(col_table.shape, jnp.bfloat16),
            pltpu.VMEM(out_table.shape[1:], jnp.float32),
            pltpu.VMEM((portion, columns), jnp.float32),
            pltpu.SMEM((2 * own_lines.shape[0], LANES), jnp.float32),
            pltpu.SMEM((2 * own_lines.shape[0] + GROUPS[-1],), jnp.int32),
            pltpu.SemaphoreType.DMA((4,)),
            pltpu.SemaphoreType.DMA((PARTS,)),
            band,
            band,
            band,
            band,
        ],
        compiler_params=pltpu.CompilerParams(vmem_limit_bytes=GRANT),
        cost_estimate=pl.CostEstimate(
            flops=2 * 128 * 4096 * 256, bytes_accessed=4 * 1024 * 1024, transcendentals=0
        ),
        name="adjoint",
    )(own, other, own_lines, other_lines, pupil, table, col_table, out_table)


def pupil_rows(phase):
    grid = jnp.arange(PUPIL, dtype=jnp.int32)
    radius = (2 * grid[:, None] - PUPIL + 1) ** 2 + (2 * grid[None, :] - PUPIL + 1) ** 2
    inside = radius <= PUPIL * PUPIL
    both = jnp.concatenate(
        [jnp.where(inside, jnp.cos(phase), 0.0), jnp.where(inside, jnp.sin(phase), 0.0)], 0
    )
    return jnp.pad(both, ((0, 0), (0, BAND - PUPIL)))


def swapped(array, sizes, steps):
    axes = tuple(sizes)
    places = np.arange(math.prod(sizes.values())).reshape(tuple(sizes.values()))
    there = places
    for dim, axis in enumerate(axes):
        there = np.take(there, np.arange(sizes[axis]) ^ steps.get(axis, 0), dim)
    turn = [(int(a), int(b)) for a, b in zip(places.ravel(), there.ravel())]
    return lax.ppermute(array, axes, turn)


def body(mask, cotangent, pupil_phase, source_weight, shift_table, source_ids, source_count):
    height, columns = mask.shape
    n_tile, n_src = lax.axis_size("tile"), lax.axis_size("src")
    col_table, row_table, out_table, out_cols = image_tables(columns, height, n_tile, n_src)
    sizes = {"src": n_src, "tile": n_tile}
    own, zeros = forward(mask, cotangent, col_table, row_table)
    ids = jnp.concatenate([source_ids, source_count[:, None]], 1) + zeros
    bit = 1
    while bit < n_src // 2:
        ids = jnp.concatenate([ids, swapped(ids, sizes, {"src": bit})], 0)
        bit *= 2
    step = 1
    while step < n_tile // 2:
        own = own + swapped(own, sizes, {"tile": step})
        step *= 2
    own_lines = slot_lines(ids + own[SUMS : SUMS + 1, : SLOTS + 1].astype(jnp.int32), shift_table.T, source_weight.reshape(-1, LANES))
    other_lines = swapped(own_lines, sizes, {"src": bit})
    other = swapped(own, sizes, {"tile": step})
    pupil = pupil_rows(pupil_phase + own[SUMS : SUMS + 1, :PUPIL])
    return adjoint(
        own, other, own_lines, other_lines, pupil, grid_tables(), out_cols, out_table, n_src
    )


def solution(mesh):
    placed = (
        P(("grp", "tile"), None),
        P(("grp", "tile"), None),
        P(),
        P(),
        P(),
        P(("grp", "src"), None),
        P(("grp", "src")),
    )
    return jax.shard_map(
        body, mesh=mesh, in_specs=placed, out_specs=P(("grp", "tile"), "src", None), check_vma=False
    )
```

```python
import functools
import math

import jax
import jax.numpy as jnp
import ml_dtypes
import numpy as np
from jax import lax
from jax.experimental import pallas as pl
from jax.experimental.pallas import tpu as pltpu
from jax.sharding import PartitionSpec as P

COLS = 2048
TILE_ROWS = 2048
BAND = 128
PUPIL = 64
SLOTS = 8
GRID = 128
CHUNKS = (1, 1, 2, 2, 1, 1)
GROUPS = (16, 20, 24, 32)
PACKS = 2
OX, OY, FACTOR, COUNT = range(4)
PARTS = 4
LANES = 128
SUMS = 2 * BAND + GRID
GRANT = 53 * 1024 * 1024

VMEM = pl.BlockSpec(memory_space=pltpu.VMEM)
SMEM = pl.BlockSpec(memory_space=pltpu.SMEM)
HBM = pl.BlockSpec(memory_space=pltpu.HBM)


def waves(positions, freqs, length):
    product = np.multiply.outer(positions, freqs) % length
    angle = product.astype(np.float64) * (2.0 * math.pi / length)
    return np.cos(angle), np.sin(angle)


def lowpass(positions, length):
    freqs = np.arange(1, PUPIL)
    step = length // GRID
    apart = np.arange(GRID)[None, :] * step - positions[:, None]
    product = (apart[:, :, None] * freqs) % length
    return (1.0 + 2.0 * np.cos(product * (2.0 * math.pi / length)).sum(2)) / GRID


def low(array):
    return np.ascontiguousarray(array).astype(ml_dtypes.bfloat16)


@functools.cache
def image_tables(columns, height, n_tile, n_src):
    band = np.arange(BAND) - BAND // 2
    cols = np.arange(columns)
    rows = np.arange(TILE_ROWS)
    cos, sin = waves(cols, band, columns)
    col_table = low(np.concatenate([cos, -sin, lowpass(cols, columns)], 1))
    cos, sin = waves(rows, band, TILE_ROWS)
    row_table = np.concatenate([cos, sin, lowpass(rows, TILE_ROWS)], 1)
    row_table = low(row_table.reshape(n_tile, height, 2 * BAND + GRID).transpose(0, 2, 1))
    portion = height // n_src
    out_table = np.concatenate([cos, -sin], 1).astype(np.float32)
    out_table = out_table.reshape(n_tile * n_src, portion, 2 * BAND)
    cos, sin = waves(cols, band, columns)
    return col_table, row_table, out_table, low(np.concatenate([cos, -sin], 1).T)


COLS_IN, COLS_OUT = slice(0, 2 * BAND), slice(2 * BAND, 2 * BAND + 2 * GRID)
ROWS_IN = slice(COLS_OUT.stop, COLS_OUT.stop + GRID)
ROWS_OUT = slice(ROWS_IN.stop, ROWS_IN.stop + 2 * PUPIL)


@functools.cache
def grid_tables():
    points = np.arange(GRID)
    band = np.arange(BAND) - BAND // 2
    cos, sin = waves(points, band, GRID)
    cols_in = np.block([[cos.T, sin.T], [-sin.T, cos.T]])
    cols_out = np.block([[cos, -sin], [sin, cos]])
    cos, sin = waves(points, np.arange(PUPIL) - PUPIL // 2, GRID)
    rows_in = np.block([[cos, -sin, sin, cos]])
    rows_out = np.block([[cos.T, sin.T], [-sin.T, cos.T]])
    return low(np.concatenate([cols_in, cols_out, rows_in, rows_out], 0))


def dot(left, right):
    return jnp.dot(left, right, preferred_element_type=jnp.float32)


def forward_kernel(
    mask, cotangent, col_table, row_table,
    partial, zeros,
    mask_v, cot_v, col_v, row_v, sems,
):
    columns = mask.shape[1]
    ends = np.cumsum(CHUNKS) * (columns // sum(CHUNKS))
    parts = [pl.ds(int(low), int(high - low)) for low, high in zip([0, *ends], ends)]
    tile = lax.axis_index("tile")
    chunk_copies = []
    for step, part in enumerate(parts):
        copies = [
            pltpu.make_async_copy(col_table.at[part, :], col_v.at[part, :], sems.at[step, 0]),
            pltpu.make_async_copy(mask.at[:, part], mask_v.at[:, part], sems.at[step, 1]),
            pltpu.make_async_copy(cotangent.at[:, part], cot_v.at[:, part], sems.at[step, 2]),
        ]
        for copy in copies:
            copy.start()
        chunk_copies.append(copies)
    row_copy = pltpu.make_async_copy(row_table.at[tile], row_v, sems.at[len(CHUNKS), 0])
    row_copy.start()

    for step, part in enumerate(parts):
        for copy in chunk_copies[step]:
            copy.wait()
        mask_add = dot(mask_v[:, part], col_v[part, : 2 * BAND])
        cot_add = dot(cot_v[:, part], col_v[part, 2 * BAND :])
        mask_part = mask_add if step == 0 else mask_part + mask_add
        cot_part = cot_add if step == 0 else cot_part + cot_add

    row_copy.wait()
    blocks = dot(row_v[: 2 * BAND, :], mask_part.astype(jnp.bfloat16))
    partial[:BAND, :] = blocks[:BAND, :BAND] + blocks[BAND:, BAND:]
    partial[BAND : 2 * BAND, :] = blocks[:BAND, BAND:] - blocks[BAND:, :BAND]
    partial[2 * BAND : SUMS, :] = dot(row_v[2 * BAND :, :], cot_part.astype(jnp.bfloat16))
    partial[SUMS:, :] = jnp.zeros((8, BAND), jnp.float32)
    zeros[...] = jnp.zeros_like(zeros)


def forward(mask, cotangent, col_table, row_table):
    height, columns = mask.shape
    return pl.pallas_call(
        forward_kernel,
        out_shape=(
            jax.ShapeDtypeStruct((SUMS + 8, BAND), jnp.float32),
            jax.ShapeDtypeStruct((1, SLOTS + 1), jnp.int32),
        ),
        in_specs=[HBM] * 4,
        out_specs=(VMEM, VMEM),
        scratch_shapes=[
            pltpu.VMEM(mask.shape, jnp.bfloat16),
            pltpu.VMEM(mask.shape, jnp.bfloat16),
            pltpu.VMEM(col_table.shape, jnp.bfloat16),
            pltpu.VMEM(row_table.shape[1:], jnp.bfloat16),
            pltpu.SemaphoreType.DMA((len(CHUNKS) + 1, 3)),
        ],
        compiler_params=pltpu.CompilerParams(vmem_limit_bytes=GRANT),
        cost_estimate=pl.CostEstimate(
            flops=2 * height * columns * SUMS, bytes_accessed=6 * 1024 * 1024, transcendentals=0
        ),
        name="forward",
    )(mask, cotangent, col_table, row_table)


def lines_kernel(ids, shift, weight, lines):
    lane = lax.broadcasted_iota(jnp.int32, (SLOTS, LANES), 1)
    place = lax.broadcasted_iota(jnp.int32, (SLOTS, LANES), 0)

    def one(row, carry):
        blocks, weights, there = [], [], jnp.full_like(lane, -1)
        for slot in range(SLOTS):
            source = ids[row, slot]
            start = pl.multiple_of(source // LANES * LANES, LANES)
            blocks.append(shift[:, pl.ds(start, LANES)])
            weights.append(weight[pl.ds(source // LANES, 1), :])
            found = jnp.where(slot < ids[row, SLOTS], source % LANES, -1)
            there = jnp.where(place == slot, found, there)
        here = lane == there
        line = jnp.zeros((SLOTS, LANES), jnp.float32)
        for dim, into in ((0, OX), (1, OY)):
            values = jnp.concatenate([block[dim : dim + 1, :] for block in blocks], 0)
            found = jnp.sum(jnp.where(here, values.astype(jnp.float32), 0.0), 1, keepdims=True)
            line = jnp.where(lane == into, found, line)
        found = jnp.sum(jnp.where(here, jnp.concatenate(weights, 0), 0.0), 1, keepdims=True)
        line = jnp.where(lane == FACTOR, found * (2.0 / SLOTS / PUPIL / PUPIL), line)
        line = jnp.where(lane == COUNT, ids[row, SLOTS].astype(jnp.float32), line)
        lines[pl.ds(pl.multiple_of(row * SLOTS, SLOTS), SLOTS), :] = line
        return carry

    lax.fori_loop(0, ids.shape[0], one, jnp.int32(0), unroll=ids.shape[0] <= 4)


def slot_lines(ids, shift, weight):
    count = ids.shape[0] * SLOTS
    return pl.pallas_call(
        lines_kernel,
        out_shape=jax.ShapeDtypeStruct((count, LANES), jnp.float32),
        in_specs=[SMEM, VMEM, VMEM],
        out_specs=VMEM,
        compiler_params=pltpu.CompilerParams(vmem_limit_bytes=2 * 1024 * 1024),
        cost_estimate=pl.CostEstimate(flops=1, bytes_accessed=1, transcendentals=0),
        name="slot_lines",
    )(ids, shift, weight)


def adjoint_kernel(
    n_src, own, other, own_lines, other_lines, pupil, table, col_table, out_table,
    result,
    spec_real, spec_imag, image, col_v, out_v, result_v, lines, used, sems, out_sems, *bands,
):
    place = lax.axis_index("tile") * n_src + lax.axis_index("src")
    out_copy = pltpu.make_async_copy(out_table.at[place], out_v, sems.at[1])
    col_copy = pltpu.make_async_copy(col_table, col_v, sems.at[2])
    half = own_lines.shape[0]
    own_copy = pltpu.make_async_copy(own_lines, lines.at[pl.ds(0, half), :], sems.at[3])
    other_copy = pltpu.make_async_copy(other_lines, lines.at[pl.ds(half, half), :], sems.at[0])
    for copy in (own_copy, other_copy, out_copy, col_copy):
        copy.start()

    scale = 1.0 / math.sqrt(TILE_ROWS * COLS)
    whole = own[:SUMS, :] + other[:SUMS, :]
    spec = (whole[: 2 * BAND] * scale).astype(jnp.bfloat16).astype(jnp.float32)
    spec_real[...] = spec[:BAND]
    spec_imag[...] = spec[BAND:]
    image[:GRID, :] = whole[2 * BAND :]
    image[GRID:, :] = whole[2 * BAND :]
    for band in bands:
        band[...] = jnp.zeros_like(band)
    for slot in range(2 * half + GROUPS[-1]):
        used[slot] = jnp.int32(0)
    own_copy.wait()
    other_copy.wait()

    def add(block, total):
        first = block * SLOTS
        for slot in range(SLOTS):
            used[total + slot] = first + slot
        return total + lines[first, COUNT].astype(jnp.int32)

    blocks = 2 * half // SLOTS
    total = lax.fori_loop(0, blocks, add, jnp.int32(0), unroll=blocks <= 8)

    def group(first, size):
        width = size // PACKS
        held, slots = [None] * PACKS, [None] * PACKS

        def amplitude(pack):
            slots[pack], parts = [], []
            for slot in range(width):
                place = first + pack * width + slot
                index = used[place]
                factor = jnp.where(place < total, lines[index, FACTOR], 0.0)
                offset_x = lines[index, OX].astype(jnp.int32)
                rows = pl.ds(lines[index, OY].astype(jnp.int32), PUPIL)
                real = pltpu.roll(pupil[:PUPIL, :], offset_x, 1)
                imag = pltpu.roll(pupil[PUPIL:, :], offset_x, 1)
                amp_real = real * spec_real[rows, :] - imag * spec_imag[rows, :]
                amp_imag = real * spec_imag[rows, :] + imag * spec_real[rows, :]
                slots[pack].append((rows, real, imag, factor))
                parts.append(jnp.concatenate([amp_real, amp_imag], 1).astype(jnp.bfloat16))
            held[pack] = jnp.concatenate(parts, 0)

        def halfway(pack):
            found = dot(held[pack], table[COLS_IN, :]).astype(jnp.bfloat16)
            parts = []
            for slot in range(width):
                block = found[slot * PUPIL : (slot + 1) * PUPIL, :]
                parts.append(jnp.concatenate([block[:, :GRID], block[:, GRID:]], 0))
            held[pack] = jnp.concatenate(parts, 1)

        def field_grad(pack):
            rows_in = table[ROWS_IN, :]
            rows_in = jnp.concatenate([rows_in[:, : 2 * PUPIL], rows_in[:, 2 * PUPIL :]], 0)
            field = dot(rows_in, held[pack])
            parts = []
            for slot in range(width):
                block = field[:, slot * GRID : (slot + 1) * GRID]
                parts.append((block * image[...]).astype(jnp.bfloat16))
            held[pack] = jnp.concatenate(parts, 1)

        def back(pack):
            found = dot(table[ROWS_OUT, :], held[pack]).astype(jnp.bfloat16)
            parts = []
            for slot in range(width):
                block = found[:, slot * GRID : (slot + 1) * GRID]
                parts.append(jnp.concatenate([block[:PUPIL], block[PUPIL:]], 1))
            held[pack] = jnp.concatenate(parts, 0)

        def gradient(pack):
            grad = dot(held[pack], table[COLS_OUT, :])
            for slot, (rows, real, imag, factor) in enumerate(slots[pack]):
                block = grad[slot * PUPIL : (slot + 1) * PUPIL, :] * factor
                grad_real, grad_imag = block[:, :BAND], block[:, BAND:]
                band_real, band_imag = bands[slot % 2], bands[2 + slot % 2]
                band_real[rows, :] = band_real[rows, :] + (real * grad_real + imag * grad_imag)
                band_imag[rows, :] = band_imag[rows, :] + (real * grad_imag - imag * grad_real)

        stages = (amplitude, halfway, field_grad, back, gradient)
        for step in range(PACKS + len(stages) - 1):
            for late, stage in reversed(list(enumerate(stages))):
                if 0 <= step - late < PACKS:
                    stage(step - late)

    largest, second = GROUPS[-1], GROUPS[-2]
    whole_groups = (total + largest - 1 - second) // largest

    def whole_group(step, carry):
        group(step * largest, largest)
        return carry

    lax.fori_loop(0, whole_groups, whole_group, jnp.int32(0))
    rest = total - whole_groups * largest
    for below, size in zip((0, *GROUPS), GROUPS[:-1]):

        @pl.when((rest > below) & (rest <= size))
        def _():
            group(whole_groups * largest, size)

    real = (bands[0][...] + bands[1][...]) * scale
    imag = (bands[2][...] + bands[3][...]) * scale
    left = jnp.concatenate(
        [jnp.concatenate([real, imag], 1), jnp.concatenate([imag, -real], 1)], 0
    ).astype(jnp.bfloat16)
    out_copy.wait()
    mixed = dot(out_v[...].astype(jnp.bfloat16), left).astype(jnp.bfloat16)
    col_copy.wait()
    width = result.shape[2] // PARTS
    copies = []
    for step in range(PARTS):
        part = pl.ds(step * width, width)
        result_v[:, part] = dot(mixed, col_v[:, part])
        copy = pltpu.make_async_copy(
            result_v.at[:, part], result.at[0, :, part], out_sems.at[step]
        )
        copy.start()
        copies.append(copy)
    for copy in copies:
        copy.wait()


def adjoint(own, other, own_lines, other_lines, pupil, table, col_table, out_table, n_src):
    portion = out_table.shape[1]
    columns = col_table.shape[1]
    band = pltpu.VMEM((BAND, BAND), jnp.float32)
    return pl.pallas_call(
        functools.partial(adjoint_kernel, n_src),
        out_shape=jax.ShapeDtypeStruct((1, portion, columns), jnp.float32),
        in_specs=[VMEM] * 6 + [HBM] * 2,
        out_specs=HBM,
        scratch_shapes=[
            band,
            band,
            pltpu.VMEM((2 * GRID, GRID), jnp.float32),
            pltpu.VMEM(col_table.shape, jnp.bfloat16),
            pltpu.VMEM(out_table.shape[1:], jnp.float32),
            pltpu.VMEM((portion, columns), jnp.float32),
            pltpu.SMEM((2 * own_lines.shape[0], LANES), jnp.float32),
            pltpu.SMEM((2 * own_lines.shape[0] + GROUPS[-1],), jnp.int32),
            pltpu.SemaphoreType.DMA((4,)),
            pltpu.SemaphoreType.DMA((PARTS,)),
            band,
            band,
            band,
            band,
        ],
        compiler_params=pltpu.CompilerParams(vmem_limit_bytes=GRANT),
        cost_estimate=pl.CostEstimate(
            flops=2 * 128 * 4096 * 256, bytes_accessed=4 * 1024 * 1024, transcendentals=0
        ),
        name="adjoint",
    )(own, other, own_lines, other_lines, pupil, table, col_table, out_table)


def pupil_rows(phase):
    grid = jnp.arange(PUPIL, dtype=jnp.int32)
    radius = (2 * grid[:, None] - PUPIL + 1) ** 2 + (2 * grid[None, :] - PUPIL + 1) ** 2
    inside = radius <= PUPIL * PUPIL
    both = jnp.concatenate(
        [jnp.where(inside, jnp.cos(phase), 0.0), jnp.where(inside, jnp.sin(phase), 0.0)], 0
    )
    return jnp.pad(both, ((0, 0), (0, BAND - PUPIL)))


def swapped(array, sizes, steps):
    axes = tuple(sizes)
    places = np.arange(math.prod(sizes.values())).reshape(tuple(sizes.values()))
    there = places
    for dim, axis in enumerate(axes):
        there = np.take(there, np.arange(sizes[axis]) ^ steps.get(axis, 0), dim)
    turn = [(int(a), int(b)) for a, b in zip(places.ravel(), there.ravel())]
    return lax.ppermute(array, axes, turn)


def body(mask, cotangent, pupil_phase, source_weight, shift_table, source_ids, source_count):
    height, columns = mask.shape
    n_tile, n_src = lax.axis_size("tile"), lax.axis_size("src")
    col_table, row_table, out_table, out_cols = image_tables(columns, height, n_tile, n_src)
    sizes = {"src": n_src, "tile": n_tile}
    own, zeros = forward(mask, cotangent, col_table, row_table)
    ids = jnp.concatenate([source_ids, source_count[:, None]], 1) + zeros
    bit = 1
    while bit < n_src // 2:
        ids = jnp.concatenate([ids, swapped(ids, sizes, {"src": bit})], 0)
        bit *= 2
    step = 1
    while step < n_tile // 2:
        own = own + swapped(own, sizes, {"tile": step})
        step *= 2
    own_lines = slot_lines(ids + own[SUMS : SUMS + 1, : SLOTS + 1].astype(jnp.int32), shift_table.T, source_weight.reshape(-1, LANES))
    other_lines = swapped(own_lines, sizes, {"src": bit})
    other = swapped(own, sizes, {"tile": step})
    pupil = pupil_rows(pupil_phase + own[SUMS : SUMS + 1, :PUPIL])
    return adjoint(
        own, other, own_lines, other_lines, pupil, grid_tables(), out_cols, out_table, n_src
    )


def solution(mesh):
    placed = (
        P(("grp", "tile"), None),
        P(("grp", "tile"), None),
        P(),
        P(),
        P(),
        P(("grp", "src"), None),
        P(("grp", "src")),
    )
    return jax.shard_map(
        body, mesh=mesh, in_specs=placed, out_specs=P(("grp", "tile"), "src", None), check_vma=False
    )
```

```python
import functools
import math

import jax
import jax.numpy as jnp
import ml_dtypes
import numpy as np
from jax import lax
from jax.experimental import pallas as pl
from jax.experimental.pallas import tpu as pltpu
from jax.sharding import PartitionSpec as P

COLS = 2048
TILE_ROWS = 2048
BAND = 128
PUPIL = 64
SLOTS = 8
GRID = 128
CHUNKS = (2, 3, 3)
GROUPS = (16, 20, 24, 32)
PACKS = 1
OX, OY, FACTOR, COUNT = range(4)
PARTS = 8
LANES = 128
SUMS = 2 * BAND + GRID
GRANT = 53 * 1024 * 1024

VMEM = pl.BlockSpec(memory_space=pltpu.VMEM)
SMEM = pl.BlockSpec(memory_space=pltpu.SMEM)
HBM = pl.BlockSpec(memory_space=pltpu.HBM)


def waves(positions, freqs, length):
    product = np.multiply.outer(positions, freqs) % length
    angle = product.astype(np.float64) * (2.0 * math.pi / length)
    return np.cos(angle), np.sin(angle)


def lowpass(positions, length):
    freqs = np.arange(1, PUPIL)
    step = length // GRID
    apart = np.arange(GRID)[None, :] * step - positions[:, None]
    product = (apart[:, :, None] * freqs) % length
    return (1.0 + 2.0 * np.cos(product * (2.0 * math.pi / length)).sum(2)) / GRID


def low(array):
    return np.ascontiguousarray(array).astype(ml_dtypes.bfloat16)


@functools.cache
def image_tables(columns, height, n_tile, n_src):
    band = np.arange(BAND) - BAND // 2
    cols = np.arange(columns)
    rows = np.arange(TILE_ROWS)
    cos, sin = waves(cols, band, columns)
    col_table = low(np.concatenate([cos, -sin, lowpass(cols, columns)], 1))
    cos, sin = waves(rows, band, TILE_ROWS)
    row_table = np.concatenate([cos, sin, lowpass(rows, TILE_ROWS)], 1)
    row_table = low(row_table.reshape(n_tile, height, 2 * BAND + GRID).transpose(0, 2, 1))
    portion = height // n_src
    out_table = np.concatenate([cos, -sin], 1).astype(np.float32)
    out_table = out_table.reshape(n_tile * n_src, portion, 2 * BAND)
    cos, sin = waves(cols, band, columns)
    return col_table, row_table, out_table, low(np.concatenate([cos, -sin], 1).T)


COLS_IN, COLS_OUT = slice(0, 2 * BAND), slice(2 * BAND, 2 * BAND + 2 * GRID)
ROWS_IN = slice(COLS_OUT.stop, COLS_OUT.stop + GRID)
ROWS_OUT = slice(ROWS_IN.stop, ROWS_IN.stop + 2 * PUPIL)


@functools.cache
def grid_tables():
    points = np.arange(GRID)
    band = np.arange(BAND) - BAND // 2
    cos, sin = waves(points, band, GRID)
    cols_in = np.block([[cos.T, sin.T], [-sin.T, cos.T]])
    cols_out = np.block([[cos, -sin], [sin, cos]])
    cos, sin = waves(points, np.arange(PUPIL) - PUPIL // 2, GRID)
    rows_in = np.block([[cos, -sin, sin, cos]])
    rows_out = np.block([[cos.T, sin.T], [-sin.T, cos.T]])
    return low(np.concatenate([cols_in, cols_out, rows_in, rows_out], 0))


def dot(left, right):
    return jnp.dot(left, right, preferred_element_type=jnp.float32)


def forward_kernel(
    mask, cotangent, col_table, row_table,
    partial, zeros,
    mask_v, cot_v, col_v, row_v, sems,
):
    columns = mask.shape[1]
    ends = np.cumsum(CHUNKS) * (columns // sum(CHUNKS))
    parts = [pl.ds(int(low), int(high - low)) for low, high in zip([0, *ends], ends)]
    tile = lax.axis_index("tile")
    chunk_copies = []
    for step, part in enumerate(parts):
        copies = [
            pltpu.make_async_copy(col_table.at[part, :], col_v.at[part, :], sems.at[step, 0]),
            pltpu.make_async_copy(mask.at[:, part], mask_v.at[:, part], sems.at[step, 1]),
            pltpu.make_async_copy(cotangent.at[:, part], cot_v.at[:, part], sems.at[step, 2]),
        ]
        for copy in copies:
            copy.start()
        chunk_copies.append(copies)
    row_copy = pltpu.make_async_copy(row_table.at[tile], row_v, sems.at[len(CHUNKS), 0])
    row_copy.start()

    for step, part in enumerate(parts):
        for copy in chunk_copies[step]:
            copy.wait()
        mask_add = dot(mask_v[:, part], col_v[part, : 2 * BAND])
        cot_add = dot(cot_v[:, part], col_v[part, 2 * BAND :])
        mask_part = mask_add if step == 0 else mask_part + mask_add
        cot_part = cot_add if step == 0 else cot_part + cot_add

    row_copy.wait()
    blocks = dot(row_v[: 2 * BAND, :], mask_part.astype(jnp.bfloat16))
    partial[:BAND, :] = blocks[:BAND, :BAND] + blocks[BAND:, BAND:]
    partial[BAND : 2 * BAND, :] = blocks[:BAND, BAND:] - blocks[BAND:, :BAND]
    partial[2 * BAND : SUMS, :] = dot(row_v[2 * BAND :, :], cot_part.astype(jnp.bfloat16))
    partial[SUMS:, :] = jnp.zeros((8, BAND), jnp.float32)
    zeros[...] = jnp.zeros_like(zeros)


def forward(mask, cotangent, col_table, row_table):
    height, columns = mask.shape
    return pl.pallas_call(
        forward_kernel,
        out_shape=(
            jax.ShapeDtypeStruct((SUMS + 8, BAND), jnp.float32),
            jax.ShapeDtypeStruct((1, SLOTS + 1), jnp.int32),
        ),
        in_specs=[HBM] * 4,
        out_specs=(VMEM, VMEM),
        scratch_shapes=[
            pltpu.VMEM(mask.shape, jnp.bfloat16),
            pltpu.VMEM(mask.shape, jnp.bfloat16),
            pltpu.VMEM(col_table.shape, jnp.bfloat16),
            pltpu.VMEM(row_table.shape[1:], jnp.bfloat16),
            pltpu.SemaphoreType.DMA((len(CHUNKS) + 1, 3)),
        ],
        compiler_params=pltpu.CompilerParams(vmem_limit_bytes=GRANT),
        cost_estimate=pl.CostEstimate(
            flops=2 * height * columns * SUMS, bytes_accessed=6 * 1024 * 1024, transcendentals=0
        ),
        name="forward",
    )(mask, cotangent, col_table, row_table)


def lines_kernel(ids, shift, weight, lines):
    lane = lax.broadcasted_iota(jnp.int32, (SLOTS, LANES), 1)
    place = lax.broadcasted_iota(jnp.int32, (SLOTS, LANES), 0)

    def one(row, carry):
        blocks, weights, there = [], [], jnp.full_like(lane, -1)
        for slot in range(SLOTS):
            source = ids[row, slot]
            start = pl.multiple_of(source // LANES * LANES, LANES)
            blocks.append(shift[:, pl.ds(start, LANES)])
            weights.append(weight[pl.ds(source // LANES, 1), :])
            found = jnp.where(slot < ids[row, SLOTS], source % LANES, -1)
            there = jnp.where(place == slot, found, there)
        here = lane == there
        line = jnp.zeros((SLOTS, LANES), jnp.float32)
        for dim, into in ((0, OX), (1, OY)):
            values = jnp.concatenate([block[dim : dim + 1, :] for block in blocks], 0)
            found = jnp.sum(jnp.where(here, values.astype(jnp.float32), 0.0), 1, keepdims=True)
            line = jnp.where(lane == into, found, line)
        found = jnp.sum(jnp.where(here, jnp.concatenate(weights, 0), 0.0), 1, keepdims=True)
        line = jnp.where(lane == FACTOR, found * (2.0 / SLOTS / PUPIL / PUPIL), line)
        line = jnp.where(lane == COUNT, ids[row, SLOTS].astype(jnp.float32), line)
        lines[pl.ds(pl.multiple_of(row * SLOTS, SLOTS), SLOTS), :] = line
        return carry

    lax.fori_loop(0, ids.shape[0], one, jnp.int32(0), unroll=ids.shape[0] <= 4)


def slot_lines(ids, shift, weight):
    count = ids.shape[0] * SLOTS
    return pl.pallas_call(
        lines_kernel,
        out_shape=jax.ShapeDtypeStruct((count, LANES), jnp.float32),
        in_specs=[SMEM, VMEM, VMEM],
        out_specs=VMEM,
        compiler_params=pltpu.CompilerParams(vmem_limit_bytes=2 * 1024 * 1024),
        cost_estimate=pl.CostEstimate(flops=1, bytes_accessed=1, transcendentals=0),
        name="slot_lines",
    )(ids, shift, weight)


def adjoint_kernel(
    n_src, own, other, own_lines, other_lines, pupil, table, col_table, out_table,
    result,
    spec_real, spec_imag, image, col_v, out_v, result_v, lines, used, sems, out_sems, *bands,
):
    place = lax.axis_index("tile") * n_src + lax.axis_index("src")
    out_copy = pltpu.make_async_copy(out_table.at[place], out_v, sems.at[1])
    col_copy = pltpu.make_async_copy(col_table, col_v, sems.at[2])
    half = own_lines.shape[0]
    own_copy = pltpu.make_async_copy(own_lines, lines.at[pl.ds(0, half), :], sems.at[3])
    other_copy = pltpu.make_async_copy(other_lines, lines.at[pl.ds(half, half), :], sems.at[0])
    for copy in (own_copy, other_copy, out_copy, col_copy):
        copy.start()

    scale = 1.0 / math.sqrt(TILE_ROWS * COLS)
    whole = own[:SUMS, :] + other[:SUMS, :]
    spec = (whole[: 2 * BAND] * scale).astype(jnp.bfloat16).astype(jnp.float32)
    spec_real[...] = spec[:BAND]
    spec_imag[...] = spec[BAND:]
    image[:GRID, :] = whole[2 * BAND :]
    image[GRID:, :] = whole[2 * BAND :]
    for band in bands:
        band[...] = jnp.zeros_like(band)
    for slot in range(2 * half + GROUPS[-1]):
        used[slot] = jnp.int32(0)
    own_copy.wait()
    other_copy.wait()

    def add(block, total):
        first = block * SLOTS
        for slot in range(SLOTS):
            used[total + slot] = first + slot
        return total + lines[first, COUNT].astype(jnp.int32)

    blocks = 2 * half // SLOTS
    total = lax.fori_loop(0, blocks, add, jnp.int32(0), unroll=blocks <= 8)

    def group(first, size):
        width = size // PACKS
        held, slots = [None] * PACKS, [None] * PACKS

        def amplitude(pack):
            slots[pack], parts = [], []
            for slot in range(width):
                place = first + pack * width + slot
                index = used[place]
                factor = jnp.where(place < total, lines[index, FACTOR], 0.0)
                offset_x = lines[index, OX].astype(jnp.int32)
                rows = pl.ds(lines[index, OY].astype(jnp.int32), PUPIL)
                real = pltpu.roll(pupil[:PUPIL, :], offset_x, 1)
                imag = pltpu.roll(pupil[PUPIL:, :], offset_x, 1)
                amp_real = real * spec_real[rows, :] - imag * spec_imag[rows, :]
                amp_imag = real * spec_imag[rows, :] + imag * spec_real[rows, :]
                slots[pack].append((rows, real, imag, factor))
                parts.append(jnp.concatenate([amp_real, amp_imag], 1).astype(jnp.bfloat16))
            held[pack] = jnp.concatenate(parts, 0)

        def halfway(pack):
            found = dot(held[pack], table[COLS_IN, :]).astype(jnp.bfloat16)
            parts = []
            for slot in range(width):
                block = found[slot * PUPIL : (slot + 1) * PUPIL, :]
                parts.append(jnp.concatenate([block[:, :GRID], block[:, GRID:]], 0))
            held[pack] = jnp.concatenate(parts, 1)

        def field_grad(pack):
            rows_in = table[ROWS_IN, :]
            rows_in = jnp.concatenate([rows_in[:, : 2 * PUPIL], rows_in[:, 2 * PUPIL :]], 0)
            field = dot(rows_in, held[pack])
            parts = []
            for slot in range(width):
                block = field[:, slot * GRID : (slot + 1) * GRID]
                parts.append((block * image[...]).astype(jnp.bfloat16))
            held[pack] = jnp.concatenate(parts, 1)

        def back(pack):
            found = dot(table[ROWS_OUT, :], held[pack]).astype(jnp.bfloat16)
            parts = []
            for slot in range(width):
                block = found[:, slot * GRID : (slot + 1) * GRID]
                parts.append(jnp.concatenate([block[:PUPIL], block[PUPIL:]], 1))
            held[pack] = jnp.concatenate(parts, 0)

        def gradient(pack):
            grad = dot(held[pack], table[COLS_OUT, :])
            for slot, (rows, real, imag, factor) in enumerate(slots[pack]):
                block = grad[slot * PUPIL : (slot + 1) * PUPIL, :] * factor
                grad_real, grad_imag = block[:, :BAND], block[:, BAND:]
                band_real, band_imag = bands[slot % 2], bands[2 + slot % 2]
                band_real[rows, :] = band_real[rows, :] + (real * grad_real + imag * grad_imag)
                band_imag[rows, :] = band_imag[rows, :] + (real * grad_imag - imag * grad_real)

        stages = (amplitude, halfway, field_grad, back, gradient)
        for step in range(PACKS + len(stages) - 1):
            for late, stage in reversed(list(enumerate(stages))):
                if 0 <= step - late < PACKS:
                    stage(step - late)

    largest, second = GROUPS[-1], GROUPS[-2]
    whole_groups = (total + largest - 1 - second) // largest

    def whole_group(step, carry):
        group(step * largest, largest)
        return carry

    lax.fori_loop(0, whole_groups, whole_group, jnp.int32(0))
    rest = total - whole_groups * largest
    for below, size in zip((0, *GROUPS), GROUPS[:-1]):

        @pl.when((rest > below) & (rest <= size))
        def _():
            group(whole_groups * largest, size)

    real = (bands[0][...] + bands[1][...]) * scale
    imag = (bands[2][...] + bands[3][...]) * scale
    left = jnp.concatenate(
        [jnp.concatenate([real, imag], 1), jnp.concatenate([imag, -real], 1)], 0
    ).astype(jnp.bfloat16)
    out_copy.wait()
    mixed = dot(out_v[...].astype(jnp.bfloat16), left).astype(jnp.bfloat16)
    col_copy.wait()
    width = result.shape[2] // PARTS
    copies = []
    for step in range(PARTS):
        part = pl.ds(step * width, width)
        result_v[:, part] = dot(mixed, col_v[:, part])
        copy = pltpu.make_async_copy(
            result_v.at[:, part], result.at[0, :, part], out_sems.at[step]
        )
        copy.start()
        copies.append(copy)
    for copy in copies:
        copy.wait()


def adjoint(own, other, own_lines, other_lines, pupil, table, col_table, out_table, n_src):
    portion = out_table.shape[1]
    columns = col_table.shape[1]
    band = pltpu.VMEM((BAND, BAND), jnp.float32)
    return pl.pallas_call(
        functools.partial(adjoint_kernel, n_src),
        out_shape=jax.ShapeDtypeStruct((1, portion, columns), jnp.float32),
        in_specs=[VMEM] * 6 + [HBM] * 2,
        out_specs=HBM,
        scratch_shapes=[
            band,
            band,
            pltpu.VMEM((2 * GRID, GRID), jnp.float32),
            pltpu.VMEM(col_table.shape, jnp.bfloat16),
            pltpu.VMEM(out_table.shape[1:], jnp.float32),
            pltpu.VMEM((portion, columns), jnp.float32),
            pltpu.SMEM((2 * own_lines.shape[0], LANES), jnp.float32),
            pltpu.SMEM((2 * own_lines.shape[0] + GROUPS[-1],), jnp.int32),
            pltpu.SemaphoreType.DMA((4,)),
            pltpu.SemaphoreType.DMA((PARTS,)),
            band,
            band,
            band,
            band,
        ],
        compiler_params=pltpu.CompilerParams(vmem_limit_bytes=GRANT),
        cost_estimate=pl.CostEstimate(
            flops=2 * 128 * 4096 * 256, bytes_accessed=4 * 1024 * 1024, transcendentals=0
        ),
        name="adjoint",
    )(own, other, own_lines, other_lines, pupil, table, col_table, out_table)


def pupil_rows(phase):
    grid = jnp.arange(PUPIL, dtype=jnp.int32)
    radius = (2 * grid[:, None] - PUPIL + 1) ** 2 + (2 * grid[None, :] - PUPIL + 1) ** 2
    inside = radius <= PUPIL * PUPIL
    both = jnp.concatenate(
        [jnp.where(inside, jnp.cos(phase), 0.0), jnp.where(inside, jnp.sin(phase), 0.0)], 0
    )
    return jnp.pad(both, ((0, 0), (0, BAND - PUPIL)))


def swapped(array, sizes, steps):
    axes = tuple(sizes)
    places = np.arange(math.prod(sizes.values())).reshape(tuple(sizes.values()))
    there = places
    for dim, axis in enumerate(axes):
        there = np.take(there, np.arange(sizes[axis]) ^ steps.get(axis, 0), dim)
    turn = [(int(a), int(b)) for a, b in zip(places.ravel(), there.ravel())]
    return lax.ppermute(array, axes, turn)


def body(mask, cotangent, pupil_phase, source_weight, shift_table, source_ids, source_count):
    height, columns = mask.shape
    n_tile, n_src = lax.axis_size("tile"), lax.axis_size("src")
    col_table, row_table, out_table, out_cols = image_tables(columns, height, n_tile, n_src)
    sizes = {"src": n_src, "tile": n_tile}
    own, zeros = forward(mask, cotangent, col_table, row_table)
    ids = jnp.concatenate([source_ids, source_count[:, None]], 1) + zeros
    bit = 1
    while bit < n_src // 2:
        ids = jnp.concatenate([ids, swapped(ids, sizes, {"src": bit})], 0)
        bit *= 2
    step = 1
    while step < n_tile // 2:
        own = own + swapped(own, sizes, {"tile": step})
        step *= 2
    own_lines = slot_lines(ids + own[SUMS : SUMS + 1, : SLOTS + 1].astype(jnp.int32), shift_table.T, source_weight.reshape(-1, LANES))
    other_lines = swapped(own_lines, sizes, {"src": bit})
    other = swapped(own, sizes, {"tile": step})
    pupil = pupil_rows(pupil_phase + own[SUMS : SUMS + 1, :PUPIL])
    return adjoint(
        own, other, own_lines, other_lines, pupil, grid_tables(), out_cols, out_table, n_src
    )


def solution(mesh):
    placed = (
        P(("grp", "tile"), None),
        P(("grp", "tile"), None),
        P(),
        P(),
        P(),
        P(("grp", "src"), None),
        P(("grp", "src")),
    )
    return jax.shard_map(
        body, mesh=mesh, in_specs=placed, out_specs=P(("grp", "tile"), "src", None), check_vma=False
    )
```

```python
import functools
import math

import jax
import jax.numpy as jnp
import ml_dtypes
import numpy as np
from jax import lax
from jax.experimental import pallas as pl
from jax.experimental.pallas import tpu as pltpu
from jax.sharding import PartitionSpec as P

COLS = 2048
TILE_ROWS = 2048
BAND = 128
PUPIL = 64
SLOTS = 8
GRID = 128
CHUNKS = (1,) * 8
GROUPS = (16, 20, 24, 32)
STEP = 8
OX, OY, FACTOR, COUNT = range(4)
PARTS = 4
LANES = 128
SUMS = 2 * BAND + GRID
GRANT = 53 * 1024 * 1024

VMEM = pl.BlockSpec(memory_space=pltpu.VMEM)
SMEM = pl.BlockSpec(memory_space=pltpu.SMEM)
HBM = pl.BlockSpec(memory_space=pltpu.HBM)


def waves(positions, freqs, length):
    product = np.multiply.outer(positions, freqs) % length
    angle = product.astype(np.float64) * (2.0 * math.pi / length)
    return np.cos(angle), np.sin(angle)


def lowpass(positions, length):
    freqs = np.arange(1, PUPIL)
    step = length // GRID
    apart = np.arange(GRID)[None, :] * step - positions[:, None]
    product = (apart[:, :, None] * freqs) % length
    return (1.0 + 2.0 * np.cos(product * (2.0 * math.pi / length)).sum(2)) / GRID


def low(array):
    return np.ascontiguousarray(array).astype(ml_dtypes.bfloat16)


@functools.cache
def image_tables(columns, height, n_tile, n_src):
    band = np.arange(BAND) - BAND // 2
    cols = np.arange(columns)
    rows = np.arange(TILE_ROWS)
    cos, sin = waves(cols, band, columns)
    col_table = low(np.concatenate([cos, -sin, lowpass(cols, columns)], 1))
    cos, sin = waves(rows, band, TILE_ROWS)
    row_table = np.concatenate([cos, sin, lowpass(rows, TILE_ROWS)], 1)
    row_table = low(row_table.reshape(n_tile, height, 2 * BAND + GRID).transpose(0, 2, 1))
    portion = height // n_src
    out_table = np.concatenate([cos, -sin], 1).astype(np.float32)
    out_table = out_table.reshape(n_tile * n_src, portion, 2 * BAND)
    cos, sin = waves(cols, band, columns)
    return col_table, row_table, out_table, low(np.concatenate([cos, -sin], 1).T)


COLS_IN, COLS_OUT = slice(0, 2 * BAND), slice(2 * BAND, 2 * BAND + 2 * GRID)
ROWS_IN = slice(COLS_OUT.stop, COLS_OUT.stop + GRID)
ROWS_OUT = slice(ROWS_IN.stop, ROWS_IN.stop + 2 * PUPIL)


@functools.cache
def grid_tables():
    points = np.arange(GRID)
    band = np.arange(BAND) - BAND // 2
    cos, sin = waves(points, band, GRID)
    cols_in = np.block([[cos.T, sin.T], [-sin.T, cos.T]])
    cols_out = np.block([[cos, -sin], [sin, cos]])
    cos, sin = waves(points, np.arange(PUPIL) - PUPIL // 2, GRID)
    rows_in = np.block([[cos, -sin, sin, cos]])
    rows_out = np.block([[cos.T, sin.T], [-sin.T, cos.T]])
    return low(np.concatenate([cols_in, cols_out, rows_in, rows_out], 0))


def dot(left, right):
    return jnp.dot(left, right, preferred_element_type=jnp.float32)


def forward_kernel(
    mask, cotangent, col_table, row_table,
    partial, zeros,
    mask_v, cot_v, col_v, row_v, sems,
):
    columns = mask.shape[1]
    ends = np.cumsum(CHUNKS) * (columns // sum(CHUNKS))
    parts = [pl.ds(int(low), int(high - low)) for low, high in zip([0, *ends], ends)]
    tile = lax.axis_index("tile")
    chunk_copies = []
    for step, part in enumerate(parts):
        copies = [
            pltpu.make_async_copy(col_table.at[part, :], col_v.at[part, :], sems.at[step, 0]),
            pltpu.make_async_copy(mask.at[:, part], mask_v.at[:, part], sems.at[step, 1]),
            pltpu.make_async_copy(cotangent.at[:, part], cot_v.at[:, part], sems.at[step, 2]),
        ]
        for copy in copies:
            copy.start()
        chunk_copies.append(copies)
    row_copy = pltpu.make_async_copy(row_table.at[tile], row_v, sems.at[len(CHUNKS), 0])
    row_copy.start()

    for step, part in enumerate(parts):
        for copy in chunk_copies[step]:
            copy.wait()
        mask_add = dot(mask_v[:, part], col_v[part, : 2 * BAND])
        cot_add = dot(cot_v[:, part], col_v[part, 2 * BAND :])
        mask_part = mask_add if step == 0 else mask_part + mask_add
        cot_part = cot_add if step == 0 else cot_part + cot_add

    row_copy.wait()
    blocks = dot(row_v[: 2 * BAND, :], mask_part.astype(jnp.bfloat16))
    partial[:BAND, :] = blocks[:BAND, :BAND] + blocks[BAND:, BAND:]
    partial[BAND : 2 * BAND, :] = blocks[:BAND, BAND:] - blocks[BAND:, :BAND]
    partial[2 * BAND : SUMS, :] = dot(row_v[2 * BAND :, :], cot_part.astype(jnp.bfloat16))
    partial[SUMS:, :] = jnp.zeros((8, BAND), jnp.float32)
    zeros[...] = jnp.zeros_like(zeros)


def forward(mask, cotangent, col_table, row_table):
    height, columns = mask.shape
    return pl.pallas_call(
        forward_kernel,
        out_shape=(
            jax.ShapeDtypeStruct((SUMS + 8, BAND), jnp.float32),
            jax.ShapeDtypeStruct((1, SLOTS + 1), jnp.int32),
        ),
        in_specs=[HBM] * 4,
        out_specs=(VMEM, VMEM),
        scratch_shapes=[
            pltpu.VMEM(mask.shape, jnp.bfloat16),
            pltpu.VMEM(mask.shape, jnp.bfloat16),
            pltpu.VMEM(col_table.shape, jnp.bfloat16),
            pltpu.VMEM(row_table.shape[1:], jnp.bfloat16),
            pltpu.SemaphoreType.DMA((len(CHUNKS) + 1, 3)),
        ],
        compiler_params=pltpu.CompilerParams(vmem_limit_bytes=GRANT),
        cost_estimate=pl.CostEstimate(
            flops=2 * height * columns * SUMS, bytes_accessed=6 * 1024 * 1024, transcendentals=0
        ),
        name="forward",
    )(mask, cotangent, col_table, row_table)


def lines_kernel(ids, shift, weight, lines):
    lane = lax.broadcasted_iota(jnp.int32, (SLOTS, LANES), 1)
    place = lax.broadcasted_iota(jnp.int32, (SLOTS, LANES), 0)

    def one(row, carry):
        blocks, weights, there = [], [], jnp.full_like(lane, -1)
        for slot in range(SLOTS):
            source = ids[row, slot]
            start = pl.multiple_of(source // LANES * LANES, LANES)
            blocks.append(shift[:, pl.ds(start, LANES)])
            weights.append(weight[pl.ds(source // LANES, 1), :])
            found = jnp.where(slot < ids[row, SLOTS], source % LANES, -1)
            there = jnp.where(place == slot, found, there)
        here = lane == there
        line = jnp.zeros((SLOTS, LANES), jnp.float32)
        for dim, into in ((0, OX), (1, OY)):
            values = jnp.concatenate([block[dim : dim + 1, :] for block in blocks], 0)
            found = jnp.sum(jnp.where(here, values.astype(jnp.float32), 0.0), 1, keepdims=True)
            line = jnp.where(lane == into, found, line)
        found = jnp.sum(jnp.where(here, jnp.concatenate(weights, 0), 0.0), 1, keepdims=True)
        line = jnp.where(lane == FACTOR, found * (2.0 / SLOTS / PUPIL / PUPIL), line)
        line = jnp.where(lane == COUNT, ids[row, SLOTS].astype(jnp.float32), line)
        lines[pl.ds(pl.multiple_of(row * SLOTS, SLOTS), SLOTS), :] = line
        return carry

    lax.fori_loop(0, ids.shape[0], one, jnp.int32(0), unroll=ids.shape[0] <= 4)


def slot_lines(ids, shift, weight):
    count = ids.shape[0] * SLOTS
    return pl.pallas_call(
        lines_kernel,
        out_shape=jax.ShapeDtypeStruct((count, LANES), jnp.float32),
        in_specs=[SMEM, VMEM, VMEM],
        out_specs=VMEM,
        compiler_params=pltpu.CompilerParams(vmem_limit_bytes=2 * 1024 * 1024),
        cost_estimate=pl.CostEstimate(flops=1, bytes_accessed=1, transcendentals=0),
        name="slot_lines",
    )(ids, shift, weight)


def adjoint_kernel(
    n_src, own, other, own_lines, other_lines, pupil, table, col_table, out_table,
    result,
    spec_real, spec_imag, image, band_real, band_imag, col_v, out_v, result_v, lines, used, sems, out_sems,
):
    place = lax.axis_index("tile") * n_src + lax.axis_index("src")
    out_copy = pltpu.make_async_copy(out_table.at[place], out_v, sems.at[1])
    col_copy = pltpu.make_async_copy(col_table, col_v, sems.at[2])
    half = own_lines.shape[0]
    own_copy = pltpu.make_async_copy(own_lines, lines.at[pl.ds(0, half), :], sems.at[3])
    other_copy = pltpu.make_async_copy(other_lines, lines.at[pl.ds(half, half), :], sems.at[0])
    for copy in (own_copy, other_copy, out_copy, col_copy):
        copy.start()

    scale = 1.0 / math.sqrt(TILE_ROWS * COLS)
    whole = own[:SUMS, :] + other[:SUMS, :]
    spec = (whole[: 2 * BAND] * scale).astype(jnp.bfloat16).astype(jnp.float32)
    for step in range(STEP):
        rows = BAND - STEP if step else BAND
        spec_real[step, :rows, :] = spec[step : step + rows]
        spec_imag[step, :rows, :] = spec[BAND + step : BAND + step + rows]
    band_real[...] = jnp.zeros_like(band_real)
    band_imag[...] = jnp.zeros_like(band_imag)
    image[:GRID, :] = whole[2 * BAND :]
    image[GRID:, :] = whole[2 * BAND :]
    for slot in range(2 * half + GROUPS[-1]):
        used[slot] = jnp.int32(0)
    own_copy.wait()
    other_copy.wait()

    def add(block, total):
        first = block * SLOTS
        for slot in range(SLOTS):
            used[total + slot] = first + slot
        return total + lines[first, COUNT].astype(jnp.int32)

    blocks = 2 * half // SLOTS
    total = lax.fori_loop(0, blocks, add, jnp.int32(0), unroll=blocks <= 8)

    def group(first, size):
        slots, amplitudes = [], []
        for slot in range(size):
            place = first + slot
            index = used[place]
            factor = jnp.where(place < total, lines[index, FACTOR], 0.0)
            offset_x = lines[index, OX].astype(jnp.int32)
            offset_y = lines[index, OY].astype(jnp.int32)
            copy = offset_y % STEP
            rows = pl.ds(pl.multiple_of(offset_y - copy, STEP), PUPIL)
            real = pltpu.roll(pupil[:PUPIL, :], offset_x, 1)
            imag = pltpu.roll(pupil[PUPIL:, :], offset_x, 1)
            here_real, here_imag = spec_real[copy, rows, :], spec_imag[copy, rows, :]
            amp_real = real * here_real - imag * here_imag
            amp_imag = real * here_imag + imag * here_real
            slots.append((copy, rows, real, imag, factor))
            amplitudes.append(jnp.concatenate([amp_real, amp_imag], 1).astype(jnp.bfloat16))
        halfway = dot(jnp.concatenate(amplitudes, 0), table[COLS_IN, :]).astype(jnp.bfloat16)
        parts = []
        for slot in range(size):
            block = halfway[slot * PUPIL : (slot + 1) * PUPIL, :]
            parts.append(jnp.concatenate([block[:, :GRID], block[:, GRID:]], 0))
        rows_in = table[ROWS_IN, :]
        rows_in = jnp.concatenate([rows_in[:, : 2 * PUPIL], rows_in[:, 2 * PUPIL :]], 0)
        field = dot(rows_in, jnp.concatenate(parts, 1))
        parts = []
        for slot in range(size):
            block = field[:, slot * GRID : (slot + 1) * GRID]
            parts.append((block * image[...]).astype(jnp.bfloat16))
        back = dot(table[ROWS_OUT, :], jnp.concatenate(parts, 1)).astype(jnp.bfloat16)
        parts = []
        for slot in range(size):
            block = back[:, slot * GRID : (slot + 1) * GRID]
            parts.append(jnp.concatenate([block[:PUPIL], block[PUPIL:]], 1))
        grad = dot(jnp.concatenate(parts, 0), table[COLS_OUT, :])
        for slot, (copy, rows, real, imag, factor) in enumerate(slots):
            block = grad[slot * PUPIL : (slot + 1) * PUPIL, :] * factor
            grad_real, grad_imag = block[:, :BAND], block[:, BAND:]
            band_real[copy, rows, :] += real * grad_real + imag * grad_imag
            band_imag[copy, rows, :] += real * grad_imag - imag * grad_real

    largest, second = GROUPS[-1], GROUPS[-2]
    whole_groups = (total + largest - 1 - second) // largest

    def whole_group(step, carry):
        group(step * largest, largest)
        return carry

    lax.fori_loop(0, whole_groups, whole_group, jnp.int32(0))
    rest = total - whole_groups * largest
    for below, size in zip((0, *GROUPS), GROUPS[:-1]):

        @pl.when((rest > below) & (rest <= size))
        def _():
            group(whole_groups * largest, size)

    for band in (band_real, band_imag):
        for step in range(1, STEP):
            rows = BAND - STEP
            band[0, step : step + rows, :] += band[step, :rows, :]
    real, imag = band_real[0] * scale, band_imag[0] * scale
    left = jnp.concatenate(
        [jnp.concatenate([real, imag], 1), jnp.concatenate([imag, -real], 1)], 0
    ).astype(jnp.bfloat16)
    out_copy.wait()
    mixed = dot(out_v[...].astype(jnp.bfloat16), left).astype(jnp.bfloat16)
    col_copy.wait()
    width = result.shape[2] // PARTS
    copies = []
    for step in range(PARTS):
        part = pl.ds(step * width, width)
        result_v[:, part] = dot(mixed, col_v[:, part])
        copy = pltpu.make_async_copy(
            result_v.at[:, part], result.at[0, :, part], out_sems.at[step]
        )
        copy.start()
        copies.append(copy)
    for copy in copies:
        copy.wait()


def adjoint(own, other, own_lines, other_lines, pupil, table, col_table, out_table, n_src):
    portion = out_table.shape[1]
    columns = col_table.shape[1]
    band = pltpu.VMEM((STEP, BAND, BAND), jnp.float32)
    return pl.pallas_call(
        functools.partial(adjoint_kernel, n_src),
        out_shape=jax.ShapeDtypeStruct((1, portion, columns), jnp.float32),
        in_specs=[VMEM] * 6 + [HBM] * 2,
        out_specs=HBM,
        scratch_shapes=[
            band,
            band,
            pltpu.VMEM((2 * GRID, GRID), jnp.float32),
            band,
            band,
            pltpu.VMEM(col_table.shape, jnp.bfloat16),
            pltpu.VMEM(out_table.shape[1:], jnp.float32),
            pltpu.VMEM((portion, columns), jnp.float32),
            pltpu.SMEM((2 * own_lines.shape[0], LANES), jnp.float32),
            pltpu.SMEM((2 * own_lines.shape[0] + GROUPS[-1],), jnp.int32),
            pltpu.SemaphoreType.DMA((4,)),
            pltpu.SemaphoreType.DMA((PARTS,)),
        ],
        compiler_params=pltpu.CompilerParams(vmem_limit_bytes=GRANT),
        cost_estimate=pl.CostEstimate(
            flops=2 * 128 * 4096 * 256, bytes_accessed=4 * 1024 * 1024, transcendentals=0
        ),
        name="adjoint",
    )(own, other, own_lines, other_lines, pupil, table, col_table, out_table)


def pupil_rows(phase):
    grid = jnp.arange(PUPIL, dtype=jnp.int32)
    radius = (2 * grid[:, None] - PUPIL + 1) ** 2 + (2 * grid[None, :] - PUPIL + 1) ** 2
    inside = radius <= PUPIL * PUPIL
    both = jnp.concatenate(
        [jnp.where(inside, jnp.cos(phase), 0.0), jnp.where(inside, jnp.sin(phase), 0.0)], 0
    )
    return jnp.pad(both, ((0, 0), (0, BAND - PUPIL)))


def swapped(array, sizes, steps):
    axes = tuple(sizes)
    places = np.arange(math.prod(sizes.values())).reshape(tuple(sizes.values()))
    there = places
    for dim, axis in enumerate(axes):
        there = np.take(there, np.arange(sizes[axis]) ^ steps.get(axis, 0), dim)
    turn = [(int(a), int(b)) for a, b in zip(places.ravel(), there.ravel())]
    return lax.ppermute(array, axes, turn)


def body(mask, cotangent, pupil_phase, source_weight, shift_table, source_ids, source_count):
    height, columns = mask.shape
    n_tile, n_src = lax.axis_size("tile"), lax.axis_size("src")
    col_table, row_table, out_table, out_cols = image_tables(columns, height, n_tile, n_src)
    sizes = {"src": n_src, "tile": n_tile}
    own, zeros = forward(mask, cotangent, col_table, row_table)
    ids = jnp.concatenate([source_ids, source_count[:, None]], 1) + zeros
    bit = 1
    while bit < n_src // 2:
        ids = jnp.concatenate([ids, swapped(ids, sizes, {"src": bit})], 0)
        bit *= 2
    step = 1
    while step < n_tile // 2:
        own = own + swapped(own, sizes, {"tile": step})
        step *= 2
    own_lines = slot_lines(ids + own[SUMS : SUMS + 1, : SLOTS + 1].astype(jnp.int32), shift_table.T, source_weight.reshape(-1, LANES))
    other_lines = swapped(own_lines, sizes, {"src": bit})
    other = swapped(own, sizes, {"tile": step})
    pupil = pupil_rows(pupil_phase + own[SUMS : SUMS + 1, :PUPIL])
    return adjoint(
        own, other, own_lines, other_lines, pupil, grid_tables(), out_cols, out_table, n_src
    )


def solution(mesh):
    placed = (
        P(("grp", "tile"), None),
        P(("grp", "tile"), None),
        P(),
        P(),
        P(),
        P(("grp", "src"), None),
        P(("grp", "src")),
    )
    return jax.shard_map(
        body, mesh=mesh, in_specs=placed, out_specs=P(("grp", "tile"), "src", None), check_vma=False
    )
```

```python
import functools
import math

import jax
import jax.numpy as jnp
import ml_dtypes
import numpy as np
from jax import lax
from jax.experimental import pallas as pl
from jax.experimental.pallas import tpu as pltpu
from jax.sharding import PartitionSpec as P

COLS = 2048
TILE_ROWS = 2048
BAND = 128
PUPIL = 64
SLOTS = 8
GRID = 128
CHUNKS = (1,) * 8
GROUPS = (16, 20, 24, 32)
OX, OY, FACTOR, COUNT = range(4)
PARTS = 4
LANES = 128
SUMS = 2 * BAND + GRID
HALF = SUMS // 2
ZEROS = 8
GRANT = 53 * 1024 * 1024

VMEM = pl.BlockSpec(memory_space=pltpu.VMEM)
SMEM = pl.BlockSpec(memory_space=pltpu.SMEM)
HBM = pl.BlockSpec(memory_space=pltpu.HBM)


def waves(positions, freqs, length):
    product = np.multiply.outer(positions, freqs) % length
    angle = product.astype(np.float64) * (2.0 * math.pi / length)
    return np.cos(angle), np.sin(angle)


def lowpass(positions, length):
    freqs = np.arange(1, PUPIL)
    step = length // GRID
    apart = np.arange(GRID)[None, :] * step - positions[:, None]
    product = (apart[:, :, None] * freqs) % length
    return (1.0 + 2.0 * np.cos(product * (2.0 * math.pi / length)).sum(2)) / GRID


def low(array):
    return np.ascontiguousarray(array).astype(ml_dtypes.bfloat16)


@functools.cache
def image_tables(columns, height, n_tile, n_src):
    band = np.arange(BAND) - BAND // 2
    cols = np.arange(columns)
    rows = np.arange(TILE_ROWS)
    cos, sin = waves(cols, band, columns)
    col_table = low(np.concatenate([cos, -sin, lowpass(cols, columns)], 1))
    cos, sin = waves(rows, band, TILE_ROWS)
    row_table = np.concatenate([cos, sin, lowpass(rows, TILE_ROWS)], 1)
    row_table = low(row_table.reshape(n_tile, height, 2 * BAND + GRID).transpose(0, 2, 1))
    portion = height // n_src
    out_table = np.concatenate([cos, -sin], 1).astype(np.float32)
    out_table = out_table.reshape(n_tile * n_src, portion, 2 * BAND)
    cos, sin = waves(cols, band, columns)
    return col_table, row_table, out_table, low(np.concatenate([cos, -sin], 1).T)


COLS_IN, COLS_OUT = slice(0, 2 * BAND), slice(2 * BAND, 2 * BAND + 2 * GRID)
ROWS_IN = slice(COLS_OUT.stop, COLS_OUT.stop + GRID)
ROWS_OUT = slice(ROWS_IN.stop, ROWS_IN.stop + 2 * PUPIL)


@functools.cache
def grid_tables():
    points = np.arange(GRID)
    band = np.arange(BAND) - BAND // 2
    cos, sin = waves(points, band, GRID)
    cols_in = np.block([[cos.T, sin.T], [-sin.T, cos.T]])
    cols_out = np.block([[cos, -sin], [sin, cos]])
    cos, sin = waves(points, np.arange(PUPIL) - PUPIL // 2, GRID)
    rows_in = np.block([[cos, -sin, sin, cos]])
    rows_out = np.block([[cos.T, sin.T], [-sin.T, cos.T]])
    return low(np.concatenate([cols_in, cols_out, rows_in, rows_out], 0))


def dot(left, right):
    return jnp.dot(left, right, preferred_element_type=jnp.float32)


def forward_kernel(
    mask, cotangent, col_table, row_table,
    keep, send, zeros,
    halves, mask_v, cot_v, col_v, row_v, sems,
):
    columns = mask.shape[1]
    ends = np.cumsum(CHUNKS) * (columns // sum(CHUNKS))
    parts = [pl.ds(int(low), int(high - low)) for low, high in zip([0, *ends], ends)]
    tile = lax.axis_index("tile")
    chunk_copies = []
    for step, part in enumerate(parts):
        copies = [
            pltpu.make_async_copy(col_table.at[part, :], col_v.at[part, :], sems.at[step, 0]),
            pltpu.make_async_copy(mask.at[:, part], mask_v.at[:, part], sems.at[step, 1]),
            pltpu.make_async_copy(cotangent.at[:, part], cot_v.at[:, part], sems.at[step, 2]),
        ]
        for copy in copies:
            copy.start()
        chunk_copies.append(copies)
    row_copy = pltpu.make_async_copy(row_table.at[tile], row_v, sems.at[len(CHUNKS), 0])
    row_copy.start()

    for step, part in enumerate(parts):
        for copy in chunk_copies[step]:
            copy.wait()
        mask_add = dot(mask_v[:, part], col_v[part, : 2 * BAND])
        cot_add = dot(cot_v[:, part], col_v[part, 2 * BAND :])
        mask_part = mask_add if step == 0 else mask_part + mask_add
        cot_part = cot_add if step == 0 else cot_part + cot_add

    row_copy.wait()
    blocks = dot(row_v[: 2 * BAND, :], mask_part.astype(jnp.bfloat16))
    image = dot(row_v[2 * BAND :, :], cot_part.astype(jnp.bfloat16))
    sums = jnp.concatenate(
        [
            blocks[:BAND, :BAND] + blocks[BAND:, BAND:],
            blocks[:BAND, BAND:] - blocks[BAND:, :BAND],
            image,
        ],
        0,
    )
    rest = jnp.zeros((ZEROS, BAND), jnp.float32)
    for half in range(2):
        halves[half] = jnp.concatenate([sums[half * HALF : (half + 1) * HALF], rest], 0)
    own_half = tile % 2
    keep[...] = halves[own_half]
    send[...] = halves[1 - own_half]
    zeros[...] = jnp.zeros_like(zeros)


def forward(mask, cotangent, col_table, row_table):
    height, columns = mask.shape
    return pl.pallas_call(
        forward_kernel,
        out_shape=(
            jax.ShapeDtypeStruct((HALF + ZEROS, BAND), jnp.float32),
            jax.ShapeDtypeStruct((HALF + ZEROS, BAND), jnp.float32),
            jax.ShapeDtypeStruct((1, SLOTS + 1), jnp.int32),
        ),
        in_specs=[HBM] * 4,
        out_specs=(VMEM, VMEM, VMEM),
        scratch_shapes=[
            pltpu.VMEM((2, HALF + ZEROS, BAND), jnp.float32),
            pltpu.VMEM(mask.shape, jnp.bfloat16),
            pltpu.VMEM(mask.shape, jnp.bfloat16),
            pltpu.VMEM(col_table.shape, jnp.bfloat16),
            pltpu.VMEM(row_table.shape[1:], jnp.bfloat16),
            pltpu.SemaphoreType.DMA((len(CHUNKS) + 1, 3)),
        ],
        compiler_params=pltpu.CompilerParams(vmem_limit_bytes=GRANT),
        cost_estimate=pl.CostEstimate(
            flops=2 * height * columns * SUMS, bytes_accessed=6 * 1024 * 1024, transcendentals=0
        ),
        name="forward",
    )(mask, cotangent, col_table, row_table)


def lines_kernel(ids, shift, weight, lines):
    lane = lax.broadcasted_iota(jnp.int32, (SLOTS, LANES), 1)
    place = lax.broadcasted_iota(jnp.int32, (SLOTS, LANES), 0)

    def one(row, carry):
        blocks, weights, there = [], [], jnp.full_like(lane, -1)
        for slot in range(SLOTS):
            source = ids[row, slot]
            start = pl.multiple_of(source // LANES * LANES, LANES)
            blocks.append(shift[:, pl.ds(start, LANES)])
            weights.append(weight[pl.ds(source // LANES, 1), :])
            found = jnp.where(slot < ids[row, SLOTS], source % LANES, -1)
            there = jnp.where(place == slot, found, there)
        here = lane == there
        line = jnp.zeros((SLOTS, LANES), jnp.float32)
        for dim, into in ((0, OX), (1, OY)):
            values = jnp.concatenate([block[dim : dim + 1, :] for block in blocks], 0)
            found = jnp.sum(jnp.where(here, values.astype(jnp.float32), 0.0), 1, keepdims=True)
            line = jnp.where(lane == into, found, line)
        found = jnp.sum(jnp.where(here, jnp.concatenate(weights, 0), 0.0), 1, keepdims=True)
        line = jnp.where(lane == FACTOR, found * (2.0 / SLOTS / PUPIL / PUPIL), line)
        line = jnp.where(lane == COUNT, ids[row, SLOTS].astype(jnp.float32), line)
        lines[pl.ds(pl.multiple_of(row * SLOTS, SLOTS), SLOTS), :] = line
        return carry

    lax.fori_loop(0, ids.shape[0], one, jnp.int32(0), unroll=ids.shape[0] <= 4)


def slot_lines(ids, shift, weight):
    count = ids.shape[0] * SLOTS
    return pl.pallas_call(
        lines_kernel,
        out_shape=jax.ShapeDtypeStruct((count, LANES), jnp.float32),
        in_specs=[SMEM, VMEM, VMEM],
        out_specs=VMEM,
        compiler_params=pltpu.CompilerParams(vmem_limit_bytes=2 * 1024 * 1024),
        cost_estimate=pl.CostEstimate(flops=1, bytes_accessed=1, transcendentals=0),
        name="slot_lines",
    )(ids, shift, weight)


def adjoint_kernel(
    n_src, own, other, own_lines, other_lines, pupil, table, col_table, out_table,
    result,
    spec_real, spec_imag, image, table_v, col_v, out_v, result_v, lines, used, sems, out_sems, *bands,
):
    place = lax.axis_index("tile") * n_src + lax.axis_index("src")
    grid_copy = pltpu.make_async_copy(table, table_v, sems.at[0])
    out_copy = pltpu.make_async_copy(out_table.at[place], out_v, sems.at[1])
    col_copy = pltpu.make_async_copy(col_table, col_v, sems.at[2])
    half = own_lines.shape[0]
    own_copy = pltpu.make_async_copy(own_lines, lines.at[pl.ds(0, half), :], sems.at[3])
    other_copy = pltpu.make_async_copy(other_lines, lines.at[pl.ds(half, half), :], sems.at[4])
    for copy in (own_copy, other_copy, grid_copy, out_copy, col_copy):
        copy.start()

    scale = 1.0 / math.sqrt(TILE_ROWS * COLS)
    first = lax.axis_index("tile") % 2 == 0
    own_half, other_half = own[:HALF, :], other[:HALF, :]
    whole = jnp.concatenate(
        [jnp.where(first, own_half, other_half), jnp.where(first, other_half, own_half)], 0
    )
    spec = (whole[: 2 * BAND] * scale).astype(jnp.bfloat16).astype(jnp.float32)
    spec_real[...] = spec[:BAND]
    spec_imag[...] = spec[BAND:]
    image[:GRID, :] = whole[2 * BAND :]
    image[GRID:, :] = whole[2 * BAND :]
    for band in bands:
        band[...] = jnp.zeros_like(band)
    for slot in range(2 * half + GROUPS[-1]):
        used[slot] = jnp.int32(0)
    own_copy.wait()
    other_copy.wait()

    def add(block, total):
        first = block * SLOTS
        for slot in range(SLOTS):
            used[total + slot] = first + slot
        return total + lines[first, COUNT].astype(jnp.int32)

    blocks = 2 * half // SLOTS
    total = lax.fori_loop(0, blocks, add, jnp.int32(0), unroll=blocks <= 8)
    grid_copy.wait()

    def group(first, size):
        starts, pupils, amplitudes = [], [], []
        for slot in range(size):
            place = first + slot
            index = used[place]
            factor = jnp.where(place < total, lines[index, FACTOR], 0.0)
            offset_x = lines[index, OX].astype(jnp.int32)
            offset_y = lines[index, OY].astype(jnp.int32)
            real = pltpu.roll(pupil[:PUPIL, :], offset_x, 1)
            imag = pltpu.roll(pupil[PUPIL:, :], offset_x, 1)
            rows = pl.ds(offset_y, PUPIL)
            amp_real = real * spec_real[rows, :] - imag * spec_imag[rows, :]
            amp_imag = real * spec_imag[rows, :] + imag * spec_real[rows, :]
            starts.append(offset_y)
            pupils.append((real, imag, factor))
            amplitudes.append(jnp.concatenate([amp_real, amp_imag], 1).astype(jnp.bfloat16))
        halfway = dot(jnp.concatenate(amplitudes, 0), table_v[COLS_IN, :]).astype(jnp.bfloat16)
        halfway = jnp.concatenate(
            [
                jnp.concatenate(
                    [
                        halfway[slot * PUPIL : (slot + 1) * PUPIL, :GRID],
                        halfway[slot * PUPIL : (slot + 1) * PUPIL, GRID:],
                    ],
                    0,
                )
                for slot in range(size)
            ],
            1,
        )
        rows_in = table_v[ROWS_IN, :]
        rows_in = jnp.concatenate([rows_in[:, : 2 * PUPIL], rows_in[:, 2 * PUPIL :]], 0)
        field = dot(rows_in, halfway)
        field_grad = jnp.concatenate(
            [
                (field[:, slot * GRID : (slot + 1) * GRID] * image[...]).astype(jnp.bfloat16)
                for slot in range(size)
            ],
            1,
        )
        back = dot(table_v[ROWS_OUT, :], field_grad).astype(jnp.bfloat16)
        back = jnp.concatenate(
            [
                jnp.concatenate(
                    [
                        back[:PUPIL, slot * GRID : (slot + 1) * GRID],
                        back[PUPIL:, slot * GRID : (slot + 1) * GRID],
                    ],
                    1,
                )
                for slot in range(size)
            ],
            0,
        )
        grad = dot(back, table_v[COLS_OUT, :])
        for slot in range(size):
            real, imag, factor = pupils[slot]
            grad_real = grad[slot * PUPIL : (slot + 1) * PUPIL, :BAND] * factor
            grad_imag = grad[slot * PUPIL : (slot + 1) * PUPIL, BAND:] * factor
            rows = pl.ds(starts[slot], PUPIL)
            band_real, band_imag = bands[slot % 2], bands[2 + slot % 2]
            band_real[rows, :] = band_real[rows, :] + (real * grad_real + imag * grad_imag)
            band_imag[rows, :] = band_imag[rows, :] + (real * grad_imag - imag * grad_real)

    largest, second = GROUPS[-1], GROUPS[-2]
    whole_groups = (total + largest - 1 - second) // largest

    def whole_group(step, carry):
        group(step * largest, largest)
        return carry

    lax.fori_loop(0, whole_groups, whole_group, jnp.int32(0))
    rest = total - whole_groups * largest
    for below, size in zip((0, *GROUPS), GROUPS[:-1]):

        @pl.when((rest > below) & (rest <= size))
        def _():
            group(whole_groups * largest, size)

    real = (bands[0][...] + bands[1][...]) * scale
    imag = (bands[2][...] + bands[3][...]) * scale
    left = jnp.concatenate(
        [jnp.concatenate([real, imag], 1), jnp.concatenate([imag, -real], 1)], 0
    ).astype(jnp.bfloat16)
    out_copy.wait()
    mixed = dot(out_v[...].astype(jnp.bfloat16), left).astype(jnp.bfloat16)
    col_copy.wait()
    width = result.shape[2] // PARTS
    copies = []
    for step in range(PARTS):
        part = pl.ds(step * width, width)
        result_v[:, part] = dot(mixed, col_v[:, part])
        copy = pltpu.make_async_copy(
            result_v.at[:, part], result.at[0, :, part], out_sems.at[step]
        )
        copy.start()
        copies.append(copy)
    for copy in copies:
        copy.wait()


def adjoint(own, other, own_lines, other_lines, pupil, table, col_table, out_table, n_src):
    portion = out_table.shape[1]
    columns = col_table.shape[1]
    band = pltpu.VMEM((BAND, BAND), jnp.float32)
    return pl.pallas_call(
        functools.partial(adjoint_kernel, n_src),
        out_shape=jax.ShapeDtypeStruct((1, portion, columns), jnp.float32),
        in_specs=[VMEM] * 5 + [HBM] * 3,
        out_specs=HBM,
        scratch_shapes=[
            band,
            band,
            pltpu.VMEM((2 * GRID, GRID), jnp.float32),
            pltpu.VMEM(table.shape, jnp.bfloat16),
            pltpu.VMEM(col_table.shape, jnp.bfloat16),
            pltpu.VMEM(out_table.shape[1:], jnp.float32),
            pltpu.VMEM((portion, columns), jnp.float32),
            pltpu.SMEM((2 * own_lines.shape[0], LANES), jnp.float32),
            pltpu.SMEM((2 * own_lines.shape[0] + GROUPS[-1],), jnp.int32),
            pltpu.SemaphoreType.DMA((5,)),
            pltpu.SemaphoreType.DMA((PARTS,)),
            band,
            band,
            band,
            band,
        ],
        compiler_params=pltpu.CompilerParams(vmem_limit_bytes=GRANT),
        cost_estimate=pl.CostEstimate(
            flops=2 * 128 * 4096 * 256, bytes_accessed=4 * 1024 * 1024, transcendentals=0
        ),
        name="adjoint",
    )(own, other, own_lines, other_lines, pupil, table, col_table, out_table)


def pupil_rows(phase):
    grid = jnp.arange(PUPIL, dtype=jnp.int32)
    radius = (2 * grid[:, None] - PUPIL + 1) ** 2 + (2 * grid[None, :] - PUPIL + 1) ** 2
    inside = radius <= PUPIL * PUPIL
    both = jnp.concatenate(
        [jnp.where(inside, jnp.cos(phase), 0.0), jnp.where(inside, jnp.sin(phase), 0.0)], 0
    )
    return jnp.pad(both, ((0, 0), (0, BAND - PUPIL)))


def swapped(array, sizes, steps):
    axes = tuple(sizes)
    places = np.arange(math.prod(sizes.values())).reshape(tuple(sizes.values()))
    there = places
    for dim, axis in enumerate(axes):
        there = np.take(there, np.arange(sizes[axis]) ^ steps.get(axis, 0), dim)
    turn = [(int(a), int(b)) for a, b in zip(places.ravel(), there.ravel())]
    return lax.ppermute(array, axes, turn)


def body(mask, cotangent, pupil_phase, source_weight, shift_table, source_ids, source_count):
    height, columns = mask.shape
    n_tile, n_src = lax.axis_size("tile"), lax.axis_size("src")
    col_table, row_table, out_table, out_cols = image_tables(columns, height, n_tile, n_src)
    sizes = {"src": n_src, "tile": n_tile}
    keep, send, zeros = forward(mask, cotangent, col_table, row_table)
    ids = jnp.concatenate([source_ids, source_count[:, None]], 1) + zeros
    bit = 1
    while bit < n_src // 2:
        ids = jnp.concatenate([ids, swapped(ids, sizes, {"src": bit})], 0)
        bit *= 2
    own = keep + swapped(send, sizes, {"tile": 1})
    own_lines = slot_lines(ids + own[HALF : HALF + 1, : SLOTS + 1].astype(jnp.int32), shift_table.T, source_weight.reshape(-1, LANES))
    other_lines = swapped(own_lines, sizes, {"src": bit})
    step = 2
    while step < n_tile:
        own = own + swapped(own, sizes, {"tile": step})
        step *= 2
    other = swapped(own, sizes, {"tile": 1})
    pupil = pupil_rows(pupil_phase + own[HALF : HALF + 1, :PUPIL])
    return adjoint(
        own, other, own_lines, other_lines, pupil, grid_tables(), out_cols, out_table, n_src
    )


def solution(mesh):
    placed = (
        P(("grp", "tile"), None),
        P(("grp", "tile"), None),
        P(),
        P(),
        P(),
        P(("grp", "src"), None),
        P(("grp", "src")),
    )
    return jax.shard_map(
        body, mesh=mesh, in_specs=placed, out_specs=P(("grp", "tile"), "src", None), check_vma=False
    )
```

```python
import functools
import math

import jax
import jax.numpy as jnp
import ml_dtypes
import numpy as np
from jax import lax
from jax.experimental import pallas as pl
from jax.experimental.pallas import tpu as pltpu
from jax.sharding import PartitionSpec as P

COLS = 2048
TILE_ROWS = 2048
BAND = 128
PUPIL = 64
SLOTS = 8
GRID = 128
CHUNKS = (1,) * 8
GROUPS = (16, 20, 24, 32)
OX, OY, FACTOR, COUNT = range(4)
PARTS = 4
LANES = 128
SUMS = 2 * BAND + GRID
HALF = SUMS // 2
ZEROS = 8
GRANT = 53 * 1024 * 1024

VMEM = pl.BlockSpec(memory_space=pltpu.VMEM)
SMEM = pl.BlockSpec(memory_space=pltpu.SMEM)
HBM = pl.BlockSpec(memory_space=pltpu.HBM)


def waves(positions, freqs, length):
    product = np.multiply.outer(positions, freqs) % length
    angle = product.astype(np.float64) * (2.0 * math.pi / length)
    return np.cos(angle), np.sin(angle)


def lowpass(positions, length):
    freqs = np.arange(1, PUPIL)
    step = length // GRID
    apart = np.arange(GRID)[None, :] * step - positions[:, None]
    product = (apart[:, :, None] * freqs) % length
    return (1.0 + 2.0 * np.cos(product * (2.0 * math.pi / length)).sum(2)) / GRID


def low(array):
    return np.ascontiguousarray(array).astype(ml_dtypes.bfloat16)


@functools.cache
def image_tables(columns, height, n_tile, n_src):
    band = np.arange(BAND) - BAND // 2
    cols = np.arange(columns)
    rows = np.arange(TILE_ROWS)
    cos, sin = waves(cols, band, columns)
    col_table = low(np.concatenate([cos, -sin, lowpass(cols, columns)], 1))
    cos, sin = waves(rows, band, TILE_ROWS)
    row_table = np.concatenate([cos, sin, lowpass(rows, TILE_ROWS)], 1)
    row_table = low(row_table.reshape(n_tile, height, 2 * BAND + GRID).transpose(0, 2, 1))
    portion = height // n_src
    out_table = np.concatenate([cos, -sin], 1).astype(np.float32)
    out_table = out_table.reshape(n_tile * n_src, portion, 2 * BAND)
    cos, sin = waves(cols, band, columns)
    return col_table, row_table, out_table, low(np.concatenate([cos, -sin], 1).T)


COLS_IN, COLS_OUT = slice(0, 2 * BAND), slice(2 * BAND, 2 * BAND + 2 * GRID)
ROWS_IN = slice(COLS_OUT.stop, COLS_OUT.stop + GRID)
ROWS_OUT = slice(ROWS_IN.stop, ROWS_IN.stop + 2 * PUPIL)


@functools.cache
def grid_tables():
    points = np.arange(GRID)
    band = np.arange(BAND) - BAND // 2
    cos, sin = waves(points, band, GRID)
    cols_in = np.block([[cos.T, sin.T], [-sin.T, cos.T]])
    cols_out = np.block([[cos, -sin], [sin, cos]])
    cos, sin = waves(points, np.arange(PUPIL) - PUPIL // 2, GRID)
    rows_in = np.block([[cos, -sin, sin, cos]])
    rows_out = np.block([[cos.T, sin.T], [-sin.T, cos.T]])
    return low(np.concatenate([cols_in, cols_out, rows_in, rows_out], 0))


def dot(left, right):
    return jnp.dot(left, right, preferred_element_type=jnp.float32)


def forward_kernel(
    mask, cotangent, col_table, row_table,
    keep, send, zeros,
    halves, mask_v, cot_v, col_v, row_v, sems,
):
    columns = mask.shape[1]
    ends = np.cumsum(CHUNKS) * (columns // sum(CHUNKS))
    parts = [pl.ds(int(low), int(high - low)) for low, high in zip([0, *ends], ends)]
    tile = lax.axis_index("tile")
    chunk_copies = []
    for step, part in enumerate(parts):
        copies = [
            pltpu.make_async_copy(col_table.at[part, :], col_v.at[part, :], sems.at[step, 0]),
            pltpu.make_async_copy(mask.at[:, part], mask_v.at[:, part], sems.at[step, 1]),
            pltpu.make_async_copy(cotangent.at[:, part], cot_v.at[:, part], sems.at[step, 2]),
        ]
        for copy in copies:
            copy.start()
        chunk_copies.append(copies)
    row_copy = pltpu.make_async_copy(row_table.at[tile], row_v, sems.at[len(CHUNKS), 0])
    row_copy.start()

    for step, part in enumerate(parts):
        for copy in chunk_copies[step]:
            copy.wait()
        mask_add = dot(mask_v[:, part], col_v[part, : 2 * BAND])
        cot_add = dot(cot_v[:, part], col_v[part, 2 * BAND :])
        mask_part = mask_add if step == 0 else mask_part + mask_add
        cot_part = cot_add if step == 0 else cot_part + cot_add

    row_copy.wait()
    blocks = dot(row_v[: 2 * BAND, :], mask_part.astype(jnp.bfloat16))
    image = dot(row_v[2 * BAND :, :], cot_part.astype(jnp.bfloat16))
    sums = jnp.concatenate(
        [
            blocks[:BAND, :BAND] + blocks[BAND:, BAND:],
            blocks[:BAND, BAND:] - blocks[BAND:, :BAND],
            image,
        ],
        0,
    )
    rest = jnp.zeros((ZEROS, BAND), jnp.float32)
    for half in range(2):
        halves[half] = jnp.concatenate([sums[half * HALF : (half + 1) * HALF], rest], 0)
    own_half = tile % 2
    keep[...] = halves[own_half]
    send[...] = halves[1 - own_half]
    zeros[...] = jnp.zeros_like(zeros)


def forward(mask, cotangent, col_table, row_table):
    height, columns = mask.shape
    return pl.pallas_call(
        forward_kernel,
        out_shape=(
            jax.ShapeDtypeStruct((HALF + ZEROS, BAND), jnp.float32),
            jax.ShapeDtypeStruct((HALF + ZEROS, BAND), jnp.float32),
            jax.ShapeDtypeStruct((1, SLOTS + 1), jnp.int32),
        ),
        in_specs=[HBM] * 4,
        out_specs=(VMEM, VMEM, VMEM),
        scratch_shapes=[
            pltpu.VMEM((2, HALF + ZEROS, BAND), jnp.float32),
            pltpu.VMEM(mask.shape, jnp.bfloat16),
            pltpu.VMEM(mask.shape, jnp.bfloat16),
            pltpu.VMEM(col_table.shape, jnp.bfloat16),
            pltpu.VMEM(row_table.shape[1:], jnp.bfloat16),
            pltpu.SemaphoreType.DMA((len(CHUNKS) + 1, 3)),
        ],
        compiler_params=pltpu.CompilerParams(vmem_limit_bytes=GRANT),
        cost_estimate=pl.CostEstimate(
            flops=2 * height * columns * SUMS, bytes_accessed=6 * 1024 * 1024, transcendentals=0
        ),
        name="forward",
    )(mask, cotangent, col_table, row_table)


def lines_kernel(ids, shift, weight, lines):
    lane = lax.broadcasted_iota(jnp.int32, (SLOTS, LANES), 1)
    place = lax.broadcasted_iota(jnp.int32, (SLOTS, LANES), 0)

    def one(row, carry):
        blocks, weights, there = [], [], jnp.full_like(lane, -1)
        for slot in range(SLOTS):
            source = ids[row, slot]
            start = pl.multiple_of(source // LANES * LANES, LANES)
            blocks.append(shift[:, pl.ds(start, LANES)])
            weights.append(weight[pl.ds(source // LANES, 1), :])
            found = jnp.where(slot < ids[row, SLOTS], source % LANES, -1)
            there = jnp.where(place == slot, found, there)
        here = lane == there
        line = jnp.zeros((SLOTS, LANES), jnp.float32)
        for dim, into in ((0, OX), (1, OY)):
            values = jnp.concatenate([block[dim : dim + 1, :] for block in blocks], 0)
            found = jnp.sum(jnp.where(here, values.astype(jnp.float32), 0.0), 1, keepdims=True)
            line = jnp.where(lane == into, found, line)
        found = jnp.sum(jnp.where(here, jnp.concatenate(weights, 0), 0.0), 1, keepdims=True)
        line = jnp.where(lane == FACTOR, found * (2.0 / SLOTS / PUPIL / PUPIL), line)
        line = jnp.where(lane == COUNT, ids[row, SLOTS].astype(jnp.float32), line)
        lines[pl.ds(pl.multiple_of(row * SLOTS, SLOTS), SLOTS), :] = line
        return carry

    lax.fori_loop(0, ids.shape[0], one, jnp.int32(0), unroll=ids.shape[0] <= 4)


def slot_lines(ids, shift, weight):
    count = ids.shape[0] * SLOTS
    return pl.pallas_call(
        lines_kernel,
        out_shape=jax.ShapeDtypeStruct((count, LANES), jnp.float32),
        in_specs=[SMEM, VMEM, VMEM],
        out_specs=VMEM,
        compiler_params=pltpu.CompilerParams(vmem_limit_bytes=2 * 1024 * 1024),
        cost_estimate=pl.CostEstimate(flops=1, bytes_accessed=1, transcendentals=0),
        name="slot_lines",
    )(ids, shift, weight)


def adjoint_kernel(
    n_src, own, other, own_lines, other_lines, pupil, table, col_table, out_table,
    result,
    spec_real, spec_imag, image, table_v, col_v, out_v, result_v, lines, used, sems, out_sems, *bands,
):
    place = lax.axis_index("tile") * n_src + lax.axis_index("src")
    grid_copy = pltpu.make_async_copy(table, table_v, sems.at[0])
    out_copy = pltpu.make_async_copy(out_table.at[place], out_v, sems.at[1])
    col_copy = pltpu.make_async_copy(col_table, col_v, sems.at[2])
    half = own_lines.shape[0]
    own_copy = pltpu.make_async_copy(own_lines, lines.at[pl.ds(0, half), :], sems.at[3])
    other_copy = pltpu.make_async_copy(other_lines, lines.at[pl.ds(half, half), :], sems.at[4])
    for copy in (own_copy, other_copy, grid_copy, out_copy, col_copy):
        copy.start()

    scale = 1.0 / math.sqrt(TILE_ROWS * COLS)
    first = lax.axis_index("tile") % 2 == 0
    own_half, other_half = own[:HALF, :], other[:HALF, :]
    whole = jnp.concatenate(
        [jnp.where(first, own_half, other_half), jnp.where(first, other_half, own_half)], 0
    )
    spec = (whole[: 2 * BAND] * scale).astype(jnp.bfloat16).astype(jnp.float32)
    spec_real[...] = spec[:BAND]
    spec_imag[...] = spec[BAND:]
    image[:GRID, :] = whole[2 * BAND :]
    image[GRID:, :] = whole[2 * BAND :]
    for band in bands:
        band[...] = jnp.zeros_like(band)
    for slot in range(2 * half + GROUPS[-1]):
        used[slot] = jnp.int32(0)
    own_copy.wait()
    other_copy.wait()

    def add(block, total):
        first = block * SLOTS
        for slot in range(SLOTS):
            used[total + slot] = first + slot
        return total + lines[first, COUNT].astype(jnp.int32)

    blocks = 2 * half // SLOTS
    total = lax.fori_loop(0, blocks, add, jnp.int32(0), unroll=blocks <= 8)
    grid_copy.wait()

    def group(first, size):
        starts, pupils, amplitudes = [], [], []
        for slot in range(size):
            place = first + slot
            index = used[place]
            factor = jnp.where(place < total, lines[index, FACTOR], 0.0)
            offset_x = lines[index, OX].astype(jnp.int32)
            offset_y = lines[index, OY].astype(jnp.int32)
            real = pltpu.roll(pupil[:PUPIL, :], offset_x, 1)
            imag = pltpu.roll(pupil[PUPIL:, :], offset_x, 1)
            rows = pl.ds(offset_y, PUPIL)
            amp_real = real * spec_real[rows, :] - imag * spec_imag[rows, :]
            amp_imag = real * spec_imag[rows, :] + imag * spec_real[rows, :]
            starts.append(offset_y)
            pupils.append((real, imag, factor))
            amplitudes.append(jnp.concatenate([amp_real, amp_imag], 1).astype(jnp.bfloat16))
        halfway = dot(jnp.concatenate(amplitudes, 0), table_v[COLS_IN, :]).astype(jnp.bfloat16)
        halfway = jnp.concatenate(
            [
                jnp.concatenate(
                    [
                        halfway[slot * PUPIL : (slot + 1) * PUPIL, :GRID],
                        halfway[slot * PUPIL : (slot + 1) * PUPIL, GRID:],
                    ],
                    0,
                )
                for slot in range(size)
            ],
            1,
        )
        rows_in = table_v[ROWS_IN, :]
        rows_in = jnp.concatenate([rows_in[:, : 2 * PUPIL], rows_in[:, 2 * PUPIL :]], 0)
        field = dot(rows_in, halfway)
        field_grad = jnp.concatenate(
            [
                (field[:, slot * GRID : (slot + 1) * GRID] * image[...]).astype(jnp.bfloat16)
                for slot in range(size)
            ],
            1,
        )
        back = dot(table_v[ROWS_OUT, :], field_grad).astype(jnp.bfloat16)
        back = jnp.concatenate(
            [
                jnp.concatenate(
                    [
                        back[:PUPIL, slot * GRID : (slot + 1) * GRID],
                        back[PUPIL:, slot * GRID : (slot + 1) * GRID],
                    ],
                    1,
                )
                for slot in range(size)
            ],
            0,
        )
        grad = dot(back, table_v[COLS_OUT, :])
        for slot in range(size):
            real, imag, factor = pupils[slot]
            grad_real = grad[slot * PUPIL : (slot + 1) * PUPIL, :BAND] * factor
            grad_imag = grad[slot * PUPIL : (slot + 1) * PUPIL, BAND:] * factor
            rows = pl.ds(starts[slot], PUPIL)
            band_real, band_imag = bands[slot % 2], bands[2 + slot % 2]
            band_real[rows, :] = band_real[rows, :] + (real * grad_real + imag * grad_imag)
            band_imag[rows, :] = band_imag[rows, :] + (real * grad_imag - imag * grad_real)

    largest, second = GROUPS[-1], GROUPS[-2]
    whole_groups = (total + largest - 1 - second) // largest

    def whole_group(step, carry):
        group(step * largest, largest)
        return carry

    lax.fori_loop(0, whole_groups, whole_group, jnp.int32(0))
    rest = total - whole_groups * largest
    for below, size in zip((0, *GROUPS), GROUPS[:-1]):

        @pl.when((rest > below) & (rest <= size))
        def _():
            group(whole_groups * largest, size)

    real = (bands[0][...] + bands[1][...]) * scale
    imag = (bands[2][...] + bands[3][...]) * scale
    left = jnp.concatenate(
        [jnp.concatenate([real, imag], 1), jnp.concatenate([imag, -real], 1)], 0
    ).astype(jnp.bfloat16)
    out_copy.wait()
    mixed = dot(out_v[...].astype(jnp.bfloat16), left).astype(jnp.bfloat16)
    col_copy.wait()
    width = result.shape[2] // PARTS
    copies = []
    for step in range(PARTS):
        part = pl.ds(step * width, width)
        result_v[:, part] = dot(mixed, col_v[:, part])
        copy = pltpu.make_async_copy(
            result_v.at[:, part], result.at[0, :, part], out_sems.at[step]
        )
        copy.start()
        copies.append(copy)
    for copy in copies:
        copy.wait()


def adjoint(own, other, own_lines, other_lines, pupil, table, col_table, out_table, n_src):
    portion = out_table.shape[1]
    columns = col_table.shape[1]
    band = pltpu.VMEM((BAND, BAND), jnp.float32)
    return pl.pallas_call(
        functools.partial(adjoint_kernel, n_src),
        out_shape=jax.ShapeDtypeStruct((1, portion, columns), jnp.float32),
        in_specs=[VMEM] * 5 + [HBM] * 3,
        out_specs=HBM,
        scratch_shapes=[
            band,
            band,
            pltpu.VMEM((2 * GRID, GRID), jnp.float32),
            pltpu.VMEM(table.shape, jnp.bfloat16),
            pltpu.VMEM(col_table.shape, jnp.bfloat16),
            pltpu.VMEM(out_table.shape[1:], jnp.float32),
            pltpu.VMEM((portion, columns), jnp.float32),
            pltpu.SMEM((2 * own_lines.shape[0], LANES), jnp.float32),
            pltpu.SMEM((2 * own_lines.shape[0] + GROUPS[-1],), jnp.int32),
            pltpu.SemaphoreType.DMA((5,)),
            pltpu.SemaphoreType.DMA((PARTS,)),
            band,
            band,
            band,
            band,
        ],
        compiler_params=pltpu.CompilerParams(vmem_limit_bytes=GRANT),
        cost_estimate=pl.CostEstimate(
            flops=2 * 128 * 4096 * 256, bytes_accessed=4 * 1024 * 1024, transcendentals=0
        ),
        name="adjoint",
    )(own, other, own_lines, other_lines, pupil, table, col_table, out_table)


def pupil_rows(phase):
    grid = 2 * np.arange(PUPIL) - PUPIL + 1
    inside = grid[:, None] ** 2 + grid[None, :] ** 2 <= PUPIL * PUPIL
    both = jnp.concatenate(
        [jnp.where(inside, jnp.cos(phase), 0.0), jnp.where(inside, jnp.sin(phase), 0.0)], 0
    )
    return jnp.pad(both, ((0, 0), (0, BAND - PUPIL)))


def swapped(array, sizes, steps):
    axes = tuple(sizes)
    places = np.arange(math.prod(sizes.values())).reshape(tuple(sizes.values()))
    there = places
    for dim, axis in enumerate(axes):
        there = np.take(there, np.arange(sizes[axis]) ^ steps.get(axis, 0), dim)
    turn = [(int(a), int(b)) for a, b in zip(places.ravel(), there.ravel())]
    return lax.ppermute(array, axes, turn)


def body(mask, cotangent, pupil_phase, source_weight, shift_table, source_ids, source_count):
    height, columns = mask.shape
    n_tile, n_src = lax.axis_size("tile"), lax.axis_size("src")
    col_table, row_table, out_table, out_cols = image_tables(columns, height, n_tile, n_src)
    sizes = {"src": n_src, "tile": n_tile}
    keep, send, zeros = forward(mask, cotangent, col_table, row_table)
    ids = jnp.concatenate([source_ids, source_count[:, None]], 1) + zeros
    bit = 1
    while bit < n_src // 2:
        ids = jnp.concatenate([ids, swapped(ids, sizes, {"src": bit})], 0)
        bit *= 2
    own = keep + swapped(send, sizes, {"tile": 1})
    after = own[HALF : HALF + 1]
    ids = ids + after[:, : SLOTS + 1].astype(jnp.int32)
    own_lines = slot_lines(ids, shift_table.T, source_weight.reshape(-1, LANES))
    pupil = pupil_rows(pupil_phase + after[:, :PUPIL])
    other_lines = swapped(own_lines, sizes, {"src": bit})
    step = 2
    while step < n_tile:
        own = own + swapped(own, sizes, {"tile": step})
        step *= 2
    other = swapped(own, sizes, {"tile": 1})
    return adjoint(
        own, other, own_lines, other_lines, pupil, grid_tables(), out_cols, out_table, n_src
    )


def solution(mesh):
    placed = (
        P(("grp", "tile"), None),
        P(("grp", "tile"), None),
        P(),
        P(),
        P(),
        P(("grp", "src"), None),
        P(("grp", "src")),
    )
    return jax.shard_map(
        body, mesh=mesh, in_specs=placed, out_specs=P(("grp", "tile"), "src", None), check_vma=False
    )
```

```python
import functools
import math

import jax
import jax.numpy as jnp
import ml_dtypes
import numpy as np
from jax import lax
from jax.experimental import pallas as pl
from jax.experimental.pallas import tpu as pltpu
from jax.sharding import PartitionSpec as P

COLS = 2048
TILE_ROWS = 2048
BAND = 128
PUPIL = 64
SLOTS = 8
GRID = 128
CHUNKS = (1,) * 8
GROUPS = (16, 20, 24, 32)
OX, OY, FACTOR, COUNT = range(4)
PARTS = 4
LANES = 128
SUMS = 2 * BAND + GRID
HALF = SUMS // 2
ZEROS = 8
GRANT = 53 * 1024 * 1024

VMEM = pl.BlockSpec(memory_space=pltpu.VMEM)
SMEM = pl.BlockSpec(memory_space=pltpu.SMEM)
HBM = pl.BlockSpec(memory_space=pltpu.HBM)


def waves(positions, freqs, length):
    product = np.multiply.outer(positions, freqs) % length
    angle = product.astype(np.float64) * (2.0 * math.pi / length)
    return np.cos(angle), np.sin(angle)


def lowpass(positions, length):
    freqs = np.arange(1, PUPIL)
    step = length // GRID
    apart = np.arange(GRID)[None, :] * step - positions[:, None]
    product = (apart[:, :, None] * freqs) % length
    return (1.0 + 2.0 * np.cos(product * (2.0 * math.pi / length)).sum(2)) / GRID


def low(array):
    return np.ascontiguousarray(array).astype(ml_dtypes.bfloat16)


@functools.cache
def image_tables(columns, height, n_tile, n_src):
    band = np.arange(BAND) - BAND // 2
    cols = np.arange(columns)
    rows = np.arange(TILE_ROWS)
    cos, sin = waves(cols, band, columns)
    col_table = low(np.concatenate([cos, -sin, lowpass(cols, columns)], 1))
    cos, sin = waves(rows, band, TILE_ROWS)
    row_table = np.concatenate([cos, sin, lowpass(rows, TILE_ROWS)], 1)
    row_table = low(row_table.reshape(n_tile, height, 2 * BAND + GRID).transpose(0, 2, 1))
    portion = height // n_src
    out_table = np.concatenate([cos, -sin], 1).astype(np.float32)
    out_table = out_table.reshape(n_tile * n_src, portion, 2 * BAND)
    cos, sin = waves(cols, band, columns)
    return col_table, row_table, out_table, low(np.concatenate([cos, -sin], 1).T)


COLS_IN, COLS_OUT = slice(0, 2 * BAND), slice(2 * BAND, 2 * BAND + 2 * GRID)
ROWS_IN = slice(COLS_OUT.stop, COLS_OUT.stop + GRID)
ROWS_OUT = slice(ROWS_IN.stop, ROWS_IN.stop + 2 * PUPIL)


@functools.cache
def grid_tables():
    points = np.arange(GRID)
    band = np.arange(BAND) - BAND // 2
    cos, sin = waves(points, band, GRID)
    cols_in = np.block([[cos.T, sin.T], [-sin.T, cos.T]])
    cols_out = np.block([[cos, -sin], [sin, cos]])
    cos, sin = waves(points, np.arange(PUPIL) - PUPIL // 2, GRID)
    rows_in = np.block([[cos, -sin, sin, cos]])
    rows_out = np.block([[cos.T, sin.T], [-sin.T, cos.T]])
    return low(np.concatenate([cols_in, cols_out, rows_in, rows_out], 0))


def dot(left, right):
    return jnp.dot(left, right, preferred_element_type=jnp.float32)


def forward_kernel(
    mask, cotangent, col_table, row_table,
    keep, send, zeros,
    halves, mask_v, cot_v, col_v, row_v, sems,
):
    columns = mask.shape[1]
    ends = np.cumsum(CHUNKS) * (columns // sum(CHUNKS))
    parts = [pl.ds(int(low), int(high - low)) for low, high in zip([0, *ends], ends)]
    tile = lax.axis_index("tile")
    chunk_copies = []
    for step, part in enumerate(parts):
        copies = [
            pltpu.make_async_copy(col_table.at[part, :], col_v.at[part, :], sems.at[step, 0]),
            pltpu.make_async_copy(mask.at[:, part], mask_v.at[:, part], sems.at[step, 1]),
            pltpu.make_async_copy(cotangent.at[:, part], cot_v.at[:, part], sems.at[step, 2]),
        ]
        for copy in copies:
            copy.start()
        chunk_copies.append(copies)
    row_copy = pltpu.make_async_copy(row_table.at[tile], row_v, sems.at[len(CHUNKS), 0])
    row_copy.start()

    for step, part in enumerate(parts):
        for copy in chunk_copies[step]:
            copy.wait()
        mask_add = dot(mask_v[:, part], col_v[part, : 2 * BAND])
        cot_add = dot(cot_v[:, part], col_v[part, 2 * BAND :])
        mask_part = mask_add if step == 0 else mask_part + mask_add
        cot_part = cot_add if step == 0 else cot_part + cot_add

    row_copy.wait()
    blocks = dot(row_v[: 2 * BAND, :], mask_part.astype(jnp.bfloat16))
    image = dot(row_v[2 * BAND :, :], cot_part.astype(jnp.bfloat16))
    sums = jnp.concatenate(
        [
            blocks[:BAND, :BAND] + blocks[BAND:, BAND:],
            blocks[:BAND, BAND:] - blocks[BAND:, :BAND],
            image,
        ],
        0,
    )
    rest = jnp.zeros((ZEROS, BAND), jnp.float32)
    for half in range(2):
        halves[half] = jnp.concatenate([sums[half * HALF : (half + 1) * HALF], rest], 0)
    own_half = tile % 2
    keep[...] = halves[own_half]
    send[...] = halves[1 - own_half]
    zeros[...] = jnp.zeros_like(zeros)


def forward(mask, cotangent, col_table, row_table):
    height, columns = mask.shape
    return pl.pallas_call(
        forward_kernel,
        out_shape=(
            jax.ShapeDtypeStruct((HALF + ZEROS, BAND), jnp.float32),
            jax.ShapeDtypeStruct((HALF + ZEROS, BAND), jnp.float32),
            jax.ShapeDtypeStruct((1, SLOTS + 1), jnp.int32),
        ),
        in_specs=[HBM] * 4,
        out_specs=(VMEM, VMEM, VMEM),
        scratch_shapes=[
            pltpu.VMEM((2, HALF + ZEROS, BAND), jnp.float32),
            pltpu.VMEM(mask.shape, jnp.bfloat16),
            pltpu.VMEM(mask.shape, jnp.bfloat16),
            pltpu.VMEM(col_table.shape, jnp.bfloat16),
            pltpu.VMEM(row_table.shape[1:], jnp.bfloat16),
            pltpu.SemaphoreType.DMA((len(CHUNKS) + 1, 3)),
        ],
        compiler_params=pltpu.CompilerParams(vmem_limit_bytes=GRANT),
        cost_estimate=pl.CostEstimate(
            flops=2 * height * columns * SUMS, bytes_accessed=6 * 1024 * 1024, transcendentals=0
        ),
        name="forward",
    )(mask, cotangent, col_table, row_table)


def lines_kernel(ids, shift, weight, lines):
    blocks = weight.shape[0]
    count = ids.shape[0] * SLOTS
    slot = lax.broadcasted_iota(jnp.int32, (SLOTS, SLOTS + 1), 0)
    column = lax.broadcasted_iota(jnp.int32, (SLOTS, SLOTS + 1), 1)
    sources, counts, used = [], [], []
    for row in range(ids.shape[0]):
        entries = jnp.broadcast_to(ids[row : row + 1, :].astype(jnp.float32), slot.shape)
        sources.append(jnp.sum(jnp.where(slot == column, entries, 0.0), 1, keepdims=True))
        counts.append(jnp.sum(jnp.where(column == SLOTS, entries, 0.0), 1, keepdims=True))
        used.append(jnp.where(slot[:, :1].astype(jnp.float32) < counts[-1], 1.0, 0.0))
    sources, counts, used = (jnp.concatenate(part, 0) for part in (sources, counts, used))
    block = jnp.floor(sources * (1.0 / LANES))

    def row_of(table, index, precision):
        lane = lax.broadcasted_iota(jnp.int32, (count, table.shape[0]), 1).astype(jnp.float32)
        pick = jnp.where(lane == index, 1.0, 0.0).astype(table.dtype)
        return jnp.dot(pick, table, precision=precision, preferred_element_type=jnp.float32)

    lane = lax.broadcasted_iota(jnp.int32, (count, LANES), 1)
    here = lane.astype(jnp.float32) == sources - block * LANES
    offsets = shift[...].astype(jnp.bfloat16)
    line = jnp.zeros((count, LANES), jnp.float32)
    for entry, found in (
        (OX, row_of(offsets, 2.0 * block, None)),
        (OY, row_of(offsets, 2.0 * block + 1.0, None)),
        (FACTOR, row_of(weight[...], block, lax.Precision.HIGHEST)),
    ):
        found = jnp.sum(jnp.where(here, found, 0.0), 1, keepdims=True) * used
        line = jnp.where(lane == entry, found, line)
    line = jnp.where(lane == FACTOR, line * (2.0 / SLOTS / PUPIL / PUPIL), line)
    lines[...] = jnp.where(lane == COUNT, counts, line)


def slot_lines(ids, shift, weight):
    count = ids.shape[0] * SLOTS
    return pl.pallas_call(
        lines_kernel,
        out_shape=jax.ShapeDtypeStruct((count, LANES), jnp.float32),
        in_specs=[VMEM, VMEM, VMEM],
        out_specs=VMEM,
        compiler_params=pltpu.CompilerParams(vmem_limit_bytes=2 * 1024 * 1024),
        cost_estimate=pl.CostEstimate(flops=1, bytes_accessed=1, transcendentals=0),
        name="slot_lines",
    )(ids, shift, weight)


def adjoint_kernel(
    n_src, own, other, own_lines, other_lines, pupil, table, col_table, out_table,
    result,
    spec_real, spec_imag, image, table_v, col_v, out_v, result_v, lines, used, sems, out_sems, *bands,
):
    place = lax.axis_index("tile") * n_src + lax.axis_index("src")
    grid_copy = pltpu.make_async_copy(table, table_v, sems.at[0])
    out_copy = pltpu.make_async_copy(out_table.at[place], out_v, sems.at[1])
    col_copy = pltpu.make_async_copy(col_table, col_v, sems.at[2])
    half = own_lines.shape[0]
    own_copy = pltpu.make_async_copy(own_lines, lines.at[pl.ds(0, half), :], sems.at[3])
    other_copy = pltpu.make_async_copy(other_lines, lines.at[pl.ds(half, half), :], sems.at[4])
    for copy in (own_copy, other_copy, grid_copy, out_copy, col_copy):
        copy.start()

    scale = 1.0 / math.sqrt(TILE_ROWS * COLS)
    first = lax.axis_index("tile") % 2 == 0
    own_half, other_half = own[:HALF, :], other[:HALF, :]
    whole = jnp.concatenate(
        [jnp.where(first, own_half, other_half), jnp.where(first, other_half, own_half)], 0
    )
    spec = (whole[: 2 * BAND] * scale).astype(jnp.bfloat16).astype(jnp.float32)
    spec_real[...] = spec[:BAND]
    spec_imag[...] = spec[BAND:]
    image[:GRID, :] = whole[2 * BAND :]
    image[GRID:, :] = whole[2 * BAND :]
    for band in bands:
        band[...] = jnp.zeros_like(band)
    for slot in range(2 * half + GROUPS[-1]):
        used[slot] = jnp.int32(0)
    own_copy.wait()
    other_copy.wait()

    def add(block, total):
        first = block * SLOTS
        for slot in range(SLOTS):
            used[total + slot] = first + slot
        return total + lines[first, COUNT].astype(jnp.int32)

    blocks = 2 * half // SLOTS
    total = lax.fori_loop(0, blocks, add, jnp.int32(0), unroll=blocks <= 8)
    grid_copy.wait()

    def group(first, size):
        starts, pupils, amplitudes = [], [], []
        for slot in range(size):
            place = first + slot
            index = used[place]
            factor = jnp.where(place < total, lines[index, FACTOR], 0.0)
            offset_x = lines[index, OX].astype(jnp.int32)
            offset_y = lines[index, OY].astype(jnp.int32)
            real = pltpu.roll(pupil[:PUPIL, :], offset_x, 1)
            imag = pltpu.roll(pupil[PUPIL:, :], offset_x, 1)
            rows = pl.ds(offset_y, PUPIL)
            amp_real = real * spec_real[rows, :] - imag * spec_imag[rows, :]
            amp_imag = real * spec_imag[rows, :] + imag * spec_real[rows, :]
            starts.append(offset_y)
            pupils.append((real, imag, factor))
            amplitudes.append(jnp.concatenate([amp_real, amp_imag], 1).astype(jnp.bfloat16))
        halfway = dot(jnp.concatenate(amplitudes, 0), table_v[COLS_IN, :]).astype(jnp.bfloat16)
        halfway = jnp.concatenate(
            [
                jnp.concatenate(
                    [
                        halfway[slot * PUPIL : (slot + 1) * PUPIL, :GRID],
                        halfway[slot * PUPIL : (slot + 1) * PUPIL, GRID:],
                    ],
                    0,
                )
                for slot in range(size)
            ],
            1,
        )
        rows_in = table_v[ROWS_IN, :]
        rows_in = jnp.concatenate([rows_in[:, : 2 * PUPIL], rows_in[:, 2 * PUPIL :]], 0)
        field = dot(rows_in, halfway)
        field_grad = jnp.concatenate(
            [
                (field[:, slot * GRID : (slot + 1) * GRID] * image[...]).astype(jnp.bfloat16)
                for slot in range(size)
            ],
            1,
        )
        back = dot(table_v[ROWS_OUT, :], field_grad).astype(jnp.bfloat16)
        back = jnp.concatenate(
            [
                jnp.concatenate(
                    [
                        back[:PUPIL, slot * GRID : (slot + 1) * GRID],
                        back[PUPIL:, slot * GRID : (slot + 1) * GRID],
                    ],
                    1,
                )
                for slot in range(size)
            ],
            0,
        )
        grad = dot(back, table_v[COLS_OUT, :])
        for slot in range(size):
            real, imag, factor = pupils[slot]
            grad_real = grad[slot * PUPIL : (slot + 1) * PUPIL, :BAND] * factor
            grad_imag = grad[slot * PUPIL : (slot + 1) * PUPIL, BAND:] * factor
            rows = pl.ds(starts[slot], PUPIL)
            band_real, band_imag = bands[slot % 2], bands[2 + slot % 2]
            band_real[rows, :] = band_real[rows, :] + (real * grad_real + imag * grad_imag)
            band_imag[rows, :] = band_imag[rows, :] + (real * grad_imag - imag * grad_real)

    largest, second = GROUPS[-1], GROUPS[-2]
    whole_groups = (total + largest - 1 - second) // largest

    def whole_group(step, carry):
        group(step * largest, largest)
        return carry

    lax.fori_loop(0, whole_groups, whole_group, jnp.int32(0))
    rest = total - whole_groups * largest
    for below, size in zip((0, *GROUPS), GROUPS[:-1]):

        @pl.when((rest > below) & (rest <= size))
        def _():
            group(whole_groups * largest, size)

    real = (bands[0][...] + bands[1][...]) * scale
    imag = (bands[2][...] + bands[3][...]) * scale
    left = jnp.concatenate(
        [jnp.concatenate([real, imag], 1), jnp.concatenate([imag, -real], 1)], 0
    ).astype(jnp.bfloat16)
    out_copy.wait()
    mixed = dot(out_v[...].astype(jnp.bfloat16), left).astype(jnp.bfloat16)
    col_copy.wait()
    width = result.shape[2] // PARTS
    copies = []
    for step in range(PARTS):
        part = pl.ds(step * width, width)
        result_v[:, part] = dot(mixed, col_v[:, part])
        copy = pltpu.make_async_copy(
            result_v.at[:, part], result.at[0, :, part], out_sems.at[step]
        )
        copy.start()
        copies.append(copy)
    for copy in copies:
        copy.wait()


def adjoint(own, other, own_lines, other_lines, pupil, table, col_table, out_table, n_src):
    portion = out_table.shape[1]
    columns = col_table.shape[1]
    band = pltpu.VMEM((BAND, BAND), jnp.float32)
    return pl.pallas_call(
        functools.partial(adjoint_kernel, n_src),
        out_shape=jax.ShapeDtypeStruct((1, portion, columns), jnp.float32),
        in_specs=[VMEM] * 5 + [HBM] * 3,
        out_specs=HBM,
        scratch_shapes=[
            band,
            band,
            pltpu.VMEM((2 * GRID, GRID), jnp.float32),
            pltpu.VMEM(table.shape, jnp.bfloat16),
            pltpu.VMEM(col_table.shape, jnp.bfloat16),
            pltpu.VMEM(out_table.shape[1:], jnp.float32),
            pltpu.VMEM((portion, columns), jnp.float32),
            pltpu.SMEM((2 * own_lines.shape[0], LANES), jnp.float32),
            pltpu.SMEM((2 * own_lines.shape[0] + GROUPS[-1],), jnp.int32),
            pltpu.SemaphoreType.DMA((5,)),
            pltpu.SemaphoreType.DMA((PARTS,)),
            band,
            band,
            band,
            band,
        ],
        compiler_params=pltpu.CompilerParams(vmem_limit_bytes=GRANT),
        cost_estimate=pl.CostEstimate(
            flops=2 * 128 * 4096 * 256, bytes_accessed=4 * 1024 * 1024, transcendentals=0
        ),
        name="adjoint",
    )(own, other, own_lines, other_lines, pupil, table, col_table, out_table)


def pupil_rows(phase):
    grid = 2 * np.arange(PUPIL) - PUPIL + 1
    inside = grid[:, None] ** 2 + grid[None, :] ** 2 <= PUPIL * PUPIL
    both = jnp.concatenate(
        [jnp.where(inside, jnp.cos(phase), 0.0), jnp.where(inside, jnp.sin(phase), 0.0)], 0
    )
    return jnp.pad(both, ((0, 0), (0, BAND - PUPIL)))


def swapped(array, sizes, steps):
    axes = tuple(sizes)
    places = np.arange(math.prod(sizes.values())).reshape(tuple(sizes.values()))
    there = places
    for dim, axis in enumerate(axes):
        there = np.take(there, np.arange(sizes[axis]) ^ steps.get(axis, 0), dim)
    turn = [(int(a), int(b)) for a, b in zip(places.ravel(), there.ravel())]
    return lax.ppermute(array, axes, turn)


def body(mask, cotangent, pupil_phase, source_weight, shift_table, source_ids, source_count):
    height, columns = mask.shape
    n_tile, n_src = lax.axis_size("tile"), lax.axis_size("src")
    col_table, row_table, out_table, out_cols = image_tables(columns, height, n_tile, n_src)
    sizes = {"src": n_src, "tile": n_tile}
    keep, send, zeros = forward(mask, cotangent, col_table, row_table)
    ids = jnp.concatenate([source_ids, source_count[:, None]], 1) + zeros
    bit = 1
    while bit < n_src // 2:
        ids = jnp.concatenate([ids, swapped(ids, sizes, {"src": bit})], 0)
        bit *= 2
    own = keep + swapped(send, sizes, {"tile": 1})
    after = own[HALF : HALF + 1]
    ids = ids + after[:, : SLOTS + 1].astype(jnp.int32)
    shift = shift_table.T.reshape(2, -1, LANES).transpose(1, 0, 2).reshape(-1, LANES)
    own_lines = slot_lines(ids, shift, source_weight.reshape(-1, LANES))
    pupil = pupil_rows(pupil_phase + after[:, :PUPIL])
    other_lines = swapped(own_lines, sizes, {"src": bit})
    step = 2
    while step < n_tile:
        own = own + swapped(own, sizes, {"tile": step})
        step *= 2
    other = swapped(own, sizes, {"tile": 1})
    return adjoint(
        own, other, own_lines, other_lines, pupil, grid_tables(), out_cols, out_table, n_src
    )


def solution(mesh):
    placed = (
        P(("grp", "tile"), None),
        P(("grp", "tile"), None),
        P(),
        P(),
        P(),
        P(("grp", "src"), None),
        P(("grp", "src")),
    )
    return jax.shard_map(
        body, mesh=mesh, in_specs=placed, out_specs=P(("grp", "tile"), "src", None), check_vma=False
    )
```

```python
import functools
import math

import jax
import jax.numpy as jnp
import ml_dtypes
import numpy as np
from jax import lax
from jax.experimental import pallas as pl
from jax.experimental.pallas import tpu as pltpu
from jax.sharding import PartitionSpec as P

COLS = 2048
TILE_ROWS = 2048
BAND = 128
PUPIL = 64
SLOTS = 8
GRID = 128
CHUNKS = (1,) * 8
GROUPS = (16, 20, 24, 32)
OX, OY, FACTOR, COUNT = range(4)
PARTS = 4
LANES = 128
SUMS = 2 * BAND + GRID
HALF = SUMS // 2
ZEROS = 8
GRANT = 53 * 1024 * 1024

VMEM = pl.BlockSpec(memory_space=pltpu.VMEM)
SMEM = pl.BlockSpec(memory_space=pltpu.SMEM)
HBM = pl.BlockSpec(memory_space=pltpu.HBM)


def waves(positions, freqs, length):
    product = np.multiply.outer(positions, freqs) % length
    angle = product.astype(np.float64) * (2.0 * math.pi / length)
    return np.cos(angle), np.sin(angle)


def lowpass(positions, length):
    freqs = np.arange(1, PUPIL)
    step = length // GRID
    apart = np.arange(GRID)[None, :] * step - positions[:, None]
    product = (apart[:, :, None] * freqs) % length
    return (1.0 + 2.0 * np.cos(product * (2.0 * math.pi / length)).sum(2)) / GRID


def low(array):
    return np.ascontiguousarray(array).astype(ml_dtypes.bfloat16)


@functools.cache
def image_tables(columns, height, n_tile, n_src):
    band = np.arange(BAND) - BAND // 2
    cols = np.arange(columns)
    rows = np.arange(TILE_ROWS)
    cos, sin = waves(cols, band, columns)
    col_table = low(np.concatenate([cos, -sin, lowpass(cols, columns)], 1))
    cos, sin = waves(rows, band, TILE_ROWS)
    row_table = np.concatenate([cos, sin, lowpass(rows, TILE_ROWS)], 1)
    row_table = low(row_table.reshape(n_tile, height, 2 * BAND + GRID).transpose(0, 2, 1))
    portion = height // n_src
    out_table = np.concatenate([cos, -sin], 1).astype(np.float32)
    out_table = out_table.reshape(n_tile * n_src, portion, 2 * BAND)
    cos, sin = waves(cols, band, columns)
    return col_table, row_table, out_table, low(np.concatenate([cos, -sin], 1).T)


COLS_IN, COLS_OUT = slice(0, 2 * BAND), slice(2 * BAND, 2 * BAND + 2 * GRID)
ROWS_IN = slice(COLS_OUT.stop, COLS_OUT.stop + GRID)
ROWS_OUT = slice(ROWS_IN.stop, ROWS_IN.stop + 2 * PUPIL)


@functools.cache
def grid_tables():
    points = np.arange(GRID)
    band = np.arange(BAND) - BAND // 2
    cos, sin = waves(points, band, GRID)
    cols_in = np.block([[cos.T, sin.T], [-sin.T, cos.T]])
    cols_out = np.block([[cos, -sin], [sin, cos]])
    cos, sin = waves(points, np.arange(PUPIL) - PUPIL // 2, GRID)
    rows_in = np.block([[cos, -sin, sin, cos]])
    rows_out = np.block([[cos.T, sin.T], [-sin.T, cos.T]])
    return low(np.concatenate([cols_in, cols_out, rows_in, rows_out], 0))


def dot(left, right):
    return jnp.dot(left, right, preferred_element_type=jnp.float32)


def forward_kernel(
    mask, cotangent, col_table, row_table,
    keep, send, zeros,
    halves, mask_v, cot_v, col_v, row_v, sems,
):
    columns = mask.shape[1]
    ends = np.cumsum(CHUNKS) * (columns // sum(CHUNKS))
    parts = [pl.ds(int(low), int(high - low)) for low, high in zip([0, *ends], ends)]
    tile = lax.axis_index("tile")
    chunk_copies = []
    for step, part in enumerate(parts):
        copies = [
            pltpu.make_async_copy(col_table.at[part, :], col_v.at[part, :], sems.at[step, 0]),
            pltpu.make_async_copy(mask.at[:, part], mask_v.at[:, part], sems.at[step, 1]),
            pltpu.make_async_copy(cotangent.at[:, part], cot_v.at[:, part], sems.at[step, 2]),
        ]
        for copy in copies:
            copy.start()
        chunk_copies.append(copies)
    row_copy = pltpu.make_async_copy(row_table.at[tile], row_v, sems.at[len(CHUNKS), 0])
    row_copy.start()

    for step, part in enumerate(parts):
        for copy in chunk_copies[step]:
            copy.wait()
        mask_add = dot(mask_v[:, part], col_v[part, : 2 * BAND])
        cot_add = dot(cot_v[:, part], col_v[part, 2 * BAND :])
        mask_part = mask_add if step == 0 else mask_part + mask_add
        cot_part = cot_add if step == 0 else cot_part + cot_add

    row_copy.wait()
    blocks = dot(row_v[: 2 * BAND, :], mask_part.astype(jnp.bfloat16))
    image = dot(row_v[2 * BAND :, :], cot_part.astype(jnp.bfloat16))
    sums = jnp.concatenate(
        [
            blocks[:BAND, :BAND] + blocks[BAND:, BAND:],
            blocks[:BAND, BAND:] - blocks[BAND:, :BAND],
            image,
        ],
        0,
    )
    rest = jnp.zeros((ZEROS, BAND), jnp.float32)
    for half in range(2):
        halves[half] = jnp.concatenate([sums[half * HALF : (half + 1) * HALF], rest], 0)
    own_half = tile % 2
    keep[...] = halves[own_half]
    send[...] = halves[1 - own_half]
    zeros[...] = jnp.zeros_like(zeros)


def forward(mask, cotangent, col_table, row_table):
    height, columns = mask.shape
    return pl.pallas_call(
        forward_kernel,
        out_shape=(
            jax.ShapeDtypeStruct((HALF + ZEROS, BAND), jnp.float32),
            jax.ShapeDtypeStruct((HALF + ZEROS, BAND), jnp.float32),
            jax.ShapeDtypeStruct((1, SLOTS + 1), jnp.int32),
        ),
        in_specs=[HBM] * 4,
        out_specs=(VMEM, VMEM, VMEM),
        scratch_shapes=[
            pltpu.VMEM((2, HALF + ZEROS, BAND), jnp.float32),
            pltpu.VMEM(mask.shape, jnp.bfloat16),
            pltpu.VMEM(mask.shape, jnp.bfloat16),
            pltpu.VMEM(col_table.shape, jnp.bfloat16),
            pltpu.VMEM(row_table.shape[1:], jnp.bfloat16),
            pltpu.SemaphoreType.DMA((len(CHUNKS) + 1, 3)),
        ],
        compiler_params=pltpu.CompilerParams(vmem_limit_bytes=GRANT),
        cost_estimate=pl.CostEstimate(
            flops=2 * height * columns * SUMS, bytes_accessed=6 * 1024 * 1024, transcendentals=0
        ),
        name="forward",
    )(mask, cotangent, col_table, row_table)


def lines_kernel(ids, shift, weight, lines):
    blocks = weight.shape[0]
    count = ids.shape[0] * SLOTS
    slot = lax.broadcasted_iota(jnp.int32, (SLOTS, SLOTS + 1), 0)
    column = lax.broadcasted_iota(jnp.int32, (SLOTS, SLOTS + 1), 1)
    sources, counts, used = [], [], []
    for row in range(ids.shape[0]):
        entries = jnp.broadcast_to(ids[row : row + 1, :].astype(jnp.float32), slot.shape)
        sources.append(jnp.sum(jnp.where(slot == column, entries, 0.0), 1, keepdims=True))
        counts.append(jnp.sum(jnp.where(column == SLOTS, entries, 0.0), 1, keepdims=True))
        used.append(jnp.where(slot[:, :1].astype(jnp.float32) < counts[-1], 1.0, 0.0))
    sources, counts, used = (jnp.concatenate(part, 0) for part in (sources, counts, used))
    block = jnp.floor(sources * (1.0 / LANES))

    def row_of(table, index, precision):
        lane = lax.broadcasted_iota(jnp.int32, (count, table.shape[0]), 1).astype(jnp.float32)
        pick = jnp.where(lane == index, 1.0, 0.0).astype(table.dtype)
        return jnp.dot(pick, table, precision=precision, preferred_element_type=jnp.float32)

    lane = lax.broadcasted_iota(jnp.int32, (count, LANES), 1)
    here = lane.astype(jnp.float32) == sources - block * LANES
    offsets = shift[...].astype(jnp.bfloat16)
    line = jnp.zeros((count, LANES), jnp.float32)
    for entry, found in (
        (OX, row_of(offsets, 2.0 * block, None)),
        (OY, row_of(offsets, 2.0 * block + 1.0, None)),
        (FACTOR, row_of(weight[...], block, lax.Precision.HIGHEST)),
    ):
        found = jnp.sum(jnp.where(here, found, 0.0), 1, keepdims=True) * used
        line = jnp.where(lane == entry, found, line)
    line = jnp.where(lane == FACTOR, line * (2.0 / SLOTS / PUPIL / PUPIL), line)
    lines[...] = jnp.where(lane == COUNT, counts, line)


def slot_lines(ids, shift, weight):
    count = ids.shape[0] * SLOTS
    return pl.pallas_call(
        lines_kernel,
        out_shape=jax.ShapeDtypeStruct((count, LANES), jnp.float32),
        in_specs=[VMEM, VMEM, VMEM],
        out_specs=VMEM,
        compiler_params=pltpu.CompilerParams(vmem_limit_bytes=2 * 1024 * 1024),
        cost_estimate=pl.CostEstimate(flops=1, bytes_accessed=1, transcendentals=0),
        name="slot_lines",
    )(ids, shift, weight)


def adjoint_kernel(
    n_src, own, other, own_lines, other_lines, pupil, table, col_table, out_table,
    result,
    spec_real, spec_imag, image, table_v, col_v, out_v, result_v, lines, used, sems, out_sems, *bands,
):
    place = lax.axis_index("tile") * n_src + lax.axis_index("src")
    grid_copy = pltpu.make_async_copy(table, table_v, sems.at[0])
    out_copy = pltpu.make_async_copy(out_table.at[place], out_v, sems.at[1])
    col_copy = pltpu.make_async_copy(col_table, col_v, sems.at[2])
    half = own_lines.shape[0]
    own_copy = pltpu.make_async_copy(own_lines, lines.at[pl.ds(0, half), :], sems.at[3])
    other_copy = pltpu.make_async_copy(other_lines, lines.at[pl.ds(half, half), :], sems.at[4])
    for copy in (own_copy, other_copy, grid_copy, out_copy, col_copy):
        copy.start()

    scale = 1.0 / math.sqrt(TILE_ROWS * COLS)
    first = lax.axis_index("tile") % 2 == 0
    own_half, other_half = own[:HALF, :], other[:HALF, :]
    whole = jnp.concatenate(
        [jnp.where(first, own_half, other_half), jnp.where(first, other_half, own_half)], 0
    )
    spec = (whole[: 2 * BAND] * scale).astype(jnp.bfloat16).astype(jnp.float32)
    spec_real[...] = spec[:BAND]
    spec_imag[...] = spec[BAND:]
    image[:GRID, :] = whole[2 * BAND :]
    image[GRID:, :] = whole[2 * BAND :]
    for band in bands:
        band[...] = jnp.zeros_like(band)
    for slot in range(2 * half + GROUPS[-1]):
        used[slot] = jnp.int32(0)
    own_copy.wait()
    other_copy.wait()

    def add(block, total):
        first = block * SLOTS
        for slot in range(SLOTS):
            used[total + slot] = first + slot
        return total + lines[first, COUNT].astype(jnp.int32)

    blocks = 2 * half // SLOTS
    total = lax.fori_loop(0, blocks, add, jnp.int32(0), unroll=blocks <= 8)
    grid_copy.wait()

    def group(first, size):
        starts, pupils, amplitudes = [], [], []
        for slot in range(size):
            place = first + slot
            index = used[place]
            factor = jnp.where(place < total, lines[index, FACTOR], 0.0)
            offset_x = lines[index, OX].astype(jnp.int32)
            offset_y = lines[index, OY].astype(jnp.int32)
            real = pltpu.roll(pupil[:PUPIL, :], offset_x, 1)
            imag = pltpu.roll(pupil[PUPIL:, :], offset_x, 1)
            rows = pl.ds(offset_y, PUPIL)
            amp_real = real * spec_real[rows, :] - imag * spec_imag[rows, :]
            amp_imag = real * spec_imag[rows, :] + imag * spec_real[rows, :]
            starts.append(offset_y)
            pupils.append((real, imag, factor))
            amplitudes.append(jnp.concatenate([amp_real, amp_imag], 1).astype(jnp.bfloat16))
        halfway = dot(jnp.concatenate(amplitudes, 0), table_v[COLS_IN, :]).astype(jnp.bfloat16)
        halfway = jnp.concatenate(
            [
                jnp.concatenate(
                    [
                        halfway[slot * PUPIL : (slot + 1) * PUPIL, :GRID],
                        halfway[slot * PUPIL : (slot + 1) * PUPIL, GRID:],
                    ],
                    0,
                )
                for slot in range(size)
            ],
            1,
        )
        rows_in = table_v[ROWS_IN, :]
        rows_in = jnp.concatenate([rows_in[:, : 2 * PUPIL], rows_in[:, 2 * PUPIL :]], 0)
        field = dot(rows_in, halfway)
        field_grad = jnp.concatenate(
            [
                (field[:, slot * GRID : (slot + 1) * GRID] * image[...]).astype(jnp.bfloat16)
                for slot in range(size)
            ],
            1,
        )
        back = dot(table_v[ROWS_OUT, :], field_grad).astype(jnp.bfloat16)
        back = jnp.concatenate(
            [
                jnp.concatenate(
                    [
                        back[:PUPIL, slot * GRID : (slot + 1) * GRID],
                        back[PUPIL:, slot * GRID : (slot + 1) * GRID],
                    ],
                    1,
                )
                for slot in range(size)
            ],
            0,
        )
        grad = dot(back, table_v[COLS_OUT, :])
        for slot in range(size):
            real, imag, factor = pupils[slot]
            grad_real = grad[slot * PUPIL : (slot + 1) * PUPIL, :BAND] * factor
            grad_imag = grad[slot * PUPIL : (slot + 1) * PUPIL, BAND:] * factor
            rows = pl.ds(starts[slot], PUPIL)
            band_real, band_imag = bands[slot % 2], bands[2 + slot % 2]
            band_real[rows, :] = band_real[rows, :] + (real * grad_real + imag * grad_imag)
            band_imag[rows, :] = band_imag[rows, :] + (real * grad_imag - imag * grad_real)

    largest, second = GROUPS[-1], GROUPS[-2]
    whole_groups = (total + largest - 1 - second) // largest

    def whole_group(step, carry):
        group(step * largest, largest)
        return carry

    lax.fori_loop(0, whole_groups, whole_group, jnp.int32(0))
    rest = total - whole_groups * largest
    for below, size in zip((0, *GROUPS), GROUPS[:-1]):

        @pl.when((rest > below) & (rest <= size))
        def _():
            group(whole_groups * largest, size)

    real = (bands[0][...] + bands[1][...]) * scale
    imag = (bands[2][...] + bands[3][...]) * scale
    left = jnp.concatenate(
        [jnp.concatenate([real, imag], 1), jnp.concatenate([imag, -real], 1)], 0
    ).astype(jnp.bfloat16)
    out_copy.wait()
    mixed = dot(out_v[...].astype(jnp.bfloat16), left).astype(jnp.bfloat16)
    col_copy.wait()
    width = result.shape[2] // PARTS
    copies = []
    for step in range(PARTS):
        part = pl.ds(step * width, width)
        result_v[:, part] = dot(mixed, col_v[:, part])
        copy = pltpu.make_async_copy(
            result_v.at[:, part], result.at[0, :, part], out_sems.at[step]
        )
        copy.start()
        copies.append(copy)
    for copy in copies:
        copy.wait()


def adjoint(own, other, own_lines, other_lines, pupil, table, col_table, out_table, n_src):
    portion = out_table.shape[1]
    columns = col_table.shape[1]
    band = pltpu.VMEM((BAND, BAND), jnp.float32)
    return pl.pallas_call(
        functools.partial(adjoint_kernel, n_src),
        out_shape=jax.ShapeDtypeStruct((1, portion, columns), jnp.float32),
        in_specs=[VMEM] * 5 + [HBM] * 3,
        out_specs=HBM,
        scratch_shapes=[
            band,
            band,
            pltpu.VMEM((2 * GRID, GRID), jnp.float32),
            pltpu.VMEM(table.shape, jnp.bfloat16),
            pltpu.VMEM(col_table.shape, jnp.bfloat16),
            pltpu.VMEM(out_table.shape[1:], jnp.float32),
            pltpu.VMEM((portion, columns), jnp.float32),
            pltpu.SMEM((2 * own_lines.shape[0], LANES), jnp.float32),
            pltpu.SMEM((2 * own_lines.shape[0] + GROUPS[-1],), jnp.int32),
            pltpu.SemaphoreType.DMA((5,)),
            pltpu.SemaphoreType.DMA((PARTS,)),
            band,
            band,
            band,
            band,
        ],
        compiler_params=pltpu.CompilerParams(vmem_limit_bytes=GRANT),
        cost_estimate=pl.CostEstimate(
            flops=2 * 128 * 4096 * 256, bytes_accessed=4 * 1024 * 1024, transcendentals=0
        ),
        name="adjoint",
    )(own, other, own_lines, other_lines, pupil, table, col_table, out_table)


def pupil_rows(phase):
    grid = 2 * np.arange(PUPIL) - PUPIL + 1
    inside = grid[:, None] ** 2 + grid[None, :] ** 2 <= PUPIL * PUPIL
    both = jnp.concatenate(
        [jnp.where(inside, jnp.cos(phase), 0.0), jnp.where(inside, jnp.sin(phase), 0.0)], 0
    )
    return jnp.pad(both, ((0, 0), (0, BAND - PUPIL)))


def swapped(array, sizes, steps):
    axes = tuple(sizes)
    places = np.arange(math.prod(sizes.values())).reshape(tuple(sizes.values()))
    there = places
    for dim, axis in enumerate(axes):
        there = np.take(there, np.arange(sizes[axis]) ^ steps.get(axis, 0), dim)
    turn = [(int(a), int(b)) for a, b in zip(places.ravel(), there.ravel())]
    return lax.ppermute(array, axes, turn)


def body(mask, cotangent, pupil_phase, source_weight, shift_table, source_ids, source_count):
    height, columns = mask.shape
    n_tile, n_src = lax.axis_size("tile"), lax.axis_size("src")
    col_table, row_table, out_table, out_cols = image_tables(columns, height, n_tile, n_src)
    sizes = {"src": n_src, "tile": n_tile}
    keep, send, zeros = forward(mask, cotangent, col_table, row_table)
    stay = [(place, place) for place in range(n_src)]
    count = lax.ppermute(source_count, "src", stay)
    ids = jnp.concatenate([source_ids, count[:, None]], 1) + zeros
    bit = 1
    while bit < n_src // 2:
        ids = jnp.concatenate([ids, swapped(ids, sizes, {"src": bit})], 0)
        bit *= 2
    own = keep + swapped(send, sizes, {"tile": 1})
    after = own[HALF : HALF + 1]
    ids = ids + after[:, : SLOTS + 1].astype(jnp.int32)
    shift = shift_table.T.reshape(2, -1, LANES).transpose(1, 0, 2).reshape(-1, LANES)
    own_lines = slot_lines(ids, shift, source_weight.reshape(-1, LANES))
    pupil = pupil_rows(pupil_phase + after[:, :PUPIL])
    other_lines = swapped(own_lines, sizes, {"src": bit})
    step = 2
    while step < n_tile:
        own = own + swapped(own, sizes, {"tile": step})
        step *= 2
    other = swapped(own, sizes, {"tile": 1})
    return adjoint(
        own, other, own_lines, other_lines, pupil, grid_tables(), out_cols, out_table, n_src
    )


def solution(mesh):
    placed = (
        P(("grp", "tile"), None),
        P(("grp", "tile"), None),
        P(),
        P(),
        P(),
        P(("grp", "src"), None),
        P(("grp", "src")),
    )
    return jax.shard_map(
        body, mesh=mesh, in_specs=placed, out_specs=P(("grp", "tile"), "src", None), check_vma=False
    )
```

```python
import functools
import math

import jax
import jax.numpy as jnp
import ml_dtypes
import numpy as np
from jax import lax
from jax.experimental import pallas as pl
from jax.experimental.pallas import tpu as pltpu
from jax.sharding import PartitionSpec as P

COLS = 2048
TILE_ROWS = 2048
BAND = 128
PUPIL = 64
SLOTS = 8
GRID = 128
CHUNKS = (1,) * 8
GROUPS = (16, 20, 24, 32)
OX, OY, FACTOR, COUNT = range(4)
PARTS = 4
LANES = 128
SUMS = 2 * BAND + GRID
HALF = SUMS // 2
ZEROS = 8
GRANT = 53 * 1024 * 1024

VMEM = pl.BlockSpec(memory_space=pltpu.VMEM)
SMEM = pl.BlockSpec(memory_space=pltpu.SMEM)
HBM = pl.BlockSpec(memory_space=pltpu.HBM)


def waves(positions, freqs, length):
    product = np.multiply.outer(positions, freqs) % length
    angle = product.astype(np.float64) * (2.0 * math.pi / length)
    return np.cos(angle), np.sin(angle)


def lowpass(positions, length):
    freqs = np.arange(1, PUPIL)
    step = length // GRID
    apart = np.arange(GRID)[None, :] * step - positions[:, None]
    product = (apart[:, :, None] * freqs) % length
    return (1.0 + 2.0 * np.cos(product * (2.0 * math.pi / length)).sum(2)) / GRID


def low(array):
    return np.ascontiguousarray(array).astype(ml_dtypes.bfloat16)


@functools.cache
def image_tables(columns, height, n_tile, n_src):
    band = np.arange(BAND) - BAND // 2
    cols = np.arange(columns)
    rows = np.arange(TILE_ROWS)
    cos, sin = waves(cols, band, columns)
    col_table = low(np.concatenate([cos, -sin, lowpass(cols, columns)], 1))
    cos, sin = waves(rows, band, TILE_ROWS)
    row_table = np.concatenate([cos, sin, lowpass(rows, TILE_ROWS)], 1)
    row_table = low(row_table.reshape(n_tile, height, 2 * BAND + GRID).transpose(0, 2, 1))
    portion = height // n_src
    out_table = np.concatenate([cos, -sin], 1).astype(np.float32)
    out_table = out_table.reshape(n_tile * n_src, portion, 2 * BAND)
    cos, sin = waves(cols, band, columns)
    return col_table, row_table, out_table, low(np.concatenate([cos, -sin], 1).T)


COLS_IN, COLS_OUT = slice(0, 2 * BAND), slice(2 * BAND, 2 * BAND + 2 * GRID)
ROWS_IN = slice(COLS_OUT.stop, COLS_OUT.stop + GRID)
ROWS_OUT = slice(ROWS_IN.stop, ROWS_IN.stop + 2 * PUPIL)


@functools.cache
def grid_tables():
    points = np.arange(GRID)
    band = np.arange(BAND) - BAND // 2
    cos, sin = waves(points, band, GRID)
    cols_in = np.block([[cos.T, sin.T], [-sin.T, cos.T]])
    cols_out = np.block([[cos, -sin], [sin, cos]])
    cos, sin = waves(points, np.arange(PUPIL) - PUPIL // 2, GRID)
    rows_in = np.block([[cos, -sin, sin, cos]])
    rows_out = np.block([[cos.T, sin.T], [-sin.T, cos.T]])
    return low(np.concatenate([cols_in, cols_out, rows_in, rows_out], 0))


def dot(left, right):
    return jnp.dot(left, right, preferred_element_type=jnp.float32)


def forward_kernel(
    mask, cotangent, col_table, row_table,
    keep, send, zeros,
    halves, mask_v, cot_v, col_v, row_v, sems,
):
    columns = mask.shape[1]
    ends = np.cumsum(CHUNKS) * (columns // sum(CHUNKS))
    parts = [pl.ds(int(low), int(high - low)) for low, high in zip([0, *ends], ends)]
    tile = lax.axis_index("tile")
    chunk_copies = []
    for step, part in enumerate(parts):
        copies = [
            pltpu.make_async_copy(col_table.at[part, :], col_v.at[part, :], sems.at[step, 0]),
            pltpu.make_async_copy(mask.at[:, part], mask_v.at[:, part], sems.at[step, 1]),
            pltpu.make_async_copy(cotangent.at[:, part], cot_v.at[:, part], sems.at[step, 2]),
        ]
        for copy in copies:
            copy.start()
        chunk_copies.append(copies)
    row_copy = pltpu.make_async_copy(row_table.at[tile], row_v, sems.at[len(CHUNKS), 0])
    row_copy.start()

    for step, part in enumerate(parts):
        for copy in chunk_copies[step]:
            copy.wait()
        mask_add = dot(mask_v[:, part], col_v[part, : 2 * BAND])
        cot_add = dot(cot_v[:, part], col_v[part, 2 * BAND :])
        mask_part = mask_add if step == 0 else mask_part + mask_add
        cot_part = cot_add if step == 0 else cot_part + cot_add

    row_copy.wait()
    blocks = dot(row_v[: 2 * BAND, :], mask_part.astype(jnp.bfloat16))
    image = dot(row_v[2 * BAND :, :], cot_part.astype(jnp.bfloat16))
    sums = jnp.concatenate(
        [
            blocks[:BAND, :BAND] + blocks[BAND:, BAND:],
            blocks[:BAND, BAND:] - blocks[BAND:, :BAND],
            image,
        ],
        0,
    )
    rest = jnp.zeros((ZEROS, BAND), jnp.float32)
    for half in range(2):
        halves[half] = jnp.concatenate([sums[half * HALF : (half + 1) * HALF], rest], 0)
    own_half = tile % 2
    keep[...] = halves[own_half]
    send[...] = halves[1 - own_half]
    zeros[...] = jnp.zeros_like(zeros)


def forward(mask, cotangent, col_table, row_table):
    height, columns = mask.shape
    return pl.pallas_call(
        forward_kernel,
        out_shape=(
            jax.ShapeDtypeStruct((HALF + ZEROS, BAND), jnp.float32),
            jax.ShapeDtypeStruct((HALF + ZEROS, BAND), jnp.float32),
            jax.ShapeDtypeStruct((1, SLOTS + 1), jnp.int32),
        ),
        in_specs=[HBM] * 4,
        out_specs=(VMEM, VMEM, VMEM),
        scratch_shapes=[
            pltpu.VMEM((2, HALF + ZEROS, BAND), jnp.float32),
            pltpu.VMEM(mask.shape, jnp.bfloat16),
            pltpu.VMEM(mask.shape, jnp.bfloat16),
            pltpu.VMEM(col_table.shape, jnp.bfloat16),
            pltpu.VMEM(row_table.shape[1:], jnp.bfloat16),
            pltpu.SemaphoreType.DMA((len(CHUNKS) + 1, 3)),
        ],
        compiler_params=pltpu.CompilerParams(vmem_limit_bytes=GRANT),
        cost_estimate=pl.CostEstimate(
            flops=2 * height * columns * SUMS, bytes_accessed=6 * 1024 * 1024, transcendentals=0
        ),
        name="forward",
    )(mask, cotangent, col_table, row_table)


def lines_kernel(ids, shift, weight, lines):
    blocks = weight.shape[0]
    count = ids.shape[0] * SLOTS
    slot = lax.broadcasted_iota(jnp.int32, (SLOTS, SLOTS + 1), 0)
    column = lax.broadcasted_iota(jnp.int32, (SLOTS, SLOTS + 1), 1)
    sources, counts, used = [], [], []
    for row in range(ids.shape[0]):
        entries = jnp.broadcast_to(ids[row : row + 1, :].astype(jnp.float32), slot.shape)
        sources.append(jnp.sum(jnp.where(slot == column, entries, 0.0), 1, keepdims=True))
        counts.append(jnp.sum(jnp.where(column == SLOTS, entries, 0.0), 1, keepdims=True))
        used.append(jnp.where(slot[:, :1].astype(jnp.float32) < counts[-1], 1.0, 0.0))
    sources, counts, used = (jnp.concatenate(part, 0) for part in (sources, counts, used))
    block = jnp.floor(sources * (1.0 / LANES))

    def row_of(table, index, precision):
        lane = lax.broadcasted_iota(jnp.int32, (count, table.shape[0]), 1).astype(jnp.float32)
        pick = jnp.where(lane == index, 1.0, 0.0).astype(table.dtype)
        return jnp.dot(pick, table, precision=precision, preferred_element_type=jnp.float32)

    lane = lax.broadcasted_iota(jnp.int32, (count, LANES), 1)
    here = lane.astype(jnp.float32) == sources - block * LANES
    offsets = shift[...].astype(jnp.bfloat16)
    line = jnp.zeros((count, LANES), jnp.float32)
    for entry, found in (
        (OX, row_of(offsets, 2.0 * block, None)),
        (OY, row_of(offsets, 2.0 * block + 1.0, None)),
        (FACTOR, row_of(weight[...], block, lax.Precision.HIGHEST)),
    ):
        found = jnp.sum(jnp.where(here, found, 0.0), 1, keepdims=True) * used
        line = jnp.where(lane == entry, found, line)
    line = jnp.where(lane == FACTOR, line * (2.0 / SLOTS / PUPIL / PUPIL), line)
    lines[...] = jnp.where(lane == COUNT, counts, line)


def slot_lines(ids, shift, weight):
    count = ids.shape[0] * SLOTS
    return pl.pallas_call(
        lines_kernel,
        out_shape=jax.ShapeDtypeStruct((count, LANES), jnp.float32),
        in_specs=[VMEM, VMEM, VMEM],
        out_specs=VMEM,
        compiler_params=pltpu.CompilerParams(vmem_limit_bytes=2 * 1024 * 1024),
        cost_estimate=pl.CostEstimate(flops=1, bytes_accessed=1, transcendentals=0),
        name="slot_lines",
    )(ids, shift, weight)


def adjoint_kernel(
    n_src, own, other, own_lines, other_lines, pupil, table, col_table, out_table,
    result,
    spec_real, spec_imag, image, table_v, col_v, out_v, result_v, lines, used, sems, out_sems, *bands,
):
    place = lax.axis_index("tile") * n_src + lax.axis_index("src")
    grid_copy = pltpu.make_async_copy(table, table_v, sems.at[0])
    out_copy = pltpu.make_async_copy(out_table.at[place], out_v, sems.at[1])
    col_copy = pltpu.make_async_copy(col_table, col_v, sems.at[2])
    half = own_lines.shape[0]
    for copy in (grid_copy, out_copy, col_copy):
        copy.start()

    scale = 1.0 / math.sqrt(TILE_ROWS * COLS)
    first = lax.axis_index("tile") % 2 == 0
    own_half, other_half = own[:HALF, :], other[:HALF, :]
    whole = jnp.concatenate(
        [jnp.where(first, own_half, other_half), jnp.where(first, other_half, own_half)], 0
    )
    spec = (whole[: 2 * BAND] * scale).astype(jnp.bfloat16).astype(jnp.float32)
    spec_real[...] = spec[:BAND]
    spec_imag[...] = spec[BAND:]
    image[:GRID, :] = whole[2 * BAND :]
    image[GRID:, :] = whole[2 * BAND :]
    for band in bands:
        band[...] = jnp.zeros_like(band)
    for slot in range(2 * half + GROUPS[-1]):
        used[slot] = jnp.int32(0)
    for part, source in enumerate((own_lines, other_lines)):
        for slot in range(half):
            line = source[slot : slot + 1, :]
            for entry in (OX, OY, FACTOR, COUNT) if slot % SLOTS == 0 else (OX, OY, FACTOR):
                lines[part * half + slot, entry] = line[0, entry]

    def add(block, total):
        first = block * SLOTS
        for slot in range(SLOTS):
            used[total + slot] = first + slot
        return total + lines[first, COUNT].astype(jnp.int32)

    blocks = 2 * half // SLOTS
    total = lax.fori_loop(0, blocks, add, jnp.int32(0), unroll=blocks <= 8)
    grid_copy.wait()

    def group(first, size):
        starts, pupils, amplitudes = [], [], []
        for slot in range(size):
            place = first + slot
            index = used[place]
            factor = jnp.where(place < total, lines[index, FACTOR], 0.0)
            offset_x = lines[index, OX].astype(jnp.int32)
            offset_y = lines[index, OY].astype(jnp.int32)
            real = pltpu.roll(pupil[:PUPIL, :], offset_x, 1)
            imag = pltpu.roll(pupil[PUPIL:, :], offset_x, 1)
            rows = pl.ds(offset_y, PUPIL)
            amp_real = real * spec_real[rows, :] - imag * spec_imag[rows, :]
            amp_imag = real * spec_imag[rows, :] + imag * spec_real[rows, :]
            starts.append(offset_y)
            pupils.append((real, imag, factor))
            amplitudes.append(jnp.concatenate([amp_real, amp_imag], 1).astype(jnp.bfloat16))
        halfway = dot(jnp.concatenate(amplitudes, 0), table_v[COLS_IN, :]).astype(jnp.bfloat16)
        halfway = jnp.concatenate(
            [
                jnp.concatenate(
                    [
                        halfway[slot * PUPIL : (slot + 1) * PUPIL, :GRID],
                        halfway[slot * PUPIL : (slot + 1) * PUPIL, GRID:],
                    ],
                    0,
                )
                for slot in range(size)
            ],
            1,
        )
        rows_in = table_v[ROWS_IN, :]
        rows_in = jnp.concatenate([rows_in[:, : 2 * PUPIL], rows_in[:, 2 * PUPIL :]], 0)
        field = dot(rows_in, halfway)
        field_grad = jnp.concatenate(
            [
                (field[:, slot * GRID : (slot + 1) * GRID] * image[...]).astype(jnp.bfloat16)
                for slot in range(size)
            ],
            1,
        )
        back = dot(table_v[ROWS_OUT, :], field_grad).astype(jnp.bfloat16)
        back = jnp.concatenate(
            [
                jnp.concatenate(
                    [
                        back[:PUPIL, slot * GRID : (slot + 1) * GRID],
                        back[PUPIL:, slot * GRID : (slot + 1) * GRID],
                    ],
                    1,
                )
                for slot in range(size)
            ],
            0,
        )
        grad = dot(back, table_v[COLS_OUT, :])
        for slot in range(size):
            real, imag, factor = pupils[slot]
            grad_real = grad[slot * PUPIL : (slot + 1) * PUPIL, :BAND] * factor
            grad_imag = grad[slot * PUPIL : (slot + 1) * PUPIL, BAND:] * factor
            rows = pl.ds(starts[slot], PUPIL)
            band_real, band_imag = bands[slot % 2], bands[2 + slot % 2]
            band_real[rows, :] = band_real[rows, :] + (real * grad_real + imag * grad_imag)
            band_imag[rows, :] = band_imag[rows, :] + (real * grad_imag - imag * grad_real)

    largest, second = GROUPS[-1], GROUPS[-2]
    whole_groups = (total + largest - 1 - second) // largest

    def whole_group(step, carry):
        group(step * largest, largest)
        return carry

    lax.fori_loop(0, whole_groups, whole_group, jnp.int32(0))
    rest = total - whole_groups * largest
    for below, size in zip((0, *GROUPS), GROUPS[:-1]):

        @pl.when((rest > below) & (rest <= size))
        def _():
            group(whole_groups * largest, size)

    real = (bands[0][...] + bands[1][...]) * scale
    imag = (bands[2][...] + bands[3][...]) * scale
    left = jnp.concatenate(
        [jnp.concatenate([real, imag], 1), jnp.concatenate([imag, -real], 1)], 0
    ).astype(jnp.bfloat16)
    out_copy.wait()
    mixed = dot(out_v[...].astype(jnp.bfloat16), left).astype(jnp.bfloat16)
    col_copy.wait()
    width = result.shape[2] // PARTS
    copies = []
    for step in range(PARTS):
        part = pl.ds(step * width, width)
        result_v[:, part] = dot(mixed, col_v[:, part])
        copy = pltpu.make_async_copy(
            result_v.at[:, part], result.at[0, :, part], out_sems.at[step]
        )
        copy.start()
        copies.append(copy)
    for copy in copies:
        copy.wait()


def adjoint(own, other, own_lines, other_lines, pupil, table, col_table, out_table, n_src):
    portion = out_table.shape[1]
    columns = col_table.shape[1]
    band = pltpu.VMEM((BAND, BAND), jnp.float32)
    return pl.pallas_call(
        functools.partial(adjoint_kernel, n_src),
        out_shape=jax.ShapeDtypeStruct((1, portion, columns), jnp.float32),
        in_specs=[VMEM] * 5 + [HBM] * 3,
        out_specs=HBM,
        scratch_shapes=[
            band,
            band,
            pltpu.VMEM((2 * GRID, GRID), jnp.float32),
            pltpu.VMEM(table.shape, jnp.bfloat16),
            pltpu.VMEM(col_table.shape, jnp.bfloat16),
            pltpu.VMEM(out_table.shape[1:], jnp.float32),
            pltpu.VMEM((portion, columns), jnp.float32),
            pltpu.SMEM((2 * own_lines.shape[0], LANES), jnp.float32),
            pltpu.SMEM((2 * own_lines.shape[0] + GROUPS[-1],), jnp.int32),
            pltpu.SemaphoreType.DMA((5,)),
            pltpu.SemaphoreType.DMA((PARTS,)),
            band,
            band,
            band,
            band,
        ],
        compiler_params=pltpu.CompilerParams(vmem_limit_bytes=GRANT),
        cost_estimate=pl.CostEstimate(
            flops=2 * 128 * 4096 * 256, bytes_accessed=4 * 1024 * 1024, transcendentals=0
        ),
        name="adjoint",
    )(own, other, own_lines, other_lines, pupil, table, col_table, out_table)


def pupil_rows(phase):
    grid = 2 * np.arange(PUPIL) - PUPIL + 1
    inside = grid[:, None] ** 2 + grid[None, :] ** 2 <= PUPIL * PUPIL
    both = jnp.concatenate(
        [jnp.where(inside, jnp.cos(phase), 0.0), jnp.where(inside, jnp.sin(phase), 0.0)], 0
    )
    return jnp.pad(both, ((0, 0), (0, BAND - PUPIL)))


def swapped(array, sizes, steps):
    axes = tuple(sizes)
    places = np.arange(math.prod(sizes.values())).reshape(tuple(sizes.values()))
    there = places
    for dim, axis in enumerate(axes):
        there = np.take(there, np.arange(sizes[axis]) ^ steps.get(axis, 0), dim)
    turn = [(int(a), int(b)) for a, b in zip(places.ravel(), there.ravel())]
    return lax.ppermute(array, axes, turn)


def body(mask, cotangent, pupil_phase, source_weight, shift_table, source_ids, source_count):
    height, columns = mask.shape
    n_tile, n_src = lax.axis_size("tile"), lax.axis_size("src")
    col_table, row_table, out_table, out_cols = image_tables(columns, height, n_tile, n_src)
    sizes = {"src": n_src, "tile": n_tile}
    keep, send, zeros = forward(mask, cotangent, col_table, row_table)
    ids = jnp.concatenate([source_ids, source_count[:, None]], 1) + zeros
    bit = 1
    while bit < n_src // 2:
        ids = jnp.concatenate([ids, swapped(ids, sizes, {"src": bit})], 0)
        bit *= 2
    own = keep + swapped(send, sizes, {"tile": 1})
    after = own[HALF : HALF + 1]
    ids = ids + after[:, : SLOTS + 1].astype(jnp.int32)
    shift = shift_table.T.reshape(2, -1, LANES).transpose(1, 0, 2).reshape(-1, LANES)
    own_lines = slot_lines(ids, shift, source_weight.reshape(-1, LANES))
    pupil = pupil_rows(pupil_phase + after[:, :PUPIL])
    other_lines = swapped(own_lines, sizes, {"src": bit})
    step = 2
    while step < n_tile:
        own = own + swapped(own, sizes, {"tile": step})
        step *= 2
    other = swapped(own, sizes, {"tile": 1})
    return adjoint(
        own, other, own_lines, other_lines, pupil, grid_tables(), out_cols, out_table, n_src
    )


def solution(mesh):
    placed = (
        P(("grp", "tile"), None),
        P(("grp", "tile"), None),
        P(),
        P(),
        P(),
        P(("grp", "src"), None),
        P(("grp", "src")),
    )
    return jax.shard_map(
        body, mesh=mesh, in_specs=placed, out_specs=P(("grp", "tile"), "src", None), check_vma=False
    )
```

```python
import functools
import math

import jax
import jax.numpy as jnp
import ml_dtypes
import numpy as np
from jax import lax
from jax.experimental import pallas as pl
from jax.experimental.pallas import tpu as pltpu
from jax.sharding import PartitionSpec as P

COLS = 2048
TILE_ROWS = 2048
BAND = 128
PUPIL = 64
SLOTS = 8
GRID = 128
CHUNKS = (1,) * 8
GROUPS = (16, 20, 24, 32)
OX, OY, FACTOR, COUNT = range(4)
PARTS = 4
LANES = 128
SUMS = 2 * BAND + GRID
HALF = SUMS // 2
ZEROS = 8
GRANT = 53 * 1024 * 1024

VMEM = pl.BlockSpec(memory_space=pltpu.VMEM)
SMEM = pl.BlockSpec(memory_space=pltpu.SMEM)
HBM = pl.BlockSpec(memory_space=pltpu.HBM)


def waves(positions, freqs, length):
    product = np.multiply.outer(positions, freqs) % length
    angle = product.astype(np.float64) * (2.0 * math.pi / length)
    return np.cos(angle), np.sin(angle)


def lowpass(positions, length):
    freqs = np.arange(1, PUPIL)
    step = length // GRID
    apart = np.arange(GRID)[None, :] * step - positions[:, None]
    product = (apart[:, :, None] * freqs) % length
    return (1.0 + 2.0 * np.cos(product * (2.0 * math.pi / length)).sum(2)) / GRID


def low(array):
    return np.ascontiguousarray(array).astype(ml_dtypes.bfloat16)


@functools.cache
def image_tables(columns, height, n_tile, n_src):
    band = np.arange(BAND) - BAND // 2
    cols = np.arange(columns)
    rows = np.arange(TILE_ROWS)
    cos, sin = waves(cols, band, columns)
    col_table = low(np.concatenate([cos, -sin, lowpass(cols, columns)], 1))
    cos, sin = waves(rows, band, TILE_ROWS)
    row_table = np.concatenate([cos, sin, lowpass(rows, TILE_ROWS)], 1)
    row_table = low(row_table.reshape(n_tile, height, 2 * BAND + GRID).transpose(0, 2, 1))
    portion = height // n_src
    out_table = np.concatenate([cos, -sin], 1).astype(np.float32)
    out_table = out_table.reshape(n_tile * n_src, portion, 2 * BAND)
    cos, sin = waves(cols, band, columns)
    return col_table, row_table, out_table, low(np.concatenate([cos, -sin], 1).T)


COLS_IN, COLS_OUT = slice(0, 2 * BAND), slice(2 * BAND, 2 * BAND + 2 * GRID)
ROWS_IN = slice(COLS_OUT.stop, COLS_OUT.stop + GRID)
ROWS_OUT = slice(ROWS_IN.stop, ROWS_IN.stop + 2 * PUPIL)


@functools.cache
def grid_tables():
    points = np.arange(GRID)
    band = np.arange(BAND) - BAND // 2
    cos, sin = waves(points, band, GRID)
    cols_in = np.block([[cos.T, sin.T], [-sin.T, cos.T]])
    cols_out = np.block([[cos, -sin], [sin, cos]])
    cos, sin = waves(points, np.arange(PUPIL) - PUPIL // 2, GRID)
    rows_in = np.block([[cos, -sin, sin, cos]])
    rows_out = np.block([[cos.T, sin.T], [-sin.T, cos.T]])
    return low(np.concatenate([cols_in, cols_out, rows_in, rows_out], 0))


def dot(left, right):
    return jnp.dot(left, right, preferred_element_type=jnp.float32)


def forward_kernel(
    mask, cotangent, col_table, row_table,
    keep, send, zeros,
    halves, mask_v, cot_v, col_v, row_v, sems,
):
    columns = mask.shape[1]
    ends = np.cumsum(CHUNKS) * (columns // sum(CHUNKS))
    parts = [pl.ds(int(low), int(high - low)) for low, high in zip([0, *ends], ends)]
    tile = lax.axis_index("tile")
    chunk_copies = []
    for step, part in enumerate(parts):
        copies = [
            pltpu.make_async_copy(col_table.at[part, :], col_v.at[part, :], sems.at[step, 0]),
            pltpu.make_async_copy(mask.at[:, part], mask_v.at[:, part], sems.at[step, 1]),
            pltpu.make_async_copy(cotangent.at[:, part], cot_v.at[:, part], sems.at[step, 2]),
        ]
        for copy in copies:
            copy.start()
        chunk_copies.append(copies)
    row_copy = pltpu.make_async_copy(row_table.at[tile], row_v, sems.at[len(CHUNKS), 0])
    row_copy.start()

    for step, part in enumerate(parts):
        for copy in chunk_copies[step]:
            copy.wait()
        mask_add = dot(mask_v[:, part], col_v[part, : 2 * BAND])
        cot_add = dot(cot_v[:, part], col_v[part, 2 * BAND :])
        mask_part = mask_add if step == 0 else mask_part + mask_add
        cot_part = cot_add if step == 0 else cot_part + cot_add

    row_copy.wait()
    blocks = dot(row_v[: 2 * BAND, :], mask_part.astype(jnp.bfloat16))
    image = dot(row_v[2 * BAND :, :], cot_part.astype(jnp.bfloat16))
    sums = jnp.concatenate(
        [
            blocks[:BAND, :BAND] + blocks[BAND:, BAND:],
            blocks[:BAND, BAND:] - blocks[BAND:, :BAND],
            image,
        ],
        0,
    )
    rest = jnp.zeros((ZEROS, BAND), jnp.float32)
    for half in range(2):
        halves[half] = jnp.concatenate([sums[half * HALF : (half + 1) * HALF], rest], 0)
    own_half = tile % 2
    keep[...] = halves[own_half]
    send[...] = halves[1 - own_half]
    zeros[...] = jnp.zeros_like(zeros)


def forward(mask, cotangent, col_table, row_table):
    height, columns = mask.shape
    return pl.pallas_call(
        forward_kernel,
        out_shape=(
            jax.ShapeDtypeStruct((HALF + ZEROS, BAND), jnp.float32),
            jax.ShapeDtypeStruct((HALF + ZEROS, BAND), jnp.float32),
            jax.ShapeDtypeStruct((1, SLOTS + 1), jnp.int32),
        ),
        in_specs=[HBM] * 4,
        out_specs=(VMEM, VMEM, VMEM),
        scratch_shapes=[
            pltpu.VMEM((2, HALF + ZEROS, BAND), jnp.float32),
            pltpu.VMEM(mask.shape, jnp.bfloat16),
            pltpu.VMEM(mask.shape, jnp.bfloat16),
            pltpu.VMEM(col_table.shape, jnp.bfloat16),
            pltpu.VMEM(row_table.shape[1:], jnp.bfloat16),
            pltpu.SemaphoreType.DMA((len(CHUNKS) + 1, 3)),
        ],
        compiler_params=pltpu.CompilerParams(vmem_limit_bytes=GRANT),
        cost_estimate=pl.CostEstimate(
            flops=2 * height * columns * SUMS, bytes_accessed=6 * 1024 * 1024, transcendentals=0
        ),
        name="forward",
    )(mask, cotangent, col_table, row_table)


def lines_kernel(ids, shift, weight, lines):
    blocks = weight.shape[0]
    count = ids.shape[0] * SLOTS
    slot = lax.broadcasted_iota(jnp.int32, (SLOTS, SLOTS + 1), 0)
    column = lax.broadcasted_iota(jnp.int32, (SLOTS, SLOTS + 1), 1)
    sources, counts, used = [], [], []
    for row in range(ids.shape[0]):
        entries = jnp.broadcast_to(ids[row : row + 1, :].astype(jnp.float32), slot.shape)
        sources.append(jnp.sum(jnp.where(slot == column, entries, 0.0), 1, keepdims=True))
        counts.append(jnp.sum(jnp.where(column == SLOTS, entries, 0.0), 1, keepdims=True))
        used.append(jnp.where(slot[:, :1].astype(jnp.float32) < counts[-1], 1.0, 0.0))
    sources, counts, used = (jnp.concatenate(part, 0) for part in (sources, counts, used))
    block = jnp.floor(sources * (1.0 / LANES))

    def row_of(table, index, precision):
        lane = lax.broadcasted_iota(jnp.int32, (count, table.shape[0]), 1).astype(jnp.float32)
        pick = jnp.where(lane == index, 1.0, 0.0).astype(table.dtype)
        return jnp.dot(pick, table, precision=precision, preferred_element_type=jnp.float32)

    lane = lax.broadcasted_iota(jnp.int32, (count, LANES), 1)
    here = lane.astype(jnp.float32) == sources - block * LANES
    offsets = shift[...].astype(jnp.bfloat16)
    line = jnp.zeros((count, LANES), jnp.float32)
    for entry, found in (
        (OX, row_of(offsets, 2.0 * block, None)),
        (OY, row_of(offsets, 2.0 * block + 1.0, None)),
        (FACTOR, row_of(weight[...], block, lax.Precision.HIGHEST)),
    ):
        found = jnp.sum(jnp.where(here, found, 0.0), 1, keepdims=True) * used
        line = jnp.where(lane == entry, found, line)
    line = jnp.where(lane == FACTOR, line * (2.0 / SLOTS / PUPIL / PUPIL), line)
    lines[...] = jnp.where(lane == COUNT, counts, line)


def slot_lines(ids, shift, weight):
    count = ids.shape[0] * SLOTS
    return pl.pallas_call(
        lines_kernel,
        out_shape=jax.ShapeDtypeStruct((count, LANES), jnp.float32),
        in_specs=[VMEM, VMEM, VMEM],
        out_specs=VMEM,
        compiler_params=pltpu.CompilerParams(vmem_limit_bytes=2 * 1024 * 1024),
        cost_estimate=pl.CostEstimate(flops=1, bytes_accessed=1, transcendentals=0),
        name="slot_lines",
    )(ids, shift, weight)


def adjoint_kernel(
    n_src, own, other, own_lines, other_lines, pupil, table, col_table, out_table,
    result,
    spec_real, spec_imag, image, col_v, out_v, result_v, lines, used, sems, out_sems, *bands,
):
    place = lax.axis_index("tile") * n_src + lax.axis_index("src")
    out_copy = pltpu.make_async_copy(out_table.at[place], out_v, sems.at[0])
    col_copy = pltpu.make_async_copy(col_table, col_v, sems.at[1])
    half = own_lines.shape[0]
    for copy in (out_copy, col_copy):
        copy.start()

    scale = 1.0 / math.sqrt(TILE_ROWS * COLS)
    first = lax.axis_index("tile") % 2 == 0
    own_half, other_half = own[:HALF, :], other[:HALF, :]
    whole = jnp.concatenate(
        [jnp.where(first, own_half, other_half), jnp.where(first, other_half, own_half)], 0
    )
    spec = (whole[: 2 * BAND] * scale).astype(jnp.bfloat16).astype(jnp.float32)
    spec_real[...] = spec[:BAND]
    spec_imag[...] = spec[BAND:]
    image[:GRID, :] = whole[2 * BAND :]
    image[GRID:, :] = whole[2 * BAND :]
    for band in bands:
        band[...] = jnp.zeros_like(band)
    for slot in range(2 * half + GROUPS[-1]):
        used[slot] = jnp.int32(0)
    for part, source in enumerate((own_lines, other_lines)):
        for slot in range(half):
            line = source[slot : slot + 1, :]
            for entry in (OX, OY, FACTOR, COUNT) if slot % SLOTS == 0 else (OX, OY, FACTOR):
                lines[part * half + slot, entry] = line[0, entry]

    def add(block, total):
        first = block * SLOTS
        for slot in range(SLOTS):
            used[total + slot] = first + slot
        return total + lines[first, COUNT].astype(jnp.int32)

    blocks = 2 * half // SLOTS
    total = lax.fori_loop(0, blocks, add, jnp.int32(0), unroll=blocks <= 8)

    def group(first, size):
        starts, pupils, amplitudes = [], [], []
        for slot in range(size):
            place = first + slot
            index = used[place]
            factor = jnp.where(place < total, lines[index, FACTOR], 0.0)
            offset_x = lines[index, OX].astype(jnp.int32)
            offset_y = lines[index, OY].astype(jnp.int32)
            real = pltpu.roll(pupil[:PUPIL, :], offset_x, 1)
            imag = pltpu.roll(pupil[PUPIL:, :], offset_x, 1)
            rows = pl.ds(offset_y, PUPIL)
            amp_real = real * spec_real[rows, :] - imag * spec_imag[rows, :]
            amp_imag = real * spec_imag[rows, :] + imag * spec_real[rows, :]
            starts.append(offset_y)
            pupils.append((real, imag, factor))
            amplitudes.append(jnp.concatenate([amp_real, amp_imag], 1).astype(jnp.bfloat16))
        halfway = dot(jnp.concatenate(amplitudes, 0), table[COLS_IN, :]).astype(jnp.bfloat16)
        halfway = jnp.concatenate(
            [
                jnp.concatenate(
                    [
                        halfway[slot * PUPIL : (slot + 1) * PUPIL, :GRID],
                        halfway[slot * PUPIL : (slot + 1) * PUPIL, GRID:],
                    ],
                    0,
                )
                for slot in range(size)
            ],
            1,
        )
        rows_in = table[ROWS_IN, :]
        rows_in = jnp.concatenate([rows_in[:, : 2 * PUPIL], rows_in[:, 2 * PUPIL :]], 0)
        field = dot(rows_in, halfway)
        field_grad = jnp.concatenate(
            [
                (field[:, slot * GRID : (slot + 1) * GRID] * image[...]).astype(jnp.bfloat16)
                for slot in range(size)
            ],
            1,
        )
        back = dot(table[ROWS_OUT, :], field_grad).astype(jnp.bfloat16)
        back = jnp.concatenate(
            [
                jnp.concatenate(
                    [
                        back[:PUPIL, slot * GRID : (slot + 1) * GRID],
                        back[PUPIL:, slot * GRID : (slot + 1) * GRID],
                    ],
                    1,
                )
                for slot in range(size)
            ],
            0,
        )
        grad = dot(back, table[COLS_OUT, :])
        for slot in range(size):
            real, imag, factor = pupils[slot]
            grad_real = grad[slot * PUPIL : (slot + 1) * PUPIL, :BAND] * factor
            grad_imag = grad[slot * PUPIL : (slot + 1) * PUPIL, BAND:] * factor
            rows = pl.ds(starts[slot], PUPIL)
            band_real, band_imag = bands[slot % 2], bands[2 + slot % 2]
            band_real[rows, :] = band_real[rows, :] + (real * grad_real + imag * grad_imag)
            band_imag[rows, :] = band_imag[rows, :] + (real * grad_imag - imag * grad_real)

    largest, second = GROUPS[-1], GROUPS[-2]
    whole_groups = (total + largest - 1 - second) // largest

    def whole_group(step, carry):
        group(step * largest, largest)
        return carry

    lax.fori_loop(0, whole_groups, whole_group, jnp.int32(0))
    rest = total - whole_groups * largest
    for below, size in zip((0, *GROUPS), GROUPS[:-1]):

        @pl.when((rest > below) & (rest <= size))
        def _():
            group(whole_groups * largest, size)

    real = (bands[0][...] + bands[1][...]) * scale
    imag = (bands[2][...] + bands[3][...]) * scale
    left = jnp.concatenate(
        [jnp.concatenate([real, imag], 1), jnp.concatenate([imag, -real], 1)], 0
    ).astype(jnp.bfloat16)
    out_copy.wait()
    mixed = dot(out_v[...].astype(jnp.bfloat16), left).astype(jnp.bfloat16)
    col_copy.wait()
    width = result.shape[2] // PARTS
    copies = []
    for step in range(PARTS):
        part = pl.ds(step * width, width)
        result_v[:, part] = dot(mixed, col_v[:, part])
        copy = pltpu.make_async_copy(
            result_v.at[:, part], result.at[0, :, part], out_sems.at[step]
        )
        copy.start()
        copies.append(copy)
    for copy in copies:
        copy.wait()


def adjoint(own, other, own_lines, other_lines, pupil, table, col_table, out_table, n_src):
    portion = out_table.shape[1]
    columns = col_table.shape[1]
    band = pltpu.VMEM((BAND, BAND), jnp.float32)
    return pl.pallas_call(
        functools.partial(adjoint_kernel, n_src),
        out_shape=jax.ShapeDtypeStruct((1, portion, columns), jnp.float32),
        in_specs=[VMEM] * 6 + [HBM] * 2,
        out_specs=HBM,
        scratch_shapes=[
            band,
            band,
            pltpu.VMEM((2 * GRID, GRID), jnp.float32),
            pltpu.VMEM(col_table.shape, jnp.bfloat16),
            pltpu.VMEM(out_table.shape[1:], jnp.float32),
            pltpu.VMEM((portion, columns), jnp.float32),
            pltpu.SMEM((2 * own_lines.shape[0], LANES), jnp.float32),
            pltpu.SMEM((2 * own_lines.shape[0] + GROUPS[-1],), jnp.int32),
            pltpu.SemaphoreType.DMA((2,)),
            pltpu.SemaphoreType.DMA((PARTS,)),
            band,
            band,
            band,
            band,
        ],
        compiler_params=pltpu.CompilerParams(vmem_limit_bytes=GRANT),
        cost_estimate=pl.CostEstimate(
            flops=2 * 128 * 4096 * 256, bytes_accessed=4 * 1024 * 1024, transcendentals=0
        ),
        name="adjoint",
    )(own, other, own_lines, other_lines, pupil, table, col_table, out_table)


def pupil_rows(phase):
    grid = 2 * np.arange(PUPIL) - PUPIL + 1
    inside = grid[:, None] ** 2 + grid[None, :] ** 2 <= PUPIL * PUPIL
    both = jnp.concatenate(
        [jnp.where(inside, jnp.cos(phase), 0.0), jnp.where(inside, jnp.sin(phase), 0.0)], 0
    )
    return jnp.pad(both, ((0, 0), (0, BAND - PUPIL)))


def swapped(array, sizes, steps):
    axes = tuple(sizes)
    places = np.arange(math.prod(sizes.values())).reshape(tuple(sizes.values()))
    there = places
    for dim, axis in enumerate(axes):
        there = np.take(there, np.arange(sizes[axis]) ^ steps.get(axis, 0), dim)
    turn = [(int(a), int(b)) for a, b in zip(places.ravel(), there.ravel())]
    return lax.ppermute(array, axes, turn)


def body(mask, cotangent, pupil_phase, source_weight, shift_table, source_ids, source_count):
    height, columns = mask.shape
    n_tile, n_src = lax.axis_size("tile"), lax.axis_size("src")
    col_table, row_table, out_table, out_cols = image_tables(columns, height, n_tile, n_src)
    sizes = {"src": n_src, "tile": n_tile}
    keep, send, zeros = forward(mask, cotangent, col_table, row_table)
    ids = jnp.concatenate([source_ids, source_count[:, None]], 1) + zeros
    bit = 1
    while bit < n_src // 2:
        ids = jnp.concatenate([ids, swapped(ids, sizes, {"src": bit})], 0)
        bit *= 2
    own = keep + swapped(send, sizes, {"tile": 1})
    after = own[HALF : HALF + 1]
    ids = ids + after[:, : SLOTS + 1].astype(jnp.int32)
    shift = shift_table.T.reshape(2, -1, LANES).transpose(1, 0, 2).reshape(-1, LANES)
    own_lines = slot_lines(ids, shift, source_weight.reshape(-1, LANES))
    pupil = pupil_rows(pupil_phase + after[:, :PUPIL])
    other_lines = swapped(own_lines, sizes, {"src": bit})
    step = 2
    while step < n_tile:
        own = own + swapped(own, sizes, {"tile": step})
        step *= 2
    other = swapped(own, sizes, {"tile": 1})
    return adjoint(
        own, other, own_lines, other_lines, pupil, grid_tables(), out_cols, out_table, n_src
    )


def solution(mesh):
    placed = (
        P(("grp", "tile"), None),
        P(("grp", "tile"), None),
        P(),
        P(),
        P(),
        P(("grp", "src"), None),
        P(("grp", "src")),
    )
    return jax.shard_map(
        body, mesh=mesh, in_specs=placed, out_specs=P(("grp", "tile"), "src", None), check_vma=False
    )
```

```python
import functools
import math

import jax
import jax.numpy as jnp
import ml_dtypes
import numpy as np
from jax import lax
from jax.experimental import pallas as pl
from jax.experimental.pallas import tpu as pltpu
from jax.sharding import PartitionSpec as P

COLS = 2048
TILE_ROWS = 2048
BAND = 128
PUPIL = 64
SLOTS = 8
GRID = 128
CHUNKS = (1,) * 8
GROUPS = (16, 20, 24, 32)
OX, OY, FACTOR, COUNT = range(4)
PARTS = 2
LANES = 128
SUMS = 2 * BAND + GRID
HALF = SUMS // 2
ZEROS = 8
GRANT = 53 * 1024 * 1024

VMEM = pl.BlockSpec(memory_space=pltpu.VMEM)
SMEM = pl.BlockSpec(memory_space=pltpu.SMEM)
HBM = pl.BlockSpec(memory_space=pltpu.HBM)


def waves(positions, freqs, length):
    product = np.multiply.outer(positions, freqs) % length
    angle = product.astype(np.float64) * (2.0 * math.pi / length)
    return np.cos(angle), np.sin(angle)


def lowpass(positions, length):
    freqs = np.arange(1, PUPIL)
    step = length // GRID
    apart = np.arange(GRID)[None, :] * step - positions[:, None]
    product = (apart[:, :, None] * freqs) % length
    return (1.0 + 2.0 * np.cos(product * (2.0 * math.pi / length)).sum(2)) / GRID


def low(array):
    return np.ascontiguousarray(array).astype(ml_dtypes.bfloat16)


@functools.cache
def image_tables(columns, height, n_tile, n_src):
    band = np.arange(BAND) - BAND // 2
    cols = np.arange(columns)
    rows = np.arange(TILE_ROWS)
    cos, sin = waves(cols, band, columns)
    col_table = low(np.concatenate([cos, -sin, lowpass(cols, columns)], 1))
    cos, sin = waves(rows, band, TILE_ROWS)
    row_table = np.concatenate([cos, sin, lowpass(rows, TILE_ROWS)], 1)
    row_table = low(row_table.reshape(n_tile, height, 2 * BAND + GRID).transpose(0, 2, 1))
    portion = height // n_src
    out_table = np.concatenate([cos, -sin], 1).astype(np.float32)
    out_table = out_table.reshape(n_tile * n_src, portion, 2 * BAND)
    cos, sin = waves(cols, band, columns)
    return col_table, row_table, out_table, low(np.concatenate([cos, -sin], 1).T)


COLS_IN, COLS_OUT = slice(0, 2 * BAND), slice(2 * BAND, 2 * BAND + 2 * GRID)
ROWS_IN = slice(COLS_OUT.stop, COLS_OUT.stop + GRID)
ROWS_OUT = slice(ROWS_IN.stop, ROWS_IN.stop + 2 * PUPIL)


@functools.cache
def grid_tables():
    points = np.arange(GRID)
    band = np.arange(BAND) - BAND // 2
    cos, sin = waves(points, band, GRID)
    cols_in = np.block([[cos.T, sin.T], [-sin.T, cos.T]])
    cols_out = np.block([[cos, -sin], [sin, cos]])
    cos, sin = waves(points, np.arange(PUPIL) - PUPIL // 2, GRID)
    rows_in = np.block([[cos, -sin, sin, cos]])
    rows_out = np.block([[cos.T, sin.T], [-sin.T, cos.T]])
    return low(np.concatenate([cols_in, cols_out, rows_in, rows_out], 0))


def dot(left, right):
    return jnp.dot(left, right, preferred_element_type=jnp.float32)


def forward_kernel(
    mask, cotangent, col_table, row_table,
    keep, send, zeros,
    halves, mask_v, cot_v, col_v, row_v, sems,
):
    columns = mask.shape[1]
    ends = np.cumsum(CHUNKS) * (columns // sum(CHUNKS))
    parts = [pl.ds(int(low), int(high - low)) for low, high in zip([0, *ends], ends)]
    tile = lax.axis_index("tile")
    chunk_copies = []
    for step, part in enumerate(parts):
        copies = [
            pltpu.make_async_copy(col_table.at[part, :], col_v.at[part, :], sems.at[step, 0]),
            pltpu.make_async_copy(mask.at[:, part], mask_v.at[:, part], sems.at[step, 1]),
            pltpu.make_async_copy(cotangent.at[:, part], cot_v.at[:, part], sems.at[step, 2]),
        ]
        for copy in copies:
            copy.start()
        chunk_copies.append(copies)
    row_copy = pltpu.make_async_copy(row_table.at[tile], row_v, sems.at[len(CHUNKS), 0])
    row_copy.start()

    for step, part in enumerate(parts):
        for copy in chunk_copies[step]:
            copy.wait()
        mask_add = dot(mask_v[:, part], col_v[part, : 2 * BAND])
        cot_add = dot(cot_v[:, part], col_v[part, 2 * BAND :])
        mask_part = mask_add if step == 0 else mask_part + mask_add
        cot_part = cot_add if step == 0 else cot_part + cot_add

    row_copy.wait()
    blocks = dot(row_v[: 2 * BAND, :], mask_part.astype(jnp.bfloat16))
    image = dot(row_v[2 * BAND :, :], cot_part.astype(jnp.bfloat16))
    sums = jnp.concatenate(
        [
            blocks[:BAND, :BAND] + blocks[BAND:, BAND:],
            blocks[:BAND, BAND:] - blocks[BAND:, :BAND],
            image,
        ],
        0,
    )
    rest = jnp.zeros((ZEROS, BAND), jnp.float32)
    for half in range(2):
        halves[half] = jnp.concatenate([sums[half * HALF : (half + 1) * HALF], rest], 0)
    own_half = tile % 2
    keep[...] = halves[own_half]
    send[...] = halves[1 - own_half]
    zeros[...] = jnp.zeros_like(zeros)


def forward(mask, cotangent, col_table, row_table):
    height, columns = mask.shape
    return pl.pallas_call(
        forward_kernel,
        out_shape=(
            jax.ShapeDtypeStruct((HALF + ZEROS, BAND), jnp.float32),
            jax.ShapeDtypeStruct((HALF + ZEROS, BAND), jnp.float32),
            jax.ShapeDtypeStruct((1, SLOTS + 1), jnp.int32),
        ),
        in_specs=[HBM] * 4,
        out_specs=(VMEM, VMEM, VMEM),
        scratch_shapes=[
            pltpu.VMEM((2, HALF + ZEROS, BAND), jnp.float32),
            pltpu.VMEM(mask.shape, jnp.bfloat16),
            pltpu.VMEM(mask.shape, jnp.bfloat16),
            pltpu.VMEM(col_table.shape, jnp.bfloat16),
            pltpu.VMEM(row_table.shape[1:], jnp.bfloat16),
            pltpu.SemaphoreType.DMA((len(CHUNKS) + 1, 3)),
        ],
        compiler_params=pltpu.CompilerParams(vmem_limit_bytes=GRANT),
        cost_estimate=pl.CostEstimate(
            flops=2 * height * columns * SUMS, bytes_accessed=6 * 1024 * 1024, transcendentals=0
        ),
        name="forward",
    )(mask, cotangent, col_table, row_table)


def lines_kernel(ids, shift, weight, lines):
    blocks = weight.shape[0]
    count = ids.shape[0] * SLOTS
    slot = lax.broadcasted_iota(jnp.int32, (SLOTS, SLOTS + 1), 0)
    column = lax.broadcasted_iota(jnp.int32, (SLOTS, SLOTS + 1), 1)
    sources, counts, used = [], [], []
    for row in range(ids.shape[0]):
        entries = jnp.broadcast_to(ids[row : row + 1, :].astype(jnp.float32), slot.shape)
        sources.append(jnp.sum(jnp.where(slot == column, entries, 0.0), 1, keepdims=True))
        counts.append(jnp.sum(jnp.where(column == SLOTS, entries, 0.0), 1, keepdims=True))
        used.append(jnp.where(slot[:, :1].astype(jnp.float32) < counts[-1], 1.0, 0.0))
    sources, counts, used = (jnp.concatenate(part, 0) for part in (sources, counts, used))
    block = jnp.floor(sources * (1.0 / LANES))

    def row_of(table, index, precision):
        lane = lax.broadcasted_iota(jnp.int32, (count, table.shape[0]), 1).astype(jnp.float32)
        pick = jnp.where(lane == index, 1.0, 0.0).astype(table.dtype)
        return jnp.dot(pick, table, precision=precision, preferred_element_type=jnp.float32)

    lane = lax.broadcasted_iota(jnp.int32, (count, LANES), 1)
    here = lane.astype(jnp.float32) == sources - block * LANES
    offsets = shift[...].astype(jnp.bfloat16)
    line = jnp.zeros((count, LANES), jnp.float32)
    for entry, found in (
        (OX, row_of(offsets, 2.0 * block, None)),
        (OY, row_of(offsets, 2.0 * block + 1.0, None)),
        (FACTOR, row_of(weight[...], block, lax.Precision.HIGHEST)),
    ):
        found = jnp.sum(jnp.where(here, found, 0.0), 1, keepdims=True) * used
        line = jnp.where(lane == entry, found, line)
    line = jnp.where(lane == FACTOR, line * (2.0 / SLOTS / PUPIL / PUPIL), line)
    lines[...] = jnp.where(lane == COUNT, counts, line)


def slot_lines(ids, shift, weight):
    count = ids.shape[0] * SLOTS
    return pl.pallas_call(
        lines_kernel,
        out_shape=jax.ShapeDtypeStruct((count, LANES), jnp.float32),
        in_specs=[VMEM, VMEM, VMEM],
        out_specs=VMEM,
        compiler_params=pltpu.CompilerParams(vmem_limit_bytes=2 * 1024 * 1024),
        cost_estimate=pl.CostEstimate(flops=1, bytes_accessed=1, transcendentals=0),
        name="slot_lines",
    )(ids, shift, weight)


def adjoint_kernel(
    n_src, own, other, own_lines, other_lines, pupil, table, col_table, out_table,
    result,
    spec_real, spec_imag, image, col_v, out_v, result_v, lines, used, sems, out_sems, *bands,
):
    place = lax.axis_index("tile") * n_src + lax.axis_index("src")
    out_copy = pltpu.make_async_copy(out_table.at[place], out_v, sems.at[0])
    col_copy = pltpu.make_async_copy(col_table, col_v, sems.at[1])
    half = own_lines.shape[0]
    for copy in (out_copy, col_copy):
        copy.start()

    scale = 1.0 / math.sqrt(TILE_ROWS * COLS)
    first = lax.axis_index("tile") % 2 == 0
    own_half, other_half = own[:HALF, :], other[:HALF, :]
    whole = jnp.concatenate(
        [jnp.where(first, own_half, other_half), jnp.where(first, other_half, own_half)], 0
    )
    spec = (whole[: 2 * BAND] * scale).astype(jnp.bfloat16).astype(jnp.float32)
    spec_real[...] = spec[:BAND]
    spec_imag[...] = spec[BAND:]
    image[:GRID, :] = whole[2 * BAND :]
    image[GRID:, :] = whole[2 * BAND :]
    for band in bands:
        band[...] = jnp.zeros_like(band)
    for slot in range(2 * half + GROUPS[-1]):
        used[slot] = jnp.int32(0)
    for part, source in enumerate((own_lines, other_lines)):
        for slot in range(half):
            line = source[slot : slot + 1, :]
            for entry in (OX, OY, FACTOR, COUNT) if slot % SLOTS == 0 else (OX, OY, FACTOR):
                lines[part * half + slot, entry] = line[0, entry]

    def add(block, total):
        first = block * SLOTS
        for slot in range(SLOTS):
            used[total + slot] = first + slot
        return total + lines[first, COUNT].astype(jnp.int32)

    blocks = 2 * half // SLOTS
    total = lax.fori_loop(0, blocks, add, jnp.int32(0), unroll=blocks <= 8)

    def group(first, size):
        starts, pupils, amplitudes = [], [], []
        for slot in range(size):
            place = first + slot
            index = used[place]
            factor = jnp.where(place < total, lines[index, FACTOR], 0.0)
            offset_x = lines[index, OX].astype(jnp.int32)
            offset_y = lines[index, OY].astype(jnp.int32)
            real = pltpu.roll(pupil[:PUPIL, :], offset_x, 1)
            imag = pltpu.roll(pupil[PUPIL:, :], offset_x, 1)
            rows = pl.ds(offset_y, PUPIL)
            amp_real = real * spec_real[rows, :] - imag * spec_imag[rows, :]
            amp_imag = real * spec_imag[rows, :] + imag * spec_real[rows, :]
            starts.append(offset_y)
            pupils.append((real, imag, factor))
            amplitudes.append(jnp.concatenate([amp_real, amp_imag], 1).astype(jnp.bfloat16))
        halfway = dot(jnp.concatenate(amplitudes, 0), table[COLS_IN, :]).astype(jnp.bfloat16)
        halfway = jnp.concatenate(
            [
                jnp.concatenate(
                    [
                        halfway[slot * PUPIL : (slot + 1) * PUPIL, :GRID],
                        halfway[slot * PUPIL : (slot + 1) * PUPIL, GRID:],
                    ],
                    0,
                )
                for slot in range(size)
            ],
            1,
        )
        rows_in = table[ROWS_IN, :]
        rows_in = jnp.concatenate([rows_in[:, : 2 * PUPIL], rows_in[:, 2 * PUPIL :]], 0)
        field = dot(rows_in, halfway)
        field_grad = jnp.concatenate(
            [
                (field[:, slot * GRID : (slot + 1) * GRID] * image[...]).astype(jnp.bfloat16)
                for slot in range(size)
            ],
            1,
        )
        back = dot(table[ROWS_OUT, :], field_grad).astype(jnp.bfloat16)
        back = jnp.concatenate(
            [
                jnp.concatenate(
                    [
                        back[:PUPIL, slot * GRID : (slot + 1) * GRID],
                        back[PUPIL:, slot * GRID : (slot + 1) * GRID],
                    ],
                    1,
                )
                for slot in range(size)
            ],
            0,
        )
        grad = dot(back, table[COLS_OUT, :])
        for slot in range(size):
            real, imag, factor = pupils[slot]
            grad_real = grad[slot * PUPIL : (slot + 1) * PUPIL, :BAND] * factor
            grad_imag = grad[slot * PUPIL : (slot + 1) * PUPIL, BAND:] * factor
            rows = pl.ds(starts[slot], PUPIL)
            band_real, band_imag = bands[slot % 2], bands[2 + slot % 2]
            band_real[rows, :] = band_real[rows, :] + (real * grad_real + imag * grad_imag)
            band_imag[rows, :] = band_imag[rows, :] + (real * grad_imag - imag * grad_real)

    largest, second = GROUPS[-1], GROUPS[-2]
    whole_groups = (total + largest - 1 - second) // largest

    def whole_group(step, carry):
        group(step * largest, largest)
        return carry

    lax.fori_loop(0, whole_groups, whole_group, jnp.int32(0))
    rest = total - whole_groups * largest
    for below, size in zip((0, *GROUPS), GROUPS[:-1]):

        @pl.when((rest > below) & (rest <= size))
        def _():
            group(whole_groups * largest, size)

    real = (bands[0][...] + bands[1][...]) * scale
    imag = (bands[2][...] + bands[3][...]) * scale
    left = jnp.concatenate(
        [jnp.concatenate([real, imag], 1), jnp.concatenate([imag, -real], 1)], 0
    ).astype(jnp.bfloat16)
    out_copy.wait()
    mixed = dot(out_v[...].astype(jnp.bfloat16), left).astype(jnp.bfloat16)
    col_copy.wait()
    width = result.shape[2] // PARTS
    copies = []
    for step in range(PARTS):
        part = pl.ds(step * width, width)
        result_v[:, part] = dot(mixed, col_v[:, part])
        copy = pltpu.make_async_copy(
            result_v.at[:, part], result.at[0, :, part], out_sems.at[step]
        )
        copy.start()
        copies.append(copy)
    for copy in copies:
        copy.wait()


def adjoint(own, other, own_lines, other_lines, pupil, table, col_table, out_table, n_src):
    portion = out_table.shape[1]
    columns = col_table.shape[1]
    band = pltpu.VMEM((BAND, BAND), jnp.float32)
    return pl.pallas_call(
        functools.partial(adjoint_kernel, n_src),
        out_shape=jax.ShapeDtypeStruct((1, portion, columns), jnp.float32),
        in_specs=[VMEM] * 6 + [HBM] * 2,
        out_specs=HBM,
        scratch_shapes=[
            band,
            band,
            pltpu.VMEM((2 * GRID, GRID), jnp.float32),
            pltpu.VMEM(col_table.shape, jnp.bfloat16),
            pltpu.VMEM(out_table.shape[1:], jnp.float32),
            pltpu.VMEM((portion, columns), jnp.float32),
            pltpu.SMEM((2 * own_lines.shape[0], LANES), jnp.float32),
            pltpu.SMEM((2 * own_lines.shape[0] + GROUPS[-1],), jnp.int32),
            pltpu.SemaphoreType.DMA((2,)),
            pltpu.SemaphoreType.DMA((PARTS,)),
            band,
            band,
            band,
            band,
        ],
        compiler_params=pltpu.CompilerParams(vmem_limit_bytes=GRANT),
        cost_estimate=pl.CostEstimate(
            flops=2 * 128 * 4096 * 256, bytes_accessed=4 * 1024 * 1024, transcendentals=0
        ),
        name="adjoint",
    )(own, other, own_lines, other_lines, pupil, table, col_table, out_table)


def pupil_rows(phase):
    grid = 2 * np.arange(PUPIL) - PUPIL + 1
    inside = grid[:, None] ** 2 + grid[None, :] ** 2 <= PUPIL * PUPIL
    both = jnp.concatenate(
        [jnp.where(inside, jnp.cos(phase), 0.0), jnp.where(inside, jnp.sin(phase), 0.0)], 0
    )
    return jnp.pad(both, ((0, 0), (0, BAND - PUPIL)))


def swapped(array, sizes, steps):
    axes = tuple(sizes)
    places = np.arange(math.prod(sizes.values())).reshape(tuple(sizes.values()))
    there = places
    for dim, axis in enumerate(axes):
        there = np.take(there, np.arange(sizes[axis]) ^ steps.get(axis, 0), dim)
    turn = [(int(a), int(b)) for a, b in zip(places.ravel(), there.ravel())]
    return lax.ppermute(array, axes, turn)


def body(mask, cotangent, pupil_phase, source_weight, shift_table, source_ids, source_count):
    height, columns = mask.shape
    n_tile, n_src = lax.axis_size("tile"), lax.axis_size("src")
    col_table, row_table, out_table, out_cols = image_tables(columns, height, n_tile, n_src)
    sizes = {"src": n_src, "tile": n_tile}
    keep, send, zeros = forward(mask, cotangent, col_table, row_table)
    ids = jnp.concatenate([source_ids, source_count[:, None]], 1) + zeros
    bit = 1
    while bit < n_src // 2:
        ids = jnp.concatenate([ids, swapped(ids, sizes, {"src": bit})], 0)
        bit *= 2
    own = keep + swapped(send, sizes, {"tile": 1})
    after = own[HALF : HALF + 1]
    ids = ids + after[:, : SLOTS + 1].astype(jnp.int32)
    shift = shift_table.T.reshape(2, -1, LANES).transpose(1, 0, 2).reshape(-1, LANES)
    own_lines = slot_lines(ids, shift, source_weight.reshape(-1, LANES))
    pupil = pupil_rows(pupil_phase + after[:, :PUPIL])
    other_lines = swapped(own_lines, sizes, {"src": bit})
    step = 2
    while step < n_tile:
        own = own + swapped(own, sizes, {"tile": step})
        step *= 2
    other = swapped(own, sizes, {"tile": 1})
    return adjoint(
        own, other, own_lines, other_lines, pupil, grid_tables(), out_cols, out_table, n_src
    )


def solution(mesh):
    placed = (
        P(("grp", "tile"), None),
        P(("grp", "tile"), None),
        P(),
        P(),
        P(),
        P(("grp", "src"), None),
        P(("grp", "src")),
    )
    return jax.shard_map(
        body, mesh=mesh, in_specs=placed, out_specs=P(("grp", "tile"), "src", None), check_vma=False
    )
```

```python
import functools
import math

import jax
import jax.numpy as jnp
import ml_dtypes
import numpy as np
from jax import lax
from jax.experimental import pallas as pl
from jax.experimental.pallas import tpu as pltpu
from jax.sharding import PartitionSpec as P

COLS = 2048
TILE_ROWS = 2048
BAND = 128
PUPIL = 64
SLOTS = 8
GRID = 128
CHUNKS = (1,) * 8
GROUPS = (16, 18, 20, 22, 24, 32)
OX, OY, FACTOR, COUNT = range(4)
PARTS = 4
LANES = 128
SUMS = 2 * BAND + GRID
HALF = SUMS // 2
ZEROS = 8
GRANT = 53 * 1024 * 1024

VMEM = pl.BlockSpec(memory_space=pltpu.VMEM)
SMEM = pl.BlockSpec(memory_space=pltpu.SMEM)
HBM = pl.BlockSpec(memory_space=pltpu.HBM)


def waves(positions, freqs, length):
    product = np.multiply.outer(positions, freqs) % length
    angle = product.astype(np.float64) * (2.0 * math.pi / length)
    return np.cos(angle), np.sin(angle)


def lowpass(positions, length):
    freqs = np.arange(1, PUPIL)
    step = length // GRID
    apart = np.arange(GRID)[None, :] * step - positions[:, None]
    product = (apart[:, :, None] * freqs) % length
    return (1.0 + 2.0 * np.cos(product * (2.0 * math.pi / length)).sum(2)) / GRID


def low(array):
    return np.ascontiguousarray(array).astype(ml_dtypes.bfloat16)


@functools.cache
def image_tables(columns, height, n_tile, n_src):
    band = np.arange(BAND) - BAND // 2
    cols = np.arange(columns)
    rows = np.arange(TILE_ROWS)
    cos, sin = waves(cols, band, columns)
    col_table = low(np.concatenate([cos, -sin, lowpass(cols, columns)], 1))
    cos, sin = waves(rows, band, TILE_ROWS)
    row_table = np.concatenate([cos, sin, lowpass(rows, TILE_ROWS)], 1)
    row_table = low(row_table.reshape(n_tile, height, 2 * BAND + GRID).transpose(0, 2, 1))
    portion = height // n_src
    out_table = np.concatenate([cos, -sin], 1).astype(np.float32)
    out_table = out_table.reshape(n_tile * n_src, portion, 2 * BAND)
    cos, sin = waves(cols, band, columns)
    return col_table, row_table, out_table, low(np.concatenate([cos, -sin], 1).T)


COLS_IN, COLS_OUT = slice(0, 2 * BAND), slice(2 * BAND, 2 * BAND + 2 * GRID)
ROWS_IN = slice(COLS_OUT.stop, COLS_OUT.stop + GRID)
ROWS_OUT = slice(ROWS_IN.stop, ROWS_IN.stop + 2 * PUPIL)


@functools.cache
def grid_tables():
    points = np.arange(GRID)
    band = np.arange(BAND) - BAND // 2
    cos, sin = waves(points, band, GRID)
    cols_in = np.block([[cos.T, sin.T], [-sin.T, cos.T]])
    cols_out = np.block([[cos, -sin], [sin, cos]])
    cos, sin = waves(points, np.arange(PUPIL) - PUPIL // 2, GRID)
    rows_in = np.block([[cos, -sin, sin, cos]])
    rows_out = np.block([[cos.T, sin.T], [-sin.T, cos.T]])
    return low(np.concatenate([cols_in, cols_out, rows_in, rows_out], 0))


def dot(left, right):
    return jnp.dot(left, right, preferred_element_type=jnp.float32)


def forward_kernel(
    mask, cotangent, col_table, row_table,
    keep, send, zeros,
    halves, mask_v, cot_v, col_v, row_v, sems,
):
    columns = mask.shape[1]
    ends = np.cumsum(CHUNKS) * (columns // sum(CHUNKS))
    parts = [pl.ds(int(low), int(high - low)) for low, high in zip([0, *ends], ends)]
    tile = lax.axis_index("tile")
    chunk_copies = []
    for step, part in enumerate(parts):
        copies = [
            pltpu.make_async_copy(col_table.at[part, :], col_v.at[part, :], sems.at[step, 0]),
            pltpu.make_async_copy(mask.at[:, part], mask_v.at[:, part], sems.at[step, 1]),
            pltpu.make_async_copy(cotangent.at[:, part], cot_v.at[:, part], sems.at[step, 2]),
        ]
        for copy in copies:
            copy.start()
        chunk_copies.append(copies)
    row_copy = pltpu.make_async_copy(row_table.at[tile], row_v, sems.at[len(CHUNKS), 0])
    row_copy.start()

    for step, part in enumerate(parts):
        for copy in chunk_copies[step]:
            copy.wait()
        mask_add = dot(mask_v[:, part], col_v[part, : 2 * BAND])
        cot_add = dot(cot_v[:, part], col_v[part, 2 * BAND :])
        mask_part = mask_add if step == 0 else mask_part + mask_add
        cot_part = cot_add if step == 0 else cot_part + cot_add

    row_copy.wait()
    blocks = dot(row_v[: 2 * BAND, :], mask_part.astype(jnp.bfloat16))
    image = dot(row_v[2 * BAND :, :], cot_part.astype(jnp.bfloat16))
    sums = jnp.concatenate(
        [
            blocks[:BAND, :BAND] + blocks[BAND:, BAND:],
            blocks[:BAND, BAND:] - blocks[BAND:, :BAND],
            image,
        ],
        0,
    )
    rest = jnp.zeros((ZEROS, BAND), jnp.float32)
    for half in range(2):
        halves[half] = jnp.concatenate([sums[half * HALF : (half + 1) * HALF], rest], 0)
    own_half = tile % 2
    keep[...] = halves[own_half]
    send[...] = halves[1 - own_half]
    zeros[...] = jnp.zeros_like(zeros)


def forward(mask, cotangent, col_table, row_table):
    height, columns = mask.shape
    return pl.pallas_call(
        forward_kernel,
        out_shape=(
            jax.ShapeDtypeStruct((HALF + ZEROS, BAND), jnp.float32),
            jax.ShapeDtypeStruct((HALF + ZEROS, BAND), jnp.float32),
            jax.ShapeDtypeStruct((1, SLOTS + 1), jnp.int32),
        ),
        in_specs=[HBM] * 4,
        out_specs=(VMEM, VMEM, VMEM),
        scratch_shapes=[
            pltpu.VMEM((2, HALF + ZEROS, BAND), jnp.float32),
            pltpu.VMEM(mask.shape, jnp.bfloat16),
            pltpu.VMEM(mask.shape, jnp.bfloat16),
            pltpu.VMEM(col_table.shape, jnp.bfloat16),
            pltpu.VMEM(row_table.shape[1:], jnp.bfloat16),
            pltpu.SemaphoreType.DMA((len(CHUNKS) + 1, 3)),
        ],
        compiler_params=pltpu.CompilerParams(vmem_limit_bytes=GRANT),
        cost_estimate=pl.CostEstimate(
            flops=2 * height * columns * SUMS, bytes_accessed=6 * 1024 * 1024, transcendentals=0
        ),
        name="forward",
    )(mask, cotangent, col_table, row_table)


def lines_kernel(ids, shift, weight, lines):
    blocks = weight.shape[0]
    count = ids.shape[0] * SLOTS
    slot = lax.broadcasted_iota(jnp.int32, (SLOTS, SLOTS + 1), 0)
    column = lax.broadcasted_iota(jnp.int32, (SLOTS, SLOTS + 1), 1)
    sources, counts, used = [], [], []
    for row in range(ids.shape[0]):
        entries = jnp.broadcast_to(ids[row : row + 1, :].astype(jnp.float32), slot.shape)
        sources.append(jnp.sum(jnp.where(slot == column, entries, 0.0), 1, keepdims=True))
        counts.append(jnp.sum(jnp.where(column == SLOTS, entries, 0.0), 1, keepdims=True))
        used.append(jnp.where(slot[:, :1].astype(jnp.float32) < counts[-1], 1.0, 0.0))
    sources, counts, used = (jnp.concatenate(part, 0) for part in (sources, counts, used))
    block = jnp.floor(sources * (1.0 / LANES))

    def row_of(table, index, precision):
        lane = lax.broadcasted_iota(jnp.int32, (count, table.shape[0]), 1).astype(jnp.float32)
        pick = jnp.where(lane == index, 1.0, 0.0).astype(table.dtype)
        return jnp.dot(pick, table, precision=precision, preferred_element_type=jnp.float32)

    lane = lax.broadcasted_iota(jnp.int32, (count, LANES), 1)
    here = lane.astype(jnp.float32) == sources - block * LANES
    offsets = shift[...].astype(jnp.bfloat16)
    line = jnp.zeros((count, LANES), jnp.float32)
    for entry, found in (
        (OX, row_of(offsets, 2.0 * block, None)),
        (OY, row_of(offsets, 2.0 * block + 1.0, None)),
        (FACTOR, row_of(weight[...], block, lax.Precision.HIGHEST)),
    ):
        found = jnp.sum(jnp.where(here, found, 0.0), 1, keepdims=True) * used
        line = jnp.where(lane == entry, found, line)
    line = jnp.where(lane == FACTOR, line * (2.0 / SLOTS / PUPIL / PUPIL), line)
    lines[...] = jnp.where(lane == COUNT, counts, line)


def slot_lines(ids, shift, weight):
    count = ids.shape[0] * SLOTS
    return pl.pallas_call(
        lines_kernel,
        out_shape=jax.ShapeDtypeStruct((count, LANES), jnp.float32),
        in_specs=[VMEM, VMEM, VMEM],
        out_specs=VMEM,
        compiler_params=pltpu.CompilerParams(vmem_limit_bytes=2 * 1024 * 1024),
        cost_estimate=pl.CostEstimate(flops=1, bytes_accessed=1, transcendentals=0),
        name="slot_lines",
    )(ids, shift, weight)


def adjoint_kernel(
    n_src, own, other, own_lines, other_lines, pupil, table, col_table, out_table,
    result,
    spec_real, spec_imag, image, col_v, out_v, result_v, lines, used, sems, out_sems, *bands,
):
    place = lax.axis_index("tile") * n_src + lax.axis_index("src")
    out_copy = pltpu.make_async_copy(out_table.at[place], out_v, sems.at[0])
    col_copy = pltpu.make_async_copy(col_table, col_v, sems.at[1])
    half = own_lines.shape[0]
    for copy in (out_copy, col_copy):
        copy.start()

    scale = 1.0 / math.sqrt(TILE_ROWS * COLS)
    first = lax.axis_index("tile") % 2 == 0
    own_half, other_half = own[:HALF, :], other[:HALF, :]
    whole = jnp.concatenate(
        [jnp.where(first, own_half, other_half), jnp.where(first, other_half, own_half)], 0
    )
    spec = (whole[: 2 * BAND] * scale).astype(jnp.bfloat16).astype(jnp.float32)
    spec_real[...] = spec[:BAND]
    spec_imag[...] = spec[BAND:]
    image[:GRID, :] = whole[2 * BAND :]
    image[GRID:, :] = whole[2 * BAND :]
    for band in bands:
        band[...] = jnp.zeros_like(band)
    for slot in range(2 * half + GROUPS[-1]):
        used[slot] = jnp.int32(0)
    for part, source in enumerate((own_lines, other_lines)):
        for slot in range(half):
            line = source[slot : slot + 1, :]
            for entry in (OX, OY, FACTOR, COUNT) if slot % SLOTS == 0 else (OX, OY, FACTOR):
                lines[part * half + slot, entry] = line[0, entry]

    def add(block, total):
        first = block * SLOTS
        for slot in range(SLOTS):
            used[total + slot] = first + slot
        return total + lines[first, COUNT].astype(jnp.int32)

    blocks = 2 * half // SLOTS
    total = lax.fori_loop(0, blocks, add, jnp.int32(0), unroll=blocks <= 8)

    def group(first, size):
        starts, pupils, amplitudes = [], [], []
        for slot in range(size):
            place = first + slot
            index = used[place]
            factor = jnp.where(place < total, lines[index, FACTOR], 0.0)
            offset_x = lines[index, OX].astype(jnp.int32)
            offset_y = lines[index, OY].astype(jnp.int32)
            real = pltpu.roll(pupil[:PUPIL, :], offset_x, 1)
            imag = pltpu.roll(pupil[PUPIL:, :], offset_x, 1)
            rows = pl.ds(offset_y, PUPIL)
            amp_real = real * spec_real[rows, :] - imag * spec_imag[rows, :]
            amp_imag = real * spec_imag[rows, :] + imag * spec_real[rows, :]
            starts.append(offset_y)
            pupils.append((real, imag, factor))
            amplitudes.append(jnp.concatenate([amp_real, amp_imag], 1).astype(jnp.bfloat16))
        halfway = dot(jnp.concatenate(amplitudes, 0), table[COLS_IN, :]).astype(jnp.bfloat16)
        halfway = jnp.concatenate(
            [
                jnp.concatenate(
                    [
                        halfway[slot * PUPIL : (slot + 1) * PUPIL, :GRID],
                        halfway[slot * PUPIL : (slot + 1) * PUPIL, GRID:],
                    ],
                    0,
                )
                for slot in range(size)
            ],
            1,
        )
        rows_in = table[ROWS_IN, :]
        rows_in = jnp.concatenate([rows_in[:, : 2 * PUPIL], rows_in[:, 2 * PUPIL :]], 0)
        field = dot(rows_in, halfway)
        field_grad = jnp.concatenate(
            [
                (field[:, slot * GRID : (slot + 1) * GRID] * image[...]).astype(jnp.bfloat16)
                for slot in range(size)
            ],
            1,
        )
        back = dot(table[ROWS_OUT, :], field_grad).astype(jnp.bfloat16)
        back = jnp.concatenate(
            [
                jnp.concatenate(
                    [
                        back[:PUPIL, slot * GRID : (slot + 1) * GRID],
                        back[PUPIL:, slot * GRID : (slot + 1) * GRID],
                    ],
                    1,
                )
                for slot in range(size)
            ],
            0,
        )
        grad = dot(back, table[COLS_OUT, :])
        for slot in range(size):
            real, imag, factor = pupils[slot]
            grad_real = grad[slot * PUPIL : (slot + 1) * PUPIL, :BAND] * factor
            grad_imag = grad[slot * PUPIL : (slot + 1) * PUPIL, BAND:] * factor
            rows = pl.ds(starts[slot], PUPIL)
            band_real, band_imag = bands[slot % 2], bands[2 + slot % 2]
            band_real[rows, :] = band_real[rows, :] + (real * grad_real + imag * grad_imag)
            band_imag[rows, :] = band_imag[rows, :] + (real * grad_imag - imag * grad_real)

    largest, second = GROUPS[-1], GROUPS[-2]
    whole_groups = (total + largest - 1 - second) // largest

    def whole_group(step, carry):
        group(step * largest, largest)
        return carry

    lax.fori_loop(0, whole_groups, whole_group, jnp.int32(0))
    rest = total - whole_groups * largest
    for below, size in zip((0, *GROUPS), GROUPS[:-1]):

        @pl.when((rest > below) & (rest <= size))
        def _():
            group(whole_groups * largest, size)

    real = (bands[0][...] + bands[1][...]) * scale
    imag = (bands[2][...] + bands[3][...]) * scale
    left = jnp.concatenate(
        [jnp.concatenate([real, imag], 1), jnp.concatenate([imag, -real], 1)], 0
    ).astype(jnp.bfloat16)
    out_copy.wait()
    mixed = dot(out_v[...].astype(jnp.bfloat16), left).astype(jnp.bfloat16)
    col_copy.wait()
    width = result.shape[2] // PARTS
    copies = []
    for step in range(PARTS):
        part = pl.ds(step * width, width)
        result_v[:, part] = dot(mixed, col_v[:, part])
        copy = pltpu.make_async_copy(
            result_v.at[:, part], result.at[0, :, part], out_sems.at[step]
        )
        copy.start()
        copies.append(copy)
    for copy in copies:
        copy.wait()


def adjoint(own, other, own_lines, other_lines, pupil, table, col_table, out_table, n_src):
    portion = out_table.shape[1]
    columns = col_table.shape[1]
    band = pltpu.VMEM((BAND, BAND), jnp.float32)
    return pl.pallas_call(
        functools.partial(adjoint_kernel, n_src),
        out_shape=jax.ShapeDtypeStruct((1, portion, columns), jnp.float32),
        in_specs=[VMEM] * 6 + [HBM] * 2,
        out_specs=HBM,
        scratch_shapes=[
            band,
            band,
            pltpu.VMEM((2 * GRID, GRID), jnp.float32),
            pltpu.VMEM(col_table.shape, jnp.bfloat16),
            pltpu.VMEM(out_table.shape[1:], jnp.float32),
            pltpu.VMEM((portion, columns), jnp.float32),
            pltpu.SMEM((2 * own_lines.shape[0], LANES), jnp.float32),
            pltpu.SMEM((2 * own_lines.shape[0] + GROUPS[-1],), jnp.int32),
            pltpu.SemaphoreType.DMA((2,)),
            pltpu.SemaphoreType.DMA((PARTS,)),
            band,
            band,
            band,
            band,
        ],
        compiler_params=pltpu.CompilerParams(vmem_limit_bytes=GRANT),
        cost_estimate=pl.CostEstimate(
            flops=2 * 128 * 4096 * 256, bytes_accessed=4 * 1024 * 1024, transcendentals=0
        ),
        name="adjoint",
    )(own, other, own_lines, other_lines, pupil, table, col_table, out_table)


def pupil_rows(phase):
    grid = 2 * np.arange(PUPIL) - PUPIL + 1
    inside = grid[:, None] ** 2 + grid[None, :] ** 2 <= PUPIL * PUPIL
    both = jnp.concatenate(
        [jnp.where(inside, jnp.cos(phase), 0.0), jnp.where(inside, jnp.sin(phase), 0.0)], 0
    )
    return jnp.pad(both, ((0, 0), (0, BAND - PUPIL)))


def swapped(array, sizes, steps):
    axes = tuple(sizes)
    places = np.arange(math.prod(sizes.values())).reshape(tuple(sizes.values()))
    there = places
    for dim, axis in enumerate(axes):
        there = np.take(there, np.arange(sizes[axis]) ^ steps.get(axis, 0), dim)
    turn = [(int(a), int(b)) for a, b in zip(places.ravel(), there.ravel())]
    return lax.ppermute(array, axes, turn)


def body(mask, cotangent, pupil_phase, source_weight, shift_table, source_ids, source_count):
    height, columns = mask.shape
    n_tile, n_src = lax.axis_size("tile"), lax.axis_size("src")
    col_table, row_table, out_table, out_cols = image_tables(columns, height, n_tile, n_src)
    sizes = {"src": n_src, "tile": n_tile}
    keep, send, zeros = forward(mask, cotangent, col_table, row_table)
    ids = jnp.concatenate([source_ids, source_count[:, None]], 1) + zeros
    bit = 1
    while bit < n_src // 2:
        ids = jnp.concatenate([ids, swapped(ids, sizes, {"src": bit})], 0)
        bit *= 2
    own = keep + swapped(send, sizes, {"tile": 1})
    after = own[HALF : HALF + 1]
    ids = ids + after[:, : SLOTS + 1].astype(jnp.int32)
    shift = shift_table.T.reshape(2, -1, LANES).transpose(1, 0, 2).reshape(-1, LANES)
    own_lines = slot_lines(ids, shift, source_weight.reshape(-1, LANES))
    pupil = pupil_rows(pupil_phase + after[:, :PUPIL])
    other_lines = swapped(own_lines, sizes, {"src": bit})
    step = 2
    while step < n_tile:
        own = own + swapped(own, sizes, {"tile": step})
        step *= 2
    other = swapped(own, sizes, {"tile": 1})
    return adjoint(
        own, other, own_lines, other_lines, pupil, grid_tables(), out_cols, out_table, n_src
    )


def solution(mesh):
    placed = (
        P(("grp", "tile"), None),
        P(("grp", "tile"), None),
        P(),
        P(),
        P(),
        P(("grp", "src"), None),
        P(("grp", "src")),
    )
    return jax.shard_map(
        body, mesh=mesh, in_specs=placed, out_specs=P(("grp", "tile"), "src", None), check_vma=False
    )
```
